32 devices in a mesh: slab: 8 (over z, y), pair: 4 (over x, core).
Axes of the slice: x: 2, y: 2, z: 4, core: 2. Of those that a mesh axis runs over, the one named last changes fastest.
Arguments:
- orbitals: bfloat16 [128, 32768], P('pair', 'slab'), may hold values from -6 to 6
- centers: int32 [128, 3], replicated, may hold values from 0 to 16
- matchings: int32 [8, 4, 16], P('slab'), may hold values from 0 to 15, as said below
Outputs:
- exchange_force: float32 [128, 32768], P('pair', 'slab')
The draws below stay inside these ranges and needn't reach their ends.
Inputs may be any that keep to these rules, and one draw needn't show every extreme that they name: `centers`: box corners relative to a common reference cell. `matchings`: entry [s, r, t] is the partner of member t of team s in round r; in each round every member has exactly one partner other than itself, and the partner's partner is the member.
All inputs are finite; a program needn't handle non-finite values.
Results may differ from the reference program's by a relative error of at most 0.0003.
Values may be sent and summed in bfloat16 or wider, within the bound.
No kernel may reach another device: no remote copies, remote signals or barrier semaphores. Data moves between devices by JAX's collectives and lax.ppermute only.
A program may use at most 128 MiB of HBM per device.

```python
import math
import jax
import jax.numpy as jnp
from jax import lax

ORB_DEV = 4
BOX = 32
ROUNDS = 4
STEPS = 16
SHIFT = 8
CUT2 = 192
CELLS = 32768
TEAMS = 8
TEAM = 16
NORB = 128
N_SLAB = 8
N_PAIR = 4


def draw_orbitals(key, part):
    key_list = jax.random.split(jax.random.fold_in(key, 29), 2)
    rough = jax.random.normal(key_list[0], (NORB, CELLS), jnp.float32)
    cell_index = jnp.arange(CELLS, dtype=jnp.int32)
    plane_coord = (cell_index // (BOX * BOX)).astype(jnp.float32)
    line_coord = (cell_index // BOX % BOX).astype(jnp.float32)
    point_coord = (cell_index % BOX).astype(jnp.float32)
    phases = jax.random.uniform(key_list[1], (NORB, 3), jnp.float32, 0.0, 2.0 * math.pi)
    angular = 2.0 * math.pi / BOX
    wave = jnp.cos(angular * plane_coord[None, :] + phases[:, 0:1])
    wave = wave + jnp.cos(angular * line_coord[None, :] + phases[:, 1:2])
    wave = (wave + jnp.cos(angular * point_coord[None, :] + phases[:, 2:3])) / 3.0
    values = 0.6 * (1.0 + 0.3 * wave) + 0.6 * rough
    return jnp.clip(values, -6.0, 6.0).astype(jnp.bfloat16)


def draw_matchings(key, part):
    key_list = jax.random.split(jax.random.fold_in(key, 17), TEAMS * ROUNDS)

    def build_matching(sub_key):
        ordering = jax.random.permutation(sub_key, TEAM).astype(jnp.int32)
        leading = ordering[0::2]
        second = ordering[1::2]
        partner = jnp.zeros((TEAM,), jnp.int32)
        partner = partner.at[leading].set(second)
        return partner.at[second].set(leading)
    return jax.vmap(build_matching)(key_list).reshape(TEAMS, ROUNDS, TEAM)


def plant(array, stream_key, low, largest):
    spot = [jax.random.randint(jax.random.fold_in(stream_key, axis), (), 0, length) for axis, length in enumerate(array.shape)]
    longest = array.shape.index(max(array.shape))
    next_to = spot[:longest] + [(spot[longest] + 1) % array.shape[longest]] + spot[longest + 1:]
    return array.at[tuple(spot)].set(low).at[tuple(next_to)].set(largest)


def setup_inputs(seed: int = 0) -> dict:
    splits = jax.random.split(jax.random.key(seed), 4)
    return {
        "orbitals": draw_orbitals(jax.random.fold_in(splits[3], 71), 0),
        "centers": plant(jax.random.randint(splits[1], (NORB, 3), 0, 2 * SHIFT + 1), jax.random.fold_in(splits[1], 1), 0, 2 * SHIFT).astype(jnp.int32),
        "matchings": draw_matchings(jax.random.fold_in(splits[3], 71), 0),
    }


SCREEN = 0.1
LOWER_BOUND = 0.1
UPPER_BOUND = 12.1


def cell_coords(box_side):
    cell_index = jnp.arange(box_side * box_side * box_side, dtype=jnp.int32)
    return cell_index // (box_side * box_side), (cell_index // box_side) % box_side, cell_index % box_side


def shift_table(offset_part, box_side):
    target = jnp.arange(box_side, dtype=jnp.int32)
    source = target[None, :, None] - offset_part.astype(jnp.int32)[:, None, None]
    return (source == target[None, None, :]).astype(jnp.float32)


def shift_rows(field, offset, box_side, shift_reach):
    row_count = field.shape[0]
    grid = field.astype(jnp.float32).reshape(row_count, box_side, box_side, box_side)
    best = lax.Precision.HIGHEST
    grid = jnp.einsum('rix,rxyz->riyz', shift_table(offset[:, 0], box_side), grid, precision=best)
    grid = jnp.einsum('riy,rxyz->rxiz', shift_table(offset[:, 1], box_side), grid, precision=best)
    grid = jnp.einsum('riz,rxyz->rxyi', shift_table(offset[:, 2], box_side), grid, precision=best)
    return grid.reshape(row_count, box_side * box_side * box_side)


def boundary_masks(box_side):
    plane_index, line_index, point_index = cell_coords(box_side)
    return jnp.stack([line_index > 0, line_index < box_side - 1, point_index > 0, point_index < box_side - 1]).astype(jnp.float32)


def apply_operator(field, box_side, masks):
    face_cells = box_side * box_side
    cell_count = field.shape[1]
    padded = jnp.pad(field, ((0, 0), (face_cells, face_cells)))

    def window(offset_cells):
        return padded[:, face_cells + offset_cells:face_cells + offset_cells + cell_count]

    neighbours = window(-face_cells) + window(face_cells)
    neighbours = neighbours + masks[0] * window(-box_side) + masks[1] * window(box_side)
    neighbours = neighbours + masks[2] * window(-1) + masks[3] * window(1)
    return (6.0 + SCREEN) * field - neighbours


def chebyshev_solve(source, box_side, sweeps):
    masks = boundary_masks(box_side)
    middle = (UPPER_BOUND + LOWER_BOUND) / 2.0
    spread = (UPPER_BOUND - LOWER_BOUND) / 2.0
    ratio = middle / spread

    def sweep(step, carry):
        solution, residual, direction, factor = carry
        solution = solution + direction
        residual = residual - apply_operator(direction, box_side, masks)
        factor_next = 1.0 / (2.0 * ratio - factor)
        direction = factor_next * factor * direction + (2.0 * factor_next / spread) * residual
        return solution, residual, direction, factor_next

    start = (jnp.zeros_like(source), source, source / middle, jnp.asarray(1.0 / ratio, source.dtype))
    return lax.fori_loop(0, sweeps, sweep, start)[0]


def pair_geometry(own_centers, partner_centers, cut_squared):
    anchor = (own_centers + partner_centers) // 2
    difference = own_centers - partner_centers
    active = (jnp.sum(difference * difference, axis=1) <= cut_squared).astype(jnp.float32)
    return own_centers - anchor, partner_centers - anchor, active


def pair_potential(own_rows, partner_rows, own_offset, partner_offset, active, box_side, shift_reach, sweeps):
    own_field = shift_rows(own_rows, own_offset, box_side, shift_reach)
    partner_field = shift_rows(partner_rows, partner_offset, box_side, shift_reach)
    density = active[:, None] * own_field * partner_field
    return chebyshev_solve(density, box_side, sweeps), own_field, partner_field


def team_forces(packed):
    team_rows, team_centers, team_matches = packed
    total = jnp.zeros(team_rows.shape, jnp.float32)
    for round_index in range(ROUNDS):
        partner = team_matches[round_index]
        own_offset, partner_offset, active = pair_geometry(team_centers, team_centers[partner], CUT2)
        potential, own_field, partner_field = pair_potential(team_rows, team_rows[partner], own_offset, partner_offset, active, BOX, SHIFT, STEPS)
        total = total + shift_rows(potential * partner_field, -own_offset, BOX, SHIFT)
    return total


def reference(orbitals, centers, matchings):
    team_rows = orbitals.reshape(N_PAIR, N_SLAB, ORB_DEV, CELLS).transpose(1, 0, 2, 3).reshape(TEAMS, TEAM, CELLS)
    team_centers = centers.reshape(N_PAIR, N_SLAB, ORB_DEV, 3).transpose(1, 0, 2, 3).reshape(TEAMS, TEAM, 3)
    forces = lax.map(team_forces, (team_rows, team_centers, matchings))
    return forces.reshape(N_SLAB, N_PAIR, ORB_DEV, CELLS).transpose(1, 0, 2, 3).reshape(NORB, CELLS)
```

```python
import functools
import math

import jax
import jax.numpy as jnp
import ml_dtypes
import numpy as np
from jax import lax
from jax.experimental import pallas as pl
from jax.experimental.pallas import tpu as pltpu
from jax.sharding import PartitionSpec as P

STEPS = 16
CUT2 = 192
REACH = 8
SCREEN = 0.1
LOWER_BOUND = 0.1
UPPER_BOUND = 12.1
LANES = 128
TILE_ROWS = 8


def split_constant(matrix):
    high = matrix.astype(ml_dtypes.bfloat16)
    low = (matrix - high.astype(np.float64)).astype(ml_dtypes.bfloat16)
    return high, low


def sine_basis(side):
    index = np.arange(1, side + 1, dtype=np.float64)
    return np.sqrt(2.0 / (side + 1)) * np.sin(np.pi * np.outer(index, index) / (side + 1))


def chebyshev_gain(side):
    shifts = -2.0 * np.cos(np.pi * np.arange(1, side + 1, dtype=np.float64) / (side + 1))
    eigenvalue = 6.0 + SCREEN + shifts[:, None, None] + shifts[None, :, None] + shifts[None, None, :]
    middle = (UPPER_BOUND + LOWER_BOUND) / 2.0
    spread = (UPPER_BOUND - LOWER_BOUND) / 2.0
    ratio = middle / spread
    total = np.zeros_like(eigenvalue)
    residual = np.ones_like(eigenvalue)
    direction = residual / middle
    factor = 1.0 / ratio
    for _ in range(STEPS):
        total = total + direction
        residual = residual - eigenvalue * direction
        factor_next = 1.0 / (2.0 * ratio - factor)
        direction = factor_next * factor * direction + 2.0 * factor_next / spread * residual
        factor = factor_next
    return total.reshape(side, side * side).astype(np.float32)


def split_pair(value):
    high = value.astype(jnp.bfloat16)
    low = (value - high.astype(jnp.float32)).astype(jnp.bfloat16)
    return high, low


def dot(left, right):
    return jnp.dot(left, right, preferred_element_type=jnp.float32)


def force_kernel(
    sizes,
    where_ref,
    match_ref,
    centers_ref,
    boxes_ref,
    mix_high_ref,
    mix_low_ref,
    gain_ref,
    basis_high_hbm,
    basis_low_hbm,
    out_ref,
    fields,
    partner,
    first_high,
    first_low,
    second_high,
    second_low,
    terms,
    total,
    basis_high,
    basis_low,
    sems,
):
    side, rounds, own_count, slab_count, pair_count = sizes
    planes = side // slab_count
    tiles = side * side // LANES
    lines = LANES // side
    pitch = side + 2 * REACH
    solves = own_count * rounds
    group = min(solves, 8)
    group_rows = group * side
    cells = tiles * LANES
    width = 2 * LANES

    high_copy = pltpu.make_async_copy(basis_high_hbm, basis_high, sems.at[0])
    low_copy = pltpu.make_async_copy(basis_low_hbm, basis_low, sems.at[1])
    high_copy.start()
    low_copy.start()

    zeros = jnp.zeros((REACH, LANES), jnp.float32)

    def clear(index, carry):
        fields[pl.ds(pl.multiple_of(index * pitch, 8), REACH), :] = zeros
        fields[pl.ds(pl.multiple_of(index * pitch + REACH + side, 8), REACH), :] = zeros
        return carry

    lax.fori_loop(0, pair_count * own_count * tiles, clear, 0, unroll=8)

    def clear_terms(index, carry):
        terms[pl.ds(pl.multiple_of(index * pitch, 8), REACH), :] = zeros
        terms[pl.ds(pl.multiple_of(index * pitch + REACH + side, 8), REACH), :] = zeros
        return carry

    lax.fori_loop(0, solves * tiles, clear_terms, 0, unroll=8)

    def unpack(index, carry):
        pair = index // slab_count
        slab = index % slab_count
        for chunk in range(own_count * planes // 2):
            block = boxes_ref[pair, slab, 16 * chunk : 16 * chunk + 16, :].astype(jnp.float32)
            for half in range(2):
                own, plane = divmod(2 * chunk + half, planes)
                start = (pair * own_count + own) * tiles * pitch + REACH + slab * planes + plane
                fields[pl.ds(start, tiles, stride=pitch), :] = block[8 * half : 8 * half + 8, :]
        return carry

    lax.fori_loop(0, pair_count * slab_count, unpack, 0)

    lane = lax.broadcasted_iota(jnp.int32, (side, LANES), 1)
    lane_row = lax.broadcasted_iota(jnp.int32, (1, LANES), 1)
    lane_line = lane_row // side
    lane_point = lane_row % side

    def rolled(ref, base, offset_x, offset_flat):
        whole = (offset_flat >> 7) & (tiles - 1)
        part = offset_flat & (LANES - 1)
        start = base * pitch + REACH - offset_x
        moved = []
        for tile in range(tiles):
            row = start + ((tile - whole) & (tiles - 1)) * pitch
            moved.append(pltpu.roll(ref[pl.ds(row, side), :], part, axis=1))
        keep = lane >= part
        return [jnp.where(keep, moved[t], moved[(t - 1) % tiles]) for t in range(tiles)]

    def geometry(index):
        own = index // rounds
        turn = index % rounds
        member = where_ref[0] * own_count + own
        mate = match_ref[turn, member]
        own_offset = []
        mate_offset = []
        distance = 0
        for axis in range(3):
            mine = centers_ref[member, axis]
            other = centers_ref[mate, axis]
            anchor = (mine + other) >> 1
            own_offset.append(mine - anchor)
            mate_offset.append(other - anchor)
            distance = distance + (mine - other) * (mine - other)
        return own, member, mate, own_offset, mate_offset, distance <= CUT2

    def densities(index, carry):
        own, member, mate, a, b, active = geometry(index)
        mine = rolled(fields, member * tiles, a[0], a[1] * side + a[2])
        other = rolled(fields, mate * tiles, b[0], b[1] * side + b[2])
        low_line = jnp.maximum(jnp.maximum(a[1], b[1]), 0)
        high_line = jnp.where(active, side + jnp.minimum(jnp.minimum(a[1], b[1]), 0), 0)
        low_point = jnp.maximum(jnp.maximum(a[2], b[2]), 0)
        high_point = side + jnp.minimum(jnp.minimum(a[2], b[2]), 0)
        point_ok = (lane_point >= low_point) & (lane_point < high_point)
        rows = pl.ds(pl.multiple_of(index * side, side), side)
        for tile in range(tiles):
            line = lane_line + tile * lines
            ok = jnp.where(point_ok & (line >= low_line) & (line < high_line), 1.0, 0.0)
            masked = other[tile] * ok
            columns = slice(tile * LANES, (tile + 1) * LANES)
            partner[rows, columns] = masked.astype(jnp.bfloat16)
            high, low = split_pair(mine[tile] * masked)
            first_high[rows, columns] = high
            first_low[rows, columns] = low
        return carry

    lax.fori_loop(0, solves, densities, 0)

    mix_high = mix_high_ref[...]
    mix_low = mix_low_ref[...]
    column_steps = cells // width
    group_steps = solves // group

    def block_of(index):
        rows = pl.ds(pl.multiple_of((index // column_steps) * group_rows, group_rows), group_rows)
        columns = pl.ds(pl.multiple_of((index % column_steps) * width, width), width)
        return rows, columns

    def along_x(index, carry):
        rows, columns = block_of(index)
        high = first_high[rows, columns]
        low = first_low[rows, columns]
        value = dot(mix_high, high) + (dot(mix_high, low) + dot(mix_low, high))
        second_high[rows, columns], second_low[rows, columns] = split_pair(value)
        return carry

    lax.fori_loop(0, group_steps * column_steps, along_x, 0)
    high_copy.wait()
    low_copy.wait()

    def in_plane(index, source_high, source_low):
        rows, columns = block_of(index)
        high = source_high[rows, :]
        low = source_low[rows, :]
        basis = basis_high[:, columns]
        return dot(high, basis) + (dot(low, basis) + dot(high, basis_low[:, columns]))

    def forward(index, carry):
        rows, columns = block_of(index)
        value = in_plane(index, second_high, second_low)
        gain = gain_ref[:, columns]
        value = (value.reshape(group, side, width) * gain[None]).reshape(group_rows, width)
        first_high[rows, columns], first_low[rows, columns] = split_pair(value)
        return carry

    lax.fori_loop(0, group_steps * column_steps, forward, 0)

    def backward(index, carry):
        rows, columns = block_of(index)
        value = in_plane(index, first_high, first_low)
        second_high[rows, columns], second_low[rows, columns] = split_pair(value)
        return carry

    lax.fori_loop(0, group_steps * column_steps, backward, 0)

    def back_along_x(index, carry):
        rows, columns = block_of(index)
        high = second_high[rows, columns]
        low = second_low[rows, columns]
        value = dot(mix_high, high) + (dot(mix_high, low) + dot(mix_low, high))
        value = value * partner[rows, columns].astype(jnp.float32)
        first_solve = (index // column_steps) * group
        first_tile = (index % column_steps) * 2
        for solve in range(group):
            for half in range(2):
                start = ((first_solve + solve) * tiles + first_tile + half) * pitch + REACH
                terms[pl.ds(pl.multiple_of(start, 8), side), :] = value[
                    solve * side : (solve + 1) * side, half * LANES : (half + 1) * LANES
                ]
        return carry

    lax.fori_loop(0, group_steps * column_steps, back_along_x, 0)

    def collect(own, carry):
        sums = None
        for turn in range(rounds):
            index = own * rounds + turn
            _, _, _, a, _, _ = geometry(index)
            term = rolled(terms, index * tiles, -a[0], -(a[1] * side + a[2]))
            sums = term if sums is None else [s + t for s, t in zip(sums, term)]
        for tile in range(tiles):
            start = (own * tiles + tile) * side
            total[pl.ds(pl.multiple_of(start, side), side), :] = sums[tile]
        return carry

    lax.fori_loop(0, own_count, collect, 0)

    def pack(slab, carry):
        for own in range(own_count):
            for plane in range(planes):
                start = own * tiles * side + slab * planes + plane
                row = (own * planes + plane) * tiles
                out_ref[slab, row : row + tiles, :] = total[pl.ds(start, tiles, stride=side), :]
        return carry

    lax.fori_loop(0, slab_count, pack, 0)


def team_forces(place, match, centers, boxes, side):
    rounds, team = match.shape
    pair_count, slab_count, rows, _ = boxes.shape
    own_count = team // pair_count
    tiles = side * side // LANES
    solves = own_count * rounds
    group = min(solves, 8)
    cells = side * side
    pitch = side + 2 * REACH
    basis = sine_basis(side)
    mix_high, mix_low = split_constant(np.kron(np.eye(group), basis))
    basis_high, basis_low = split_constant(np.kron(basis, basis))
    gain = chebyshev_gain(side)
    sizes = (side, rounds, own_count, slab_count, pair_count)
    scalars = pl.BlockSpec(memory_space=pltpu.SMEM)
    vectors = pl.BlockSpec(memory_space=pltpu.VMEM)
    wide = pltpu.VMEM((solves * side, cells), jnp.bfloat16)
    flops = 2 * solves * side * 3 * 2 * (cells * cells + cells * group * side)
    return pl.pallas_call(
        functools.partial(force_kernel, sizes),
        out_shape=jax.ShapeDtypeStruct((slab_count, rows, LANES), jnp.float32),
        in_specs=[scalars] * 3 + [vectors] * 4 + [pl.BlockSpec(memory_space=pl.ANY)] * 2,
        out_specs=vectors,
        scratch_shapes=[
            pltpu.VMEM((team * tiles * pitch, LANES), jnp.float32),
            wide,
            wide,
            wide,
            wide,
            wide,
            pltpu.VMEM((solves * tiles * pitch, LANES), jnp.float32),
            pltpu.VMEM((own_count * tiles * side, LANES), jnp.float32),
            pltpu.VMEM((cells, cells), jnp.bfloat16),
            pltpu.VMEM((cells, cells), jnp.bfloat16),
            pltpu.SemaphoreType.DMA((2,)),
        ],
        compiler_params=pltpu.CompilerParams(vmem_limit_bytes=40 * 1024 * 1024),
        cost_estimate=pl.CostEstimate(flops=flops, bytes_accessed=8 * 1024 * 1024, transcendentals=0),
    )(
        place,
        match,
        centers,
        boxes,
        jnp.asarray(mix_high),
        jnp.asarray(mix_low),
        jnp.asarray(gain),
        jnp.asarray(basis_high),
        jnp.asarray(basis_low),
    )


def shards(orbitals, centers, matchings):
    slab_count = lax.axis_size("slab")
    pair_count = lax.axis_size("pair")
    slab_index = lax.axis_index("slab")
    pair_index = lax.axis_index("pair")
    local_rows, plane_cells = orbitals.shape
    own_count = local_rows // slab_count
    side = round((plane_cells * slab_count) ** (1.0 / 3.0))
    match = matchings[0]
    team = match.shape[1]
    team_centers = lax.dynamic_index_in_dim(
        centers.reshape(pair_count, slab_count, own_count, 3), slab_index, 1, keepdims=False
    ).reshape(team, 3)
    place = pair_index.astype(jnp.int32).reshape(1)
    rows = own_count * plane_cells // LANES
    sent = orbitals.reshape(slab_count, rows, LANES)
    boxes = lax.all_to_all(sent, "slab", split_axis=0, concat_axis=0, tiled=True)
    gathered = lax.all_gather(boxes, "pair", axis=0, tiled=False)
    force = team_forces(place, match, team_centers, gathered, side)
    planes = lax.all_to_all(force, "slab", split_axis=0, concat_axis=0, tiled=True)
    return planes.reshape(local_rows, plane_cells)


def solution(mesh):
    in_specs = (P("pair", "slab"), P(), P("slab", None, None))
    out_specs = P("pair", "slab")
    return jax.shard_map(shards, mesh=mesh, in_specs=in_specs, out_specs=out_specs, check_vma=False)
```

```python
import functools

import jax
import jax.numpy as jnp
import ml_dtypes
import numpy as np
from jax import lax
from jax.experimental import pallas as pl
from jax.experimental.pallas import tpu as pltpu
from jax.sharding import PartitionSpec as P

STEPS = 16
CUT2 = 192
REACH = 8
SCREEN = 0.1
LOWER_BOUND = 0.1
UPPER_BOUND = 12.1
LANES = 128
CORES = 2


def split_constant(matrix):
    high = matrix.astype(ml_dtypes.bfloat16)
    low = (matrix - high.astype(np.float64)).astype(ml_dtypes.bfloat16)
    return high, low


def sine_basis(side):
    index = np.arange(1, side + 1, dtype=np.float64)
    return np.sqrt(2.0 / (side + 1)) * np.sin(np.pi * np.outer(index, index) / (side + 1))


def chebyshev_gain(side):
    shifts = -2.0 * np.cos(np.pi * np.arange(1, side + 1, dtype=np.float64) / (side + 1))
    eigenvalue = 6.0 + SCREEN + shifts[:, None, None] + shifts[None, :, None] + shifts[None, None, :]
    middle = (UPPER_BOUND + LOWER_BOUND) / 2.0
    spread = (UPPER_BOUND - LOWER_BOUND) / 2.0
    ratio = middle / spread
    total = np.zeros_like(eigenvalue)
    residual = np.ones_like(eigenvalue)
    direction = residual / middle
    factor = 1.0 / ratio
    for _ in range(STEPS):
        total = total + direction
        residual = residual - eigenvalue * direction
        factor_next = 1.0 / (2.0 * ratio - factor)
        direction = factor_next * factor * direction + 2.0 * factor_next / spread * residual
        factor = factor_next
    return total.reshape(side, side * side).astype(np.float32)


def split_pair(value):
    high = value.astype(jnp.bfloat16)
    low = (value - high.astype(jnp.float32)).astype(jnp.bfloat16)
    return high, low


def dot(left, right):
    return jnp.dot(left, right, preferred_element_type=jnp.float32)


def force_kernel(
    sizes,
    where_ref,
    match_ref,
    centers_ref,
    *refs,
):
    side, rounds, own_count, slab_count, pair_count = sizes
    block_count = slab_count * pair_count
    block_refs = refs[:block_count]
    constant_refs = refs[block_count : block_count + 5]
    out_refs = refs[block_count + 5 : block_count + 5 + slab_count]
    scratch = refs[block_count + 5 + slab_count :]
    force_body(sizes, where_ref, match_ref, centers_ref, block_refs, constant_refs, out_refs, *scratch)


def force_body(
    sizes,
    where_ref,
    match_ref,
    centers_ref,
    block_refs,
    constant_refs,
    out_refs,
    boxes_ref,
    mix_high_ref,
    mix_low_ref,
    gain_ref,
    fields,
    partner,
    first_high,
    first_low,
    second_high,
    second_low,
    terms,
    total,
    basis_high,
    basis_low,
    sems,
):
    side, rounds, own_count, slab_count, pair_count = sizes
    planes = side // slab_count
    tiles = side * side // LANES
    lines = LANES // side
    pitch = side + 2 * REACH
    solves = own_count * rounds
    group = min(solves, 8)
    group_rows = group * side
    cells = tiles * LANES
    width = 2 * LANES

    slab_index = where_ref[0]
    pair_index = where_ref[1]
    copies = []
    for index, (pair, slab) in enumerate(block_places(slab_index, pair_index, slab_count, pair_count)):
        copies.append(
            pltpu.make_async_copy(block_refs[index], boxes_ref.at[pair, slab], sems.at[index])
        )
    constants = (mix_high_ref, mix_low_ref, gain_ref, basis_high, basis_low)
    constant_copies = []
    for index, (source, target) in enumerate(zip(constant_refs, constants)):
        constant_copies.append(pltpu.make_async_copy(source, target, sems.at[len(copies) + index]))
    for copy in copies + constant_copies:
        copy.start()

    zeros = jnp.zeros((REACH, LANES), jnp.float32)

    def clear(index, carry):
        fields[pl.ds(pl.multiple_of(index * pitch, 8), REACH), :] = zeros
        fields[pl.ds(pl.multiple_of(index * pitch + REACH + side, 8), REACH), :] = zeros
        return carry

    lax.fori_loop(0, pair_count * own_count * tiles, clear, 0, unroll=8)

    def clear_terms(index, carry):
        terms[pl.ds(pl.multiple_of(index * pitch, 8), REACH), :] = zeros
        terms[pl.ds(pl.multiple_of(index * pitch + REACH + side, 8), REACH), :] = zeros
        return carry

    lax.fori_loop(0, solves * tiles, clear_terms, 0, unroll=8)

    for copy in copies:
        copy.wait()

    def unpack(index, carry):
        pair = index // slab_count
        slab = index % slab_count
        for chunk in range(own_count * planes // 2):
            block = boxes_ref[pair, slab, 16 * chunk : 16 * chunk + 16, :].astype(jnp.float32)
            for half in range(2):
                own, plane = divmod(2 * chunk + half, planes)
                start = (pair * own_count + own) * tiles * pitch + REACH + slab * planes + plane
                fields[pl.ds(start, tiles, stride=pitch), :] = block[8 * half : 8 * half + 8, :]
        return carry

    lax.fori_loop(0, pair_count * slab_count, unpack, 0)

    lane = lax.broadcasted_iota(jnp.int32, (side, LANES), 1)
    lane_row = lax.broadcasted_iota(jnp.int32, (1, LANES), 1)
    lane_line = lane_row // side
    lane_point = lane_row % side

    def rolled(ref, base, offset_x, offset_flat):
        whole = (offset_flat >> 7) & (tiles - 1)
        part = offset_flat & (LANES - 1)
        start = base * pitch + REACH - offset_x
        moved = []
        for tile in range(tiles):
            row = start + ((tile - whole) & (tiles - 1)) * pitch
            moved.append(pltpu.roll(ref[pl.ds(row, side), :], part, axis=1))
        keep = lane >= part
        return [jnp.where(keep, moved[t], moved[(t - 1) % tiles]) for t in range(tiles)]

    def geometry(index):
        own = index // rounds
        turn = index % rounds
        member = pair_index * own_count + own
        mate = match_ref[turn, member]
        own_offset = []
        mate_offset = []
        distance = 0
        for axis in range(3):
            mine = centers_ref[member, axis]
            other = centers_ref[mate, axis]
            anchor = (mine + other) >> 1
            own_offset.append(mine - anchor)
            mate_offset.append(other - anchor)
            distance = distance + (mine - other) * (mine - other)
        return own, member, mate, own_offset, mate_offset, distance <= CUT2

    def densities(index, carry):
        own, member, mate, a, b, active = geometry(index)
        mine = rolled(fields, member * tiles, a[0], a[1] * side + a[2])
        other = rolled(fields, mate * tiles, b[0], b[1] * side + b[2])
        low_line = jnp.maximum(jnp.maximum(a[1], b[1]), 0)
        high_line = jnp.where(active, side + jnp.minimum(jnp.minimum(a[1], b[1]), 0), 0)
        low_point = jnp.maximum(jnp.maximum(a[2], b[2]), 0)
        high_point = side + jnp.minimum(jnp.minimum(a[2], b[2]), 0)
        point_ok = (lane_point >= low_point) & (lane_point < high_point)
        rows = pl.ds(pl.multiple_of(index * side, side), side)
        for tile in range(tiles):
            line = lane_line + tile * lines
            ok = jnp.where(point_ok & (line >= low_line) & (line < high_line), 1.0, 0.0)
            masked = other[tile] * ok
            columns = slice(tile * LANES, (tile + 1) * LANES)
            partner[rows, columns] = masked.astype(jnp.bfloat16)
            high, low = split_pair(mine[tile] * masked)
            first_high[rows, columns] = high
            first_low[rows, columns] = low
        return carry

    lax.fori_loop(0, solves, densities, 0)

    for copy in constant_copies:
        copy.wait()
    mix_high = mix_high_ref[...]
    mix_low = mix_low_ref[...]
    column_steps = cells // width
    group_steps = solves // group

    def block_of(index):
        rows = pl.ds(pl.multiple_of((index // column_steps) * group_rows, group_rows), group_rows)
        columns = pl.ds(pl.multiple_of((index % column_steps) * width, width), width)
        return rows, columns

    def along_x(index, carry):
        rows, columns = block_of(index)
        high = first_high[rows, columns]
        low = first_low[rows, columns]
        value = dot(mix_high, high) + (dot(mix_high, low) + dot(mix_low, high))
        second_high[rows, columns], second_low[rows, columns] = split_pair(value)
        return carry

    lax.fori_loop(0, group_steps * column_steps, along_x, 0)

    def in_plane(index, source_high, source_low):
        rows, columns = block_of(index)
        high = source_high[rows, :]
        low = source_low[rows, :]
        basis = basis_high[:, columns]
        return dot(high, basis) + (dot(low, basis) + dot(high, basis_low[:, columns]))

    def forward(index, carry):
        rows, columns = block_of(index)
        value = in_plane(index, second_high, second_low)
        gain = gain_ref[:, columns]
        value = (value.reshape(group, side, width) * gain[None]).reshape(group_rows, width)
        first_high[rows, columns], first_low[rows, columns] = split_pair(value)
        return carry

    lax.fori_loop(0, group_steps * column_steps, forward, 0)

    def backward(index, carry):
        rows, columns = block_of(index)
        value = in_plane(index, first_high, first_low)
        second_high[rows, columns], second_low[rows, columns] = split_pair(value)
        return carry

    lax.fori_loop(0, group_steps * column_steps, backward, 0)

    def back_along_x(index, carry):
        rows, columns = block_of(index)
        high = second_high[rows, columns]
        low = second_low[rows, columns]
        value = dot(mix_high, high) + (dot(mix_high, low) + dot(mix_low, high))
        value = value * partner[rows, columns].astype(jnp.float32)
        first_solve = (index // column_steps) * group
        first_tile = (index % column_steps) * 2
        for solve in range(group):
            for half in range(2):
                start = ((first_solve + solve) * tiles + first_tile + half) * pitch + REACH
                terms[pl.ds(pl.multiple_of(start, 8), side), :] = value[
                    solve * side : (solve + 1) * side, half * LANES : (half + 1) * LANES
                ]
        return carry

    lax.fori_loop(0, group_steps * column_steps, back_along_x, 0)

    def collect(own, carry):
        sums = None
        for turn in range(rounds):
            index = own * rounds + turn
            _, _, _, a, _, _ = geometry(index)
            term = rolled(terms, index * tiles, -a[0], -(a[1] * side + a[2]))
            sums = term if sums is None else [s + t for s, t in zip(sums, term)]
        for tile in range(tiles):
            start = (own * tiles + tile) * side
            total[pl.ds(pl.multiple_of(start, side), side), :] = sums[tile]
        return carry

    lax.fori_loop(0, own_count, collect, 0)

    for step in range(slab_count):
        slab = (slab_index + step) % slab_count
        for own in range(own_count):
            for plane in range(planes):
                start = own * tiles * side + slab * planes + plane
                row = (own * planes + plane) * tiles
                out_refs[step][row : row + tiles, :] = total[pl.ds(start, tiles, stride=side), :]


def block_places(slab_index, pair_index, slab_count, pair_count):
    chips = pair_count // CORES
    chip = pair_index // CORES
    core = pair_index % CORES
    for core_step in range(CORES):
        for chip_step in range(chips):
            pair = (chip + chips - chip_step) % chips * CORES + (core + core_step) % CORES
            for step in range(slab_count):
                yield pair, (slab_index + slab_count - step) % slab_count


def gather_boxes(blocks, slab_count, pair_count):
    chips = pair_count // CORES
    own = [blocks[0]]
    for step in range(1, slab_count):
        perm = [(i, (i + step) % slab_count) for i in range(slab_count)]
        own.append(lax.ppermute(blocks[step], "slab", perm))
    pieces = [own]
    for step in range(1, chips):
        perm = [(i, (i + step * CORES) % pair_count) for i in range(pair_count)]
        pieces.append([lax.ppermute(block, "pair", perm) for block in own])
    swap = [(i, i ^ 1) for i in range(pair_count)]
    other = [[lax.ppermute(block, "pair", swap) for block in piece] for piece in pieces]
    return [block for piece in pieces + other for block in piece]


def pack_kernel(sizes, where_ref, orbitals_ref, *refs):
    own_count, slab_count = sizes
    out_refs, lines = refs[:slab_count], refs[slab_count]
    row_count, cells = orbitals_ref.shape
    tiles = cells // LANES
    for tile in range(tiles):
        columns = slice(tile * LANES, (tile + 1) * LANES)
        lines[tile * row_count : (tile + 1) * row_count, :] = orbitals_ref[:, columns].astype(jnp.float32)
    for step in range(slab_count):
        first = (where_ref[0] + step) % slab_count * own_count
        for chunk in range(own_count * tiles // 16):
            halves = []
            for half in range(2):
                own, tile = divmod(16 * chunk + 8 * half, tiles)
                halves.append(lines[pl.ds(tile * row_count + first + own, 8, stride=row_count), :])
            out_refs[step][16 * chunk : 16 * chunk + 16, :] = jnp.concatenate(halves, axis=0).astype(
                jnp.bfloat16
            )


def pack(place, orbitals, own_count, slab_count):
    row_count, cells = orbitals.shape
    rows = own_count * cells // LANES
    vectors = pl.BlockSpec(memory_space=pltpu.VMEM)
    return pl.pallas_call(
        functools.partial(pack_kernel, (own_count, slab_count)),
        out_shape=[jax.ShapeDtypeStruct((rows, LANES), jnp.bfloat16)] * slab_count,
        in_specs=[pl.BlockSpec(memory_space=pltpu.SMEM), vectors],
        out_specs=[vectors] * slab_count,
        scratch_shapes=[pltpu.VMEM((row_count * cells // LANES, LANES), jnp.float32)],
    )(place, orbitals)


def unpack_kernel(sizes, where_ref, *refs):
    own_count, slab_count = sizes
    block_refs, out_ref, lines = refs[:slab_count], refs[slab_count], refs[slab_count + 1]
    row_count, cells = out_ref.shape
    tiles = cells // LANES
    for step in range(slab_count):
        first = (where_ref[0] + slab_count - step) % slab_count * own_count
        for own in range(own_count):
            for tile in range(0, tiles, 8):
                start = tile * row_count + first + own
                row = own * tiles + tile
                lines[pl.ds(start, 8, stride=row_count), :] = block_refs[step][row : row + 8, :]
    for tile in range(tiles):
        columns = slice(tile * LANES, (tile + 1) * LANES)
        out_ref[:, columns] = lines[tile * row_count : (tile + 1) * row_count, :]


def unpack(place, blocks, own_count, cells):
    slab_count = len(blocks)
    row_count = own_count * slab_count
    vectors = pl.BlockSpec(memory_space=pltpu.VMEM)
    return pl.pallas_call(
        functools.partial(unpack_kernel, (own_count, slab_count)),
        out_shape=jax.ShapeDtypeStruct((row_count, cells), jnp.float32),
        in_specs=[pl.BlockSpec(memory_space=pltpu.SMEM)] + [vectors] * slab_count,
        out_specs=vectors,
        scratch_shapes=[pltpu.VMEM((row_count * cells // LANES, LANES), jnp.float32)],
    )(place, *blocks)


def team_forces(place, match, centers, blocks, side, slab_count, pair_count):
    rounds, team = match.shape
    rows = blocks[0].shape[0]
    own_count = team // pair_count
    tiles = side * side // LANES
    solves = own_count * rounds
    group = min(solves, 8)
    cells = side * side
    pitch = side + 2 * REACH
    basis = sine_basis(side)
    mix_high, mix_low = split_constant(np.kron(np.eye(group), basis))
    basis_high, basis_low = split_constant(np.kron(basis, basis))
    gain = chebyshev_gain(side)
    sizes = (side, rounds, own_count, slab_count, pair_count)
    scalars = pl.BlockSpec(memory_space=pltpu.SMEM)
    vectors = pl.BlockSpec(memory_space=pltpu.VMEM)
    wide = pltpu.VMEM((solves * side, cells), jnp.bfloat16)
    flops = 2 * solves * side * 3 * 2 * (cells * cells + cells * group * side)
    return pl.pallas_call(
        functools.partial(force_kernel, sizes),
        out_shape=[jax.ShapeDtypeStruct((rows, LANES), jnp.float32)] * slab_count,
        in_specs=[scalars] * 3 + [pl.BlockSpec(memory_space=pl.ANY)] * (len(blocks) + 5),
        out_specs=[vectors] * slab_count,
        scratch_shapes=[
            pltpu.VMEM((pair_count, slab_count, rows, LANES), jnp.bfloat16),
            pltpu.VMEM((group * side, group * side), jnp.bfloat16),
            pltpu.VMEM((group * side, group * side), jnp.bfloat16),
            pltpu.VMEM((side, cells), jnp.float32),
            pltpu.VMEM((team * tiles * pitch, LANES), jnp.float32),
            wide,
            wide,
            wide,
            wide,
            wide,
            pltpu.VMEM((solves * tiles * pitch, LANES), jnp.float32),
            pltpu.VMEM((own_count * tiles * side, LANES), jnp.float32),
            pltpu.VMEM((cells, cells), jnp.bfloat16),
            pltpu.VMEM((cells, cells), jnp.bfloat16),
            pltpu.SemaphoreType.DMA((len(blocks) + 5,)),
        ],
        compiler_params=pltpu.CompilerParams(vmem_limit_bytes=40 * 1024 * 1024),
        cost_estimate=pl.CostEstimate(flops=flops, bytes_accessed=8 * 1024 * 1024, transcendentals=0),
    )(
        place,
        match,
        centers,
        *blocks,
        jnp.asarray(mix_high),
        jnp.asarray(mix_low),
        jnp.asarray(gain),
        jnp.asarray(basis_high),
        jnp.asarray(basis_low),
    )


def shards(orbitals, centers, matchings):
    slab_count = lax.axis_size("slab")
    pair_count = lax.axis_size("pair")
    slab_index = lax.axis_index("slab")
    pair_index = lax.axis_index("pair")
    local_rows, plane_cells = orbitals.shape
    own_count = local_rows // slab_count
    side = round((plane_cells * slab_count) ** (1.0 / 3.0))
    match = matchings[0]
    team = match.shape[1]
    team_centers = lax.dynamic_index_in_dim(
        centers.reshape(pair_count, slab_count, own_count, 3), slab_index, 1, keepdims=False
    ).reshape(team, 3)
    place = jnp.stack([slab_index, pair_index]).astype(jnp.int32)
    blocks = pack(place, orbitals, own_count, slab_count)
    team_blocks = gather_boxes(blocks, slab_count, pair_count)
    forces = team_forces(place, match, team_centers, team_blocks, side, slab_count, pair_count)
    received = [forces[0]]
    for step in range(1, slab_count):
        perm = [(i, (i + step) % slab_count) for i in range(slab_count)]
        received.append(lax.ppermute(forces[step], "slab", perm))
    return unpack(place, received, own_count, plane_cells)


def solution(mesh):
    in_specs = (P("pair", "slab"), P(), P("slab", None, None))
    out_specs = P("pair", "slab")
    return jax.shard_map(shards, mesh=mesh, in_specs=in_specs, out_specs=out_specs, check_vma=False)
```

```python
import functools

import jax
import jax.numpy as jnp
import ml_dtypes
import numpy as np
from jax import lax
from jax.experimental import pallas as pl
from jax.experimental.pallas import tpu as pltpu
from jax.sharding import PartitionSpec as P

STEPS = 16
CUT2 = 192
REACH = 8
SCREEN = 0.1
LOWER_BOUND = 0.1
UPPER_BOUND = 12.1
LANES = 128
CORES = 2


def split_constant(matrix):
    high = matrix.astype(ml_dtypes.bfloat16)
    low = (matrix - high.astype(np.float64)).astype(ml_dtypes.bfloat16)
    return high, low


def sine_basis(side):
    index = np.arange(1, side + 1, dtype=np.float64)
    return np.sqrt(2.0 / (side + 1)) * np.sin(np.pi * np.outer(index, index) / (side + 1))


def chebyshev_gain(side):
    shifts = -2.0 * np.cos(np.pi * np.arange(1, side + 1, dtype=np.float64) / (side + 1))
    eigenvalue = 6.0 + SCREEN + shifts[:, None, None] + shifts[None, :, None] + shifts[None, None, :]
    middle = (UPPER_BOUND + LOWER_BOUND) / 2.0
    spread = (UPPER_BOUND - LOWER_BOUND) / 2.0
    ratio = middle / spread
    total = np.zeros_like(eigenvalue)
    residual = np.ones_like(eigenvalue)
    direction = residual / middle
    factor = 1.0 / ratio
    for _ in range(STEPS):
        total = total + direction
        residual = residual - eigenvalue * direction
        factor_next = 1.0 / (2.0 * ratio - factor)
        direction = factor_next * factor * direction + 2.0 * factor_next / spread * residual
        factor = factor_next
    return total.reshape(side, side * side).astype(np.float32)


def split_pair(value):
    high = value.astype(jnp.bfloat16)
    low = (value - high.astype(jnp.float32)).astype(jnp.bfloat16)
    return high, low


def dot(left, right):
    return jnp.dot(left, right, preferred_element_type=jnp.float32)


def partner_of(index, step, count):
    if count & (count - 1) == 0:
        return index ^ step, index ^ step
    return (index + step) % count, (index + count - step) % count


def slab_step(turn, core):
    return CORES * turn + CORES - 1 - core


def block_places(slab_index, pair_index, slab_count, pair_count):
    chips = pair_count // CORES
    chip = pair_index // CORES
    for core_step in range(CORES):
        core = (pair_index + core_step) % CORES
        for chip_step in range(chips):
            for turn in range(slab_count // CORES):
                step = slab_step(turn, core)
                yield (chip + chips - chip_step) % chips, partner_of(slab_index, step, slab_count)[1]


def force_kernel(sizes, match_ref, centers_ref, *refs):
    slab_count, pair_count = sizes[3:]
    block_count = slab_count * pair_count // CORES
    block_refs = refs[:block_count]
    constant_refs = refs[block_count : block_count + 5]
    out_refs = refs[block_count + 5 : block_count + 5 + slab_count]
    scratch = refs[block_count + 5 + slab_count :]
    force_body(sizes, match_ref, centers_ref, block_refs, constant_refs, out_refs, *scratch)


def force_body(
    sizes,
    match_hbm,
    centers_hbm,
    block_refs,
    constant_refs,
    out_refs,
    match_ref,
    centers_ref,
    boxes_ref,
    mix_high_ref,
    mix_low_ref,
    gain_ref,
    fields,
    partner,
    first_high,
    first_low,
    second_high,
    second_low,
    terms,
    total,
    basis_high,
    basis_low,
    sems,
):
    side, rounds, own_count, slab_count, pair_count = sizes
    planes = side // slab_count
    tiles = side * side // LANES
    lines = LANES // side
    pitch = side + 2 * REACH
    solves = own_count * rounds
    group = min(solves, 8)
    group_rows = group * side
    cells = tiles * LANES
    width = 2 * LANES
    slab_index = lax.axis_index("slab")
    pair_index = lax.axis_index("pair")

    targets = [boxes_ref.at[place] for place in block_places(slab_index, pair_index, slab_count, pair_count)]
    sources = list(block_refs) + [match_hbm, centers_hbm]
    targets += [match_ref, centers_ref]
    copies = []
    for source, target in zip(sources, targets):
        copies.append(pltpu.make_async_copy(source, target, sems.at[len(copies)]))
    constants = (mix_high_ref, mix_low_ref, gain_ref, basis_high, basis_low)
    constant_copies = []
    for index, (source, target) in enumerate(zip(constant_refs, constants)):
        constant_copies.append(pltpu.make_async_copy(source, target, sems.at[len(copies) + index]))
    for copy in copies + constant_copies:
        copy.start()

    zeros = jnp.zeros((REACH, LANES), jnp.float32)

    def clear(index, carry):
        fields[pl.ds(pl.multiple_of(index * pitch, 8), REACH), :] = zeros
        fields[pl.ds(pl.multiple_of(index * pitch + REACH + side, 8), REACH), :] = zeros
        return carry

    lax.fori_loop(0, pair_count * own_count * tiles, clear, 0, unroll=8)

    def clear_terms(index, carry):
        terms[pl.ds(pl.multiple_of(index * pitch, 8), REACH), :] = zeros
        terms[pl.ds(pl.multiple_of(index * pitch + REACH + side, 8), REACH), :] = zeros
        return carry

    lax.fori_loop(0, solves * tiles, clear_terms, 0, unroll=8)

    for copy in copies:
        copy.wait()

    def spread(index, carry):
        chip = index // slab_count
        slab = index % slab_count
        for chunk in range(CORES * own_count * planes // 2):
            block = boxes_ref[chip, slab, 16 * chunk : 16 * chunk + 16, :].astype(jnp.float32)
            for half in range(2):
                member, plane = divmod(2 * chunk + half, planes)
                start = (chip * CORES * own_count + member) * tiles * pitch + REACH + slab * planes + plane
                fields[pl.ds(start, tiles, stride=pitch), :] = block[8 * half : 8 * half + 8, :]
        return carry

    lax.fori_loop(0, pair_count // CORES * slab_count, spread, 0)

    lane = lax.broadcasted_iota(jnp.int32, (side, LANES), 1)
    lane_row = lax.broadcasted_iota(jnp.int32, (1, LANES), 1)
    lane_line = lane_row // side
    lane_point = lane_row % side

    def rolled(ref, base, offset_x, offset_flat):
        whole = (offset_flat >> 7) & (tiles - 1)
        part = offset_flat & (LANES - 1)
        start = base * pitch + REACH - offset_x
        moved = []
        for tile in range(tiles):
            row = start + ((tile - whole) & (tiles - 1)) * pitch
            moved.append(pltpu.roll(ref[pl.ds(row, side), :], part, axis=1))
        keep = lane >= part
        return [jnp.where(keep, moved[t], moved[(t - 1) % tiles]) for t in range(tiles)]

    def orbital_of(member):
        return (member // own_count * slab_count + slab_index) * own_count + member % own_count

    def geometry(index):
        own = index // rounds
        turn = index % rounds
        member = pair_index * own_count + own
        mate = match_ref[0, turn, member]
        own_offset = []
        mate_offset = []
        distance = 0
        for axis in range(3):
            mine = centers_ref[axis, orbital_of(member)]
            other = centers_ref[axis, orbital_of(mate)]
            anchor = (mine + other) >> 1
            own_offset.append(mine - anchor)
            mate_offset.append(other - anchor)
            distance = distance + (mine - other) * (mine - other)
        return own, member, mate, own_offset, mate_offset, distance <= CUT2

    def densities(index, carry):
        own, member, mate, a, b, active = geometry(index)
        mine = rolled(fields, member * tiles, a[0], a[1] * side + a[2])
        other = rolled(fields, mate * tiles, b[0], b[1] * side + b[2])
        low_line = jnp.maximum(jnp.maximum(a[1], b[1]), 0)
        high_line = jnp.where(active, side + jnp.minimum(jnp.minimum(a[1], b[1]), 0), 0)
        low_point = jnp.maximum(jnp.maximum(a[2], b[2]), 0)
        high_point = side + jnp.minimum(jnp.minimum(a[2], b[2]), 0)
        point_ok = (lane_point >= low_point) & (lane_point < high_point)
        rows = pl.ds(pl.multiple_of(index * side, side), side)
        for tile in range(tiles):
            line = lane_line + tile * lines
            ok = jnp.where(point_ok & (line >= low_line) & (line < high_line), 1.0, 0.0)
            masked = other[tile] * ok
            columns = slice(tile * LANES, (tile + 1) * LANES)
            partner[rows, columns] = masked.astype(jnp.bfloat16)
            high, low = split_pair(mine[tile] * masked)
            first_high[rows, columns] = high
            first_low[rows, columns] = low
        return carry

    lax.fori_loop(0, solves, densities, 0)

    for copy in constant_copies:
        copy.wait()
    mix_high = mix_high_ref[...]
    mix_low = mix_low_ref[...]
    column_steps = cells // width
    group_steps = solves // group

    def block_of(index):
        rows = pl.ds(pl.multiple_of((index // column_steps) * group_rows, group_rows), group_rows)
        columns = pl.ds(pl.multiple_of((index % column_steps) * width, width), width)
        return rows, columns

    def along_x(index, carry):
        rows, columns = block_of(index)
        high = first_high[rows, columns]
        low = first_low[rows, columns]
        value = dot(mix_high, high) + (dot(mix_high, low) + dot(mix_low, high))
        second_high[rows, columns], second_low[rows, columns] = split_pair(value)
        return carry

    lax.fori_loop(0, group_steps * column_steps, along_x, 0)

    def in_plane(index, source_high, source_low):
        rows, columns = block_of(index)
        high = source_high[rows, :]
        low = source_low[rows, :]
        basis = basis_high[:, columns]
        return dot(high, basis) + (dot(low, basis) + dot(high, basis_low[:, columns]))

    def forward(index, carry):
        rows, columns = block_of(index)
        value = in_plane(index, second_high, second_low)
        gain = gain_ref[:, columns]
        value = (value.reshape(group, side, width) * gain[None]).reshape(group_rows, width)
        first_high[rows, columns], first_low[rows, columns] = split_pair(value)
        return carry

    lax.fori_loop(0, group_steps * column_steps, forward, 0)

    def backward(index, carry):
        rows, columns = block_of(index)
        value = in_plane(index, first_high, first_low)
        second_high[rows, columns], second_low[rows, columns] = split_pair(value)
        return carry

    lax.fori_loop(0, group_steps * column_steps, backward, 0)

    def back_along_x(index, carry):
        rows, columns = block_of(index)
        high = second_high[rows, columns]
        low = second_low[rows, columns]
        value = dot(mix_high, high) + (dot(mix_high, low) + dot(mix_low, high))
        value = value * partner[rows, columns].astype(jnp.float32)
        first_solve = (index // column_steps) * group
        first_tile = (index % column_steps) * 2
        for solve in range(group):
            for half in range(2):
                start = ((first_solve + solve) * tiles + first_tile + half) * pitch + REACH
                terms[pl.ds(pl.multiple_of(start, 8), side), :] = value[
                    solve * side : (solve + 1) * side, half * LANES : (half + 1) * LANES
                ]
        return carry

    lax.fori_loop(0, group_steps * column_steps, back_along_x, 0)

    def collect(own, carry):
        sums = None
        for turn in range(rounds):
            index = own * rounds + turn
            _, _, _, a, _, _ = geometry(index)
            term = rolled(terms, index * tiles, -a[0], -(a[1] * side + a[2]))
            sums = term if sums is None else [s + t for s, t in zip(sums, term)]
        for tile in range(tiles):
            start = (own * tiles + tile) * side
            total[pl.ds(pl.multiple_of(start, side), side), :] = sums[tile]
        return carry

    lax.fori_loop(0, own_count, collect, 0)

    for step in range(slab_count):
        slab = partner_of(slab_index, step, slab_count)[0]
        for own in range(own_count):
            for plane in range(planes):
                start = own * tiles * side + slab * planes + plane
                row = (own * planes + plane) * tiles
                out_refs[step][row : row + tiles, :] = total[pl.ds(start, tiles, stride=side), :]


def gather_boxes(blocks, slab_count, pair_count):
    chips = pair_count // CORES
    own = []
    for turn, block in enumerate(blocks):
        perm = []
        for slab in range(slab_count):
            for pair in range(pair_count):
                target = partner_of(slab, slab_step(turn, pair % CORES), slab_count)[0]
                perm.append((slab * pair_count + pair, target * pair_count + pair))
        own.append((turn, lax.ppermute(block, ("slab", "pair"), perm)))
    pieces = [own]
    for step in range(1, chips):
        perm = [(i, (i + step * CORES) % pair_count) for i in range(pair_count)]
        pieces.append([(turn, lax.ppermute(block, "pair", perm)) for turn, block in own])
    other = [[(turn, swap_cores(block, pair_count)) for turn, block in piece] for piece in pieces]
    return [block for piece in pieces + other for _, block in sorted(piece, key=lambda item: item[0])]


def swap_cores(block, pair_count):
    return lax.ppermute(block, "pair", [(i, i ^ 1) for i in range(pair_count)])


def pack_kernel(sizes, *refs):
    own_count, slab_count = sizes
    orbital_refs, out_refs, lines = refs[:CORES], refs[CORES:-1], refs[-1]
    row_count, cells = orbital_refs[0].shape
    tiles = cells // LANES
    slab_index = lax.axis_index("slab")
    core = lax.axis_index("pair") % CORES
    for side in range(CORES):
        base = (core ^ side) * tiles * row_count
        for tile in range(tiles):
            columns = slice(tile * LANES, (tile + 1) * LANES)
            rows = pl.ds(pl.multiple_of(base + tile * row_count, 8), row_count)
            lines[rows, :] = orbital_refs[side][:, columns].astype(jnp.float32)
    for turn, out_ref in enumerate(out_refs):
        first = partner_of(slab_index, slab_step(turn, core), slab_count)[0] * own_count
        for chunk in range(CORES * own_count * tiles // 16):
            halves = []
            for half in range(2):
                member, tile = divmod(16 * chunk + 8 * half, tiles)
                side, own = divmod(member, own_count)
                start = (side * tiles + tile) * row_count + first + own
                halves.append(lines[pl.ds(start, 8, stride=row_count), :])
            block = jnp.concatenate(halves, axis=0).astype(jnp.bfloat16)
            out_ref[16 * chunk : 16 * chunk + 16, :] = block


def pack(orbitals, other, own_count, slab_count):
    row_count, cells = orbitals.shape
    rows = CORES * own_count * cells // LANES
    vectors = pl.BlockSpec(memory_space=pltpu.VMEM)
    turns = slab_count // CORES
    return pl.pallas_call(
        functools.partial(pack_kernel, (own_count, slab_count)),
        out_shape=[jax.ShapeDtypeStruct((rows, LANES), jnp.bfloat16)] * turns,
        in_specs=[vectors] * CORES,
        out_specs=[vectors] * turns,
        scratch_shapes=[pltpu.VMEM((CORES * row_count * cells // LANES, LANES), jnp.float32)],
    )(orbitals, other)


def unpack_kernel(sizes, *refs):
    own_count, slab_count = sizes
    block_refs, out_ref, blocks, lines, sems = refs[:slab_count], *refs[slab_count:]
    row_count, cells = out_ref.shape
    tiles = cells // LANES
    slab_index = lax.axis_index("slab")
    copies = []
    for step in range(slab_count):
        copies.append(pltpu.make_async_copy(block_refs[step], blocks.at[step], sems.at[step]))
        copies[-1].start()
    for step in range(slab_count):
        copies[step].wait()
        first = partner_of(slab_index, step, slab_count)[1] * own_count
        for own in range(own_count):
            for tile in range(0, tiles, 8):
                start = tile * row_count + first + own
                row = own * tiles + tile
                lines[pl.ds(start, 8, stride=row_count), :] = blocks[step, row : row + 8, :]
    for tile in range(tiles):
        columns = slice(tile * LANES, (tile + 1) * LANES)
        out_ref[:, columns] = lines[tile * row_count : (tile + 1) * row_count, :]


def unpack(blocks, own_count, cells):
    slab_count = len(blocks)
    row_count = own_count * slab_count
    return pl.pallas_call(
        functools.partial(unpack_kernel, (own_count, slab_count)),
        out_shape=jax.ShapeDtypeStruct((row_count, cells), jnp.float32),
        in_specs=[pl.BlockSpec(memory_space=pl.ANY)] * slab_count,
        out_specs=pl.BlockSpec(memory_space=pltpu.VMEM),
        scratch_shapes=[
            pltpu.VMEM((slab_count,) + blocks[0].shape, jnp.float32),
            pltpu.VMEM((row_count * cells // LANES, LANES), jnp.float32),
            pltpu.SemaphoreType.DMA((slab_count,)),
        ],
    )(*blocks)


def team_forces(match, centers, blocks, side, slab_count, pair_count):
    _, rounds, team = match.shape
    rows = blocks[0].shape[0] // CORES
    own_count = team // pair_count
    tiles = side * side // LANES
    solves = own_count * rounds
    group = min(solves, 8)
    cells = side * side
    pitch = side + 2 * REACH
    basis = sine_basis(side)
    mix_high, mix_low = split_constant(np.kron(np.eye(group), basis))
    basis_high, basis_low = split_constant(np.kron(basis, basis))
    gain = chebyshev_gain(side)
    sizes = (side, rounds, own_count, slab_count, pair_count)
    either = pl.BlockSpec(memory_space=pl.ANY)
    distant = pl.BlockSpec(memory_space=pltpu.HBM)
    vectors = pl.BlockSpec(memory_space=pltpu.VMEM)
    wide = pltpu.VMEM((solves * side, cells), jnp.bfloat16)
    flops = 2 * solves * side * 3 * 2 * (cells * cells + cells * group * side)
    return pl.pallas_call(
        functools.partial(force_kernel, sizes),
        out_shape=[jax.ShapeDtypeStruct((rows, LANES), jnp.float32)] * slab_count,
        in_specs=[distant] * 2 + [either] * len(blocks) + [distant] * 5,
        out_specs=[vectors] * slab_count,
        scratch_shapes=[
            pltpu.SMEM(match.shape, jnp.int32),
            pltpu.SMEM(centers.shape, jnp.int32),
            pltpu.VMEM((pair_count // CORES, slab_count, CORES * rows, LANES), jnp.bfloat16),
            pltpu.VMEM((group * side, group * side), jnp.bfloat16),
            pltpu.VMEM((group * side, group * side), jnp.bfloat16),
            pltpu.VMEM((side, cells), jnp.float32),
            pltpu.VMEM((team * tiles * pitch, LANES), jnp.float32),
            wide,
            wide,
            wide,
            wide,
            wide,
            pltpu.VMEM((solves * tiles * pitch, LANES), jnp.float32),
            pltpu.VMEM((own_count * tiles * side, LANES), jnp.float32),
            pltpu.VMEM((cells, cells), jnp.bfloat16),
            pltpu.VMEM((cells, cells), jnp.bfloat16),
            pltpu.SemaphoreType.DMA((len(blocks) + 7,)),
        ],
        compiler_params=pltpu.CompilerParams(vmem_limit_bytes=40 * 1024 * 1024),
        cost_estimate=pl.CostEstimate(flops=flops, bytes_accessed=8 * 1024 * 1024, transcendentals=0),
    )(
        match,
        centers,
        *blocks,
        jnp.asarray(mix_high),
        jnp.asarray(mix_low),
        jnp.asarray(gain),
        jnp.asarray(basis_high),
        jnp.asarray(basis_low),
    )


def shards(orbitals, centers, matchings):
    slab_count = lax.axis_size("slab")
    pair_count = lax.axis_size("pair")
    local_rows, plane_cells = orbitals.shape
    own_count = local_rows // slab_count
    side = round((plane_cells * slab_count) ** (1.0 / 3.0))
    other = swap_cores(orbitals, pair_count)
    blocks = pack(orbitals, other, own_count, slab_count)
    team_blocks = gather_boxes(blocks, slab_count, pair_count)
    forces = team_forces(matchings, centers.T, team_blocks, side, slab_count, pair_count)
    received = [forces[0]]
    for step in range(1, slab_count):
        perm = [(i, partner_of(i, step, slab_count)[0]) for i in range(slab_count)]
        received.append(lax.ppermute(forces[step], "slab", perm))
    return unpack(received, own_count, plane_cells)


def solution(mesh):
    in_specs = (P("pair", "slab"), P(), P("slab", None, None))
    out_specs = P("pair", "slab")
    return jax.shard_map(shards, mesh=mesh, in_specs=in_specs, out_specs=out_specs, check_vma=False)
```

```python
import functools

import jax
import jax.numpy as jnp
import ml_dtypes
import numpy as np
from jax import lax
from jax.experimental import pallas as pl
from jax.experimental.pallas import tpu as pltpu
from jax.sharding import PartitionSpec as P

STEPS = 16
CUT2 = 192
REACH = 8
SCREEN = 0.1
LOWER_BOUND = 0.1
UPPER_BOUND = 12.1
LANES = 128
CORES = 2


def split_constant(matrix):
    high = matrix.astype(ml_dtypes.bfloat16)
    low = (matrix - high.astype(np.float64)).astype(ml_dtypes.bfloat16)
    return high, low


def sine_basis(side):
    index = np.arange(1, side + 1, dtype=np.float64)
    return np.sqrt(2.0 / (side + 1)) * np.sin(np.pi * np.outer(index, index) / (side + 1))


def chebyshev_gain(side):
    shifts = -2.0 * np.cos(np.pi * np.arange(1, side + 1, dtype=np.float64) / (side + 1))
    eigenvalue = 6.0 + SCREEN + shifts[:, None, None] + shifts[None, :, None] + shifts[None, None, :]
    middle = (UPPER_BOUND + LOWER_BOUND) / 2.0
    spread = (UPPER_BOUND - LOWER_BOUND) / 2.0
    ratio = middle / spread
    total = np.zeros_like(eigenvalue)
    residual = np.ones_like(eigenvalue)
    direction = residual / middle
    factor = 1.0 / ratio
    for _ in range(STEPS):
        total = total + direction
        residual = residual - eigenvalue * direction
        factor_next = 1.0 / (2.0 * ratio - factor)
        direction = factor_next * factor * direction + 2.0 * factor_next / spread * residual
        factor = factor_next
    return total.reshape(side, side * side).astype(np.float32)


def split_pair(value):
    high = value.astype(jnp.bfloat16)
    low = (value - high.astype(jnp.float32)).astype(jnp.bfloat16)
    return high, low


def dot(left, right):
    return jnp.dot(left, right, preferred_element_type=jnp.float32)


def partner_of(index, step, count):
    if count & (count - 1) == 0:
        return index ^ step, index ^ step
    return (index + step) % count, (index + count - step) % count


def slab_step(turn, core):
    return CORES * turn + CORES - 1 - core


def block_places(slab_index, pair_index, slab_count, pair_count):
    chips = pair_count // CORES
    chip = pair_index // CORES
    for core_step in range(CORES):
        core = (pair_index + core_step) % CORES
        for chip_step in range(chips):
            for turn in range(slab_count // CORES):
                step = slab_step(turn, core)
                yield (chip + chips - chip_step) % chips, partner_of(slab_index, step, slab_count)[1]


def force_kernel(sizes, match_ref, centers_ref, *refs):
    slab_count, pair_count = sizes[3:]
    block_count = slab_count * pair_count // CORES
    block_refs = refs[:block_count]
    constant_refs = refs[block_count : block_count + 6]
    out_refs = refs[block_count + 6 : block_count + 6 + slab_count]
    scratch = refs[block_count + 6 + slab_count :]
    force_body(sizes, match_ref, centers_ref, block_refs, constant_refs, out_refs, *scratch)


def force_body(
    sizes,
    match_hbm,
    centers_hbm,
    block_refs,
    constant_refs,
    out_refs,
    match_ref,
    centers_ref,
    boxes_ref,
    mix_ref,
    gain_ref,
    there_high,
    there_low,
    back_high,
    back_low,
    fields,
    partner,
    first,
    second,
    terms,
    total,
    sems,
):
    side, rounds, own_count, slab_count, pair_count = sizes
    planes = side // slab_count
    tiles = side * side // LANES
    lines = LANES // side
    pitch = side + 2 * REACH
    solves = own_count * rounds
    group = min(solves, 8)
    group_rows = group * side
    cells = tiles * LANES
    width = 2 * LANES
    slab_index = lax.axis_index("slab")
    pair_index = lax.axis_index("pair")

    targets = [boxes_ref.at[place] for place in block_places(slab_index, pair_index, slab_count, pair_count)]
    sources = list(block_refs) + [match_hbm, centers_hbm]
    targets += [match_ref, centers_ref]
    copies = []
    for source, target in zip(sources, targets):
        copies.append(pltpu.make_async_copy(source, target, sems.at[len(copies)]))
    constants = (mix_ref, gain_ref, there_high, there_low, back_high, back_low)
    constant_copies = []
    for index, (source, target) in enumerate(zip(constant_refs, constants)):
        constant_copies.append(pltpu.make_async_copy(source, target, sems.at[len(copies) + index]))
    for copy in copies + constant_copies:
        copy.start()

    zeros = jnp.zeros((REACH, LANES), jnp.float32)

    def clear(index, carry):
        fields[pl.ds(pl.multiple_of(index * pitch, 8), REACH), :] = zeros
        fields[pl.ds(pl.multiple_of(index * pitch + REACH + side, 8), REACH), :] = zeros
        return carry

    lax.fori_loop(0, pair_count * own_count * tiles, clear, 0, unroll=8)

    def clear_terms(index, carry):
        terms[pl.ds(pl.multiple_of(index * pitch, 8), REACH), :] = zeros
        terms[pl.ds(pl.multiple_of(index * pitch + REACH + side, 8), REACH), :] = zeros
        return carry

    lax.fori_loop(0, solves * tiles, clear_terms, 0, unroll=8)

    for copy in copies:
        copy.wait()

    def spread(index, carry):
        chip = index // slab_count
        slab = index % slab_count
        for chunk in range(CORES * own_count * planes // 2):
            block = boxes_ref[chip, slab, 16 * chunk : 16 * chunk + 16, :].astype(jnp.float32)
            for half in range(2):
                member, plane = divmod(2 * chunk + half, planes)
                start = (chip * CORES * own_count + member) * tiles * pitch + REACH + slab * planes + plane
                fields[pl.ds(start, tiles, stride=pitch), :] = block[8 * half : 8 * half + 8, :]
        return carry

    lax.fori_loop(0, pair_count // CORES * slab_count, spread, 0)

    step_rows = 16
    lane = lax.broadcasted_iota(jnp.int32, (step_rows, LANES), 1)
    lane_row = lax.broadcasted_iota(jnp.int32, (1, LANES), 1)
    lane_line = lane_row // side
    lane_point = lane_row % side

    def rolled(ref, base, row, offset_x, offset_flat):
        whole = (offset_flat >> 7) & (tiles - 1)
        part = offset_flat & (LANES - 1)
        start = base * pitch + REACH + row - offset_x
        moved = []
        for tile in range(tiles):
            first_row = start + ((tile - whole) & (tiles - 1)) * pitch
            moved.append(pltpu.roll(ref[pl.ds(first_row, step_rows), :], part, axis=1))
        keep = lane >= part
        return [jnp.where(keep, moved[t], moved[(t - 1) % tiles]) for t in range(tiles)]

    def mirrored(tile):
        line = lax.broadcasted_iota(jnp.int32, tile.shape, 1) // side
        result = None
        for index in range(lines):
            amount = (2 * index - lines + 1) * side % LANES
            if index < 2:
                moved = pltpu.roll(tile, amount, axis=1)
                result = moved if result is None else jnp.where(line % 2 == index, moved, result)
        return result

    def orbital_of(member):
        return (member // own_count * slab_count + slab_index) * own_count + member % own_count

    def geometry(index):
        own = index // rounds
        turn = index % rounds
        member = pair_index * own_count + own
        mate = match_ref[0, turn, member]
        own_offset = []
        mate_offset = []
        distance = 0
        for axis in range(3):
            mine = centers_ref[axis, orbital_of(member)]
            other = centers_ref[axis, orbital_of(mate)]
            anchor = (mine + other) >> 1
            own_offset.append(mine - anchor)
            mate_offset.append(other - anchor)
            distance = distance + (mine - other) * (mine - other)
        return own, member, mate, own_offset, mate_offset, distance <= CUT2

    row_count = solves * side
    half_tiles = tiles // 2
    half_cells = cells // 2

    def store_split(ref, start, count, columns, value):
        high, low = split_pair(value)
        if isinstance(start, int):
            ref[start : start + count, columns] = high
            ref[row_count + start : row_count + start + count, columns] = low
        else:
            ref[pl.ds(pl.multiple_of(start, count), count), columns] = high
            ref[pl.ds(pl.multiple_of(row_count + start, count), count), columns] = low

    def densities(step, carry):
        index = step // (side // step_rows)
        row = step % (side // step_rows) * step_rows
        own, member, mate, a, b, active = geometry(index)
        mine = rolled(fields, member * tiles, row, a[0], a[1] * side + a[2])
        other = rolled(fields, mate * tiles, row, b[0], b[1] * side + b[2])
        low_line = jnp.maximum(jnp.maximum(a[1], b[1]), 0)
        high_line = jnp.where(active, side + jnp.minimum(jnp.minimum(a[1], b[1]), 0), 0)
        low_point = jnp.maximum(jnp.maximum(a[2], b[2]), 0)
        high_point = side + jnp.minimum(jnp.minimum(a[2], b[2]), 0)
        point_ok = (lane_point >= low_point) & (lane_point < high_point)
        start = step * step_rows
        rows = pl.ds(pl.multiple_of(start, step_rows), step_rows)
        density = []
        for tile in range(tiles):
            line = lane_line + tile * lines
            ok = jnp.where(point_ok & (line >= low_line) & (line < high_line), 1.0, 0.0)
            masked = other[tile] * ok
            partner[rows, tile * LANES : (tile + 1) * LANES] = masked.astype(jnp.bfloat16)
            density.append(mine[tile] * masked)
        for tile in range(half_tiles):
            mirror = mirrored(density[tiles - 1 - tile])
            for parity, value in enumerate((density[tile] + mirror, density[tile] - mirror)):
                column = parity * half_cells + tile * LANES
                store_split(first, start, step_rows, slice(column, column + LANES), value)
        return carry

    lax.fori_loop(0, solves * side // step_rows, densities, 0, unroll=2)

    for copy in constant_copies:
        copy.wait()

    def along_x(start, columns, source):
        high = source[start : start + group_rows, columns]
        low = source[row_count + start : row_count + start + group_rows, columns]
        value = dot(mix_ref[...], high)
        return value[:group_rows] + (value[group_rows:] + dot(mix_ref[:group_rows, :], low))

    def in_plane(parity, columns, source, high_ref, low_ref):
        inner = slice(parity * half_cells, (parity + 1) * half_cells)
        value = dot(source[:, inner], high_ref[parity, :, columns])
        rest = dot(source[:row_count, inner], low_ref[parity, :, columns])
        return value[:row_count] + (value[row_count:] + rest)

    for start in range(0, row_count, group_rows):
        for column in range(0, cells, width):
            columns = slice(column, column + width)
            store_split(second, start, group_rows, columns, along_x(start, columns, first))

    for parity in range(2):
        for column in range(0, half_cells, width):
            columns = slice(column, column + width)
            value = in_plane(parity, columns, second, there_high, there_low)
            columns = slice(parity * half_cells + column, parity * half_cells + column + width)
            gain = gain_ref[:, columns]
            value = (value.reshape(solves, side, width) * gain[None]).reshape(row_count, width)
            store_split(first, 0, row_count, columns, value)

    for parity in range(2):
        for column in range(0, half_cells, width):
            value = in_plane(parity, slice(column, column + width), first, back_high, back_low)
            columns = slice(parity * half_cells + column, parity * half_cells + column + width)
            store_split(second, 0, row_count, columns, value)

    for start in range(0, row_count, group_rows):
        for column in range(0, half_cells, width):
            even = along_x(start, slice(column, column + width), second)
            odd = along_x(start, slice(half_cells + column, half_cells + column + width), second)
            for part in range(width // LANES):
                tile = column // LANES + part
                lanes = slice(part * LANES, (part + 1) * LANES)
                near = even[:, lanes] + odd[:, lanes]
                far = mirrored(even[:, lanes] - odd[:, lanes])
                for place, value in ((tile, near), (tiles - 1 - tile, far)):
                    columns = slice(place * LANES, (place + 1) * LANES)
                    value = value * partner[start : start + group_rows, columns].astype(jnp.float32)
                    for solve in range(group):
                        row = ((start // side + solve) * tiles + place) * pitch + REACH
                        terms[row : row + side, :] = value[solve * side : (solve + 1) * side, :]

    def collect(step, carry):
        own = step // (side // step_rows)
        row = step % (side // step_rows) * step_rows
        sums = None
        for turn in range(rounds):
            index = own * rounds + turn
            _, _, _, a, _, _ = geometry(index)
            term = rolled(terms, index * tiles, row, -a[0], -(a[1] * side + a[2]))
            sums = term if sums is None else [s + t for s, t in zip(sums, term)]
        for tile in range(tiles):
            start = (own * tiles + tile) * side + row
            total[pl.ds(pl.multiple_of(start, step_rows), step_rows), :] = sums[tile]
        return carry

    lax.fori_loop(0, own_count * side // step_rows, collect, 0)

    for step in range(slab_count):
        slab = partner_of(slab_index, step, slab_count)[0]
        for own in range(own_count):
            for plane in range(planes):
                start = own * tiles * side + slab * planes + plane
                row = (own * planes + plane) * tiles
                out_refs[step][row : row + tiles, :] = total[pl.ds(start, tiles, stride=side), :]


def gather_boxes(blocks, slab_count, pair_count):
    chips = pair_count // CORES
    own = []
    for turn in reversed(range(len(blocks))):
        block = blocks[turn]
        perm = []
        for slab in range(slab_count):
            for pair in range(pair_count):
                target = partner_of(slab, slab_step(turn, pair % CORES), slab_count)[0]
                perm.append((slab * pair_count + pair, target * pair_count + pair))
        own.append((turn, lax.ppermute(block, ("slab", "pair"), perm)))
    pieces = [own]
    for step in range(1, chips):
        perm = [(i, (i + step * CORES) % pair_count) for i in range(pair_count)]
        pieces.append([(turn, lax.ppermute(block, "pair", perm)) for turn, block in own])
    other = [[(turn, swap_cores(block, pair_count)) for turn, block in piece] for piece in pieces]
    return [block for piece in pieces + other for _, block in sorted(piece, key=lambda item: item[0])]


def swap_cores(block, pair_count):
    return lax.ppermute(block, "pair", [(i, i ^ 1) for i in range(pair_count)])


def pack_kernel(sizes, *refs):
    own_count, slab_count = sizes
    orbital_refs, out_refs, lines = refs[:CORES], refs[CORES:-1], refs[-1]
    row_count, cells = orbital_refs[0].shape
    tiles = cells // LANES
    slab_index = lax.axis_index("slab")
    core = lax.axis_index("pair") % CORES
    for side in range(CORES):
        base = (core ^ side) * tiles * row_count
        for tile in range(tiles):
            columns = slice(tile * LANES, (tile + 1) * LANES)
            rows = pl.ds(pl.multiple_of(base + tile * row_count, 8), row_count)
            lines[rows, :] = orbital_refs[side][:, columns].astype(jnp.float32)
    for turn, out_ref in enumerate(out_refs):
        first = partner_of(slab_index, slab_step(turn, core), slab_count)[0] * own_count
        for chunk in range(CORES * own_count * tiles // 16):
            halves = []
            for half in range(2):
                member, tile = divmod(16 * chunk + 8 * half, tiles)
                side, own = divmod(member, own_count)
                start = (side * tiles + tile) * row_count + first + own
                halves.append(lines[pl.ds(start, 8, stride=row_count), :])
            block = jnp.concatenate(halves, axis=0).astype(jnp.bfloat16)
            out_ref[16 * chunk : 16 * chunk + 16, :] = block


def pack(orbitals, other, own_count, slab_count):
    row_count, cells = orbitals.shape
    rows = CORES * own_count * cells // LANES
    vectors = pl.BlockSpec(memory_space=pltpu.VMEM)
    turns = slab_count // CORES
    return pl.pallas_call(
        functools.partial(pack_kernel, (own_count, slab_count)),
        out_shape=[jax.ShapeDtypeStruct((rows, LANES), jnp.bfloat16)] * turns,
        in_specs=[vectors] * CORES,
        out_specs=[vectors] * turns,
        scratch_shapes=[pltpu.VMEM((CORES * row_count * cells // LANES, LANES), jnp.float32)],
    )(orbitals, other)


def unpack_kernel(sizes, *refs):
    own_count, slab_count = sizes
    block_refs, out_ref, blocks, lines, sems = refs[:slab_count], *refs[slab_count:]
    row_count, cells = out_ref.shape
    tiles = cells // LANES
    slab_index = lax.axis_index("slab")
    copies = []
    for step in range(slab_count):
        copies.append(pltpu.make_async_copy(block_refs[step], blocks.at[step], sems.at[step]))
        copies[-1].start()
    for step in range(slab_count):
        copies[step].wait()
        first = partner_of(slab_index, step, slab_count)[1] * own_count
        for own in range(own_count):
            for tile in range(0, tiles, 8):
                start = tile * row_count + first + own
                row = own * tiles + tile
                lines[pl.ds(start, 8, stride=row_count), :] = blocks[step, row : row + 8, :]
    for tile in range(tiles):
        columns = slice(tile * LANES, (tile + 1) * LANES)
        out_ref[:, columns] = lines[tile * row_count : (tile + 1) * row_count, :]


def unpack(blocks, own_count, cells):
    slab_count = len(blocks)
    row_count = own_count * slab_count
    return pl.pallas_call(
        functools.partial(unpack_kernel, (own_count, slab_count)),
        out_shape=jax.ShapeDtypeStruct((row_count, cells), jnp.float32),
        in_specs=[pl.BlockSpec(memory_space=pl.ANY)] * slab_count,
        out_specs=pl.BlockSpec(memory_space=pltpu.VMEM),
        scratch_shapes=[
            pltpu.VMEM((slab_count,) + blocks[0].shape, jnp.float32),
            pltpu.VMEM((row_count * cells // LANES, LANES), jnp.float32),
            pltpu.SemaphoreType.DMA((slab_count,)),
        ],
    )(*blocks)


def team_forces(match, centers, blocks, side, slab_count, pair_count):
    _, rounds, team = match.shape
    rows = blocks[0].shape[0] // CORES
    own_count = team // pair_count
    tiles = side * side // LANES
    solves = own_count * rounds
    group = min(solves, 8)
    cells = side * side
    pitch = side + 2 * REACH
    basis = sine_basis(side)
    mix = np.concatenate(split_constant(np.kron(np.eye(group), basis)), axis=0)
    there = np.stack([np.kron(basis[parity::2, : side // 2].T, basis) for parity in range(2)])
    gain = chebyshev_gain(side).reshape(side, side, side)
    gain = np.concatenate([gain[:, parity::2].reshape(side, -1) for parity in range(2)], axis=1)
    constants = (mix, gain, *split_constant(there), *split_constant(there.transpose(0, 2, 1)))
    sizes = (side, rounds, own_count, slab_count, pair_count)
    either = pl.BlockSpec(memory_space=pl.ANY)
    distant = pl.BlockSpec(memory_space=pltpu.HBM)
    vectors = pl.BlockSpec(memory_space=pltpu.VMEM)
    wide = pltpu.VMEM((2 * solves * side, cells), jnp.bfloat16)
    flops = 2 * solves * side * 3 * 2 * (cells * cells // 2 + cells * group * side)
    return pl.pallas_call(
        functools.partial(force_kernel, sizes),
        out_shape=[jax.ShapeDtypeStruct((rows, LANES), jnp.float32)] * slab_count,
        in_specs=[distant] * 2 + [either] * len(blocks) + [distant] * len(constants),
        out_specs=[vectors] * slab_count,
        scratch_shapes=[
            pltpu.SMEM(match.shape, jnp.int32),
            pltpu.SMEM(centers.shape, jnp.int32),
            pltpu.VMEM((pair_count // CORES, slab_count, CORES * rows, LANES), jnp.bfloat16),
            *[pltpu.VMEM(constant.shape, constant.dtype) for constant in constants],
            pltpu.VMEM((team * tiles * pitch, LANES), jnp.float32),
            pltpu.VMEM((solves * side, cells), jnp.bfloat16),
            wide,
            wide,
            pltpu.VMEM((solves * tiles * pitch, LANES), jnp.float32),
            pltpu.VMEM((own_count * tiles * side, LANES), jnp.float32),
            pltpu.SemaphoreType.DMA((len(blocks) + 2 + len(constants),)),
        ],
        compiler_params=pltpu.CompilerParams(vmem_limit_bytes=60 * 1024 * 1024),
        cost_estimate=pl.CostEstimate(flops=flops, bytes_accessed=8 * 1024 * 1024, transcendentals=0),
    )(
        match,
        centers,
        *blocks,
        *[jnp.asarray(constant) for constant in constants],
    )


def shards(orbitals, centers, matchings):
    slab_count = lax.axis_size("slab")
    pair_count = lax.axis_size("pair")
    local_rows, plane_cells = orbitals.shape
    own_count = local_rows // slab_count
    side = round((plane_cells * slab_count) ** (1.0 / 3.0))
    other = swap_cores(orbitals, pair_count)
    blocks = pack(orbitals, other, own_count, slab_count)
    team_blocks = gather_boxes(blocks, slab_count, pair_count)
    forces = team_forces(matchings, centers.T, team_blocks, side, slab_count, pair_count)
    received = [forces[0]]
    for step in reversed(range(1, slab_count)):
        perm = [(i, partner_of(i, step, slab_count)[0]) for i in range(slab_count)]
        received.insert(1, lax.ppermute(forces[step], "slab", perm))
    return unpack(received, own_count, plane_cells)


def solution(mesh):
    in_specs = (P("pair", "slab"), P(), P("slab", None, None))
    out_specs = P("pair", "slab")
    return jax.shard_map(shards, mesh=mesh, in_specs=in_specs, out_specs=out_specs, check_vma=False)
```

```python
import functools

import jax
import jax.numpy as jnp
import ml_dtypes
import numpy as np
from jax import lax
from jax.experimental import pallas as pl
from jax.experimental.pallas import tpu as pltpu
from jax.sharding import PartitionSpec as P

STEPS = 16
CUT2 = 192
REACH = 8
SCREEN = 0.1
LOWER_BOUND = 0.1
UPPER_BOUND = 12.1
LANES = 128
CORES = 2


def split_constant(matrix):
    high = matrix.astype(ml_dtypes.bfloat16)
    low = (matrix - high.astype(np.float64)).astype(ml_dtypes.bfloat16)
    return high, low


def sine_basis(side):
    index = np.arange(1, side + 1, dtype=np.float64)
    return np.sqrt(2.0 / (side + 1)) * np.sin(np.pi * np.outer(index, index) / (side + 1))


def chebyshev_gain(side):
    shifts = -2.0 * np.cos(np.pi * np.arange(1, side + 1, dtype=np.float64) / (side + 1))
    eigenvalue = 6.0 + SCREEN + shifts[:, None, None] + shifts[None, :, None] + shifts[None, None, :]
    middle = (UPPER_BOUND + LOWER_BOUND) / 2.0
    spread = (UPPER_BOUND - LOWER_BOUND) / 2.0
    ratio = middle / spread
    total = np.zeros_like(eigenvalue)
    residual = np.ones_like(eigenvalue)
    direction = residual / middle
    factor = 1.0 / ratio
    for _ in range(STEPS):
        total = total + direction
        residual = residual - eigenvalue * direction
        factor_next = 1.0 / (2.0 * ratio - factor)
        direction = factor_next * factor * direction + 2.0 * factor_next / spread * residual
        factor = factor_next
    return total.reshape(side, side * side).astype(np.float32)


def split_pair(value):
    high = value.astype(jnp.bfloat16)
    low = (value - high.astype(jnp.float32)).astype(jnp.bfloat16)
    return high, low


def dot(left, right):
    return jnp.dot(left, right, preferred_element_type=jnp.float32)


def partner_of(index, step, count):
    if count & (count - 1) == 0:
        return index ^ step, index ^ step
    return (index + step) % count, (index + count - step) % count


def slab_step(turn, core):
    return CORES * turn + CORES - 1 - core


def turn_groups(slab_count):
    turns = list(reversed(range(slab_count // CORES)))
    middle = (len(turns) + 1) // 2
    return [group for group in (turns[:middle], turns[middle:]) if group]


def block_places(slab_index, pair_index, slab_count, pair_count):
    chips = pair_count // CORES
    chip = pair_index // CORES
    for core_step in range(CORES):
        core = (pair_index + core_step) % CORES
        for chip_step in range(chips):
            source = (chip + chips - chip_step) % chips
            for turns in turn_groups(slab_count):
                steps = [slab_step(turn, core) for turn in turns]
                yield [(source, partner_of(slab_index, step, slab_count)[1]) for step in steps]


def force_kernel(sizes, match_ref, centers_ref, *refs):
    slab_count, pair_count = sizes[3:]
    block_count = len(turn_groups(slab_count)) * pair_count
    block_refs = refs[:block_count]
    constant_refs = refs[block_count : block_count + 6]
    out_refs = refs[block_count + 6 : block_count + 6 + slab_count]
    scratch = refs[block_count + 6 + slab_count :]
    force_body(sizes, match_ref, centers_ref, block_refs, constant_refs, out_refs, *scratch)


def force_body(
    sizes,
    match_hbm,
    centers_hbm,
    block_refs,
    constant_refs,
    out_refs,
    match_ref,
    centers_ref,
    boxes_ref,
    mix_ref,
    gain_ref,
    there_high,
    there_low,
    back_high,
    back_low,
    fields,
    partner,
    first,
    second,
    terms,
    total,
    sems,
):
    side, rounds, own_count, slab_count, pair_count = sizes
    planes = side // slab_count
    tiles = side * side // LANES
    lines = LANES // side
    pitch = side + 2 * REACH
    solves = own_count * rounds
    group = min(solves, 8)
    group_rows = group * side
    cells = tiles * LANES
    width = 2 * LANES
    slab_index = lax.axis_index("slab")
    pair_index = lax.axis_index("pair")

    sources = [match_hbm, centers_hbm]
    targets = [match_ref, centers_ref]
    block_rows = boxes_ref.shape[2]
    places = block_places(slab_index, pair_index, slab_count, pair_count)
    for block_ref, group_places in zip(block_refs, places):
        for index, place in enumerate(group_places):
            sources.append(block_ref.at[index * block_rows : (index + 1) * block_rows])
            targets.append(boxes_ref.at[place])
    copies = []
    for source, target in zip(sources, targets):
        copies.append(pltpu.make_async_copy(source, target, sems.at[len(copies)]))
    constants = (mix_ref, gain_ref, there_high, there_low, back_high, back_low)
    constant_copies = []
    for index, (source, target) in enumerate(zip(constant_refs, constants)):
        constant_copies.append(pltpu.make_async_copy(source, target, sems.at[len(copies) + index]))
    for copy in copies + constant_copies:
        copy.start()

    zeros = jnp.zeros((REACH, LANES), jnp.float32)

    def clear(index, carry):
        fields[pl.ds(pl.multiple_of(index * pitch, 8), REACH), :] = zeros
        fields[pl.ds(pl.multiple_of(index * pitch + REACH + side, 8), REACH), :] = zeros
        return carry

    lax.fori_loop(0, pair_count * own_count * tiles, clear, 0, unroll=8)

    def clear_terms(index, carry):
        terms[pl.ds(pl.multiple_of(index * pitch, 8), REACH), :] = zeros
        terms[pl.ds(pl.multiple_of(index * pitch + REACH + side, 8), REACH), :] = zeros
        return carry

    lax.fori_loop(0, solves * tiles, clear_terms, 0, unroll=8)

    for copy in copies:
        copy.wait()

    def spread(index, carry):
        chip = index // slab_count
        slab = index % slab_count
        for chunk in range(CORES * own_count * planes // 2):
            block = boxes_ref[chip, slab, 16 * chunk : 16 * chunk + 16, :].astype(jnp.float32)
            for half in range(2):
                member, plane = divmod(2 * chunk + half, planes)
                start = (chip * CORES * own_count + member) * tiles * pitch + REACH + slab * planes + plane
                fields[pl.ds(start, tiles, stride=pitch), :] = block[8 * half : 8 * half + 8, :]
        return carry

    lax.fori_loop(0, pair_count // CORES * slab_count, spread, 0)

    step_rows = 16
    lane = lax.broadcasted_iota(jnp.int32, (step_rows, LANES), 1)
    lane_row = lax.broadcasted_iota(jnp.int32, (1, LANES), 1)
    lane_line = lane_row // side
    lane_point = lane_row % side

    def rolled(ref, base, row, offset_x, offset_flat):
        whole = (offset_flat >> 7) & (tiles - 1)
        part = offset_flat & (LANES - 1)
        start = base * pitch + REACH + row - offset_x
        moved = []
        for tile in range(tiles):
            first_row = start + ((tile - whole) & (tiles - 1)) * pitch
            moved.append(pltpu.roll(ref[pl.ds(first_row, step_rows), :], part, axis=1))
        keep = lane >= part
        return [jnp.where(keep, moved[t], moved[(t - 1) % tiles]) for t in range(tiles)]

    def mirrored(tile):
        line = lax.broadcasted_iota(jnp.int32, tile.shape, 1) // side
        result = None
        for index in range(lines):
            amount = (2 * index - lines + 1) * side % LANES
            if index < 2:
                moved = pltpu.roll(tile, amount, axis=1)
                result = moved if result is None else jnp.where(line % 2 == index, moved, result)
        return result

    def orbital_of(member):
        return (member // own_count * slab_count + slab_index) * own_count + member % own_count

    def geometry(index):
        own = index // rounds
        turn = index % rounds
        member = pair_index * own_count + own
        mate = match_ref[0, turn, member]
        own_offset = []
        mate_offset = []
        distance = 0
        for axis in range(3):
            mine = centers_ref[axis, orbital_of(member)]
            other = centers_ref[axis, orbital_of(mate)]
            anchor = (mine + other) >> 1
            own_offset.append(mine - anchor)
            mate_offset.append(other - anchor)
            distance = distance + (mine - other) * (mine - other)
        return own, member, mate, own_offset, mate_offset, distance <= CUT2

    row_count = solves * side
    half_tiles = tiles // 2
    half_cells = cells // 2

    def store_split(ref, start, count, columns, value):
        high, low = split_pair(value)
        if isinstance(start, int):
            ref[start : start + count, columns] = high
            ref[row_count + start : row_count + start + count, columns] = low
        else:
            ref[pl.ds(pl.multiple_of(start, count), count), columns] = high
            ref[pl.ds(pl.multiple_of(row_count + start, count), count), columns] = low

    def densities(step, carry):
        index = step // (side // step_rows)
        row = step % (side // step_rows) * step_rows
        own, member, mate, a, b, active = geometry(index)
        mine = rolled(fields, member * tiles, row, a[0], a[1] * side + a[2])
        other = rolled(fields, mate * tiles, row, b[0], b[1] * side + b[2])
        low_line = jnp.maximum(jnp.maximum(a[1], b[1]), 0)
        high_line = jnp.where(active, side + jnp.minimum(jnp.minimum(a[1], b[1]), 0), 0)
        low_point = jnp.maximum(jnp.maximum(a[2], b[2]), 0)
        high_point = side + jnp.minimum(jnp.minimum(a[2], b[2]), 0)
        point_ok = (lane_point >= low_point) & (lane_point < high_point)
        start = step * step_rows
        rows = pl.ds(pl.multiple_of(start, step_rows), step_rows)
        density = []
        for tile in range(tiles):
            line = lane_line + tile * lines
            ok = jnp.where(point_ok & (line >= low_line) & (line < high_line), 1.0, 0.0)
            masked = other[tile] * ok
            partner[rows, tile * LANES : (tile + 1) * LANES] = masked.astype(jnp.bfloat16)
            density.append(mine[tile] * masked)
        for tile in range(half_tiles):
            mirror = mirrored(density[tiles - 1 - tile])
            for parity, value in enumerate((density[tile] + mirror, density[tile] - mirror)):
                column = parity * half_cells + tile * LANES
                store_split(first, start, step_rows, slice(column, column + LANES), value)
        return carry

    lax.fori_loop(0, solves * side // step_rows, densities, 0, unroll=2)

    for copy in constant_copies:
        copy.wait()

    def along_x(start, columns, source):
        high = source[start : start + group_rows, columns]
        low = source[row_count + start : row_count + start + group_rows, columns]
        value = dot(mix_ref[...], high)
        return value[:group_rows] + (value[group_rows:] + dot(mix_ref[:group_rows, :], low))

    def in_plane(parity, columns, source, high_ref, low_ref):
        inner = slice(parity * half_cells, (parity + 1) * half_cells)
        value = dot(source[:, inner], high_ref[parity, :, columns])
        rest = dot(source[:row_count, inner], low_ref[parity, :, columns])
        return value[:row_count] + (value[row_count:] + rest)

    for start in range(0, row_count, group_rows):
        for column in range(0, cells, width):
            columns = slice(column, column + width)
            store_split(second, start, group_rows, columns, along_x(start, columns, first))

    for parity in range(2):
        for column in range(0, half_cells, width):
            columns = slice(column, column + width)
            value = in_plane(parity, columns, second, there_high, there_low)
            columns = slice(parity * half_cells + column, parity * half_cells + column + width)
            gain = gain_ref[:, columns]
            value = (value.reshape(solves, side, width) * gain[None]).reshape(row_count, width)
            store_split(first, 0, row_count, columns, value)

    for parity in range(2):
        for column in range(0, half_cells, width):
            value = in_plane(parity, slice(column, column + width), first, back_high, back_low)
            columns = slice(parity * half_cells + column, parity * half_cells + column + width)
            store_split(second, 0, row_count, columns, value)

    for start in range(0, row_count, group_rows):
        for column in range(0, half_cells, width):
            even = along_x(start, slice(column, column + width), second)
            odd = along_x(start, slice(half_cells + column, half_cells + column + width), second)
            for part in range(width // LANES):
                tile = column // LANES + part
                lanes = slice(part * LANES, (part + 1) * LANES)
                near = even[:, lanes] + odd[:, lanes]
                far = mirrored(even[:, lanes] - odd[:, lanes])
                for place, value in ((tile, near), (tiles - 1 - tile, far)):
                    columns = slice(place * LANES, (place + 1) * LANES)
                    value = value * partner[start : start + group_rows, columns].astype(jnp.float32)
                    for solve in range(group):
                        row = ((start // side + solve) * tiles + place) * pitch + REACH
                        terms[row : row + side, :] = value[solve * side : (solve + 1) * side, :]

    def collect(step, carry):
        own = step // (side // step_rows)
        row = step % (side // step_rows) * step_rows
        sums = None
        for turn in range(rounds):
            index = own * rounds + turn
            _, _, _, a, _, _ = geometry(index)
            term = rolled(terms, index * tiles, row, -a[0], -(a[1] * side + a[2]))
            sums = term if sums is None else [s + t for s, t in zip(sums, term)]
        for tile in range(tiles):
            start = (own * tiles + tile) * side + row
            total[pl.ds(pl.multiple_of(start, step_rows), step_rows), :] = sums[tile]
        return carry

    lax.fori_loop(0, own_count * side // step_rows, collect, 0)

    for step in range(slab_count):
        slab = partner_of(slab_index, step, slab_count)[0]
        for own in range(own_count):
            for plane in range(planes):
                start = own * tiles * side + slab * planes + plane
                row = (own * planes + plane) * tiles
                out_refs[step][row : row + tiles, :] = total[pl.ds(start, tiles, stride=side), :]


def gather_boxes(blocks, slab_count, pair_count):
    chips = pair_count // CORES
    arrived = {}
    for turns in turn_groups(slab_count):
        for turn in turns:
            perm = []
            for slab in range(slab_count):
                for pair in range(pair_count):
                    target = partner_of(slab, slab_step(turn, pair % CORES), slab_count)[0]
                    perm.append((slab * pair_count + pair, target * pair_count + pair))
            arrived[turn] = lax.ppermute(blocks[turn], ("slab", "pair"), perm)
    own = [jnp.concatenate([arrived[t] for t in turns]) for turns in turn_groups(slab_count)]
    pieces = [own]
    for step in range(1, chips):
        perm = [(i, (i + step * CORES) % pair_count) for i in range(pair_count)]
        pieces.append([lax.ppermute(block, "pair", perm) for block in own])
    other = [[swap_cores(block, pair_count) for block in piece] for piece in pieces]
    return [block for piece in pieces + other for block in piece]


def swap_cores(block, pair_count):
    return lax.ppermute(block, "pair", [(i, i ^ 1) for i in range(pair_count)])


def pack_kernel(sizes, *refs):
    own_count, slab_count = sizes
    orbital_refs, out_refs, lines = refs[:CORES], refs[CORES:-1], refs[-1]
    row_count, cells = orbital_refs[0].shape
    tiles = cells // LANES
    slab_index = lax.axis_index("slab")
    core = lax.axis_index("pair") % CORES
    for side in range(CORES):
        base = (core ^ side) * tiles * row_count
        for tile in range(tiles):
            columns = slice(tile * LANES, (tile + 1) * LANES)
            rows = pl.ds(pl.multiple_of(base + tile * row_count, 8), row_count)
            lines[rows, :] = orbital_refs[side][:, columns].astype(jnp.float32)
    for turn, out_ref in enumerate(out_refs):
        first = partner_of(slab_index, slab_step(turn, core), slab_count)[0] * own_count
        for chunk in range(CORES * own_count * tiles // 16):
            halves = []
            for half in range(2):
                member, tile = divmod(16 * chunk + 8 * half, tiles)
                side, own = divmod(member, own_count)
                start = (side * tiles + tile) * row_count + first + own
                halves.append(lines[pl.ds(start, 8, stride=row_count), :])
            block = jnp.concatenate(halves, axis=0).astype(jnp.bfloat16)
            out_ref[16 * chunk : 16 * chunk + 16, :] = block


def pack(orbitals, other, own_count, slab_count):
    row_count, cells = orbitals.shape
    rows = CORES * own_count * cells // LANES
    vectors = pl.BlockSpec(memory_space=pltpu.VMEM)
    turns = slab_count // CORES
    return pl.pallas_call(
        functools.partial(pack_kernel, (own_count, slab_count)),
        out_shape=[jax.ShapeDtypeStruct((rows, LANES), jnp.bfloat16)] * turns,
        in_specs=[vectors] * CORES,
        out_specs=[vectors] * turns,
        scratch_shapes=[pltpu.VMEM((CORES * row_count * cells // LANES, LANES), jnp.float32)],
    )(orbitals, other)


def unpack_kernel(sizes, *refs):
    own_count, slab_count = sizes
    block_refs, out_ref, blocks, lines, sems = refs[:slab_count], *refs[slab_count:]
    row_count, cells = out_ref.shape
    tiles = cells // LANES
    slab_index = lax.axis_index("slab")
    copies = []
    for index in range(slab_count):
        copies.append(pltpu.make_async_copy(block_refs[index], blocks.at[index], sems.at[index]))
        copies[-1].start()
    for index in reversed(range(slab_count)):
        step = slab_count - 1 - index
        copies[index].wait()
        first = partner_of(slab_index, step, slab_count)[1] * own_count
        for own in range(own_count):
            for tile in range(0, tiles, 8):
                start = tile * row_count + first + own
                row = own * tiles + tile
                lines[pl.ds(start, 8, stride=row_count), :] = blocks[index, row : row + 8, :]
    for tile in range(tiles):
        columns = slice(tile * LANES, (tile + 1) * LANES)
        out_ref[:, columns] = lines[tile * row_count : (tile + 1) * row_count, :]


def unpack(blocks, own_count, cells):
    slab_count = len(blocks)
    row_count = own_count * slab_count
    return pl.pallas_call(
        functools.partial(unpack_kernel, (own_count, slab_count)),
        out_shape=jax.ShapeDtypeStruct((row_count, cells), jnp.float32),
        in_specs=[pl.BlockSpec(memory_space=pl.ANY)] * slab_count,
        out_specs=pl.BlockSpec(memory_space=pltpu.VMEM),
        scratch_shapes=[
            pltpu.VMEM((slab_count,) + blocks[0].shape, jnp.float32),
            pltpu.VMEM((row_count * cells // LANES, LANES), jnp.float32),
            pltpu.SemaphoreType.DMA((slab_count,)),
        ],
    )(*blocks)


def team_forces(match, centers, blocks, side, slab_count, pair_count):
    _, rounds, team = match.shape
    own_count = team // pair_count
    rows = own_count * side * side // LANES * (side // slab_count)
    block_count = slab_count * pair_count // CORES
    tiles = side * side // LANES
    solves = own_count * rounds
    group = min(solves, 8)
    cells = side * side
    pitch = side + 2 * REACH
    basis = sine_basis(side)
    mix = np.concatenate(split_constant(np.kron(np.eye(group), basis)), axis=0)
    there = np.stack([np.kron(basis[parity::2, : side // 2].T, basis) for parity in range(2)])
    gain = chebyshev_gain(side).reshape(side, side, side)
    gain = np.concatenate([gain[:, parity::2].reshape(side, -1) for parity in range(2)], axis=1)
    constants = (mix, gain, *split_constant(there), *split_constant(there.transpose(0, 2, 1)))
    sizes = (side, rounds, own_count, slab_count, pair_count)
    either = pl.BlockSpec(memory_space=pl.ANY)
    distant = pl.BlockSpec(memory_space=pltpu.HBM)
    vectors = pl.BlockSpec(memory_space=pltpu.VMEM)
    wide = pltpu.VMEM((2 * solves * side, cells), jnp.bfloat16)
    flops = 2 * solves * side * 3 * 2 * (cells * cells // 2 + cells * group * side)
    return pl.pallas_call(
        functools.partial(force_kernel, sizes),
        out_shape=[jax.ShapeDtypeStruct((rows, LANES), jnp.float32)] * slab_count,
        in_specs=[distant] * 2 + [either] * len(blocks) + [distant] * len(constants),
        out_specs=[vectors] * slab_count,
        scratch_shapes=[
            pltpu.SMEM(match.shape, jnp.int32),
            pltpu.SMEM(centers.shape, jnp.int32),
            pltpu.VMEM((pair_count // CORES, slab_count, CORES * rows, LANES), jnp.bfloat16),
            *[pltpu.VMEM(constant.shape, constant.dtype) for constant in constants],
            pltpu.VMEM((team * tiles * pitch, LANES), jnp.float32),
            pltpu.VMEM((solves * side, cells), jnp.bfloat16),
            wide,
            wide,
            pltpu.VMEM((solves * tiles * pitch, LANES), jnp.float32),
            pltpu.VMEM((own_count * tiles * side, LANES), jnp.float32),
            pltpu.SemaphoreType.DMA((block_count + 2 + len(constants),)),
        ],
        compiler_params=pltpu.CompilerParams(vmem_limit_bytes=60 * 1024 * 1024),
        cost_estimate=pl.CostEstimate(flops=flops, bytes_accessed=8 * 1024 * 1024, transcendentals=0),
    )(
        match,
        centers,
        *blocks,
        *[jnp.asarray(constant) for constant in constants],
    )


def shards(orbitals, centers, matchings):
    slab_count = lax.axis_size("slab")
    pair_count = lax.axis_size("pair")
    local_rows, plane_cells = orbitals.shape
    own_count = local_rows // slab_count
    side = round((plane_cells * slab_count) ** (1.0 / 3.0))
    other = swap_cores(orbitals, pair_count)
    blocks = pack(orbitals, other, own_count, slab_count)
    team_blocks = gather_boxes(blocks, slab_count, pair_count)
    forces = team_forces(matchings, centers.T, team_blocks, side, slab_count, pair_count)
    received = []
    for step in reversed(range(1, slab_count)):
        perm = [(i, partner_of(i, step, slab_count)[0]) for i in range(slab_count)]
        received.append(lax.ppermute(forces[step], "slab", perm))
    return unpack(received + [forces[0]], own_count, plane_cells)


def solution(mesh):
    in_specs = (P("pair", "slab"), P(), P("slab", None, None))
    out_specs = P("pair", "slab")
    return jax.shard_map(shards, mesh=mesh, in_specs=in_specs, out_specs=out_specs, check_vma=False)
```

```python
import functools

import jax
import jax.numpy as jnp
import ml_dtypes
import numpy as np
from jax import lax
from jax.experimental import pallas as pl
from jax.experimental.pallas import tpu as pltpu
from jax.sharding import PartitionSpec as P

STEPS = 16
CUT2 = 192
REACH = 8
SCREEN = 0.1
LOWER_BOUND = 0.1
UPPER_BOUND = 12.1
LANES = 128
CORES = 2
CODE_LIMIT = 32767.0
FACTOR_UNIT = 8192.0
LOWEST_EXPONENT = -120.0
TINY = 1e-37
HEADER_ROWS = 16


def split_constant(matrix):
    high = matrix.astype(ml_dtypes.bfloat16)
    low = (matrix - high.astype(np.float64)).astype(ml_dtypes.bfloat16)
    return high, low


def sine_basis(side):
    index = np.arange(1, side + 1, dtype=np.float64)
    return np.sqrt(2.0 / (side + 1)) * np.sin(np.pi * np.outer(index, index) / (side + 1))


def chebyshev_gain(side):
    shifts = -2.0 * np.cos(np.pi * np.arange(1, side + 1, dtype=np.float64) / (side + 1))
    eigenvalue = 6.0 + SCREEN + shifts[:, None, None] + shifts[None, :, None] + shifts[None, None, :]
    middle = (UPPER_BOUND + LOWER_BOUND) / 2.0
    spread = (UPPER_BOUND - LOWER_BOUND) / 2.0
    ratio = middle / spread
    total = np.zeros_like(eigenvalue)
    residual = np.ones_like(eigenvalue)
    direction = residual / middle
    factor = 1.0 / ratio
    for _ in range(STEPS):
        total = total + direction
        residual = residual - eigenvalue * direction
        factor_next = 1.0 / (2.0 * ratio - factor)
        direction = factor_next * factor * direction + 2.0 * factor_next / spread * residual
        factor = factor_next
    return total.reshape(side, side * side).astype(np.float32)


def split_pair(value):
    high = value.astype(jnp.bfloat16)
    low = (value - high.astype(jnp.float32)).astype(jnp.bfloat16)
    return high, low


def dot(left, right):
    return jnp.dot(left, right, preferred_element_type=jnp.float32)


def partner_of(index, step, count):
    if count & (count - 1) == 0:
        return index ^ step, index ^ step
    return (index + step) % count, (index + count - step) % count


def slab_step(turn, core):
    return CORES * turn + CORES - 1 - core


def turn_groups(slab_count):
    turns = list(reversed(range(slab_count // CORES)))
    middle = (len(turns) + 1) // 2
    return [group for group in (turns[:middle], turns[middle:]) if group]


def block_places(slab_index, pair_index, slab_count, pair_count):
    chips = pair_count // CORES
    chip = pair_index // CORES
    for core_step in range(CORES):
        core = (pair_index + core_step) % CORES
        for chip_step in range(chips):
            source = (chip + chips - chip_step) % chips
            for turns in turn_groups(slab_count):
                steps = [slab_step(turn, core) for turn in turns]
                yield [(source, partner_of(slab_index, step, slab_count)[1]) for step in steps]


def force_kernel(sizes, match_ref, centers_ref, *refs):
    slab_count, pair_count = sizes[3:]
    block_count = len(turn_groups(slab_count)) * pair_count
    block_refs = refs[:block_count]
    constant_refs = refs[block_count : block_count + 6]
    out_refs = refs[block_count + 6 : block_count + 6 + slab_count]
    scratch = refs[block_count + 6 + slab_count :]
    force_body(sizes, match_ref, centers_ref, block_refs, constant_refs, out_refs, *scratch)


def force_body(
    sizes,
    match_hbm,
    centers_hbm,
    block_refs,
    constant_refs,
    out_refs,
    match_ref,
    centers_ref,
    boxes_ref,
    mix_ref,
    gain_ref,
    there_high,
    there_low,
    back_high,
    back_low,
    fields,
    partner,
    first,
    second,
    terms,
    total,
    sems,
):
    side, rounds, own_count, slab_count, pair_count = sizes
    planes = side // slab_count
    tiles = side * side // LANES
    lines = LANES // side
    pitch = side + 2 * REACH
    solves = own_count * rounds
    group = min(solves, 8)
    group_rows = group * side
    cells = tiles * LANES
    width = 2 * LANES
    slab_index = lax.axis_index("slab")
    pair_index = lax.axis_index("pair")

    sources = [match_hbm, centers_hbm]
    targets = [match_ref, centers_ref]
    block_rows = boxes_ref.shape[2]
    places = block_places(slab_index, pair_index, slab_count, pair_count)
    for block_ref, group_places in zip(block_refs, places):
        for index, place in enumerate(group_places):
            sources.append(block_ref.at[index * block_rows : (index + 1) * block_rows])
            targets.append(boxes_ref.at[place])
    copies = []
    for source, target in zip(sources, targets):
        copies.append(pltpu.make_async_copy(source, target, sems.at[len(copies)]))
    constants = (mix_ref, gain_ref, there_high, there_low, back_high, back_low)
    constant_copies = []
    for index, (source, target) in enumerate(zip(constant_refs, constants)):
        constant_copies.append(pltpu.make_async_copy(source, target, sems.at[len(copies) + index]))
    for copy in copies + constant_copies:
        copy.start()

    zeros = jnp.zeros((REACH, LANES), jnp.float32)

    def clear(index, carry):
        fields[pl.ds(pl.multiple_of(index * pitch, 8), REACH), :] = zeros
        fields[pl.ds(pl.multiple_of(index * pitch + REACH + side, 8), REACH), :] = zeros
        return carry

    lax.fori_loop(0, pair_count * own_count * tiles, clear, 0, unroll=8)

    def clear_terms(index, carry):
        terms[pl.ds(pl.multiple_of(index * pitch, 8), REACH), :] = zeros
        terms[pl.ds(pl.multiple_of(index * pitch + REACH + side, 8), REACH), :] = zeros
        return carry

    lax.fori_loop(0, solves * tiles, clear_terms, 0, unroll=8)

    for copy in copies:
        copy.wait()

    def spread(index, carry):
        chip = index // slab_count
        slab = index % slab_count
        for chunk in range(CORES * own_count * planes // 2):
            block = boxes_ref[chip, slab, 16 * chunk : 16 * chunk + 16, :].astype(jnp.float32)
            for half in range(2):
                member, plane = divmod(2 * chunk + half, planes)
                start = (chip * CORES * own_count + member) * tiles * pitch + REACH + slab * planes + plane
                fields[pl.ds(start, tiles, stride=pitch), :] = block[8 * half : 8 * half + 8, :]
        return carry

    lax.fori_loop(0, pair_count // CORES * slab_count, spread, 0)

    step_rows = 16
    lane = lax.broadcasted_iota(jnp.int32, (step_rows, LANES), 1)
    lane_row = lax.broadcasted_iota(jnp.int32, (1, LANES), 1)
    lane_line = lane_row // side
    lane_point = lane_row % side

    def rolled(ref, base, row, offset_x, offset_flat):
        whole = (offset_flat >> 7) & (tiles - 1)
        part = offset_flat & (LANES - 1)
        start = base * pitch + REACH + row - offset_x
        moved = []
        for tile in range(tiles):
            first_row = start + ((tile - whole) & (tiles - 1)) * pitch
            moved.append(pltpu.roll(ref[pl.ds(first_row, step_rows), :], part, axis=1))
        keep = lane >= part
        return [jnp.where(keep, moved[t], moved[(t - 1) % tiles]) for t in range(tiles)]

    def mirrored(tile):
        line = lax.broadcasted_iota(jnp.int32, tile.shape, 1) // side
        result = None
        for index in range(lines):
            amount = (2 * index - lines + 1) * side % LANES
            if index < 2:
                moved = pltpu.roll(tile, amount, axis=1)
                result = moved if result is None else jnp.where(line % 2 == index, moved, result)
        return result

    def orbital_of(member):
        return (member // own_count * slab_count + slab_index) * own_count + member % own_count

    def geometry(index):
        own = index // rounds
        turn = index % rounds
        member = pair_index * own_count + own
        mate = match_ref[0, turn, member]
        own_offset = []
        mate_offset = []
        distance = 0
        for axis in range(3):
            mine = centers_ref[axis, orbital_of(member)]
            other = centers_ref[axis, orbital_of(mate)]
            anchor = (mine + other) >> 1
            own_offset.append(mine - anchor)
            mate_offset.append(other - anchor)
            distance = distance + (mine - other) * (mine - other)
        return own, member, mate, own_offset, mate_offset, distance <= CUT2

    row_count = solves * side
    half_tiles = tiles // 2
    half_cells = cells // 2

    def store_split(ref, start, count, columns, value):
        high, low = split_pair(value)
        if isinstance(start, int):
            ref[start : start + count, columns] = high
            ref[row_count + start : row_count + start + count, columns] = low
        else:
            ref[pl.ds(pl.multiple_of(start, count), count), columns] = high
            ref[pl.ds(pl.multiple_of(row_count + start, count), count), columns] = low

    def densities(step, carry):
        index = step // (side // step_rows)
        row = step % (side // step_rows) * step_rows
        own, member, mate, a, b, active = geometry(index)
        mine = rolled(fields, member * tiles, row, a[0], a[1] * side + a[2])
        other = rolled(fields, mate * tiles, row, b[0], b[1] * side + b[2])
        low_line = jnp.maximum(jnp.maximum(a[1], b[1]), 0)
        high_line = jnp.where(active, side + jnp.minimum(jnp.minimum(a[1], b[1]), 0), 0)
        low_point = jnp.maximum(jnp.maximum(a[2], b[2]), 0)
        high_point = side + jnp.minimum(jnp.minimum(a[2], b[2]), 0)
        point_ok = (lane_point >= low_point) & (lane_point < high_point)
        start = step * step_rows
        rows = pl.ds(pl.multiple_of(start, step_rows), step_rows)
        density = []
        for tile in range(tiles):
            line = lane_line + tile * lines
            ok = jnp.where(point_ok & (line >= low_line) & (line < high_line), 1.0, 0.0)
            masked = other[tile] * ok
            partner[rows, tile * LANES : (tile + 1) * LANES] = masked.astype(jnp.bfloat16)
            density.append(mine[tile] * masked)
        for tile in range(half_tiles):
            mirror = mirrored(density[tiles - 1 - tile])
            for parity, value in enumerate((density[tile] + mirror, density[tile] - mirror)):
                column = parity * half_cells + tile * LANES
                store_split(first, start, step_rows, slice(column, column + LANES), value)
        return carry

    lax.fori_loop(0, solves * side // step_rows, densities, 0, unroll=2)

    for copy in constant_copies:
        copy.wait()

    def along_x(start, columns, source):
        high = source[start : start + group_rows, columns]
        low = source[row_count + start : row_count + start + group_rows, columns]
        value = dot(mix_ref[...], high)
        return value[:group_rows] + (value[group_rows:] + dot(mix_ref[:group_rows, :], low))

    def in_plane(parity, columns, source, high_ref, low_ref):
        inner = slice(parity * half_cells, (parity + 1) * half_cells)
        value = dot(source[:, inner], high_ref[parity, :, columns])
        rest = dot(source[:row_count, inner], low_ref[parity, :, columns])
        return value[:row_count] + (value[row_count:] + rest)

    for start in range(0, row_count, group_rows):
        for column in range(0, cells, width):
            columns = slice(column, column + width)
            store_split(second, start, group_rows, columns, along_x(start, columns, first))

    for parity in range(2):
        for column in range(0, half_cells, width):
            columns = slice(column, column + width)
            value = in_plane(parity, columns, second, there_high, there_low)
            columns = slice(parity * half_cells + column, parity * half_cells + column + width)
            gain = gain_ref[:, columns]
            value = (value.reshape(solves, side, width) * gain[None]).reshape(row_count, width)
            store_split(first, 0, row_count, columns, value)

    for parity in range(2):
        for column in range(0, half_cells, width):
            value = in_plane(parity, slice(column, column + width), first, back_high, back_low)
            columns = slice(parity * half_cells + column, parity * half_cells + column + width)
            store_split(second, 0, row_count, columns, value)

    for start in range(0, row_count, group_rows):
        for column in range(0, half_cells, width):
            even = along_x(start, slice(column, column + width), second)
            odd = along_x(start, slice(half_cells + column, half_cells + column + width), second)
            for part in range(width // LANES):
                tile = column // LANES + part
                lanes = slice(part * LANES, (part + 1) * LANES)
                near = even[:, lanes] + odd[:, lanes]
                far = mirrored(even[:, lanes] - odd[:, lanes])
                for place, value in ((tile, near), (tiles - 1 - tile, far)):
                    columns = slice(place * LANES, (place + 1) * LANES)
                    value = value * partner[start : start + group_rows, columns].astype(jnp.float32)
                    for solve in range(group):
                        row = ((start // side + solve) * tiles + place) * pitch + REACH
                        terms[row : row + side, :] = value[solve * side : (solve + 1) * side, :]

    def collect(step, carry):
        own = step // (side // step_rows)
        row = step % (side // step_rows) * step_rows
        sums = None
        for turn in range(rounds):
            index = own * rounds + turn
            _, _, _, a, _, _ = geometry(index)
            term = rolled(terms, index * tiles, row, -a[0], -(a[1] * side + a[2]))
            sums = term if sums is None else [s + t for s, t in zip(sums, term)]
        for tile in range(tiles):
            start = (own * tiles + tile) * side + row
            total[pl.ds(pl.multiple_of(start, step_rows), step_rows), :] = sums[tile]
        return carry

    lax.fori_loop(0, own_count * side // step_rows, collect, 0)

    lane_index = lax.broadcasted_iota(jnp.int32, (tiles, LANES), 1)
    for step in range(slab_count):
        slab = partner_of(slab_index, step, slab_count)[0]
        exponents = jnp.zeros((tiles, LANES), jnp.float32)
        factors = jnp.zeros((tiles, LANES), jnp.float32)
        codes = []
        for chunk in range(own_count * planes):
            own, plane = divmod(chunk, planes)
            start = own * tiles * side + slab * planes + plane
            value = total[pl.ds(start, tiles, stride=side), :]
            code, exponent, factor = encode(value)
            codes.append(code)
            exponents = jnp.where(lane_index == chunk, exponent, exponents)
            factors = jnp.where(lane_index == chunk, factor, factors)
            if chunk % 2:
                pair = jnp.concatenate(codes[-2:], axis=0)
                out_refs[step][tiles * (chunk - 1) : tiles * (chunk + 1), :] = whole_codes(pair)
        header = jnp.concatenate([exponents, factors], axis=0)
        out_refs[step][tiles * own_count * planes :, :] = whole_codes(header)


def whole_codes(value):
    return value.astype(jnp.int32).astype(jnp.int16)


def encode(value):
    largest = jnp.max(jnp.abs(value), axis=1, keepdims=True)
    exponent = jnp.maximum(jnp.floor(jnp.log2(jnp.maximum(largest, TINY))), LOWEST_EXPONENT)
    lifted = 1.0 / jnp.exp2(exponent)
    factor = jnp.maximum(jnp.ceil(largest * lifted * FACTOR_UNIT), 1.0)
    code = jnp.floor(value * lifted * (CODE_LIMIT * FACTOR_UNIT / factor) + 0.5)
    return jnp.clip(code, -CODE_LIMIT, CODE_LIMIT), exponent, factor


def gather_boxes(blocks, slab_count, pair_count):
    chips = pair_count // CORES
    arrived = {}
    for turns in turn_groups(slab_count):
        for turn in turns:
            perm = []
            for slab in range(slab_count):
                for pair in range(pair_count):
                    target = partner_of(slab, slab_step(turn, pair % CORES), slab_count)[0]
                    perm.append((slab * pair_count + pair, target * pair_count + pair))
            arrived[turn] = lax.ppermute(blocks[turn], ("slab", "pair"), perm)
    own = [jnp.concatenate([arrived[t] for t in turns]) for turns in turn_groups(slab_count)]
    pieces = [own]
    for step in range(1, chips):
        perm = [(i, (i + step * CORES) % pair_count) for i in range(pair_count)]
        pieces.append([lax.ppermute(block, "pair", perm) for block in own])
    other = [[swap_cores(block, pair_count) for block in piece] for piece in pieces]
    return [block for piece in pieces + other for block in piece]


def swap_cores(block, pair_count):
    return lax.ppermute(block, "pair", [(i, i ^ 1) for i in range(pair_count)])


def pack_kernel(sizes, *refs):
    own_count, slab_count = sizes
    orbital_refs, out_refs, lines = refs[:CORES], refs[CORES:-1], refs[-1]
    row_count, cells = orbital_refs[0].shape
    tiles = cells // LANES
    slab_index = lax.axis_index("slab")
    core = lax.axis_index("pair") % CORES
    for side in range(CORES):
        base = (core ^ side) * tiles * row_count
        for tile in range(tiles):
            columns = slice(tile * LANES, (tile + 1) * LANES)
            rows = pl.ds(pl.multiple_of(base + tile * row_count, 8), row_count)
            lines[rows, :] = orbital_refs[side][:, columns].astype(jnp.float32)
    for turn, out_ref in enumerate(out_refs):
        first = partner_of(slab_index, slab_step(turn, core), slab_count)[0] * own_count
        for chunk in range(CORES * own_count * tiles // 16):
            halves = []
            for half in range(2):
                member, tile = divmod(16 * chunk + 8 * half, tiles)
                side, own = divmod(member, own_count)
                start = (side * tiles + tile) * row_count + first + own
                halves.append(lines[pl.ds(start, 8, stride=row_count), :])
            block = jnp.concatenate(halves, axis=0).astype(jnp.bfloat16)
            out_ref[16 * chunk : 16 * chunk + 16, :] = block


def pack(orbitals, other, own_count, slab_count):
    row_count, cells = orbitals.shape
    rows = CORES * own_count * cells // LANES
    vectors = pl.BlockSpec(memory_space=pltpu.VMEM)
    turns = slab_count // CORES
    return pl.pallas_call(
        functools.partial(pack_kernel, (own_count, slab_count)),
        out_shape=[jax.ShapeDtypeStruct((rows, LANES), jnp.bfloat16)] * turns,
        in_specs=[vectors] * CORES,
        out_specs=[vectors] * turns,
        scratch_shapes=[pltpu.VMEM((CORES * row_count * cells // LANES, LANES), jnp.float32)],
        compiler_params=pltpu.CompilerParams(vmem_limit_bytes=60 * 1024 * 1024),
    )(orbitals, other)


def unpack_kernel(sizes, *refs):
    own_count, slab_count, tiles = sizes
    block_refs, out_ref, blocks, sems = refs[:slab_count], *refs[slab_count:]
    slab_index = lax.axis_index("slab")
    copies = []
    for index in range(slab_count):
        copies.append(pltpu.make_async_copy(block_refs[index], blocks.at[index], sems.at[index]))
        copies[-1].start()
    for index in reversed(range(slab_count)):
        step = slab_count - 1 - index
        copies[index].wait()
        first = partner_of(slab_index, step, slab_count)[1] * own_count
        row_count = own_count * tiles
        header = blocks[index, row_count:, :].astype(jnp.int32).astype(jnp.float32)
        units = jnp.exp2(header[:8, :])
        factors = header[8:, :] * (1.0 / (CODE_LIMIT * FACTOR_UNIT))
        for pair in range(row_count // 16):
            codes = blocks[index, 16 * pair : 16 * pair + 16, :].astype(jnp.int32).astype(jnp.float32)
            for half in range(2):
                chunk = 2 * pair + half
                own, tile = divmod(8 * chunk, tiles)
                row = first + own
                start = (row // 8 * tiles + tile) * 8 + row % 8
                value = codes[8 * half : 8 * half + 8, :] * factors[:, chunk : chunk + 1]
                out_ref[pl.ds(start, 8, stride=8), :] = value * units[:, chunk : chunk + 1]


def unpack(blocks, own_count, cells):
    slab_count = len(blocks)
    row_count = own_count * slab_count
    tiles = cells // LANES
    out = pl.pallas_call(
        functools.partial(unpack_kernel, (own_count, slab_count, tiles)),
        out_shape=jax.ShapeDtypeStruct((row_count * tiles, LANES), jnp.float32),
        in_specs=[pl.BlockSpec(memory_space=pl.ANY)] * slab_count,
        out_specs=pl.BlockSpec(memory_space=pltpu.VMEM),
        scratch_shapes=[
            pltpu.VMEM((slab_count,) + blocks[0].shape, jnp.int16),
            pltpu.SemaphoreType.DMA((slab_count,)),
        ],
    )(*blocks)
    return out.reshape(row_count // 8, tiles, 8, LANES).transpose(0, 2, 1, 3).reshape(row_count, cells)


def team_forces(match, centers, blocks, side, slab_count, pair_count):
    _, rounds, team = match.shape
    own_count = team // pair_count
    rows = own_count * side * side // LANES * (side // slab_count)
    block_count = slab_count * pair_count // CORES
    tiles = side * side // LANES
    solves = own_count * rounds
    group = min(solves, 8)
    cells = side * side
    pitch = side + 2 * REACH
    basis = sine_basis(side)
    mix = np.concatenate(split_constant(np.kron(np.eye(group), basis)), axis=0)
    there = np.stack([np.kron(basis[parity::2, : side // 2].T, basis) for parity in range(2)])
    gain = chebyshev_gain(side).reshape(side, side, side)
    gain = np.concatenate([gain[:, parity::2].reshape(side, -1) for parity in range(2)], axis=1)
    constants = (mix, gain, *split_constant(there), *split_constant(there.transpose(0, 2, 1)))
    sizes = (side, rounds, own_count, slab_count, pair_count)
    either = pl.BlockSpec(memory_space=pl.ANY)
    distant = pl.BlockSpec(memory_space=pltpu.HBM)
    vectors = pl.BlockSpec(memory_space=pltpu.VMEM)
    wide = pltpu.VMEM((2 * solves * side, cells), jnp.bfloat16)
    flops = 2 * solves * side * 3 * 2 * (cells * cells // 2 + cells * group * side)
    return pl.pallas_call(
        functools.partial(force_kernel, sizes),
        out_shape=[jax.ShapeDtypeStruct((rows + HEADER_ROWS, LANES), jnp.int16)] * slab_count,
        in_specs=[distant] * 2 + [either] * len(blocks) + [distant] * len(constants),
        out_specs=[vectors] * slab_count,
        scratch_shapes=[
            pltpu.SMEM(match.shape, jnp.int32),
            pltpu.SMEM(centers.shape, jnp.int32),
            pltpu.VMEM((pair_count // CORES, slab_count, CORES * rows, LANES), jnp.bfloat16),
            *[pltpu.VMEM(constant.shape, constant.dtype) for constant in constants],
            pltpu.VMEM((team * tiles * pitch, LANES), jnp.float32),
            pltpu.VMEM((solves * side, cells), jnp.bfloat16),
            wide,
            wide,
            pltpu.VMEM((solves * tiles * pitch, LANES), jnp.float32),
            pltpu.VMEM((own_count * tiles * side, LANES), jnp.float32),
            pltpu.SemaphoreType.DMA((block_count + 2 + len(constants),)),
        ],
        compiler_params=pltpu.CompilerParams(vmem_limit_bytes=60 * 1024 * 1024),
        cost_estimate=pl.CostEstimate(flops=flops, bytes_accessed=8 * 1024 * 1024, transcendentals=0),
    )(
        match,
        centers,
        *blocks,
        *[jnp.asarray(constant) for constant in constants],
    )


def shards(orbitals, centers, matchings):
    slab_count = lax.axis_size("slab")
    pair_count = lax.axis_size("pair")
    local_rows, plane_cells = orbitals.shape
    own_count = local_rows // slab_count
    side = round((plane_cells * slab_count) ** (1.0 / 3.0))
    other = swap_cores(orbitals, pair_count)
    blocks = pack(orbitals, other, own_count, slab_count)
    team_blocks = gather_boxes(blocks, slab_count, pair_count)
    forces = team_forces(matchings, centers.T, team_blocks, side, slab_count, pair_count)
    received = []
    for step in reversed(range(1, slab_count)):
        perm = [(i, partner_of(i, step, slab_count)[0]) for i in range(slab_count)]
        received.append(lax.ppermute(forces[step], "slab", perm))
    return unpack(received + [forces[0]], own_count, plane_cells)


def solution(mesh):
    in_specs = (P("pair", "slab"), P(), P("slab", None, None))
    out_specs = P("pair", "slab")
    return jax.shard_map(shards, mesh=mesh, in_specs=in_specs, out_specs=out_specs, check_vma=False)
```

```python
import functools

import jax
import jax.numpy as jnp
import ml_dtypes
import numpy as np
from jax import lax
from jax.experimental import pallas as pl
from jax.experimental.pallas import tpu as pltpu
from jax.sharding import PartitionSpec as P

STEPS = 16
CUT2 = 192
REACH = 8
SCREEN = 0.1
LOWER_BOUND = 0.1
UPPER_BOUND = 12.1
LANES = 128
CORES = 2
CODE_LIMIT = 32767.0
FACTOR_UNIT = 8192.0
LOWEST_EXPONENT = -120.0
TINY = 1e-37
HEADER_ROWS = 16


def split_constant(matrix):
    high = matrix.astype(ml_dtypes.bfloat16)
    low = (matrix - high.astype(np.float64)).astype(ml_dtypes.bfloat16)
    return high, low


def sine_basis(side):
    index = np.arange(1, side + 1, dtype=np.float64)
    return np.sqrt(2.0 / (side + 1)) * np.sin(np.pi * np.outer(index, index) / (side + 1))


def chebyshev_gain(side):
    shifts = -2.0 * np.cos(np.pi * np.arange(1, side + 1, dtype=np.float64) / (side + 1))
    eigenvalue = 6.0 + SCREEN + shifts[:, None, None] + shifts[None, :, None] + shifts[None, None, :]
    middle = (UPPER_BOUND + LOWER_BOUND) / 2.0
    spread = (UPPER_BOUND - LOWER_BOUND) / 2.0
    ratio = middle / spread
    total = np.zeros_like(eigenvalue)
    residual = np.ones_like(eigenvalue)
    direction = residual / middle
    factor = 1.0 / ratio
    for _ in range(STEPS):
        total = total + direction
        residual = residual - eigenvalue * direction
        factor_next = 1.0 / (2.0 * ratio - factor)
        direction = factor_next * factor * direction + 2.0 * factor_next / spread * residual
        factor = factor_next
    return total.reshape(side, side * side).astype(np.float32)


def split_pair(value):
    high = value.astype(jnp.bfloat16)
    low = (value - high.astype(jnp.float32)).astype(jnp.bfloat16)
    return high, low


def dot(left, right):
    return jnp.dot(left, right, preferred_element_type=jnp.float32)


def piece_places(pair_index, pair_count):
    chips = pair_count // CORES
    chip = pair_index // CORES
    for core_step in range(CORES):
        for chip_step in range(chips):
            yield (chip + chips - chip_step) % chips * CORES + (pair_index + core_step) % CORES


def force_kernel(sizes, match_ref, centers_ref, *refs):
    pair_count = sizes[4]
    block_refs, constant_refs = refs[:pair_count], refs[pair_count : pair_count + 6]
    out_ref, scratch = refs[pair_count + 6], refs[pair_count + 7 :]
    force_body(sizes, match_ref, centers_ref, block_refs, constant_refs, out_ref, *scratch)


def force_body(
    sizes,
    match_hbm,
    centers_hbm,
    block_refs,
    constant_refs,
    out_ref,
    match_ref,
    centers_ref,
    boxes_ref,
    mix_ref,
    gain_ref,
    there_high,
    there_low,
    back_high,
    back_low,
    fields,
    partner,
    first,
    second,
    terms,
    total,
    sems,
):
    side, rounds, own_count, slab_count, pair_count = sizes
    planes = side // slab_count
    tiles = side * side // LANES
    lines = LANES // side
    pitch = side + 2 * REACH
    solves = own_count * rounds
    group = min(solves, 8)
    group_rows = group * side
    cells = tiles * LANES
    width = 2 * LANES
    slab_index = lax.axis_index("slab")
    pair_index = lax.axis_index("pair")

    sources = [match_hbm, centers_hbm, *block_refs]
    targets = [match_ref, centers_ref]
    targets += [boxes_ref.at[pair] for pair in piece_places(pair_index, pair_count)]
    copies = []
    for source, target in zip(sources, targets):
        copies.append(pltpu.make_async_copy(source, target, sems.at[len(copies)]))
    constants = (mix_ref, gain_ref, there_high, there_low, back_high, back_low)
    constant_copies = []
    for index, (source, target) in enumerate(zip(constant_refs, constants)):
        constant_copies.append(pltpu.make_async_copy(source, target, sems.at[len(copies) + index]))
    for copy in copies + constant_copies:
        copy.start()

    zeros = jnp.zeros((REACH, LANES), jnp.float32)

    def clear(index, carry):
        fields[pl.ds(pl.multiple_of(index * pitch, 8), REACH), :] = zeros
        fields[pl.ds(pl.multiple_of(index * pitch + REACH + side, 8), REACH), :] = zeros
        return carry

    lax.fori_loop(0, pair_count * own_count * tiles, clear, 0, unroll=8)

    def clear_terms(index, carry):
        terms[pl.ds(pl.multiple_of(index * pitch, 8), REACH), :] = zeros
        terms[pl.ds(pl.multiple_of(index * pitch + REACH + side, 8), REACH), :] = zeros
        return carry

    lax.fori_loop(0, solves * tiles, clear_terms, 0, unroll=8)

    for copy in copies:
        copy.wait()

    def spread(index, carry):
        pair = index // slab_count
        slab = index % slab_count
        for chunk in range(own_count * planes // 2):
            block = boxes_ref[pair, slab, 16 * chunk : 16 * chunk + 16, :].astype(jnp.float32)
            for half in range(2):
                own, plane = divmod(2 * chunk + half, planes)
                start = (pair * own_count + own) * tiles * pitch + REACH + slab * planes + plane
                fields[pl.ds(start, tiles, stride=pitch), :] = block[8 * half : 8 * half + 8, :]
        return carry

    lax.fori_loop(0, pair_count * slab_count, spread, 0)

    step_rows = 16
    lane = lax.broadcasted_iota(jnp.int32, (step_rows, LANES), 1)
    lane_row = lax.broadcasted_iota(jnp.int32, (1, LANES), 1)
    lane_line = lane_row // side
    lane_point = lane_row % side

    def rolled(ref, base, row, offset_x, offset_flat):
        whole = (offset_flat >> 7) & (tiles - 1)
        part = offset_flat & (LANES - 1)
        start = base * pitch + REACH + row - offset_x
        moved = []
        for tile in range(tiles):
            first_row = start + ((tile - whole) & (tiles - 1)) * pitch
            moved.append(pltpu.roll(ref[pl.ds(first_row, step_rows), :], part, axis=1))
        keep = lane >= part
        return [jnp.where(keep, moved[t], moved[(t - 1) % tiles]) for t in range(tiles)]

    def mirrored(tile):
        line = lax.broadcasted_iota(jnp.int32, tile.shape, 1) // side
        result = None
        for index in range(lines):
            amount = (2 * index - lines + 1) * side % LANES
            if index < 2:
                moved = pltpu.roll(tile, amount, axis=1)
                result = moved if result is None else jnp.where(line % 2 == index, moved, result)
        return result

    def orbital_of(member):
        return (member // own_count * slab_count + slab_index) * own_count + member % own_count

    def geometry(index):
        own = index // rounds
        turn = index % rounds
        member = pair_index * own_count + own
        mate = match_ref[0, turn, member]
        own_offset = []
        mate_offset = []
        distance = 0
        for axis in range(3):
            mine = centers_ref[axis, orbital_of(member)]
            other = centers_ref[axis, orbital_of(mate)]
            anchor = (mine + other) >> 1
            own_offset.append(mine - anchor)
            mate_offset.append(other - anchor)
            distance = distance + (mine - other) * (mine - other)
        return own, member, mate, own_offset, mate_offset, distance <= CUT2

    row_count = solves * side
    half_tiles = tiles // 2
    half_cells = cells // 2

    def store_split(ref, start, count, columns, value):
        high, low = split_pair(value)
        if isinstance(start, int):
            ref[start : start + count, columns] = high
            ref[row_count + start : row_count + start + count, columns] = low
        else:
            ref[pl.ds(pl.multiple_of(start, count), count), columns] = high
            ref[pl.ds(pl.multiple_of(row_count + start, count), count), columns] = low

    def densities(step, carry):
        index = step // (side // step_rows)
        row = step % (side // step_rows) * step_rows
        own, member, mate, a, b, active = geometry(index)
        mine = rolled(fields, member * tiles, row, a[0], a[1] * side + a[2])
        other = rolled(fields, mate * tiles, row, b[0], b[1] * side + b[2])
        low_line = jnp.maximum(jnp.maximum(a[1], b[1]), 0)
        high_line = jnp.where(active, side + jnp.minimum(jnp.minimum(a[1], b[1]), 0), 0)
        low_point = jnp.maximum(jnp.maximum(a[2], b[2]), 0)
        high_point = side + jnp.minimum(jnp.minimum(a[2], b[2]), 0)
        point_ok = (lane_point >= low_point) & (lane_point < high_point)
        start = step * step_rows
        rows = pl.ds(pl.multiple_of(start, step_rows), step_rows)
        density = []
        for tile in range(tiles):
            line = lane_line + tile * lines
            ok = jnp.where(point_ok & (line >= low_line) & (line < high_line), 1.0, 0.0)
            masked = other[tile] * ok
            partner[rows, tile * LANES : (tile + 1) * LANES] = masked.astype(jnp.bfloat16)
            density.append(mine[tile] * masked)
        for tile in range(half_tiles):
            mirror = mirrored(density[tiles - 1 - tile])
            for parity, value in enumerate((density[tile] + mirror, density[tile] - mirror)):
                column = parity * half_cells + tile * LANES
                store_split(first, start, step_rows, slice(column, column + LANES), value)
        return carry

    lax.fori_loop(0, solves * side // step_rows, densities, 0, unroll=2)

    for copy in constant_copies:
        copy.wait()

    def along_x(start, columns, source):
        high = source[start : start + group_rows, columns]
        low = source[row_count + start : row_count + start + group_rows, columns]
        value = dot(mix_ref[...], high)
        return value[:group_rows] + (value[group_rows:] + dot(mix_ref[:group_rows, :], low))

    def in_plane(parity, columns, source, high_ref, low_ref):
        inner = slice(parity * half_cells, (parity + 1) * half_cells)
        value = dot(source[:, inner], high_ref[parity, :, columns])
        rest = dot(source[:row_count, inner], low_ref[parity, :, columns])
        return value[:row_count] + (value[row_count:] + rest)

    for start in range(0, row_count, group_rows):
        for column in range(0, cells, width):
            columns = slice(column, column + width)
            store_split(second, start, group_rows, columns, along_x(start, columns, first))

    for parity in range(2):
        for column in range(0, half_cells, width):
            columns = slice(column, column + width)
            value = in_plane(parity, columns, second, there_high, there_low)
            columns = slice(parity * half_cells + column, parity * half_cells + column + width)
            gain = gain_ref[:, columns]
            value = (value.reshape(solves, side, width) * gain[None]).reshape(row_count, width)
            store_split(first, 0, row_count, columns, value)

    for parity in range(2):
        for column in range(0, half_cells, width):
            value = in_plane(parity, slice(column, column + width), first, back_high, back_low)
            columns = slice(parity * half_cells + column, parity * half_cells + column + width)
            store_split(second, 0, row_count, columns, value)

    for start in range(0, row_count, group_rows):
        for column in range(0, half_cells, width):
            even = along_x(start, slice(column, column + width), second)
            odd = along_x(start, slice(half_cells + column, half_cells + column + width), second)
            for part in range(width // LANES):
                tile = column // LANES + part
                lanes = slice(part * LANES, (part + 1) * LANES)
                near = even[:, lanes] + odd[:, lanes]
                far = mirrored(even[:, lanes] - odd[:, lanes])
                for place, value in ((tile, near), (tiles - 1 - tile, far)):
                    columns = slice(place * LANES, (place + 1) * LANES)
                    value = value * partner[start : start + group_rows, columns].astype(jnp.float32)
                    for solve in range(group):
                        row = ((start // side + solve) * tiles + place) * pitch + REACH
                        terms[row : row + side, :] = value[solve * side : (solve + 1) * side, :]

    def collect(step, carry):
        own = step // (side // step_rows)
        row = step % (side // step_rows) * step_rows
        sums = None
        for turn in range(rounds):
            index = own * rounds + turn
            _, _, _, a, _, _ = geometry(index)
            term = rolled(terms, index * tiles, row, -a[0], -(a[1] * side + a[2]))
            sums = term if sums is None else [s + t for s, t in zip(sums, term)]
        for tile in range(tiles):
            start = (own * tiles + tile) * side + row
            total[pl.ds(pl.multiple_of(start, step_rows), step_rows), :] = sums[tile]
        return carry

    lax.fori_loop(0, own_count * side // step_rows, collect, 0)

    lane_index = lax.broadcasted_iota(jnp.int32, (tiles, LANES), 1)
    for slab in range(slab_count):
        exponents = jnp.zeros((tiles, LANES), jnp.float32)
        factors = jnp.zeros((tiles, LANES), jnp.float32)
        codes = []
        for chunk in range(own_count * planes):
            own, plane = divmod(chunk, planes)
            start = own * tiles * side + slab * planes + plane
            value = total[pl.ds(start, tiles, stride=side), :]
            code, exponent, factor = encode(value)
            codes.append(code)
            exponents = jnp.where(lane_index == chunk, exponent, exponents)
            factors = jnp.where(lane_index == chunk, factor, factors)
            if chunk % 2:
                pair = jnp.concatenate(codes[-2:], axis=0)
                out_ref[slab, tiles * (chunk - 1) : tiles * (chunk + 1), :] = whole_codes(pair)
        header = jnp.concatenate([exponents, factors], axis=0)
        out_ref[slab, tiles * own_count * planes :, :] = whole_codes(header)


def whole_codes(value):
    return value.astype(jnp.int32).astype(jnp.int16)


def encode(value):
    largest = jnp.max(jnp.abs(value), axis=1, keepdims=True)
    exponent = jnp.maximum(jnp.floor(jnp.log2(jnp.maximum(largest, TINY))), LOWEST_EXPONENT)
    lifted = 1.0 / jnp.exp2(exponent)
    factor = jnp.maximum(jnp.ceil(largest * lifted * FACTOR_UNIT), 1.0)
    code = jnp.floor(value * lifted * (CODE_LIMIT * FACTOR_UNIT / factor) + 0.5)
    return jnp.clip(code, -CODE_LIMIT, CODE_LIMIT), exponent, factor


def gather_boxes(boxes, pair_count):
    pieces = [boxes]
    for step in range(1, pair_count // CORES):
        perm = [(i, (i + step * CORES) % pair_count) for i in range(pair_count)]
        pieces.append(lax.ppermute(boxes, "pair", perm))
    swap = [(i, i ^ 1) for i in range(pair_count)]
    return pieces + [lax.ppermute(piece, "pair", swap) for piece in pieces]


def unpack_kernel(sizes, blocks_ref, out_ref):
    own_count, tiles = sizes
    row_count = own_count * tiles
    for slab in range(blocks_ref.shape[0]):
        header = blocks_ref[slab, row_count:, :].astype(jnp.int32).astype(jnp.float32)
        units = jnp.exp2(header[:8, :])
        factors = header[8:, :] * (1.0 / (CODE_LIMIT * FACTOR_UNIT))
        for pair in range(row_count // 16):
            codes = blocks_ref[slab, 16 * pair : 16 * pair + 16, :].astype(jnp.int32).astype(jnp.float32)
            for half in range(2):
                chunk = 2 * pair + half
                own, tile = divmod(8 * chunk, tiles)
                row = slab * own_count + own
                start = (row // 8 * tiles + tile) * 8 + row % 8
                value = codes[8 * half : 8 * half + 8, :] * factors[:, chunk : chunk + 1]
                out_ref[pl.ds(start, 8, stride=8), :] = value * units[:, chunk : chunk + 1]


def unpack(blocks, own_count, cells):
    row_count = own_count * blocks.shape[0]
    tiles = cells // LANES
    vectors = pl.BlockSpec(memory_space=pltpu.VMEM)
    out = pl.pallas_call(
        functools.partial(unpack_kernel, (own_count, tiles)),
        out_shape=jax.ShapeDtypeStruct((row_count * tiles, LANES), jnp.float32),
        in_specs=[vectors],
        out_specs=vectors,
    )(blocks)
    return out.reshape(row_count // 8, tiles, 8, LANES).transpose(0, 2, 1, 3).reshape(row_count, cells)


def team_forces(match, centers, blocks, side, slab_count, pair_count):
    _, rounds, team = match.shape
    own_count = team // pair_count
    rows = own_count * side * side // LANES * (side // slab_count)
    tiles = side * side // LANES
    solves = own_count * rounds
    group = min(solves, 8)
    cells = side * side
    pitch = side + 2 * REACH
    basis = sine_basis(side)
    mix = np.concatenate(split_constant(np.kron(np.eye(group), basis)), axis=0)
    there = np.stack([np.kron(basis[parity::2, : side // 2].T, basis) for parity in range(2)])
    gain = chebyshev_gain(side).reshape(side, side, side)
    gain = np.concatenate([gain[:, parity::2].reshape(side, -1) for parity in range(2)], axis=1)
    constants = (mix, gain, *split_constant(there), *split_constant(there.transpose(0, 2, 1)))
    sizes = (side, rounds, own_count, slab_count, pair_count)
    either = pl.BlockSpec(memory_space=pl.ANY)
    distant = pl.BlockSpec(memory_space=pltpu.HBM)
    vectors = pl.BlockSpec(memory_space=pltpu.VMEM)
    wide = pltpu.VMEM((2 * solves * side, cells), jnp.bfloat16)
    flops = 2 * solves * side * 3 * 2 * (cells * cells // 2 + cells * group * side)
    return pl.pallas_call(
        functools.partial(force_kernel, sizes),
        out_shape=jax.ShapeDtypeStruct((slab_count, rows + HEADER_ROWS, LANES), jnp.int16),
        in_specs=[distant] * 2 + [either] * len(blocks) + [distant] * len(constants),
        out_specs=vectors,
        scratch_shapes=[
            pltpu.SMEM(match.shape, jnp.int32),
            pltpu.SMEM(centers.shape, jnp.int32),
            pltpu.VMEM((pair_count, slab_count, rows, LANES), jnp.bfloat16),
            *[pltpu.VMEM(constant.shape, constant.dtype) for constant in constants],
            pltpu.VMEM((team * tiles * pitch, LANES), jnp.float32),
            pltpu.VMEM((solves * side, cells), jnp.bfloat16),
            wide,
            wide,
            pltpu.VMEM((solves * tiles * pitch, LANES), jnp.float32),
            pltpu.VMEM((own_count * tiles * side, LANES), jnp.float32),
            pltpu.SemaphoreType.DMA((pair_count + 2 + len(constants),)),
        ],
        compiler_params=pltpu.CompilerParams(vmem_limit_bytes=60 * 1024 * 1024),
        cost_estimate=pl.CostEstimate(flops=flops, bytes_accessed=8 * 1024 * 1024, transcendentals=0),
    )(
        match,
        centers,
        *blocks,
        *[jnp.asarray(constant) for constant in constants],
    )


def shards(orbitals, centers, matchings):
    slab_count = lax.axis_size("slab")
    pair_count = lax.axis_size("pair")
    local_rows, plane_cells = orbitals.shape
    own_count = local_rows // slab_count
    side = round((plane_cells * slab_count) ** (1.0 / 3.0))
    blocks = orbitals.reshape(slab_count, own_count * plane_cells // LANES, LANES)
    boxes = lax.all_to_all(blocks, "slab", split_axis=0, concat_axis=0, tiled=True)
    pieces = gather_boxes(boxes, pair_count)
    codes = team_forces(matchings, centers.T, pieces, side, slab_count, pair_count)
    codes = lax.all_to_all(codes, "slab", split_axis=0, concat_axis=0, tiled=True)
    return unpack(codes, own_count, plane_cells)


def solution(mesh):
    in_specs = (P("pair", "slab"), P(), P("slab", None, None))
    out_specs = P("pair", "slab")
    return jax.shard_map(shards, mesh=mesh, in_specs=in_specs, out_specs=out_specs, check_vma=False)
```

```python
import functools

import jax
import jax.numpy as jnp
import ml_dtypes
import numpy as np
from jax import lax
from jax.experimental import pallas as pl
from jax.experimental.pallas import tpu as pltpu
from jax.sharding import PartitionSpec as P

STEPS = 16
CUT2 = 192
REACH = 8
SCREEN = 0.1
LOWER_BOUND = 0.1
UPPER_BOUND = 12.1
LANES = 128
CORES = 2
CODE_LIMIT = 32767.0
FACTOR_UNIT = 8192.0
LOWEST_EXPONENT = -120.0
TINY = 1e-37
HEADER_ROWS = 16


def split_constant(matrix):
    high = matrix.astype(ml_dtypes.bfloat16)
    low = (matrix - high.astype(np.float64)).astype(ml_dtypes.bfloat16)
    return high, low


def sine_basis(side):
    index = np.arange(1, side + 1, dtype=np.float64)
    return np.sqrt(2.0 / (side + 1)) * np.sin(np.pi * np.outer(index, index) / (side + 1))


def chebyshev_gain(side):
    shifts = -2.0 * np.cos(np.pi * np.arange(1, side + 1, dtype=np.float64) / (side + 1))
    eigenvalue = 6.0 + SCREEN + shifts[:, None, None] + shifts[None, :, None] + shifts[None, None, :]
    middle = (UPPER_BOUND + LOWER_BOUND) / 2.0
    spread = (UPPER_BOUND - LOWER_BOUND) / 2.0
    ratio = middle / spread
    total = np.zeros_like(eigenvalue)
    residual = np.ones_like(eigenvalue)
    direction = residual / middle
    factor = 1.0 / ratio
    for _ in range(STEPS):
        total = total + direction
        residual = residual - eigenvalue * direction
        factor_next = 1.0 / (2.0 * ratio - factor)
        direction = factor_next * factor * direction + 2.0 * factor_next / spread * residual
        factor = factor_next
    return total.reshape(side, side * side).astype(np.float32)


def split_pair(value):
    high = value.astype(jnp.bfloat16)
    low = (value - high.astype(jnp.float32)).astype(jnp.bfloat16)
    return high, low


def dot(left, right):
    return jnp.dot(left, right, preferred_element_type=jnp.float32)


def partner_of(index, step, count):
    if count & (count - 1) == 0:
        return index ^ step, index ^ step
    return (index + step) % count, (index + count - step) % count


def piece_places(pair_index, pair_count):
    chips = pair_count // CORES
    chip = pair_index // CORES
    for core_step in range(CORES):
        for chip_step in range(chips):
            yield (chip + chips - chip_step) % chips * CORES + (pair_index + core_step) % CORES


def force_kernel(sizes, match_ref, centers_ref, *refs):
    slab_count, pair_count = sizes[3:]
    block_refs, refs = refs[:pair_count], refs[pair_count:]
    constant_refs, refs = refs[:6], refs[6:]
    out_refs, scratch = refs[:slab_count], refs[slab_count:]
    force_body(sizes, match_ref, centers_ref, block_refs, constant_refs, out_refs, *scratch)


def force_body(
    sizes,
    match_hbm,
    centers_hbm,
    block_refs,
    constant_refs,
    out_refs,
    match_ref,
    centers_ref,
    boxes_ref,
    mix_ref,
    gain_ref,
    there_high,
    there_low,
    back_high,
    back_low,
    fields,
    partner,
    first,
    second,
    terms,
    total,
    sems,
):
    side, rounds, own_count, slab_count, pair_count = sizes
    planes = side // slab_count
    tiles = side * side // LANES
    lines = LANES // side
    pitch = side + 2 * REACH
    solves = own_count * rounds
    group = min(solves, 8)
    group_rows = group * side
    cells = tiles * LANES
    width = 2 * LANES
    slab_index = lax.axis_index("slab")
    pair_index = lax.axis_index("pair")

    sources = [match_hbm, centers_hbm, *block_refs]
    targets = [match_ref, centers_ref]
    targets += [boxes_ref.at[pair] for pair in piece_places(pair_index, pair_count)]
    copies = []
    for source, target in zip(sources, targets):
        copies.append(pltpu.make_async_copy(source, target, sems.at[len(copies)]))
    constants = (mix_ref, gain_ref, there_high, there_low, back_high, back_low)
    constant_copies = []
    for index, (source, target) in enumerate(zip(constant_refs, constants)):
        constant_copies.append(pltpu.make_async_copy(source, target, sems.at[len(copies) + index]))
    for copy in copies + constant_copies:
        copy.start()

    zeros = jnp.zeros((REACH, LANES), jnp.float32)

    def clear(index, carry):
        fields[pl.ds(pl.multiple_of(index * pitch, 8), REACH), :] = zeros
        fields[pl.ds(pl.multiple_of(index * pitch + REACH + side, 8), REACH), :] = zeros
        return carry

    lax.fori_loop(0, pair_count * own_count * tiles, clear, 0, unroll=8)

    def clear_terms(index, carry):
        terms[pl.ds(pl.multiple_of(index * pitch, 8), REACH), :] = zeros
        terms[pl.ds(pl.multiple_of(index * pitch + REACH + side, 8), REACH), :] = zeros
        return carry

    lax.fori_loop(0, solves * tiles, clear_terms, 0, unroll=8)

    for copy in copies:
        copy.wait()

    def spread(index, carry):
        pair = index // slab_count
        slab = index % slab_count
        for chunk in range(own_count * planes // 2):
            block = boxes_ref[pair, slab, 16 * chunk : 16 * chunk + 16, :].astype(jnp.float32)
            for half in range(2):
                own, plane = divmod(2 * chunk + half, planes)
                start = (pair * own_count + own) * tiles * pitch + REACH + slab * planes + plane
                fields[pl.ds(start, tiles, stride=pitch), :] = block[8 * half : 8 * half + 8, :]
        return carry

    lax.fori_loop(0, pair_count * slab_count, spread, 0)

    step_rows = 16
    lane = lax.broadcasted_iota(jnp.int32, (step_rows, LANES), 1)
    lane_row = lax.broadcasted_iota(jnp.int32, (1, LANES), 1)
    lane_line = lane_row // side
    lane_point = lane_row % side

    def rolled(ref, base, row, offset_x, offset_flat):
        whole = (offset_flat >> 7) & (tiles - 1)
        part = offset_flat & (LANES - 1)
        start = base * pitch + REACH + row - offset_x
        moved = []
        for tile in range(tiles):
            first_row = start + ((tile - whole) & (tiles - 1)) * pitch
            moved.append(pltpu.roll(ref[pl.ds(first_row, step_rows), :], part, axis=1))
        keep = lane >= part
        return [jnp.where(keep, moved[t], moved[(t - 1) % tiles]) for t in range(tiles)]

    def mirrored(tile):
        line = lax.broadcasted_iota(jnp.int32, tile.shape, 1) // side
        result = None
        for index in range(lines):
            amount = (2 * index - lines + 1) * side % LANES
            if index < 2:
                moved = pltpu.roll(tile, amount, axis=1)
                result = moved if result is None else jnp.where(line % 2 == index, moved, result)
        return result

    def orbital_of(member):
        return (member // own_count * slab_count + slab_index) * own_count + member % own_count

    def geometry(index):
        own = index // rounds
        turn = index % rounds
        member = pair_index * own_count + own
        mate = match_ref[0, turn, member]
        own_offset = []
        mate_offset = []
        distance = 0
        for axis in range(3):
            mine = centers_ref[axis, orbital_of(member)]
            other = centers_ref[axis, orbital_of(mate)]
            anchor = (mine + other) >> 1
            own_offset.append(mine - anchor)
            mate_offset.append(other - anchor)
            distance = distance + (mine - other) * (mine - other)
        return own, member, mate, own_offset, mate_offset, distance <= CUT2

    row_count = solves * side
    half_tiles = tiles // 2
    half_cells = cells // 2

    def store_split(ref, start, count, columns, value):
        high, low = split_pair(value)
        if isinstance(start, int):
            ref[start : start + count, columns] = high
            ref[row_count + start : row_count + start + count, columns] = low
        else:
            ref[pl.ds(pl.multiple_of(start, count), count), columns] = high
            ref[pl.ds(pl.multiple_of(row_count + start, count), count), columns] = low

    def densities(step, carry):
        index = step // (side // step_rows)
        row = step % (side // step_rows) * step_rows
        own, member, mate, a, b, active = geometry(index)
        mine = rolled(fields, member * tiles, row, a[0], a[1] * side + a[2])
        other = rolled(fields, mate * tiles, row, b[0], b[1] * side + b[2])
        low_line = jnp.maximum(jnp.maximum(a[1], b[1]), 0)
        high_line = jnp.where(active, side + jnp.minimum(jnp.minimum(a[1], b[1]), 0), 0)
        low_point = jnp.maximum(jnp.maximum(a[2], b[2]), 0)
        high_point = side + jnp.minimum(jnp.minimum(a[2], b[2]), 0)
        point_ok = (lane_point >= low_point) & (lane_point < high_point)
        start = step * step_rows
        rows = pl.ds(pl.multiple_of(start, step_rows), step_rows)
        density = []
        for tile in range(tiles):
            line = lane_line + tile * lines
            ok = jnp.where(point_ok & (line >= low_line) & (line < high_line), 1.0, 0.0)
            masked = other[tile] * ok
            partner[rows, tile * LANES : (tile + 1) * LANES] = masked.astype(jnp.bfloat16)
            density.append(mine[tile] * masked)
        for tile in range(half_tiles):
            mirror = mirrored(density[tiles - 1 - tile])
            for parity, value in enumerate((density[tile] + mirror, density[tile] - mirror)):
                column = parity * half_cells + tile * LANES
                store_split(first, start, step_rows, slice(column, column + LANES), value)
        return carry

    lax.fori_loop(0, solves * side // step_rows, densities, 0, unroll=2)

    for copy in constant_copies:
        copy.wait()

    def along_x(start, columns, source):
        high = source[start : start + group_rows, columns]
        low = source[row_count + start : row_count + start + group_rows, columns]
        return dot(mix_ref[...], jnp.concatenate([high, low, high], axis=0))

    def in_plane(parity, columns, source, high_ref, low_ref):
        inner = slice(parity * half_cells, (parity + 1) * half_cells)
        high = source[:row_count, inner]
        low = source[row_count:, inner]
        basis = high_ref[parity, :, columns]
        rest = low_ref[parity, :, columns]
        left = jnp.concatenate([high, low, high], axis=1)
        return dot(left, jnp.concatenate([basis, basis, rest], axis=0))

    for start in range(0, row_count, group_rows):
        for column in range(0, cells, width):
            columns = slice(column, column + width)
            store_split(second, start, group_rows, columns, along_x(start, columns, first))

    for parity in range(2):
        for column in range(0, half_cells, width):
            columns = slice(column, column + width)
            value = in_plane(parity, columns, second, there_high, there_low)
            columns = slice(parity * half_cells + column, parity * half_cells + column + width)
            gain = gain_ref[:, columns]
            value = (value.reshape(solves, side, width) * gain[None]).reshape(row_count, width)
            store_split(first, 0, row_count, columns, value)

    for parity in range(2):
        for column in range(0, half_cells, width):
            value = in_plane(parity, slice(column, column + width), first, back_high, back_low)
            columns = slice(parity * half_cells + column, parity * half_cells + column + width)
            store_split(second, 0, row_count, columns, value)

    for start in range(0, row_count, group_rows):
        for column in range(0, half_cells, width):
            even = along_x(start, slice(column, column + width), second)
            odd = along_x(start, slice(half_cells + column, half_cells + column + width), second)
            for part in range(width // LANES):
                tile = column // LANES + part
                lanes = slice(part * LANES, (part + 1) * LANES)
                near = even[:, lanes] + odd[:, lanes]
                far = mirrored(even[:, lanes] - odd[:, lanes])
                for place, value in ((tile, near), (tiles - 1 - tile, far)):
                    columns = slice(place * LANES, (place + 1) * LANES)
                    value = value * partner[start : start + group_rows, columns].astype(jnp.float32)
                    for solve in range(group):
                        row = ((start // side + solve) * tiles + place) * pitch + REACH
                        terms[row : row + side, :] = value[solve * side : (solve + 1) * side, :]

    def collect(step, carry):
        own = step // (side // step_rows)
        row = step % (side // step_rows) * step_rows
        sums = None
        for turn in range(rounds):
            index = own * rounds + turn
            _, _, _, a, _, _ = geometry(index)
            term = rolled(terms, index * tiles, row, -a[0], -(a[1] * side + a[2]))
            sums = term if sums is None else [s + t for s, t in zip(sums, term)]
        for tile in range(tiles):
            start = (own * tiles + tile) * side + row
            total[pl.ds(pl.multiple_of(start, step_rows), step_rows), :] = sums[tile]
        return carry

    lax.fori_loop(0, own_count * side // step_rows, collect, 0)

    lane_index = lax.broadcasted_iota(jnp.int32, (tiles, LANES), 1)
    for step in range(slab_count):
        slab = partner_of(slab_index, step, slab_count)[0]
        exponents = jnp.zeros((tiles, LANES), jnp.float32)
        factors = jnp.zeros((tiles, LANES), jnp.float32)
        codes = []
        for chunk in range(own_count * planes):
            own, plane = divmod(chunk, planes)
            start = own * tiles * side + slab * planes + plane
            value = total[pl.ds(start, tiles, stride=side), :]
            code, exponent, factor = encode(value)
            codes.append(code)
            exponents = jnp.where(lane_index == chunk, exponent, exponents)
            factors = jnp.where(lane_index == chunk, factor, factors)
            if chunk % 2:
                pair = jnp.concatenate(codes[-2:], axis=0)
                out_refs[step][tiles * (chunk - 1) : tiles * (chunk + 1), :] = whole_codes(pair)
        header = jnp.concatenate([exponents, factors], axis=0)
        out_refs[step][tiles * own_count * planes :, :] = whole_codes(header)


def whole_codes(value):
    return value.astype(jnp.int32).astype(jnp.int16)


def encode(value):
    largest = jnp.max(jnp.abs(value), axis=1, keepdims=True)
    exponent = jnp.maximum(jnp.floor(jnp.log2(jnp.maximum(largest, TINY))), LOWEST_EXPONENT)
    lifted = 1.0 / jnp.exp2(exponent)
    factor = jnp.maximum(jnp.ceil(largest * lifted * FACTOR_UNIT), 1.0)
    code = jnp.floor(value * lifted * (CODE_LIMIT * FACTOR_UNIT / factor) + 0.5)
    return jnp.clip(code, -CODE_LIMIT, CODE_LIMIT), exponent, factor


def gather_boxes(boxes, pair_count):
    pieces = [boxes]
    for step in range(1, pair_count // CORES):
        perm = [(i, (i + step * CORES) % pair_count) for i in range(pair_count)]
        pieces.append(lax.ppermute(boxes, "pair", perm))
    swap = [(i, i ^ 1) for i in range(pair_count)]
    return pieces + [lax.ppermute(piece, "pair", swap) for piece in pieces]


def unpack_kernel(sizes, *refs):
    own_count, slab_count, tiles = sizes
    block_refs, out_ref, blocks, sems = refs[:slab_count], *refs[slab_count:]
    slab_index = lax.axis_index("slab")
    copies = []
    for index in range(slab_count):
        copies.append(pltpu.make_async_copy(block_refs[index], blocks.at[index], sems.at[index]))
        copies[-1].start()
    for index in reversed(range(slab_count)):
        step = slab_count - 1 - index
        copies[index].wait()
        first = partner_of(slab_index, step, slab_count)[1] * own_count
        row_count = own_count * tiles
        header = blocks[index, row_count:, :].astype(jnp.int32).astype(jnp.float32)
        units = jnp.exp2(header[:8, :])
        factors = header[8:, :] * (1.0 / (CODE_LIMIT * FACTOR_UNIT))
        for pair in range(row_count // 16):
            codes = blocks[index, 16 * pair : 16 * pair + 16, :].astype(jnp.int32).astype(jnp.float32)
            for half in range(2):
                chunk = 2 * pair + half
                own, tile = divmod(8 * chunk, tiles)
                row = first + own
                start = (row // 8 * tiles + tile) * 8 + row % 8
                value = codes[8 * half : 8 * half + 8, :] * factors[:, chunk : chunk + 1]
                out_ref[pl.ds(start, 8, stride=8), :] = value * units[:, chunk : chunk + 1]


def unpack(blocks, own_count, cells):
    slab_count = len(blocks)
    row_count = own_count * slab_count
    tiles = cells // LANES
    out = pl.pallas_call(
        functools.partial(unpack_kernel, (own_count, slab_count, tiles)),
        out_shape=jax.ShapeDtypeStruct((row_count * tiles, LANES), jnp.float32),
        in_specs=[pl.BlockSpec(memory_space=pl.ANY)] * slab_count,
        out_specs=pl.BlockSpec(memory_space=pltpu.VMEM),
        scratch_shapes=[
            pltpu.VMEM((slab_count,) + blocks[0].shape, jnp.int16),
            pltpu.SemaphoreType.DMA((slab_count,)),
        ],
    )(*blocks)
    return out.reshape(row_count // 8, tiles, 8, LANES).transpose(0, 2, 1, 3).reshape(row_count, cells)


def team_forces(match, centers, blocks, side, slab_count, pair_count):
    _, rounds, team = match.shape
    own_count = team // pair_count
    rows = own_count * side * side // LANES * (side // slab_count)
    tiles = side * side // LANES
    solves = own_count * rounds
    group = min(solves, 8)
    cells = side * side
    pitch = side + 2 * REACH
    basis = sine_basis(side)
    mix_high, mix_low = split_constant(np.kron(np.eye(group), basis))
    mix = np.concatenate([mix_high, mix_high, mix_low], axis=1)
    there = np.stack([np.kron(basis[parity::2, : side // 2].T, basis) for parity in range(2)])
    gain = chebyshev_gain(side).reshape(side, side, side)
    gain = np.concatenate([gain[:, parity::2].reshape(side, -1) for parity in range(2)], axis=1)
    constants = (mix, gain, *split_constant(there), *split_constant(there.transpose(0, 2, 1)))
    sizes = (side, rounds, own_count, slab_count, pair_count)
    either = pl.BlockSpec(memory_space=pl.ANY)
    distant = pl.BlockSpec(memory_space=pltpu.HBM)
    vectors = pl.BlockSpec(memory_space=pltpu.VMEM)
    wide = pltpu.VMEM((2 * solves * side, cells), jnp.bfloat16)
    flops = 2 * solves * side * 3 * 2 * (cells * cells // 2 + cells * group * side)
    return pl.pallas_call(
        functools.partial(force_kernel, sizes),
        out_shape=[jax.ShapeDtypeStruct((rows + HEADER_ROWS, LANES), jnp.int16)] * slab_count,
        in_specs=[distant] * 2 + [either] * len(blocks) + [distant] * len(constants),
        out_specs=[vectors] * slab_count,
        scratch_shapes=[
            pltpu.SMEM(match.shape, jnp.int32),
            pltpu.SMEM(centers.shape, jnp.int32),
            pltpu.VMEM((pair_count, slab_count, rows, LANES), jnp.bfloat16),
            *[pltpu.VMEM(constant.shape, constant.dtype) for constant in constants],
            pltpu.VMEM((team * tiles * pitch, LANES), jnp.float32),
            pltpu.VMEM((solves * side, cells), jnp.bfloat16),
            wide,
            wide,
            pltpu.VMEM((solves * tiles * pitch, LANES), jnp.float32),
            pltpu.VMEM((own_count * tiles * side, LANES), jnp.float32),
            pltpu.SemaphoreType.DMA((pair_count + 2 + len(constants),)),
        ],
        compiler_params=pltpu.CompilerParams(vmem_limit_bytes=60 * 1024 * 1024),
        cost_estimate=pl.CostEstimate(flops=flops, bytes_accessed=8 * 1024 * 1024, transcendentals=0),
    )(
        match,
        centers,
        *blocks,
        *[jnp.asarray(constant) for constant in constants],
    )


def shards(orbitals, centers, matchings):
    slab_count = lax.axis_size("slab")
    pair_count = lax.axis_size("pair")
    local_rows, plane_cells = orbitals.shape
    own_count = local_rows // slab_count
    side = round((plane_cells * slab_count) ** (1.0 / 3.0))
    blocks = orbitals.reshape(slab_count, own_count * plane_cells // LANES, LANES)
    boxes = lax.all_to_all(blocks, "slab", split_axis=0, concat_axis=0, tiled=True)
    pieces = gather_boxes(boxes, pair_count)
    codes = team_forces(matchings, centers.T, pieces, side, slab_count, pair_count)
    received = []
    for step in reversed(range(1, slab_count)):
        perm = [(i, partner_of(i, step, slab_count)[0]) for i in range(slab_count)]
        received.append(lax.ppermute(codes[step], "slab", perm))
    return unpack(received + [codes[0]], own_count, plane_cells)


def solution(mesh):
    in_specs = (P("pair", "slab"), P(), P("slab", None, None))
    out_specs = P("pair", "slab")
    return jax.shard_map(shards, mesh=mesh, in_specs=in_specs, out_specs=out_specs, check_vma=False)
```

```python
import functools

import jax
import jax.numpy as jnp
import ml_dtypes
import numpy as np
from jax import lax
from jax.experimental import pallas as pl
from jax.experimental.pallas import tpu as pltpu
from jax.sharding import PartitionSpec as P

STEPS = 16
CUT2 = 192
REACH = 8
SCREEN = 0.1
LOWER_BOUND = 0.1
UPPER_BOUND = 12.1
LANES = 128
CORES = 2
CODE_LIMIT = 32767.0
FACTOR_UNIT = 8192.0
LOWEST_EXPONENT = -120.0
TINY = 1e-37
HEADER_ROWS = 16


def split_constant(matrix):
    high = matrix.astype(ml_dtypes.bfloat16)
    low = (matrix - high.astype(np.float64)).astype(ml_dtypes.bfloat16)
    return high, low


def sine_basis(side):
    index = np.arange(1, side + 1, dtype=np.float64)
    return np.sqrt(2.0 / (side + 1)) * np.sin(np.pi * np.outer(index, index) / (side + 1))


def chebyshev_gain(side):
    shifts = -2.0 * np.cos(np.pi * np.arange(1, side + 1, dtype=np.float64) / (side + 1))
    eigenvalue = 6.0 + SCREEN + shifts[:, None, None] + shifts[None, :, None] + shifts[None, None, :]
    middle = (UPPER_BOUND + LOWER_BOUND) / 2.0
    spread = (UPPER_BOUND - LOWER_BOUND) / 2.0
    ratio = middle / spread
    total = np.zeros_like(eigenvalue)
    residual = np.ones_like(eigenvalue)
    direction = residual / middle
    factor = 1.0 / ratio
    for _ in range(STEPS):
        total = total + direction
        residual = residual - eigenvalue * direction
        factor_next = 1.0 / (2.0 * ratio - factor)
        direction = factor_next * factor * direction + 2.0 * factor_next / spread * residual
        factor = factor_next
    return total.reshape(side, side * side).astype(np.float32)


def split_pair(value):
    high = value.astype(jnp.bfloat16)
    low = (value - high.astype(jnp.float32)).astype(jnp.bfloat16)
    return high, low


def dot(left, right):
    return jnp.dot(left, right, preferred_element_type=jnp.float32)


def partner_of(index, step, count):
    if count & (count - 1) == 0:
        return index ^ step, index ^ step
    return (index + step) % count, (index + count - step) % count


def pair_geometry(sizes, match_ref, centers_ref, index):
    _, rounds, own_count, slab_count, _ = sizes
    slab_index = lax.axis_index("slab")
    pair_index = lax.axis_index("pair")

    def orbital_of(member):
        return (member // own_count * slab_count + slab_index) * own_count + member % own_count

    member = pair_index * own_count + index // rounds
    mate = match_ref[0, index % rounds, member]
    own_offset = []
    mate_offset = []
    distance = 0
    for axis in range(3):
        mine = centers_ref[axis, orbital_of(member)]
        other = centers_ref[axis, orbital_of(mate)]
        anchor = (mine + other) >> 1
        own_offset.append(mine - anchor)
        mate_offset.append(other - anchor)
        distance = distance + (mine - other) * (mine - other)
    return member, mate, own_offset, mate_offset, distance <= CUT2


def box_shape(sizes):
    side = sizes[0]
    return side * side // LANES, LANES // side, side + 2 * REACH


def clear_edges(sizes, ref, first, count):
    side = sizes[0]
    tiles, _, pitch = box_shape(sizes)
    zeros = jnp.zeros((REACH, LANES), jnp.float32)

    def clear(index, carry):
        start = (first * tiles + index) * pitch
        ref[pl.ds(pl.multiple_of(start, 8), REACH), :] = zeros
        ref[pl.ds(pl.multiple_of(start + REACH + side, 8), REACH), :] = zeros
        return carry

    lax.fori_loop(0, count * tiles, clear, 0, unroll=8)


def spread(sizes, boxes_ref, fields, pair):
    side, _, own_count, slab_count, _ = sizes
    planes = side // slab_count
    tiles, _, pitch = box_shape(sizes)

    def spread_slab(slab, carry):
        for chunk in range(own_count * planes // 2):
            block = boxes_ref[pair, slab, 16 * chunk : 16 * chunk + 16, :].astype(jnp.float32)
            for half in range(2):
                own, plane = divmod(2 * chunk + half, planes)
                start = (pair * own_count + own) * tiles * pitch + REACH + slab * planes + plane
                fields[pl.ds(start, tiles, stride=pitch), :] = block[8 * half : 8 * half + 8, :]
        return carry

    lax.fori_loop(0, slab_count, spread_slab, 0)


def rolled(sizes, ref, box, row, rows, offset_x, offset_flat):
    tiles, _, pitch = box_shape(sizes)
    whole = (offset_flat >> 7) & (tiles - 1)
    part = offset_flat & (LANES - 1)
    start = box * tiles * pitch + REACH + row - offset_x
    moved = []
    for tile in range(tiles):
        first_row = start + ((tile - whole) & (tiles - 1)) * pitch
        moved.append(pltpu.roll(ref[pl.ds(first_row, rows), :], part, axis=1))
    keep = lax.broadcasted_iota(jnp.int32, (rows, LANES), 1) >= part
    return [jnp.where(keep, moved[t], moved[(t - 1) % tiles]) for t in range(tiles)]


def place_partner(sizes, fields, box, own_offset, offset, active, out_ref, rows):
    side = sizes[0]
    tiles, lines, _ = box_shape(sizes)
    placed = rolled(sizes, fields, box, 0, side, offset[0], offset[1] * side + offset[2])
    lane = lax.broadcasted_iota(jnp.int32, (1, LANES), 1)
    lows = [jnp.maximum(jnp.maximum(a, b), 0) for a, b in zip(own_offset, offset)]
    highs = [side + jnp.minimum(jnp.minimum(a, b), 0) for a, b in zip(own_offset, offset)]
    point_ok = (lane % side >= lows[2]) & (lane % side < highs[2]) & active
    for tile in range(tiles):
        line = lane // side + tile * lines
        ok = jnp.where(point_ok & (line >= lows[1]) & (line < highs[1]), 1.0, 0.0)
        out_ref[rows, tile * LANES : (tile + 1) * LANES] = (placed[tile] * ok).astype(jnp.bfloat16)


def near_kernel(
    sizes, match_hbm, centers_hbm, own_hbm, other_hbm, mine_ref, partner_ref, match_ref, centers_ref, boxes_ref, fields, sems
):
    side, rounds, own_count, _, _ = sizes
    tiles, _, _ = box_shape(sizes)
    pair_index = lax.axis_index("pair")
    core = pair_index % CORES
    first_member = pair_index // CORES * CORES * own_count
    sources = (match_hbm, centers_hbm, own_hbm, other_hbm)
    targets = (match_ref, centers_ref, boxes_ref.at[core], boxes_ref.at[1 - core])
    copies = [pltpu.make_async_copy(s, t, sems.at[i]) for i, (s, t) in enumerate(zip(sources, targets))]
    for copy in copies:
        copy.start()
    clear_edges(sizes, fields, 0, CORES * own_count)
    for copy in copies:
        copy.wait()
    for pair in range(CORES):
        spread(sizes, boxes_ref, fields, pair)

    def place(index, carry):
        member, mate, a, b, active = pair_geometry(sizes, match_ref, centers_ref, index)
        rows = pl.ds(pl.multiple_of(index * side, side), side)
        placed = rolled(sizes, fields, member - first_member, 0, side, a[0], a[1] * side + a[2])
        for tile in range(tiles):
            mine_ref[rows, tile * LANES : (tile + 1) * LANES] = placed[tile].astype(jnp.bfloat16)
        local = mate - first_member

        @pl.when((local >= 0) & (local < CORES * own_count))
        def _():
            place_partner(sizes, fields, local, a, b, active, partner_ref, rows)

        return carry

    lax.fori_loop(0, own_count * rounds, place, 0)


def force_kernel(sizes, match_hbm, centers_hbm, mine_hbm, partner_hbm, *refs):
    side, rounds, own_count, slab_count, pair_count = sizes
    piece_hbm, refs = refs[: pair_count - CORES], refs[pair_count - CORES :]
    constant_hbm, refs = refs[:6], refs[6:]
    out_refs, refs = refs[:slab_count], refs[slab_count:]
    match_ref, centers_ref, mine, partner, boxes_ref, *refs = refs
    constants, refs = refs[:6], refs[6:]
    mix_ref, gain_ref, there_high, there_low, back_high, back_low = constants
    fields, first, second, terms, total, sems = refs
    planes = side // slab_count
    tiles, lines, pitch = box_shape(sizes)
    solves = own_count * rounds
    group = min(solves, 8)
    group_rows = group * side
    cells = tiles * LANES
    width = 2 * LANES
    slab_index = lax.axis_index("slab")
    pair_index = lax.axis_index("pair")
    core = pair_index % CORES
    chip = pair_index // CORES
    chips = pair_count // CORES
    first_member = chip * CORES * own_count

    places = [
        (chip + chips - step) % chips * CORES + (core + core_step) % CORES
        for core_step in range(CORES)
        for step in range(1, chips)
    ]
    sources = [match_hbm, centers_hbm, *piece_hbm, mine_hbm, partner_hbm, *constant_hbm]
    targets = [match_ref, centers_ref, *[boxes_ref.at[pair] for pair in places], mine, partner, *constants]
    copies = [pltpu.make_async_copy(s, t, sems.at[i]) for i, (s, t) in enumerate(zip(sources, targets))]
    for copy in copies:
        copy.start()
    for pair in places:
        clear_edges(sizes, fields, pair * own_count, own_count)
    clear_edges(sizes, terms, 0, solves)
    boxes_count = 2 + len(places)
    for copy in copies[:boxes_count]:
        copy.wait()
    for pair in places:
        spread(sizes, boxes_ref, fields, pair)
    for copy in copies[boxes_count : boxes_count + 2]:
        copy.wait()

    def place(index, carry):
        _, mate, a, b, active = pair_geometry(sizes, match_ref, centers_ref, index)
        local = mate - first_member

        @pl.when((local < 0) | (local >= CORES * own_count))
        def _():
            rows = pl.ds(pl.multiple_of(index * side, side), side)
            place_partner(sizes, fields, mate, a, b, active, partner, rows)

        return carry

    lax.fori_loop(0, solves, place, 0)

    row_count = solves * side
    half_tiles = tiles // 2
    half_cells = cells // 2

    def mirrored(tile):
        line = lax.broadcasted_iota(jnp.int32, tile.shape, 1) // side
        result = None
        for index in range(lines):
            amount = (2 * index - lines + 1) * side % LANES
            if index < 2:
                moved = pltpu.roll(tile, amount, axis=1)
                result = moved if result is None else jnp.where(line % 2 == index, moved, result)
        return result

    def store_split(ref, start, count, columns, value):
        high, low = split_pair(value)
        if isinstance(start, int):
            ref[start : start + count, columns] = high
            ref[row_count + start : row_count + start + count, columns] = low
        else:
            ref[pl.ds(pl.multiple_of(start, count), count), columns] = high
            ref[pl.ds(pl.multiple_of(row_count + start, count), count), columns] = low

    def densities(index, carry):
        start = index * side
        rows = pl.ds(pl.multiple_of(start, side), side)

        def density(tile):
            columns = slice(tile * LANES, (tile + 1) * LANES)
            return mine[rows, columns].astype(jnp.float32) * partner[rows, columns].astype(jnp.float32)

        for tile in range(half_tiles):
            near = density(tile)
            far = mirrored(density(tiles - 1 - tile))
            for parity, value in enumerate((near + far, near - far)):
                column = parity * half_cells + tile * LANES
                store_split(first, start, side, slice(column, column + LANES), value)
        return carry

    lax.fori_loop(0, solves, densities, 0, unroll=2)

    for copy in copies[boxes_count + 2 :]:
        copy.wait()

    def along_x(start, columns, source):
        high = source[start : start + group_rows, columns]
        low = source[row_count + start : row_count + start + group_rows, columns]
        return dot(mix_ref[...], jnp.concatenate([high, low, high], axis=0))

    def in_plane(parity, columns, source, high_ref, low_ref):
        inner = slice(parity * half_cells, (parity + 1) * half_cells)
        high = source[:row_count, inner]
        low = source[row_count:, inner]
        basis = high_ref[parity, :, columns]
        rest = low_ref[parity, :, columns]
        left = jnp.concatenate([high, low, high], axis=1)
        return dot(left, jnp.concatenate([basis, basis, rest], axis=0))

    for start in range(0, row_count, group_rows):
        for column in range(0, cells, width):
            columns = slice(column, column + width)
            store_split(second, start, group_rows, columns, along_x(start, columns, first))

    for parity in range(2):
        for column in range(0, half_cells, width):
            columns = slice(column, column + width)
            value = in_plane(parity, columns, second, there_high, there_low)
            columns = slice(parity * half_cells + column, parity * half_cells + column + width)
            gain = gain_ref[:, columns]
            value = (value.reshape(solves, side, width) * gain[None]).reshape(row_count, width)
            store_split(first, 0, row_count, columns, value)

    for parity in range(2):
        for column in range(0, half_cells, width):
            value = in_plane(parity, slice(column, column + width), first, back_high, back_low)
            columns = slice(parity * half_cells + column, parity * half_cells + column + width)
            store_split(second, 0, row_count, columns, value)

    for start in range(0, row_count, group_rows):
        for column in range(0, half_cells, width):
            even = along_x(start, slice(column, column + width), second)
            odd = along_x(start, slice(half_cells + column, half_cells + column + width), second)
            for part in range(width // LANES):
                tile = column // LANES + part
                lanes = slice(part * LANES, (part + 1) * LANES)
                near = even[:, lanes] + odd[:, lanes]
                far = mirrored(even[:, lanes] - odd[:, lanes])
                for place, value in ((tile, near), (tiles - 1 - tile, far)):
                    columns = slice(place * LANES, (place + 1) * LANES)
                    value = value * partner[start : start + group_rows, columns].astype(jnp.float32)
                    for solve in range(group):
                        row = ((start // side + solve) * tiles + place) * pitch + REACH
                        terms[row : row + side, :] = value[solve * side : (solve + 1) * side, :]

    step_rows = 16

    def collect(step, carry):
        own = step // (side // step_rows)
        row = step % (side // step_rows) * step_rows
        sums = None
        for turn in range(rounds):
            index = own * rounds + turn
            _, _, a, _, _ = pair_geometry(sizes, match_ref, centers_ref, index)
            term = rolled(sizes, terms, index, row, step_rows, -a[0], -(a[1] * side + a[2]))
            sums = term if sums is None else [s + t for s, t in zip(sums, term)]
        for tile in range(tiles):
            start = (own * tiles + tile) * side + row
            total[pl.ds(pl.multiple_of(start, step_rows), step_rows), :] = sums[tile]
        return carry

    lax.fori_loop(0, own_count * side // step_rows, collect, 0)

    lane_index = lax.broadcasted_iota(jnp.int32, (tiles, LANES), 1)
    for step in range(slab_count):
        slab = partner_of(slab_index, step, slab_count)[0]
        exponents = jnp.zeros((tiles, LANES), jnp.float32)
        factors = jnp.zeros((tiles, LANES), jnp.float32)
        codes = []
        for chunk in range(own_count * planes):
            own, plane = divmod(chunk, planes)
            start = own * tiles * side + slab * planes + plane
            value = total[pl.ds(start, tiles, stride=side), :]
            code, exponent, factor = encode(value)
            codes.append(code)
            exponents = jnp.where(lane_index == chunk, exponent, exponents)
            factors = jnp.where(lane_index == chunk, factor, factors)
            if chunk % 2:
                pair = jnp.concatenate(codes[-2:], axis=0)
                out_refs[step][tiles * (chunk - 1) : tiles * (chunk + 1), :] = whole_codes(pair)
        header = jnp.concatenate([exponents, factors], axis=0)
        out_refs[step][tiles * own_count * planes :, :] = whole_codes(header)


def whole_codes(value):
    return value.astype(jnp.int32).astype(jnp.int16)


def encode(value):
    largest = jnp.max(jnp.abs(value), axis=1, keepdims=True)
    exponent = jnp.maximum(jnp.floor(jnp.log2(jnp.maximum(largest, TINY))), LOWEST_EXPONENT)
    lifted = 1.0 / jnp.exp2(exponent)
    factor = jnp.maximum(jnp.ceil(largest * lifted * FACTOR_UNIT), 1.0)
    code = jnp.floor(value * lifted * (CODE_LIMIT * FACTOR_UNIT / factor) + 0.5)
    return jnp.clip(code, -CODE_LIMIT, CODE_LIMIT), exponent, factor


def swap_cores(block, pair_count):
    return lax.ppermute(block, "pair", [(i, i ^ 1) for i in range(pair_count)])


def gather_chips(boxes, pair_count):
    pieces = []
    for step in range(1, pair_count // CORES):
        perm = [(i, (i + step * CORES) % pair_count) for i in range(pair_count)]
        pieces.append(lax.ppermute(boxes, "pair", perm))
    return pieces


def unpack_kernel(sizes, *refs):
    own_count, slab_count, tiles = sizes
    block_refs, out_ref, blocks, sems = refs[:slab_count], *refs[slab_count:]
    slab_index = lax.axis_index("slab")
    copies = []
    for index in range(slab_count):
        copies.append(pltpu.make_async_copy(block_refs[index], blocks.at[index], sems.at[index]))
        copies[-1].start()
    for index in reversed(range(slab_count)):
        step = slab_count - 1 - index
        copies[index].wait()
        first = partner_of(slab_index, step, slab_count)[1] * own_count
        row_count = own_count * tiles
        header = blocks[index, row_count:, :].astype(jnp.int32).astype(jnp.float32)
        units = jnp.exp2(header[:8, :])
        factors = header[8:, :] * (1.0 / (CODE_LIMIT * FACTOR_UNIT))
        for pair in range(row_count // 16):
            codes = blocks[index, 16 * pair : 16 * pair + 16, :].astype(jnp.int32).astype(jnp.float32)
            for half in range(2):
                chunk = 2 * pair + half
                own, tile = divmod(8 * chunk, tiles)
                row = first + own
                start = (row // 8 * tiles + tile) * 8 + row % 8
                value = codes[8 * half : 8 * half + 8, :] * factors[:, chunk : chunk + 1]
                out_ref[pl.ds(start, 8, stride=8), :] = value * units[:, chunk : chunk + 1]


def unpack(blocks, own_count, cells):
    slab_count = len(blocks)
    row_count = own_count * slab_count
    tiles = cells // LANES
    out = pl.pallas_call(
        functools.partial(unpack_kernel, (own_count, slab_count, tiles)),
        out_shape=jax.ShapeDtypeStruct((row_count * tiles, LANES), jnp.float32),
        in_specs=[pl.BlockSpec(memory_space=pl.ANY)] * slab_count,
        out_specs=pl.BlockSpec(memory_space=pltpu.VMEM),
        scratch_shapes=[
            pltpu.VMEM((slab_count,) + blocks[0].shape, jnp.int16),
            pltpu.SemaphoreType.DMA((slab_count,)),
        ],
        compiler_params=pltpu.CompilerParams(vmem_limit_bytes=8 * 1024 * 1024),
    )(*blocks)
    return out.reshape(row_count // 8, tiles, 8, LANES).transpose(0, 2, 1, 3).reshape(row_count, cells)


def place_near(sizes, match, centers, boxes, other):
    side, rounds, own_count, slab_count, _ = sizes
    tiles, _, pitch = box_shape(sizes)
    placed = (own_count * rounds * side, side * side)
    either = pl.BlockSpec(memory_space=pl.ANY)
    vectors = pl.BlockSpec(memory_space=pltpu.VMEM)
    return pl.pallas_call(
        functools.partial(near_kernel, sizes),
        out_shape=[jax.ShapeDtypeStruct(placed, jnp.bfloat16)] * 2,
        in_specs=[either] * 4,
        out_specs=[vectors] * 2,
        scratch_shapes=[
            pltpu.SMEM(match.shape, jnp.int32),
            pltpu.SMEM(centers.shape, jnp.int32),
            pltpu.VMEM((CORES,) + boxes.shape, jnp.bfloat16),
            pltpu.VMEM((CORES * own_count * tiles * pitch, LANES), jnp.float32),
            pltpu.SemaphoreType.DMA((4,)),
        ],
        compiler_params=pltpu.CompilerParams(vmem_limit_bytes=32 * 1024 * 1024),
        cost_estimate=pl.CostEstimate(flops=5 * 10**9, bytes_accessed=4 * 1024 * 1024, transcendentals=0),
    )(match, centers, boxes, other)


def team_forces(sizes, match, centers, mine, partner, pieces):
    side, rounds, own_count, slab_count, pair_count = sizes
    tiles, _, pitch = box_shape(sizes)
    _, rows, _ = pieces[0].shape
    solves = own_count * rounds
    group = min(solves, 8)
    cells = side * side
    basis = sine_basis(side)
    mix_high, mix_low = split_constant(np.kron(np.eye(group), basis))
    mix = np.concatenate([mix_high, mix_high, mix_low], axis=1)
    there = np.stack([np.kron(basis[parity::2, : side // 2].T, basis) for parity in range(2)])
    gain = chebyshev_gain(side).reshape(side, side, side)
    gain = np.concatenate([gain[:, parity::2].reshape(side, -1) for parity in range(2)], axis=1)
    constants = (mix, gain, *split_constant(there), *split_constant(there.transpose(0, 2, 1)))
    either = pl.BlockSpec(memory_space=pl.ANY)
    distant = pl.BlockSpec(memory_space=pltpu.HBM)
    vectors = pl.BlockSpec(memory_space=pltpu.VMEM)
    wide = pltpu.VMEM((2 * solves * side, cells), jnp.bfloat16)
    flops = 2 * solves * side * 3 * 2 * (cells * cells // 2 + cells * group * side)
    inputs = [match, centers, mine, partner, *pieces, *[jnp.asarray(constant) for constant in constants]]
    return pl.pallas_call(
        functools.partial(force_kernel, sizes),
        out_shape=[jax.ShapeDtypeStruct((rows + HEADER_ROWS, LANES), jnp.int16)] * slab_count,
        in_specs=[distant] * 2 + [either] * (len(inputs) - 2 - len(constants)) + [distant] * len(constants),
        out_specs=[vectors] * slab_count,
        scratch_shapes=[
            pltpu.SMEM(match.shape, jnp.int32),
            pltpu.SMEM(centers.shape, jnp.int32),
            pltpu.VMEM(mine.shape, jnp.bfloat16),
            pltpu.VMEM(partner.shape, jnp.bfloat16),
            pltpu.VMEM((pair_count, slab_count, rows, LANES), jnp.bfloat16),
            *[pltpu.VMEM(constant.shape, constant.dtype) for constant in constants],
            pltpu.VMEM((own_count * pair_count * tiles * pitch, LANES), jnp.float32),
            wide,
            wide,
            pltpu.VMEM((solves * tiles * pitch, LANES), jnp.float32),
            pltpu.VMEM((own_count * tiles * side, LANES), jnp.float32),
            pltpu.SemaphoreType.DMA((len(inputs),)),
        ],
        compiler_params=pltpu.CompilerParams(vmem_limit_bytes=60 * 1024 * 1024),
        cost_estimate=pl.CostEstimate(flops=flops, bytes_accessed=8 * 1024 * 1024, transcendentals=0),
    )(*inputs)


def shards(orbitals, centers, matchings):
    slab_count = lax.axis_size("slab")
    pair_count = lax.axis_size("pair")
    local_rows, plane_cells = orbitals.shape
    own_count = local_rows // slab_count
    side = round((plane_cells * slab_count) ** (1.0 / 3.0))
    blocks = orbitals.reshape(slab_count, own_count * plane_cells // LANES, LANES)
    boxes = lax.all_to_all(blocks, "slab", split_axis=0, concat_axis=0, tiled=True)
    sizes = (side, matchings.shape[1], own_count, slab_count, pair_count)
    pieces = gather_chips(boxes, pair_count)
    mine, partner = place_near(sizes, matchings, centers.T, boxes, swap_cores(boxes, pair_count))
    pieces, mine, partner = lax.optimization_barrier((pieces, mine, partner))
    pieces = pieces + [swap_cores(piece, pair_count) for piece in pieces]
    codes = team_forces(sizes, matchings, centers.T, mine, partner, pieces)
    received = []
    for step in reversed(range(1, slab_count)):
        perm = [(i, partner_of(i, step, slab_count)[0]) for i in range(slab_count)]
        received.append(lax.ppermute(codes[step], "slab", perm))
    return unpack(received + [codes[0]], own_count, plane_cells)


def solution(mesh):
    in_specs = (P("pair", "slab"), P(), P("slab", None, None))
    out_specs = P("pair", "slab")
    return jax.shard_map(shards, mesh=mesh, in_specs=in_specs, out_specs=out_specs, check_vma=False)
```

```python
import functools

import jax
import jax.numpy as jnp
import ml_dtypes
import numpy as np
from jax import lax
from jax.experimental import pallas as pl
from jax.experimental.pallas import tpu as pltpu
from jax.sharding import PartitionSpec as P

STEPS = 16
CUT2 = 192
REACH = 8
SCREEN = 0.1
LOWER_BOUND = 0.1
UPPER_BOUND = 12.1
LANES = 128
CORES = 2
CODE_LIMIT = 32767.0
FACTOR_UNIT = 8192.0
LOWEST_EXPONENT = -120.0
TINY = 1e-37
HEADER_ROWS = 16


def split_constant(matrix):
    high = matrix.astype(ml_dtypes.bfloat16)
    low = (matrix - high.astype(np.float64)).astype(ml_dtypes.bfloat16)
    return high, low


def sine_basis(side):
    index = np.arange(1, side + 1, dtype=np.float64)
    return np.sqrt(2.0 / (side + 1)) * np.sin(np.pi * np.outer(index, index) / (side + 1))


def chebyshev_gain(side):
    shifts = -2.0 * np.cos(np.pi * np.arange(1, side + 1, dtype=np.float64) / (side + 1))
    eigenvalue = 6.0 + SCREEN + shifts[:, None, None] + shifts[None, :, None] + shifts[None, None, :]
    middle = (UPPER_BOUND + LOWER_BOUND) / 2.0
    spread = (UPPER_BOUND - LOWER_BOUND) / 2.0
    ratio = middle / spread
    total = np.zeros_like(eigenvalue)
    residual = np.ones_like(eigenvalue)
    direction = residual / middle
    factor = 1.0 / ratio
    for _ in range(STEPS):
        total = total + direction
        residual = residual - eigenvalue * direction
        factor_next = 1.0 / (2.0 * ratio - factor)
        direction = factor_next * factor * direction + 2.0 * factor_next / spread * residual
        factor = factor_next
    return total.reshape(side, side * side).astype(np.float32)


def split_pair(value):
    high = value.astype(jnp.bfloat16)
    low = (value - high.astype(jnp.float32)).astype(jnp.bfloat16)
    return high, low


def dot(left, right):
    return jnp.dot(left, right, preferred_element_type=jnp.float32)


def partner_of(index, step, count):
    if count & (count - 1) == 0:
        return index ^ step, index ^ step
    return (index + step) % count, (index + count - step) % count


def pair_geometry(sizes, match_ref, centers_ref, index):
    _, rounds, own_count, slab_count, _ = sizes
    slab_index = lax.axis_index("slab")
    pair_index = lax.axis_index("pair")

    def orbital_of(member):
        return (member // own_count * slab_count + slab_index) * own_count + member % own_count

    member = pair_index * own_count + index // rounds
    mate = match_ref[0, index % rounds, member]
    own_offset = []
    mate_offset = []
    distance = 0
    for axis in range(3):
        mine = centers_ref[axis, orbital_of(member)]
        other = centers_ref[axis, orbital_of(mate)]
        anchor = (mine + other) >> 1
        own_offset.append(mine - anchor)
        mate_offset.append(other - anchor)
        distance = distance + (mine - other) * (mine - other)
    return member, mate, own_offset, mate_offset, distance <= CUT2


def box_shape(sizes):
    side = sizes[0]
    return side * side // LANES, LANES // side, side + 2 * REACH


def clear_edges(sizes, ref, first, count):
    side = sizes[0]
    tiles, _, pitch = box_shape(sizes)
    zeros = jnp.zeros((REACH, LANES), jnp.float32)

    def clear(index, carry):
        start = (first * tiles + index) * pitch
        ref[pl.ds(pl.multiple_of(start, 8), REACH), :] = zeros
        ref[pl.ds(pl.multiple_of(start + REACH + side, 8), REACH), :] = zeros
        return carry

    lax.fori_loop(0, count * tiles, clear, 0, unroll=8)


def spread(sizes, boxes_ref, fields, pair):
    side, _, own_count, slab_count, _ = sizes
    planes = side // slab_count
    tiles, _, pitch = box_shape(sizes)

    def spread_slab(slab, carry):
        for chunk in range(own_count * planes // 2):
            block = boxes_ref[pair, slab, 16 * chunk : 16 * chunk + 16, :].astype(jnp.float32)
            for half in range(2):
                own, plane = divmod(2 * chunk + half, planes)
                start = (pair * own_count + own) * tiles * pitch + REACH + slab * planes + plane
                fields[pl.ds(start, tiles, stride=pitch), :] = block[8 * half : 8 * half + 8, :]
        return carry

    lax.fori_loop(0, slab_count, spread_slab, 0)


def rolled(sizes, ref, box, row, rows, offset_x, offset_flat):
    tiles, _, pitch = box_shape(sizes)
    whole = (offset_flat >> 7) & (tiles - 1)
    part = offset_flat & (LANES - 1)
    start = box * tiles * pitch + REACH + row - offset_x
    moved = []
    for tile in range(tiles):
        first_row = start + ((tile - whole) & (tiles - 1)) * pitch
        moved.append(pltpu.roll(ref[pl.ds(first_row, rows), :], part, axis=1))
    keep = lax.broadcasted_iota(jnp.int32, (rows, LANES), 1) >= part
    return [jnp.where(keep, moved[t], moved[(t - 1) % tiles]) for t in range(tiles)]


def place_partner(sizes, fields, box, own_offset, offset, active, out_ref, rows):
    side = sizes[0]
    tiles, lines, _ = box_shape(sizes)
    placed = rolled(sizes, fields, box, 0, side, offset[0], offset[1] * side + offset[2])
    lane = lax.broadcasted_iota(jnp.int32, (1, LANES), 1)
    lows = [jnp.maximum(jnp.maximum(a, b), 0) for a, b in zip(own_offset, offset)]
    highs = [side + jnp.minimum(jnp.minimum(a, b), 0) for a, b in zip(own_offset, offset)]
    point_ok = (lane % side >= lows[2]) & (lane % side < highs[2]) & active
    for tile in range(tiles):
        line = lane // side + tile * lines
        ok = jnp.where(point_ok & (line >= lows[1]) & (line < highs[1]), 1.0, 0.0)
        out_ref[rows, tile * LANES : (tile + 1) * LANES] = (placed[tile] * ok).astype(jnp.bfloat16)


def near_kernel(
    sizes, match_hbm, centers_hbm, own_hbm, other_hbm, mine_ref, partner_ref, match_ref, centers_ref, boxes_ref, fields, sems
):
    side, rounds, own_count, _, _ = sizes
    tiles, _, _ = box_shape(sizes)
    pair_index = lax.axis_index("pair")
    core = pair_index % CORES
    first_member = pair_index // CORES * CORES * own_count
    sources = (match_hbm, centers_hbm, own_hbm, other_hbm)
    targets = (match_ref, centers_ref, boxes_ref.at[core], boxes_ref.at[1 - core])
    copies = [pltpu.make_async_copy(s, t, sems.at[i]) for i, (s, t) in enumerate(zip(sources, targets))]
    for copy in copies:
        copy.start()
    clear_edges(sizes, fields, 0, CORES * own_count)
    for copy in copies:
        copy.wait()
    for pair in range(CORES):
        spread(sizes, boxes_ref, fields, pair)

    def place(index, carry):
        member, mate, a, b, active = pair_geometry(sizes, match_ref, centers_ref, index)
        rows = pl.ds(pl.multiple_of(index * side, side), side)
        placed = rolled(sizes, fields, member - first_member, 0, side, a[0], a[1] * side + a[2])
        for tile in range(tiles):
            mine_ref[rows, tile * LANES : (tile + 1) * LANES] = placed[tile].astype(jnp.bfloat16)
        local = mate - first_member

        @pl.when((local >= 0) & (local < CORES * own_count))
        def _():
            place_partner(sizes, fields, local, a, b, active, partner_ref, rows)

        return carry

    lax.fori_loop(0, own_count * rounds, place, 0)


def force_kernel(sizes, match_hbm, centers_hbm, mine_hbm, partner_hbm, *refs):
    side, rounds, own_count, slab_count, pair_count = sizes
    piece_hbm, refs = refs[: pair_count - CORES], refs[pair_count - CORES :]
    constant_hbm, refs = refs[:6], refs[6:]
    out_refs, refs = refs[:slab_count], refs[slab_count:]
    match_ref, centers_ref, mine, partner, boxes_ref, *refs = refs
    constants, refs = refs[:6], refs[6:]
    mix_ref, gain_ref, there_high, there_low, back_high, back_low = constants
    fields, first, second, terms, total, sems = refs
    planes = side // slab_count
    tiles, lines, pitch = box_shape(sizes)
    solves = own_count * rounds
    group = min(solves, 8)
    group_rows = group * side
    cells = tiles * LANES
    width = 2 * LANES
    slab_index = lax.axis_index("slab")
    pair_index = lax.axis_index("pair")
    core = pair_index % CORES
    chip = pair_index // CORES
    chips = pair_count // CORES
    first_member = chip * CORES * own_count

    places = [
        (chip + chips - step) % chips * CORES + (core + core_step) % CORES
        for core_step in range(CORES)
        for step in range(1, chips)
    ]
    sources = [match_hbm, centers_hbm, *piece_hbm, mine_hbm, partner_hbm, *constant_hbm]
    targets = [match_ref, centers_ref, *[boxes_ref.at[pair] for pair in places], mine, partner, *constants]
    copies = [pltpu.make_async_copy(s, t, sems.at[i]) for i, (s, t) in enumerate(zip(sources, targets))]
    for copy in copies:
        copy.start()
    for pair in places:
        clear_edges(sizes, fields, pair * own_count, own_count)
    clear_edges(sizes, terms, 0, solves)
    boxes_count = 2 + len(places)
    for copy in copies[:boxes_count]:
        copy.wait()
    for pair in places:
        spread(sizes, boxes_ref, fields, pair)
    for copy in copies[boxes_count : boxes_count + 2]:
        copy.wait()

    def place(index, carry):
        _, mate, a, b, active = pair_geometry(sizes, match_ref, centers_ref, index)
        local = mate - first_member

        @pl.when((local < 0) | (local >= CORES * own_count))
        def _():
            rows = pl.ds(pl.multiple_of(index * side, side), side)
            place_partner(sizes, fields, mate, a, b, active, partner, rows)

        return carry

    lax.fori_loop(0, solves, place, 0)

    row_count = solves * side
    half_tiles = tiles // 2
    half_cells = cells // 2

    def mirrored(tile):
        line = lax.broadcasted_iota(jnp.int32, tile.shape, 1) // side
        result = None
        for index in range(lines):
            amount = (2 * index - lines + 1) * side % LANES
            if index < 2:
                moved = pltpu.roll(tile, amount, axis=1)
                result = moved if result is None else jnp.where(line % 2 == index, moved, result)
        return result

    def store_split(ref, start, count, columns, value):
        high, low = split_pair(value)
        if isinstance(start, int):
            ref[start : start + count, columns] = high
            ref[row_count + start : row_count + start + count, columns] = low
        else:
            ref[pl.ds(pl.multiple_of(start, count), count), columns] = high
            ref[pl.ds(pl.multiple_of(row_count + start, count), count), columns] = low

    def densities(index, carry):
        start = index * side
        rows = pl.ds(pl.multiple_of(start, side), side)

        def density(tile):
            columns = slice(tile * LANES, (tile + 1) * LANES)
            return mine[rows, columns].astype(jnp.float32) * partner[rows, columns].astype(jnp.float32)

        for tile in range(half_tiles):
            near = density(tile)
            far = mirrored(density(tiles - 1 - tile))
            for parity, value in enumerate((near + far, near - far)):
                column = parity * half_cells + tile * LANES
                store_split(first, start, side, slice(column, column + LANES), value)
        return carry

    lax.fori_loop(0, solves, densities, 0, unroll=2)

    mix_copy, gain_copy, *matrix_copies = copies[boxes_count + 2 :]
    mix_copy.wait()

    def along_x(start, columns, source):
        high = source[start : start + group_rows, columns]
        low = source[row_count + start : row_count + start + group_rows, columns]
        return dot(mix_ref[...], jnp.concatenate([high, low, high], axis=0))

    def in_plane(parity, columns, source, high_ref, low_ref):
        inner = slice(parity * half_cells, (parity + 1) * half_cells)
        high = source[:row_count, inner]
        low = source[row_count:, inner]
        basis = high_ref[parity, :, columns]
        rest = low_ref[parity, :, columns]
        left = jnp.concatenate([high, low, high], axis=1)
        return dot(left, jnp.concatenate([basis, basis, rest], axis=0))

    for start in range(0, row_count, group_rows):
        for column in range(0, cells, width):
            columns = slice(column, column + width)
            store_split(second, start, group_rows, columns, along_x(start, columns, first))

    for copy in (gain_copy, *matrix_copies[:2]):
        copy.wait()
    for parity in range(2):
        for column in range(0, half_cells, width):
            columns = slice(column, column + width)
            value = in_plane(parity, columns, second, there_high, there_low)
            columns = slice(parity * half_cells + column, parity * half_cells + column + width)
            gain = gain_ref[:, columns]
            value = (value.reshape(solves, side, width) * gain[None]).reshape(row_count, width)
            store_split(first, 0, row_count, columns, value)

    for copy in matrix_copies[2:]:
        copy.wait()
    for parity in range(2):
        for column in range(0, half_cells, width):
            value = in_plane(parity, slice(column, column + width), first, back_high, back_low)
            columns = slice(parity * half_cells + column, parity * half_cells + column + width)
            store_split(second, 0, row_count, columns, value)

    for start in range(0, row_count, group_rows):
        for column in range(0, half_cells, width):
            even = along_x(start, slice(column, column + width), second)
            odd = along_x(start, slice(half_cells + column, half_cells + column + width), second)
            for part in range(width // LANES):
                tile = column // LANES + part
                lanes = slice(part * LANES, (part + 1) * LANES)
                near = even[:, lanes] + odd[:, lanes]
                far = mirrored(even[:, lanes] - odd[:, lanes])
                for place, value in ((tile, near), (tiles - 1 - tile, far)):
                    columns = slice(place * LANES, (place + 1) * LANES)
                    value = value * partner[start : start + group_rows, columns].astype(jnp.float32)
                    for solve in range(group):
                        row = ((start // side + solve) * tiles + place) * pitch + REACH
                        terms[row : row + side, :] = value[solve * side : (solve + 1) * side, :]

    step_rows = 16

    def collect(step, carry):
        own = step // (side // step_rows)
        row = step % (side // step_rows) * step_rows
        sums = None
        for turn in range(rounds):
            index = own * rounds + turn
            _, _, a, _, _ = pair_geometry(sizes, match_ref, centers_ref, index)
            term = rolled(sizes, terms, index, row, step_rows, -a[0], -(a[1] * side + a[2]))
            sums = term if sums is None else [s + t for s, t in zip(sums, term)]
        for tile in range(tiles):
            start = (own * tiles + tile) * side + row
            total[pl.ds(pl.multiple_of(start, step_rows), step_rows), :] = sums[tile]
        return carry

    lax.fori_loop(0, own_count * side // step_rows, collect, 0)

    lane_index = lax.broadcasted_iota(jnp.int32, (tiles, LANES), 1)
    for step in range(slab_count):
        slab = partner_of(slab_index, step, slab_count)[0]
        exponents = jnp.zeros((tiles, LANES), jnp.float32)
        factors = jnp.zeros((tiles, LANES), jnp.float32)
        codes = []
        for chunk in range(own_count * planes):
            own, plane = divmod(chunk, planes)
            start = own * tiles * side + slab * planes + plane
            value = total[pl.ds(start, tiles, stride=side), :]
            code, exponent, factor = encode(value)
            codes.append(code)
            exponents = jnp.where(lane_index == chunk, exponent, exponents)
            factors = jnp.where(lane_index == chunk, factor, factors)
            if chunk % 2:
                pair = jnp.concatenate(codes[-2:], axis=0)
                out_refs[step][tiles * (chunk - 1) : tiles * (chunk + 1), :] = whole_codes(pair)
        header = jnp.concatenate([exponents, factors], axis=0)
        out_refs[step][tiles * own_count * planes :, :] = whole_codes(header)


def whole_codes(value):
    return value.astype(jnp.int32).astype(jnp.int16)


def encode(value):
    largest = jnp.max(jnp.abs(value), axis=1, keepdims=True)
    exponent = jnp.maximum(jnp.floor(jnp.log2(jnp.maximum(largest, TINY))), LOWEST_EXPONENT)
    lifted = 1.0 / jnp.exp2(exponent)
    factor = jnp.maximum(jnp.ceil(largest * lifted * FACTOR_UNIT), 1.0)
    code = jnp.floor(value * lifted * (CODE_LIMIT * FACTOR_UNIT / factor) + 0.5)
    return jnp.clip(code, -CODE_LIMIT, CODE_LIMIT), exponent, factor


def swap_cores(block, pair_count):
    return lax.ppermute(block, "pair", [(i, i ^ 1) for i in range(pair_count)])


def gather_chips(boxes, pair_count):
    pieces = []
    for step in range(1, pair_count // CORES):
        perm = [(i, (i + step * CORES) % pair_count) for i in range(pair_count)]
        pieces.append(lax.ppermute(boxes, "pair", perm))
    return pieces


def unpack_kernel(sizes, *refs):
    own_count, slab_count, tiles = sizes
    block_refs, out_ref, blocks, sems = refs[:slab_count], *refs[slab_count:]
    slab_index = lax.axis_index("slab")
    copies = []
    for index in range(slab_count):
        copies.append(pltpu.make_async_copy(block_refs[index], blocks.at[index], sems.at[index]))
        copies[-1].start()
    for index in reversed(range(slab_count)):
        step = slab_count - 1 - index
        copies[index].wait()
        first = partner_of(slab_index, step, slab_count)[1] * own_count
        row_count = own_count * tiles
        header = blocks[index, row_count:, :].astype(jnp.int32).astype(jnp.float32)
        units = jnp.exp2(header[:8, :])
        factors = header[8:, :] * (1.0 / (CODE_LIMIT * FACTOR_UNIT))
        for pair in range(row_count // 16):
            codes = blocks[index, 16 * pair : 16 * pair + 16, :].astype(jnp.int32).astype(jnp.float32)
            for half in range(2):
                chunk = 2 * pair + half
                own, tile = divmod(8 * chunk, tiles)
                row = first + own
                start = (row // 8 * tiles + tile) * 8 + row % 8
                value = codes[8 * half : 8 * half + 8, :] * factors[:, chunk : chunk + 1]
                out_ref[pl.ds(start, 8, stride=8), :] = value * units[:, chunk : chunk + 1]


def unpack(blocks, own_count, cells):
    slab_count = len(blocks)
    row_count = own_count * slab_count
    tiles = cells // LANES
    out = pl.pallas_call(
        functools.partial(unpack_kernel, (own_count, slab_count, tiles)),
        out_shape=jax.ShapeDtypeStruct((row_count * tiles, LANES), jnp.float32),
        in_specs=[pl.BlockSpec(memory_space=pl.ANY)] * slab_count,
        out_specs=pl.BlockSpec(memory_space=pltpu.VMEM),
        scratch_shapes=[
            pltpu.VMEM((slab_count,) + blocks[0].shape, jnp.int16),
            pltpu.SemaphoreType.DMA((slab_count,)),
        ],
        compiler_params=pltpu.CompilerParams(vmem_limit_bytes=8 * 1024 * 1024),
    )(*blocks)
    return out.reshape(row_count // 8, tiles, 8, LANES).transpose(0, 2, 1, 3).reshape(row_count, cells)


def place_near(sizes, match, centers, boxes, other):
    side, rounds, own_count, slab_count, _ = sizes
    tiles, _, pitch = box_shape(sizes)
    placed = (own_count * rounds * side, side * side)
    either = pl.BlockSpec(memory_space=pl.ANY)
    vectors = pl.BlockSpec(memory_space=pltpu.VMEM)
    return pl.pallas_call(
        functools.partial(near_kernel, sizes),
        out_shape=[jax.ShapeDtypeStruct(placed, jnp.bfloat16)] * 2,
        in_specs=[either] * 4,
        out_specs=[vectors] * 2,
        scratch_shapes=[
            pltpu.SMEM(match.shape, jnp.int32),
            pltpu.SMEM(centers.shape, jnp.int32),
            pltpu.VMEM((CORES,) + boxes.shape, jnp.bfloat16),
            pltpu.VMEM((CORES * own_count * tiles * pitch, LANES), jnp.float32),
            pltpu.SemaphoreType.DMA((4,)),
        ],
        compiler_params=pltpu.CompilerParams(vmem_limit_bytes=60 * 1024 * 1024),
        cost_estimate=pl.CostEstimate(flops=5 * 10**9, bytes_accessed=4 * 1024 * 1024, transcendentals=0),
    )(match, centers, boxes, other)


def team_forces(sizes, match, centers, mine, partner, pieces):
    side, rounds, own_count, slab_count, pair_count = sizes
    tiles, _, pitch = box_shape(sizes)
    _, rows, _ = pieces[0].shape
    solves = own_count * rounds
    group = min(solves, 8)
    cells = side * side
    basis = sine_basis(side)
    mix_high, mix_low = split_constant(np.kron(np.eye(group), basis))
    mix = np.concatenate([mix_high, mix_high, mix_low], axis=1)
    there = np.stack([np.kron(basis[parity::2, : side // 2].T, basis) for parity in range(2)])
    gain = chebyshev_gain(side).reshape(side, side, side)
    gain = np.concatenate([gain[:, parity::2].reshape(side, -1) for parity in range(2)], axis=1)
    constants = (mix, gain, *split_constant(there), *split_constant(there.transpose(0, 2, 1)))
    either = pl.BlockSpec(memory_space=pl.ANY)
    distant = pl.BlockSpec(memory_space=pltpu.HBM)
    vectors = pl.BlockSpec(memory_space=pltpu.VMEM)
    wide = pltpu.VMEM((2 * solves * side, cells), jnp.bfloat16)
    flops = 2 * solves * side * 3 * 2 * (cells * cells // 2 + cells * group * side)
    inputs = [match, centers, mine, partner, *pieces, *[jnp.asarray(constant) for constant in constants]]
    return pl.pallas_call(
        functools.partial(force_kernel, sizes),
        out_shape=[jax.ShapeDtypeStruct((rows + HEADER_ROWS, LANES), jnp.int16)] * slab_count,
        in_specs=[distant] * 2 + [either] * (len(inputs) - 2 - len(constants)) + [distant] * len(constants),
        out_specs=[vectors] * slab_count,
        scratch_shapes=[
            pltpu.SMEM(match.shape, jnp.int32),
            pltpu.SMEM(centers.shape, jnp.int32),
            pltpu.VMEM(mine.shape, jnp.bfloat16),
            pltpu.VMEM(partner.shape, jnp.bfloat16),
            pltpu.VMEM((pair_count, slab_count, rows, LANES), jnp.bfloat16),
            *[pltpu.VMEM(constant.shape, constant.dtype) for constant in constants],
            pltpu.VMEM((own_count * pair_count * tiles * pitch, LANES), jnp.float32),
            wide,
            wide,
            pltpu.VMEM((solves * tiles * pitch, LANES), jnp.float32),
            pltpu.VMEM((own_count * tiles * side, LANES), jnp.float32),
            pltpu.SemaphoreType.DMA((len(inputs),)),
        ],
        compiler_params=pltpu.CompilerParams(vmem_limit_bytes=60 * 1024 * 1024),
        cost_estimate=pl.CostEstimate(flops=flops, bytes_accessed=8 * 1024 * 1024, transcendentals=0),
    )(*inputs)


def shards(orbitals, centers, matchings):
    slab_count = lax.axis_size("slab")
    pair_count = lax.axis_size("pair")
    local_rows, plane_cells = orbitals.shape
    own_count = local_rows // slab_count
    side = round((plane_cells * slab_count) ** (1.0 / 3.0))
    blocks = orbitals.reshape(slab_count, own_count * plane_cells // LANES, LANES)
    boxes = lax.all_to_all(blocks, "slab", split_axis=0, concat_axis=0, tiled=True)
    sizes = (side, matchings.shape[1], own_count, slab_count, pair_count)
    pieces = gather_chips(boxes, pair_count)
    mine, partner = place_near(sizes, matchings, centers.T, boxes, swap_cores(boxes, pair_count))
    pieces, mine, partner = lax.optimization_barrier((pieces, mine, partner))
    pieces = pieces + [swap_cores(piece, pair_count) for piece in pieces]
    codes = team_forces(sizes, matchings, centers.T, mine, partner, pieces)
    received = []
    for step in reversed(range(1, slab_count)):
        perm = [(i, partner_of(i, step, slab_count)[0]) for i in range(slab_count)]
        received.append(lax.ppermute(codes[step], "slab", perm))
    return unpack(received + [codes[0]], own_count, plane_cells)


def solution(mesh):
    in_specs = (P("pair", "slab"), P(), P("slab", None, None))
    out_specs = P("pair", "slab")
    return jax.shard_map(shards, mesh=mesh, in_specs=in_specs, out_specs=out_specs, check_vma=False)
```

```python
import functools

import jax
import jax.numpy as jnp
import ml_dtypes
import numpy as np
from jax import lax
from jax.experimental import pallas as pl
from jax.experimental.pallas import tpu as pltpu
from jax.sharding import PartitionSpec as P

STEPS = 16
CUT2 = 192
REACH = 8
SCREEN = 0.1
LOWER_BOUND = 0.1
UPPER_BOUND = 12.1
LANES = 128
CORES = 2
CODE_LIMIT = 32767.0
FACTOR_UNIT = 8192.0
LOWEST_EXPONENT = -120.0
TINY = 1e-37
HEADER_ROWS = 16


def split_constant(matrix):
    high = matrix.astype(ml_dtypes.bfloat16)
    low = (matrix - high.astype(np.float64)).astype(ml_dtypes.bfloat16)
    return high, low


def sine_basis(side):
    index = np.arange(1, side + 1, dtype=np.float64)
    return np.sqrt(2.0 / (side + 1)) * np.sin(np.pi * np.outer(index, index) / (side + 1))


def chebyshev_gain(side):
    shifts = -2.0 * np.cos(np.pi * np.arange(1, side + 1, dtype=np.float64) / (side + 1))
    eigenvalue = 6.0 + SCREEN + shifts[:, None, None] + shifts[None, :, None] + shifts[None, None, :]
    middle = (UPPER_BOUND + LOWER_BOUND) / 2.0
    spread = (UPPER_BOUND - LOWER_BOUND) / 2.0
    ratio = middle / spread
    total = np.zeros_like(eigenvalue)
    residual = np.ones_like(eigenvalue)
    direction = residual / middle
    factor = 1.0 / ratio
    for _ in range(STEPS):
        total = total + direction
        residual = residual - eigenvalue * direction
        factor_next = 1.0 / (2.0 * ratio - factor)
        direction = factor_next * factor * direction + 2.0 * factor_next / spread * residual
        factor = factor_next
    return total.reshape(side, side * side).astype(np.float32)


def split_pair(value):
    high = value.astype(jnp.bfloat16)
    low = (value - high.astype(jnp.float32)).astype(jnp.bfloat16)
    return high, low


def dot(left, right):
    return jnp.dot(left, right, preferred_element_type=jnp.float32)


def partner_of(index, step, count):
    if count & (count - 1) == 0:
        return index ^ step, index ^ step
    return (index + step) % count, (index + count - step) % count


def pair_geometry(sizes, match_ref, centers_ref, index):
    _, rounds, own_count, slab_count, _ = sizes
    slab_index = lax.axis_index("slab")
    pair_index = lax.axis_index("pair")

    def orbital_of(member):
        return (member // own_count * slab_count + slab_index) * own_count + member % own_count

    member = pair_index * own_count + index // rounds
    mate = match_ref[0, index % rounds, member]
    own_offset = []
    mate_offset = []
    distance = 0
    for axis in range(3):
        mine = centers_ref[axis, orbital_of(member)]
        other = centers_ref[axis, orbital_of(mate)]
        anchor = (mine + other) >> 1
        own_offset.append(mine - anchor)
        mate_offset.append(other - anchor)
        distance = distance + (mine - other) * (mine - other)
    return member, mate, own_offset, mate_offset, distance <= CUT2


def box_shape(sizes):
    side = sizes[0]
    return side * side // LANES, LANES // side, side + 2 * REACH


def clear_edges(sizes, ref, first, count):
    side = sizes[0]
    tiles, _, pitch = box_shape(sizes)
    zeros = jnp.zeros((REACH, LANES), jnp.float32)

    def clear(index, carry):
        start = (first * tiles + index) * pitch
        ref[pl.ds(pl.multiple_of(start, 8), REACH), :] = zeros
        ref[pl.ds(pl.multiple_of(start + REACH + side, 8), REACH), :] = zeros
        return carry

    lax.fori_loop(0, count * tiles, clear, 0, unroll=8)


def spread(sizes, boxes_ref, fields, pair):
    side, _, own_count, slab_count, _ = sizes
    planes = side // slab_count
    tiles, _, pitch = box_shape(sizes)

    def spread_slab(slab, carry):
        for chunk in range(own_count * planes // 2):
            block = boxes_ref[pair, slab, 16 * chunk : 16 * chunk + 16, :].astype(jnp.float32)
            for half in range(2):
                own, plane = divmod(2 * chunk + half, planes)
                start = (pair * own_count + own) * tiles * pitch + REACH + slab * planes + plane
                fields[pl.ds(start, tiles, stride=pitch), :] = block[8 * half : 8 * half + 8, :]
        return carry

    lax.fori_loop(0, slab_count, spread_slab, 0)


def rolled(sizes, ref, box, row, rows, offset_x, offset_flat):
    tiles, _, pitch = box_shape(sizes)
    whole = (offset_flat >> 7) & (tiles - 1)
    part = offset_flat & (LANES - 1)
    start = box * tiles * pitch + REACH + row - offset_x
    moved = []
    for tile in range(tiles):
        first_row = start + ((tile - whole) & (tiles - 1)) * pitch
        moved.append(pltpu.roll(ref[pl.ds(first_row, rows), :], part, axis=1))
    keep = lax.broadcasted_iota(jnp.int32, (rows, LANES), 1) >= part
    return [jnp.where(keep, moved[t], moved[(t - 1) % tiles]) for t in range(tiles)]


def place_partner(sizes, fields, box, own_offset, offset, active, out_ref, rows):
    side = sizes[0]
    tiles, lines, _ = box_shape(sizes)
    placed = rolled(sizes, fields, box, 0, side, offset[0], offset[1] * side + offset[2])
    lane = lax.broadcasted_iota(jnp.int32, (1, LANES), 1)
    lows = [jnp.maximum(jnp.maximum(a, b), 0) for a, b in zip(own_offset, offset)]
    highs = [side + jnp.minimum(jnp.minimum(a, b), 0) for a, b in zip(own_offset, offset)]
    point_ok = (lane % side >= lows[2]) & (lane % side < highs[2]) & active
    for tile in range(tiles):
        line = lane // side + tile * lines
        ok = jnp.where(point_ok & (line >= lows[1]) & (line < highs[1]), 1.0, 0.0)
        out_ref[rows, tile * LANES : (tile + 1) * LANES] = (placed[tile] * ok).astype(jnp.bfloat16)


def own_kernel(
    sizes, match_hbm, centers_hbm, own_hbm, mine_ref, partner_ref, match_ref, centers_ref, boxes_ref, fields, sems
):
    side, rounds, own_count, _, _ = sizes
    tiles, _, _ = box_shape(sizes)
    first_member = lax.axis_index("pair") * own_count
    sources = (match_hbm, centers_hbm, own_hbm)
    targets = (match_ref, centers_ref, boxes_ref.at[0])
    copies = [pltpu.make_async_copy(s, t, sems.at[i]) for i, (s, t) in enumerate(zip(sources, targets))]
    for copy in copies:
        copy.start()
    clear_edges(sizes, fields, 0, own_count)
    for copy in copies:
        copy.wait()
    spread(sizes, boxes_ref, fields, 0)

    def place(index, carry):
        member, mate, a, b, active = pair_geometry(sizes, match_ref, centers_ref, index)
        rows = pl.ds(pl.multiple_of(index * side, side), side)
        placed = rolled(sizes, fields, member - first_member, 0, side, a[0], a[1] * side + a[2])
        for tile in range(tiles):
            mine_ref[rows, tile * LANES : (tile + 1) * LANES] = placed[tile].astype(jnp.bfloat16)
        local = mate - first_member

        @pl.when((local >= 0) & (local < own_count))
        def _():
            place_partner(sizes, fields, local, a, b, active, partner_ref, rows)

        return carry

    lax.fori_loop(0, own_count * rounds, place, 0)


def force_kernel(sizes, match_hbm, centers_hbm, mine_hbm, partner_hbm, *refs):
    side, rounds, own_count, slab_count, pair_count = sizes
    piece_hbm, refs = refs[: pair_count - 1], refs[pair_count - 1 :]
    constant_hbm, refs = refs[:6], refs[6:]
    out_refs, refs = refs[:slab_count], refs[slab_count:]
    match_ref, centers_ref, mine, partner, boxes_ref, *refs = refs
    constants, refs = refs[:6], refs[6:]
    mix_ref, gain_ref, there_high, there_low, back_high, back_low = constants
    fields, first, second, terms, total, sems = refs
    planes = side // slab_count
    tiles, lines, pitch = box_shape(sizes)
    solves = own_count * rounds
    group = min(solves, 8)
    group_rows = group * side
    cells = tiles * LANES
    width = cells // 2
    slab_index = lax.axis_index("slab")
    pair_index = lax.axis_index("pair")
    core = pair_index % CORES
    chip = pair_index // CORES
    chips = pair_count // CORES
    first_member = pair_index * own_count

    places = [
        (chip + chips - step) % chips * CORES + (core + core_step) % CORES
        for core_step in range(CORES)
        for step in range(chips)
    ]
    places = places[1:]
    sources = [match_hbm, centers_hbm, *piece_hbm, mine_hbm, partner_hbm, *constant_hbm]
    targets = [match_ref, centers_ref, *[boxes_ref.at[pair] for pair in places], mine, partner, *constants]
    copies = [pltpu.make_async_copy(s, t, sems.at[i]) for i, (s, t) in enumerate(zip(sources, targets))]
    for copy in copies:
        copy.start()
    for pair in places:
        clear_edges(sizes, fields, pair * own_count, own_count)
    clear_edges(sizes, terms, 0, solves)
    boxes_count = 2 + len(places)
    for copy in copies[:boxes_count]:
        copy.wait()
    for pair in places:
        spread(sizes, boxes_ref, fields, pair)
    for copy in copies[boxes_count : boxes_count + 2]:
        copy.wait()

    def place(index, carry):
        _, mate, a, b, active = pair_geometry(sizes, match_ref, centers_ref, index)
        local = mate - first_member

        @pl.when((local < 0) | (local >= own_count))
        def _():
            rows = pl.ds(pl.multiple_of(index * side, side), side)
            place_partner(sizes, fields, mate, a, b, active, partner, rows)

        return carry

    lax.fori_loop(0, solves, place, 0)

    row_count = solves * side
    half_tiles = tiles // 2
    half_cells = cells // 2

    def mirrored(tile):
        line = lax.broadcasted_iota(jnp.int32, tile.shape, 1) // side
        result = None
        for index in range(lines):
            amount = (2 * index - lines + 1) * side % LANES
            if index < 2:
                moved = pltpu.roll(tile, amount, axis=1)
                result = moved if result is None else jnp.where(line % 2 == index, moved, result)
        return result

    def store_split(ref, start, count, columns, value):
        high, low = split_pair(value)
        if isinstance(start, int):
            ref[start : start + count, columns] = high
            ref[row_count + start : row_count + start + count, columns] = low
        else:
            ref[pl.ds(pl.multiple_of(start, count), count), columns] = high
            ref[pl.ds(pl.multiple_of(row_count + start, count), count), columns] = low

    def densities(index, carry):
        start = index * side
        rows = pl.ds(pl.multiple_of(start, side), side)

        def density(tile):
            columns = slice(tile * LANES, (tile + 1) * LANES)
            return mine[rows, columns].astype(jnp.float32) * partner[rows, columns].astype(jnp.float32)

        for tile in range(half_tiles):
            near = density(tile)
            far = mirrored(density(tiles - 1 - tile))
            for parity, value in enumerate((near + far, near - far)):
                column = parity * half_cells + tile * LANES
                store_split(first, start, side, slice(column, column + LANES), value)
        return carry

    lax.fori_loop(0, solves, densities, 0, unroll=2)

    mix_copy, gain_copy, *matrix_copies = copies[boxes_count + 2 :]
    mix_copy.wait()

    def along_x(start, columns, source):
        high = source[start : start + group_rows, columns]
        low = source[row_count + start : row_count + start + group_rows, columns]
        return dot(mix_ref[...], jnp.concatenate([high, low, high], axis=0))

    def in_plane(parity, columns, source, high_ref, low_ref):
        inner = slice(parity * half_cells, (parity + 1) * half_cells)
        high = source[:row_count, inner]
        low = source[row_count:, inner]
        basis = high_ref[parity, :, columns]
        rest = low_ref[parity, :, columns]
        left = jnp.concatenate([high, low, high], axis=1)
        return dot(left, jnp.concatenate([basis, basis, rest], axis=0))

    for start in range(0, row_count, group_rows):
        columns = slice(0, cells)
        store_split(second, start, group_rows, columns, along_x(start, columns, first))

    for copy in (gain_copy, *matrix_copies[:2]):
        copy.wait()
    for parity in range(2):
        for column in range(0, half_cells, width):
            columns = slice(column, column + width)
            value = in_plane(parity, columns, second, there_high, there_low)
            columns = slice(parity * half_cells + column, parity * half_cells + column + width)
            gain = gain_ref[:, columns]
            value = (value.reshape(solves, side, width) * gain[None]).reshape(row_count, width)
            store_split(first, 0, row_count, columns, value)

    for copy in matrix_copies[2:]:
        copy.wait()
    for parity in range(2):
        for column in range(0, half_cells, width):
            value = in_plane(parity, slice(column, column + width), first, back_high, back_low)
            columns = slice(parity * half_cells + column, parity * half_cells + column + width)
            store_split(second, 0, row_count, columns, value)

    for start in range(0, row_count, group_rows):
        for column in range(0, half_cells, width):
            even = along_x(start, slice(column, column + width), second)
            odd = along_x(start, slice(half_cells + column, half_cells + column + width), second)
            for part in range(width // LANES):
                tile = column // LANES + part
                lanes = slice(part * LANES, (part + 1) * LANES)
                near = even[:, lanes] + odd[:, lanes]
                far = mirrored(even[:, lanes] - odd[:, lanes])
                for place, value in ((tile, near), (tiles - 1 - tile, far)):
                    columns = slice(place * LANES, (place + 1) * LANES)
                    value = value * partner[start : start + group_rows, columns].astype(jnp.float32)
                    for solve in range(group):
                        row = ((start // side + solve) * tiles + place) * pitch + REACH
                        terms[row : row + side, :] = value[solve * side : (solve + 1) * side, :]

    step_rows = 16

    def collect(step, carry):
        own = step // (side // step_rows)
        row = step % (side // step_rows) * step_rows
        sums = None
        for turn in range(rounds):
            index = own * rounds + turn
            _, _, a, _, _ = pair_geometry(sizes, match_ref, centers_ref, index)
            term = rolled(sizes, terms, index, row, step_rows, -a[0], -(a[1] * side + a[2]))
            sums = term if sums is None else [s + t for s, t in zip(sums, term)]
        for tile in range(tiles):
            start = (own * tiles + tile) * side + row
            total[pl.ds(pl.multiple_of(start, step_rows), step_rows), :] = sums[tile]
        return carry

    lax.fori_loop(0, own_count * side // step_rows, collect, 0)

    lane_index = lax.broadcasted_iota(jnp.int32, (tiles, LANES), 1)
    for step in range(slab_count):
        slab = partner_of(slab_index, step, slab_count)[0]
        exponents = jnp.zeros((tiles, LANES), jnp.float32)
        factors = jnp.zeros((tiles, LANES), jnp.float32)
        codes = []
        for chunk in range(own_count * planes):
            own, plane = divmod(chunk, planes)
            start = own * tiles * side + slab * planes + plane
            value = total[pl.ds(start, tiles, stride=side), :]
            code, exponent, factor = encode(value)
            codes.append(code)
            exponents = jnp.where(lane_index == chunk, exponent, exponents)
            factors = jnp.where(lane_index == chunk, factor, factors)
            if chunk % 2:
                pair = jnp.concatenate(codes[-2:], axis=0)
                out_refs[step][tiles * (chunk - 1) : tiles * (chunk + 1), :] = whole_codes(pair)
        header = jnp.concatenate([exponents, factors], axis=0)
        out_refs[step][tiles * own_count * planes :, :] = whole_codes(header)


def whole_codes(value):
    return value.astype(jnp.int32).astype(jnp.int16)


def encode(value):
    largest = jnp.max(jnp.abs(value), axis=1, keepdims=True)
    exponent = jnp.maximum(jnp.floor(jnp.log2(jnp.maximum(largest, TINY))), LOWEST_EXPONENT)
    lifted = 1.0 / jnp.exp2(exponent)
    factor = jnp.maximum(jnp.ceil(largest * lifted * FACTOR_UNIT), 1.0)
    code = jnp.floor(value * lifted * (CODE_LIMIT * FACTOR_UNIT / factor) + 0.5)
    return jnp.clip(code, -CODE_LIMIT, CODE_LIMIT), exponent, factor


def swap_cores(block, pair_count):
    return lax.ppermute(block, "pair", [(i, i ^ 1) for i in range(pair_count)])


def gather_chips(boxes, pair_count):
    pieces = []
    for step in range(1, pair_count // CORES):
        perm = [(i, (i + step * CORES) % pair_count) for i in range(pair_count)]
        pieces.append(lax.ppermute(boxes, "pair", perm))
    return pieces


def unpack_kernel(sizes, *refs):
    own_count, slab_count, tiles = sizes
    block_refs, out_ref, blocks, sems = refs[:slab_count], *refs[slab_count:]
    slab_index = lax.axis_index("slab")
    copies = []
    for index in range(slab_count):
        copies.append(pltpu.make_async_copy(block_refs[index], blocks.at[index], sems.at[index]))
        copies[-1].start()
    for index in reversed(range(slab_count)):
        step = slab_count - 1 - index
        copies[index].wait()
        first = partner_of(slab_index, step, slab_count)[1] * own_count
        row_count = own_count * tiles
        header = blocks[index, row_count:, :].astype(jnp.int32).astype(jnp.float32)
        units = jnp.exp2(header[:8, :])
        factors = header[8:, :] * (1.0 / (CODE_LIMIT * FACTOR_UNIT))
        for pair in range(row_count // 16):
            codes = blocks[index, 16 * pair : 16 * pair + 16, :].astype(jnp.int32).astype(jnp.float32)
            for half in range(2):
                chunk = 2 * pair + half
                own, tile = divmod(8 * chunk, tiles)
                row = first + own
                start = (row // 8 * tiles + tile) * 8 + row % 8
                value = codes[8 * half : 8 * half + 8, :] * factors[:, chunk : chunk + 1]
                out_ref[pl.ds(start, 8, stride=8), :] = value * units[:, chunk : chunk + 1]


def unpack(blocks, own_count, cells):
    slab_count = len(blocks)
    row_count = own_count * slab_count
    tiles = cells // LANES
    out = pl.pallas_call(
        functools.partial(unpack_kernel, (own_count, slab_count, tiles)),
        out_shape=jax.ShapeDtypeStruct((row_count * tiles, LANES), jnp.float32),
        in_specs=[pl.BlockSpec(memory_space=pl.ANY)] * slab_count,
        out_specs=pl.BlockSpec(memory_space=pltpu.VMEM),
        scratch_shapes=[
            pltpu.VMEM((slab_count,) + blocks[0].shape, jnp.int16),
            pltpu.SemaphoreType.DMA((slab_count,)),
        ],
        compiler_params=pltpu.CompilerParams(vmem_limit_bytes=8 * 1024 * 1024),
    )(*blocks)
    return out.reshape(row_count // 8, tiles, 8, LANES).transpose(0, 2, 1, 3).reshape(row_count, cells)


def place_own(sizes, match, centers, boxes):
    side, rounds, own_count, slab_count, _ = sizes
    tiles, _, pitch = box_shape(sizes)
    placed = (own_count * rounds * side, side * side)
    either = pl.BlockSpec(memory_space=pl.ANY)
    vectors = pl.BlockSpec(memory_space=pltpu.VMEM)
    return pl.pallas_call(
        functools.partial(own_kernel, sizes),
        out_shape=[jax.ShapeDtypeStruct(placed, jnp.bfloat16)] * 2,
        in_specs=[either] * 3,
        out_specs=[vectors] * 2,
        scratch_shapes=[
            pltpu.SMEM(match.shape, jnp.int32),
            pltpu.SMEM(centers.shape, jnp.int32),
            pltpu.VMEM((1,) + boxes.shape, jnp.bfloat16),
            pltpu.VMEM((own_count * tiles * pitch, LANES), jnp.float32),
            pltpu.SemaphoreType.DMA((3,)),
        ],
        compiler_params=pltpu.CompilerParams(vmem_limit_bytes=60 * 1024 * 1024),
        cost_estimate=pl.CostEstimate(flops=5 * 10**9, bytes_accessed=4 * 1024 * 1024, transcendentals=0),
    )(match, centers, boxes)


def team_forces(sizes, match, centers, mine, partner, pieces):
    side, rounds, own_count, slab_count, pair_count = sizes
    tiles, _, pitch = box_shape(sizes)
    _, rows, _ = pieces[0].shape
    solves = own_count * rounds
    group = min(solves, 8)
    cells = side * side
    basis = sine_basis(side)
    mix_high, mix_low = split_constant(np.kron(np.eye(group), basis))
    mix = np.concatenate([mix_high, mix_high, mix_low], axis=1)
    there = np.stack([np.kron(basis[parity::2, : side // 2].T, basis) for parity in range(2)])
    gain = chebyshev_gain(side).reshape(side, side, side)
    gain = np.concatenate([gain[:, parity::2].reshape(side, -1) for parity in range(2)], axis=1)
    constants = (mix, gain, *split_constant(there), *split_constant(there.transpose(0, 2, 1)))
    either = pl.BlockSpec(memory_space=pl.ANY)
    distant = pl.BlockSpec(memory_space=pltpu.HBM)
    vectors = pl.BlockSpec(memory_space=pltpu.VMEM)
    wide = pltpu.VMEM((2 * solves * side, cells), jnp.bfloat16)
    flops = 2 * solves * side * 3 * 2 * (cells * cells // 2 + cells * group * side)
    inputs = [match, centers, mine, partner, *pieces, *[jnp.asarray(constant) for constant in constants]]
    return pl.pallas_call(
        functools.partial(force_kernel, sizes),
        out_shape=[jax.ShapeDtypeStruct((rows + HEADER_ROWS, LANES), jnp.int16)] * slab_count,
        in_specs=[distant] * 2 + [either] * (len(inputs) - 2 - len(constants)) + [distant] * len(constants),
        out_specs=[vectors] * slab_count,
        scratch_shapes=[
            pltpu.SMEM(match.shape, jnp.int32),
            pltpu.SMEM(centers.shape, jnp.int32),
            pltpu.VMEM(mine.shape, jnp.bfloat16),
            pltpu.VMEM(partner.shape, jnp.bfloat16),
            pltpu.VMEM((pair_count, slab_count, rows, LANES), jnp.bfloat16),
            *[pltpu.VMEM(constant.shape, constant.dtype) for constant in constants],
            pltpu.VMEM((own_count * pair_count * tiles * pitch, LANES), jnp.float32),
            wide,
            wide,
            pltpu.VMEM((solves * tiles * pitch, LANES), jnp.float32),
            pltpu.VMEM((own_count * tiles * side, LANES), jnp.float32),
            pltpu.SemaphoreType.DMA((len(inputs),)),
        ],
        compiler_params=pltpu.CompilerParams(vmem_limit_bytes=60 * 1024 * 1024),
        cost_estimate=pl.CostEstimate(flops=flops, bytes_accessed=8 * 1024 * 1024, transcendentals=0),
    )(*inputs)


def shards(orbitals, centers, matchings):
    slab_count = lax.axis_size("slab")
    pair_count = lax.axis_size("pair")
    local_rows, plane_cells = orbitals.shape
    own_count = local_rows // slab_count
    side = round((plane_cells * slab_count) ** (1.0 / 3.0))
    blocks = orbitals.reshape(slab_count, own_count * plane_cells // LANES, LANES)
    boxes = lax.all_to_all(blocks, "slab", split_axis=0, concat_axis=0, tiled=True)
    sizes = (side, matchings.shape[1], own_count, slab_count, pair_count)
    pieces = gather_chips(boxes, pair_count)
    mine, partner = place_own(sizes, matchings, centers.T, boxes)
    boxes, mine, partner = lax.optimization_barrier((boxes, mine, partner))
    swapped = [swap_cores(boxes, pair_count)]
    pieces, mine, partner = lax.optimization_barrier((pieces, mine, partner))
    pieces = pieces + swapped + [swap_cores(piece, pair_count) for piece in pieces]
    codes = team_forces(sizes, matchings, centers.T, mine, partner, pieces)
    received = []
    for step in reversed(range(1, slab_count)):
        perm = [(i, partner_of(i, step, slab_count)[0]) for i in range(slab_count)]
        received.append(lax.ppermute(codes[step], "slab", perm))
    return unpack(received + [codes[0]], own_count, plane_cells)


def solution(mesh):
    in_specs = (P("pair", "slab"), P(), P("slab", None, None))
    out_specs = P("pair", "slab")
    return jax.shard_map(shards, mesh=mesh, in_specs=in_specs, out_specs=out_specs, check_vma=False)
```

```python
import functools

import jax
import jax.numpy as jnp
import ml_dtypes
import numpy as np
from jax import lax
from jax.experimental import pallas as pl
from jax.experimental.pallas import tpu as pltpu
from jax.sharding import PartitionSpec as P

STEPS = 16
CUT2 = 192
REACH = 8
SCREEN = 0.1
LOWER_BOUND = 0.1
UPPER_BOUND = 12.1
LANES = 128
CORES = 2
CODE_LIMIT = 32767.0
FACTOR_UNIT = 8192.0
LOWEST_EXPONENT = -120.0
TINY = 1e-37
HEADER_ROWS = 16


def split_constant(matrix):
    high = matrix.astype(ml_dtypes.bfloat16)
    low = (matrix - high.astype(np.float64)).astype(ml_dtypes.bfloat16)
    return high, low


def sine_basis(side):
    index = np.arange(1, side + 1, dtype=np.float64)
    return np.sqrt(2.0 / (side + 1)) * np.sin(np.pi * np.outer(index, index) / (side + 1))


def chebyshev_gain(side):
    shifts = -2.0 * np.cos(np.pi * np.arange(1, side + 1, dtype=np.float64) / (side + 1))
    eigenvalue = 6.0 + SCREEN + shifts[:, None, None] + shifts[None, :, None] + shifts[None, None, :]
    middle = (UPPER_BOUND + LOWER_BOUND) / 2.0
    spread = (UPPER_BOUND - LOWER_BOUND) / 2.0
    ratio = middle / spread
    total = np.zeros_like(eigenvalue)
    residual = np.ones_like(eigenvalue)
    direction = residual / middle
    factor = 1.0 / ratio
    for _ in range(STEPS):
        total = total + direction
        residual = residual - eigenvalue * direction
        factor_next = 1.0 / (2.0 * ratio - factor)
        direction = factor_next * factor * direction + 2.0 * factor_next / spread * residual
        factor = factor_next
    return total.reshape(side, side * side).astype(np.float32)


def split_pair(value):
    high = value.astype(jnp.bfloat16)
    low = (value - high.astype(jnp.float32)).astype(jnp.bfloat16)
    return high, low


def dot(left, right):
    return jnp.dot(left, right, preferred_element_type=jnp.float32)


def partner_of(index, step, count):
    if count & (count - 1) == 0:
        return index ^ step, index ^ step
    return (index + step) % count, (index + count - step) % count


def pair_geometry(sizes, match_ref, centers_ref, index):
    _, rounds, own_count, slab_count, _ = sizes
    slab_index = lax.axis_index("slab")
    pair_index = lax.axis_index("pair")

    def orbital_of(member):
        return (member // own_count * slab_count + slab_index) * own_count + member % own_count

    member = pair_index * own_count + index // rounds
    mate = match_ref[0, index % rounds, member]
    own_offset = []
    mate_offset = []
    distance = 0
    for axis in range(3):
        mine = centers_ref[axis, orbital_of(member)]
        other = centers_ref[axis, orbital_of(mate)]
        anchor = (mine + other) >> 1
        own_offset.append(mine - anchor)
        mate_offset.append(other - anchor)
        distance = distance + (mine - other) * (mine - other)
    return member, mate, own_offset, mate_offset, distance <= CUT2


def box_shape(sizes):
    side = sizes[0]
    return side * side // LANES, LANES // side, side + 2 * REACH


def clear_edges(sizes, ref, first, count):
    side = sizes[0]
    tiles, _, pitch = box_shape(sizes)
    zeros = jnp.zeros((REACH, LANES), jnp.float32)

    def clear(index, carry):
        start = (first * tiles + index) * pitch
        ref[pl.ds(pl.multiple_of(start, 8), REACH), :] = zeros
        ref[pl.ds(pl.multiple_of(start + REACH + side, 8), REACH), :] = zeros
        return carry

    lax.fori_loop(0, count * tiles, clear, 0, unroll=8)


def spread(sizes, boxes_ref, fields, pair):
    side, _, own_count, slab_count, _ = sizes
    planes = side // slab_count
    tiles, _, pitch = box_shape(sizes)

    def spread_slab(slab, carry):
        for chunk in range(own_count * planes // 2):
            block = boxes_ref[pair, slab, 16 * chunk : 16 * chunk + 16, :].astype(jnp.float32)
            for half in range(2):
                own, plane = divmod(2 * chunk + half, planes)
                start = (pair * own_count + own) * tiles * pitch + REACH + slab * planes + plane
                fields[pl.ds(start, tiles, stride=pitch), :] = block[8 * half : 8 * half + 8, :]
        return carry

    lax.fori_loop(0, slab_count, spread_slab, 0, unroll=4)


def rolled(sizes, ref, box, row, rows, offset_x, offset_flat):
    tiles, _, pitch = box_shape(sizes)
    whole = (offset_flat >> 7) & (tiles - 1)
    part = offset_flat & (LANES - 1)
    start = box * tiles * pitch + REACH + row - offset_x
    moved = []
    for tile in range(tiles):
        first_row = start + ((tile - whole) & (tiles - 1)) * pitch
        moved.append(pltpu.roll(ref[pl.ds(first_row, rows), :], part, axis=1))
    keep = lax.broadcasted_iota(jnp.int32, (rows, LANES), 1) >= part
    return [jnp.where(keep, moved[t], moved[(t - 1) % tiles]) for t in range(tiles)]


def place_partner(sizes, fields, box, own_offset, offset, active, out_ref, rows):
    side = sizes[0]
    tiles, lines, _ = box_shape(sizes)
    placed = rolled(sizes, fields, box, 0, side, offset[0], offset[1] * side + offset[2])
    lane = lax.broadcasted_iota(jnp.int32, (1, LANES), 1)
    lows = [jnp.maximum(jnp.maximum(a, b), 0) for a, b in zip(own_offset, offset)]
    highs = [side + jnp.minimum(jnp.minimum(a, b), 0) for a, b in zip(own_offset, offset)]
    point_ok = (lane % side >= lows[2]) & (lane % side < highs[2]) & active
    for tile in range(tiles):
        line = lane // side + tile * lines
        ok = jnp.where(point_ok & (line >= lows[1]) & (line < highs[1]), 1.0, 0.0)
        out_ref[rows, tile * LANES : (tile + 1) * LANES] = (placed[tile] * ok).astype(jnp.bfloat16)


def own_kernel(
    sizes, match_hbm, centers_hbm, own_hbm, mine_ref, partner_ref, match_ref, centers_ref, boxes_ref, fields, sems
):
    side, rounds, own_count, _, _ = sizes
    tiles, _, _ = box_shape(sizes)
    first_member = lax.axis_index("pair") * own_count
    sources = (match_hbm, centers_hbm, own_hbm)
    targets = (match_ref, centers_ref, boxes_ref.at[0])
    copies = [pltpu.make_async_copy(s, t, sems.at[i]) for i, (s, t) in enumerate(zip(sources, targets))]
    for copy in copies:
        copy.start()
    clear_edges(sizes, fields, 0, own_count)
    for copy in copies:
        copy.wait()
    spread(sizes, boxes_ref, fields, 0)

    def place(index, carry):
        member, mate, a, b, active = pair_geometry(sizes, match_ref, centers_ref, index)
        rows = pl.ds(pl.multiple_of(index * side, side), side)
        placed = rolled(sizes, fields, member - first_member, 0, side, a[0], a[1] * side + a[2])
        for tile in range(tiles):
            mine_ref[rows, tile * LANES : (tile + 1) * LANES] = placed[tile].astype(jnp.bfloat16)
        local = mate - first_member

        @pl.when((local >= 0) & (local < own_count))
        def _():
            place_partner(sizes, fields, local, a, b, active, partner_ref, rows)

        return carry

    lax.fori_loop(0, own_count * rounds, place, 0)


def force_kernel(sizes, match_hbm, centers_hbm, mine_hbm, partner_hbm, *refs):
    side, rounds, own_count, slab_count, pair_count = sizes
    piece_hbm, refs = refs[: pair_count - 1], refs[pair_count - 1 :]
    constant_hbm, refs = refs[:6], refs[6:]
    out_refs, refs = refs[:slab_count], refs[slab_count:]
    match_ref, centers_ref, mine, partner, boxes_ref, *refs = refs
    constants, refs = refs[:6], refs[6:]
    mix_ref, gain_ref, there_high, there_low, back_high, back_low = constants
    fields, first, second, terms, total, sems = refs
    planes = side // slab_count
    tiles, lines, pitch = box_shape(sizes)
    solves = own_count * rounds
    group = min(solves, 8)
    group_rows = group * side
    cells = tiles * LANES
    width = cells // 2
    slab_index = lax.axis_index("slab")
    pair_index = lax.axis_index("pair")
    core = pair_index % CORES
    chip = pair_index // CORES
    chips = pair_count // CORES
    first_member = pair_index * own_count

    places = [
        (chip + chips - step) % chips * CORES + (core + core_step) % CORES
        for core_step in range(CORES)
        for step in range(chips)
    ]
    places = places[1:]
    sources = [match_hbm, centers_hbm, *piece_hbm, mine_hbm, partner_hbm, *constant_hbm]
    targets = [match_ref, centers_ref, *[boxes_ref.at[pair] for pair in places], mine, partner, *constants]
    copies = [pltpu.make_async_copy(s, t, sems.at[i]) for i, (s, t) in enumerate(zip(sources, targets))]
    for copy in copies:
        copy.start()
    for pair in places:
        clear_edges(sizes, fields, pair * own_count, own_count)
    clear_edges(sizes, terms, 0, solves)
    boxes_count = 2 + len(places)
    for copy in copies[:boxes_count]:
        copy.wait()
    for pair in places:
        spread(sizes, boxes_ref, fields, pair)
    for copy in copies[boxes_count : boxes_count + 2]:
        copy.wait()

    def place(index, carry):
        _, mate, a, b, active = pair_geometry(sizes, match_ref, centers_ref, index)
        local = mate - first_member

        @pl.when((local < 0) | (local >= own_count))
        def _():
            rows = pl.ds(pl.multiple_of(index * side, side), side)
            place_partner(sizes, fields, mate, a, b, active, partner, rows)

        return carry

    lax.fori_loop(0, solves, place, 0)

    row_count = solves * side
    half_tiles = tiles // 2
    half_cells = cells // 2

    def mirrored(tile):
        line = lax.broadcasted_iota(jnp.int32, tile.shape, 1) // side
        result = None
        for index in range(lines):
            amount = (2 * index - lines + 1) * side % LANES
            if index < 2:
                moved = pltpu.roll(tile, amount, axis=1)
                result = moved if result is None else jnp.where(line % 2 == index, moved, result)
        return result

    def store_split(ref, start, count, columns, value):
        high, low = split_pair(value)
        ref[start : start + count, columns] = high
        ref[row_count + start : row_count + start + count, columns] = low

    def densities(index):
        start = index * side
        rows = slice(start, start + side)

        def density(tile):
            columns = slice(tile * LANES, (tile + 1) * LANES)
            return mine[rows, columns].astype(jnp.float32) * partner[rows, columns].astype(jnp.float32)

        for tile in range(half_tiles):
            near = density(tile)
            far = mirrored(density(tiles - 1 - tile))
            for parity, value in enumerate((near + far, near - far)):
                column = parity * half_cells + tile * LANES
                store_split(first, start, side, slice(column, column + LANES), value)

    mix_copy, gain_copy, *matrix_copies = copies[boxes_count + 2 :]
    mix_copy.wait()

    def along_x(start, columns, source):
        high = source[start : start + group_rows, columns]
        low = source[row_count + start : row_count + start + group_rows, columns]
        return dot(mix_ref[...], jnp.concatenate([high, low, high], axis=0))

    def in_plane(parity, columns, source, high_ref, low_ref):
        inner = slice(parity * half_cells, (parity + 1) * half_cells)
        high = source[:row_count, inner]
        low = source[row_count:, inner]
        basis = high_ref[parity, :, columns]
        rest = low_ref[parity, :, columns]
        left = jnp.concatenate([high, low, high], axis=1)
        return dot(left, jnp.concatenate([basis, basis, rest], axis=0))

    for start in range(0, row_count, group_rows):
        for index in range(start // side, (start + group_rows) // side):
            densities(index)
        columns = slice(0, cells)
        store_split(second, start, group_rows, columns, along_x(start, columns, first))

    for copy in (gain_copy, *matrix_copies[:2]):
        copy.wait()
    for parity in range(2):
        for column in range(0, half_cells, width):
            columns = slice(column, column + width)
            value = in_plane(parity, columns, second, there_high, there_low)
            columns = slice(parity * half_cells + column, parity * half_cells + column + width)
            gain = gain_ref[:, columns]
            value = (value.reshape(solves, side, width) * gain[None]).reshape(row_count, width)
            store_split(first, 0, row_count, columns, value)

    for copy in matrix_copies[2:]:
        copy.wait()
    for parity in range(2):
        for column in range(0, half_cells, width):
            value = in_plane(parity, slice(column, column + width), first, back_high, back_low)
            columns = slice(parity * half_cells + column, parity * half_cells + column + width)
            store_split(second, 0, row_count, columns, value)

    for start in range(0, row_count, group_rows):
        for column in range(0, half_cells, width):
            even = along_x(start, slice(column, column + width), second)
            odd = along_x(start, slice(half_cells + column, half_cells + column + width), second)
            for part in range(width // LANES):
                tile = column // LANES + part
                lanes = slice(part * LANES, (part + 1) * LANES)
                near = even[:, lanes] + odd[:, lanes]
                far = mirrored(even[:, lanes] - odd[:, lanes])
                for place, value in ((tile, near), (tiles - 1 - tile, far)):
                    columns = slice(place * LANES, (place + 1) * LANES)
                    value = value * partner[start : start + group_rows, columns].astype(jnp.float32)
                    for solve in range(group):
                        row = ((start // side + solve) * tiles + place) * pitch + REACH
                        terms[row : row + side, :] = value[solve * side : (solve + 1) * side, :]

    step_rows = 16

    def collect(step, carry):
        own = step // (side // step_rows)
        row = step % (side // step_rows) * step_rows
        sums = None
        for turn in range(rounds):
            index = own * rounds + turn
            _, _, a, _, _ = pair_geometry(sizes, match_ref, centers_ref, index)
            term = rolled(sizes, terms, index, row, step_rows, -a[0], -(a[1] * side + a[2]))
            sums = term if sums is None else [s + t for s, t in zip(sums, term)]
        for tile in range(tiles):
            start = (own * tiles + tile) * side + row
            total[pl.ds(pl.multiple_of(start, step_rows), step_rows), :] = sums[tile]
        return carry

    lax.fori_loop(0, own_count * side // step_rows, collect, 0, unroll=2)

    lane_index = lax.broadcasted_iota(jnp.int32, (tiles, LANES), 1)
    for step in range(slab_count):
        slab = partner_of(slab_index, step, slab_count)[0]
        exponents = jnp.zeros((tiles, LANES), jnp.float32)
        factors = jnp.zeros((tiles, LANES), jnp.float32)
        codes = []
        for chunk in range(own_count * planes):
            own, plane = divmod(chunk, planes)
            start = own * tiles * side + slab * planes + plane
            value = total[pl.ds(start, tiles, stride=side), :]
            code, exponent, factor = encode(value)
            codes.append(code)
            exponents = jnp.where(lane_index == chunk, exponent, exponents)
            factors = jnp.where(lane_index == chunk, factor, factors)
            if chunk % 2:
                pair = jnp.concatenate(codes[-2:], axis=0)
                out_refs[step][tiles * (chunk - 1) : tiles * (chunk + 1), :] = whole_codes(pair)
        header = jnp.concatenate([exponents, factors], axis=0)
        out_refs[step][tiles * own_count * planes :, :] = whole_codes(header)


def whole_codes(value):
    return value.astype(jnp.int32).astype(jnp.int16)


def encode(value):
    largest = jnp.max(jnp.abs(value), axis=1, keepdims=True)
    exponent = jnp.maximum(jnp.floor(jnp.log2(jnp.maximum(largest, TINY))), LOWEST_EXPONENT)
    lifted = 1.0 / jnp.exp2(exponent)
    factor = jnp.maximum(jnp.ceil(largest * lifted * FACTOR_UNIT), 1.0)
    code = jnp.floor(value * lifted * (CODE_LIMIT * FACTOR_UNIT / factor) + 0.5)
    return jnp.clip(code, -CODE_LIMIT, CODE_LIMIT), exponent, factor


def swap_cores(block, pair_count):
    return lax.ppermute(block, "pair", [(i, i ^ 1) for i in range(pair_count)])


def gather_chips(boxes, pair_count):
    pieces = []
    for step in range(1, pair_count // CORES):
        perm = [(i, (i + step * CORES) % pair_count) for i in range(pair_count)]
        pieces.append(lax.ppermute(boxes, "pair", perm))
    return pieces


def unpack_kernel(sizes, *refs):
    own_count, slab_count, tiles = sizes
    block_refs, out_ref, blocks, sems = refs[:slab_count], *refs[slab_count:]
    slab_index = lax.axis_index("slab")
    copies = []
    for index in range(slab_count):
        copies.append(pltpu.make_async_copy(block_refs[index], blocks.at[index], sems.at[index]))
        copies[-1].start()
    for index in reversed(range(slab_count)):
        step = slab_count - 1 - index
        copies[index].wait()
        first = partner_of(slab_index, step, slab_count)[1] * own_count
        row_count = own_count * tiles
        header = blocks[index, row_count:, :].astype(jnp.int32).astype(jnp.float32)
        units = jnp.exp2(header[:8, :])
        factors = header[8:, :] * (1.0 / (CODE_LIMIT * FACTOR_UNIT))
        for pair in range(row_count // 16):
            codes = blocks[index, 16 * pair : 16 * pair + 16, :].astype(jnp.int32).astype(jnp.float32)
            for half in range(2):
                chunk = 2 * pair + half
                own, tile = divmod(8 * chunk, tiles)
                row = first + own
                start = (row // 8 * tiles + tile) * 8 + row % 8
                value = codes[8 * half : 8 * half + 8, :] * factors[:, chunk : chunk + 1]
                out_ref[pl.ds(start, 8, stride=8), :] = value * units[:, chunk : chunk + 1]


def unpack(blocks, own_count, cells):
    slab_count = len(blocks)
    row_count = own_count * slab_count
    tiles = cells // LANES
    out = pl.pallas_call(
        functools.partial(unpack_kernel, (own_count, slab_count, tiles)),
        out_shape=jax.ShapeDtypeStruct((row_count * tiles, LANES), jnp.float32),
        in_specs=[pl.BlockSpec(memory_space=pl.ANY)] * slab_count,
        out_specs=pl.BlockSpec(memory_space=pltpu.VMEM),
        scratch_shapes=[
            pltpu.VMEM((slab_count,) + blocks[0].shape, jnp.int16),
            pltpu.SemaphoreType.DMA((slab_count,)),
        ],
        compiler_params=pltpu.CompilerParams(vmem_limit_bytes=8 * 1024 * 1024),
    )(*blocks)
    return out.reshape(row_count // 8, tiles, 8, LANES).transpose(0, 2, 1, 3).reshape(row_count, cells)


def place_own(sizes, match, centers, boxes):
    side, rounds, own_count, slab_count, _ = sizes
    tiles, _, pitch = box_shape(sizes)
    placed = (own_count * rounds * side, side * side)
    either = pl.BlockSpec(memory_space=pl.ANY)
    vectors = pl.BlockSpec(memory_space=pltpu.VMEM)
    return pl.pallas_call(
        functools.partial(own_kernel, sizes),
        out_shape=[jax.ShapeDtypeStruct(placed, jnp.bfloat16)] * 2,
        in_specs=[either] * 3,
        out_specs=[vectors] * 2,
        scratch_shapes=[
            pltpu.SMEM(match.shape, jnp.int32),
            pltpu.SMEM(centers.shape, jnp.int32),
            pltpu.VMEM((1,) + boxes.shape, jnp.bfloat16),
            pltpu.VMEM((own_count * tiles * pitch, LANES), jnp.float32),
            pltpu.SemaphoreType.DMA((3,)),
        ],
        compiler_params=pltpu.CompilerParams(vmem_limit_bytes=60 * 1024 * 1024),
        cost_estimate=pl.CostEstimate(flops=5 * 10**9, bytes_accessed=4 * 1024 * 1024, transcendentals=0),
    )(match, centers, boxes)


def team_forces(sizes, match, centers, mine, partner, pieces):
    side, rounds, own_count, slab_count, pair_count = sizes
    tiles, _, pitch = box_shape(sizes)
    _, rows, _ = pieces[0].shape
    solves = own_count * rounds
    group = min(solves, 8)
    cells = side * side
    basis = sine_basis(side)
    mix_high, mix_low = split_constant(np.kron(np.eye(group), basis))
    mix = np.concatenate([mix_high, mix_high, mix_low], axis=1)
    there = np.stack([np.kron(basis[parity::2, : side // 2].T, basis) for parity in range(2)])
    gain = chebyshev_gain(side).reshape(side, side, side)
    gain = np.concatenate([gain[:, parity::2].reshape(side, -1) for parity in range(2)], axis=1)
    constants = (mix, gain, *split_constant(there), *split_constant(there.transpose(0, 2, 1)))
    either = pl.BlockSpec(memory_space=pl.ANY)
    distant = pl.BlockSpec(memory_space=pltpu.HBM)
    vectors = pl.BlockSpec(memory_space=pltpu.VMEM)
    wide = pltpu.VMEM((2 * solves * side, cells), jnp.bfloat16)
    flops = 2 * solves * side * 3 * 2 * (cells * cells // 2 + cells * group * side)
    inputs = [match, centers, mine, partner, *pieces, *[jnp.asarray(constant) for constant in constants]]
    return pl.pallas_call(
        functools.partial(force_kernel, sizes),
        out_shape=[jax.ShapeDtypeStruct((rows + HEADER_ROWS, LANES), jnp.int16)] * slab_count,
        in_specs=[distant] * 2 + [either] * (len(inputs) - 2 - len(constants)) + [distant] * len(constants),
        out_specs=[vectors] * slab_count,
        scratch_shapes=[
            pltpu.SMEM(match.shape, jnp.int32),
            pltpu.SMEM(centers.shape, jnp.int32),
            pltpu.VMEM(mine.shape, jnp.bfloat16),
            pltpu.VMEM(partner.shape, jnp.bfloat16),
            pltpu.VMEM((pair_count, slab_count, rows, LANES), jnp.bfloat16),
            *[pltpu.VMEM(constant.shape, constant.dtype) for constant in constants],
            pltpu.VMEM((own_count * pair_count * tiles * pitch, LANES), jnp.float32),
            wide,
            wide,
            pltpu.VMEM((solves * tiles * pitch, LANES), jnp.float32),
            pltpu.VMEM((own_count * tiles * side, LANES), jnp.float32),
            pltpu.SemaphoreType.DMA((len(inputs),)),
        ],
        compiler_params=pltpu.CompilerParams(vmem_limit_bytes=60 * 1024 * 1024),
        cost_estimate=pl.CostEstimate(flops=flops, bytes_accessed=8 * 1024 * 1024, transcendentals=0),
    )(*inputs)


def shards(orbitals, centers, matchings):
    slab_count = lax.axis_size("slab")
    pair_count = lax.axis_size("pair")
    local_rows, plane_cells = orbitals.shape
    own_count = local_rows // slab_count
    side = round((plane_cells * slab_count) ** (1.0 / 3.0))
    blocks = orbitals.reshape(slab_count, own_count * plane_cells // LANES, LANES)
    boxes = lax.all_to_all(blocks, "slab", split_axis=0, concat_axis=0, tiled=True)
    sizes = (side, matchings.shape[1], own_count, slab_count, pair_count)
    pieces = gather_chips(boxes, pair_count)
    mine, partner = place_own(sizes, matchings, centers.T, boxes)
    boxes, mine, partner = lax.optimization_barrier((boxes, mine, partner))
    swapped = [swap_cores(boxes, pair_count)]
    pieces, mine, partner = lax.optimization_barrier((pieces, mine, partner))
    pieces = pieces + swapped + [swap_cores(piece, pair_count) for piece in pieces]
    codes = team_forces(sizes, matchings, centers.T, mine, partner, pieces)
    received = []
    for step in reversed(range(1, slab_count)):
        perm = [(i, partner_of(i, step, slab_count)[0]) for i in range(slab_count)]
        received.append(lax.ppermute(codes[step], "slab", perm))
    return unpack(received + [codes[0]], own_count, plane_cells)


def solution(mesh):
    in_specs = (P("pair", "slab"), P(), P("slab", None, None))
    out_specs = P("pair", "slab")
    return jax.shard_map(shards, mesh=mesh, in_specs=in_specs, out_specs=out_specs, check_vma=False)
```

```python
import functools

import jax
import jax.numpy as jnp
import ml_dtypes
import numpy as np
from jax import lax
from jax.experimental import pallas as pl
from jax.experimental.pallas import tpu as pltpu
from jax.sharding import PartitionSpec as P

STEPS = 16
CUT2 = 192
REACH = 8
SCREEN = 0.1
LOWER_BOUND = 0.1
UPPER_BOUND = 12.1
LANES = 128
CORES = 2
CODE_LIMIT = 32767.0
FACTOR_UNIT = 8192.0
LOWEST_EXPONENT = -120.0
TINY = 1e-37
HEADER_ROWS = 16


def split_constant(matrix):
    high = matrix.astype(ml_dtypes.bfloat16)
    low = (matrix - high.astype(np.float64)).astype(ml_dtypes.bfloat16)
    return high, low


def sine_basis(side):
    index = np.arange(1, side + 1, dtype=np.float64)
    return np.sqrt(2.0 / (side + 1)) * np.sin(np.pi * np.outer(index, index) / (side + 1))


def chebyshev_gain(side):
    shifts = -2.0 * np.cos(np.pi * np.arange(1, side + 1, dtype=np.float64) / (side + 1))
    eigenvalue = 6.0 + SCREEN + shifts[:, None, None] + shifts[None, :, None] + shifts[None, None, :]
    middle = (UPPER_BOUND + LOWER_BOUND) / 2.0
    spread = (UPPER_BOUND - LOWER_BOUND) / 2.0
    ratio = middle / spread
    total = np.zeros_like(eigenvalue)
    residual = np.ones_like(eigenvalue)
    direction = residual / middle
    factor = 1.0 / ratio
    for _ in range(STEPS):
        total = total + direction
        residual = residual - eigenvalue * direction
        factor_next = 1.0 / (2.0 * ratio - factor)
        direction = factor_next * factor * direction + 2.0 * factor_next / spread * residual
        factor = factor_next
    return total.reshape(side, side * side).astype(np.float32)


def split_pair(value):
    high = value.astype(jnp.bfloat16)
    low = (value - high.astype(jnp.float32)).astype(jnp.bfloat16)
    return high, low


def dot(left, right):
    return jnp.dot(left, right, preferred_element_type=jnp.float32)


def partner_of(index, step, count):
    if count & (count - 1) == 0:
        return index ^ step, index ^ step
    return (index + step) % count, (index + count - step) % count


def pair_geometry(sizes, match_ref, centers_ref, index):
    _, rounds, own_count, slab_count, _ = sizes
    slab_index = lax.axis_index("slab")
    pair_index = lax.axis_index("pair")

    def orbital_of(member):
        return (member // own_count * slab_count + slab_index) * own_count + member % own_count

    member = pair_index * own_count + index // rounds
    mate = match_ref[0, index % rounds, member]
    own_offset = []
    mate_offset = []
    distance = 0
    for axis in range(3):
        mine = centers_ref[axis, orbital_of(member)]
        other = centers_ref[axis, orbital_of(mate)]
        anchor = (mine + other) >> 1
        own_offset.append(mine - anchor)
        mate_offset.append(other - anchor)
        distance = distance + (mine - other) * (mine - other)
    return member, mate, own_offset, mate_offset, distance <= CUT2


def box_shape(sizes):
    side = sizes[0]
    return side * side // LANES, LANES // side, side + 2 * REACH


def clear_edges(sizes, ref, first, count):
    side = sizes[0]
    tiles, _, pitch = box_shape(sizes)
    zeros = jnp.zeros((REACH, LANES), jnp.float32)

    def clear(index, carry):
        start = (first * tiles + index) * pitch
        ref[pl.ds(pl.multiple_of(start, 8), REACH), :] = zeros
        ref[pl.ds(pl.multiple_of(start + REACH + side, 8), REACH), :] = zeros
        return carry

    lax.fori_loop(0, count * tiles, clear, 0, unroll=8)


def spread(sizes, boxes_ref, fields, pair):
    side, _, own_count, slab_count, _ = sizes
    planes = side // slab_count
    tiles, _, pitch = box_shape(sizes)

    def spread_slab(slab, carry):
        for chunk in range(own_count * planes // 2):
            block = boxes_ref[pair, slab, 16 * chunk : 16 * chunk + 16, :].astype(jnp.float32)
            for half in range(2):
                own, plane = divmod(2 * chunk + half, planes)
                start = (pair * own_count + own) * tiles * pitch + REACH + slab * planes + plane
                fields[pl.ds(start, tiles, stride=pitch), :] = block[8 * half : 8 * half + 8, :]
        return carry

    lax.fori_loop(0, slab_count, spread_slab, 0, unroll=4)


def rolled(sizes, ref, box, row, rows, offset_x, offset_flat):
    tiles, _, pitch = box_shape(sizes)
    whole = (offset_flat >> 7) & (tiles - 1)
    part = offset_flat & (LANES - 1)
    start = box * tiles * pitch + REACH + row - offset_x
    moved = []
    for tile in range(tiles):
        first_row = start + ((tile - whole) & (tiles - 1)) * pitch
        moved.append(pltpu.roll(ref[pl.ds(first_row, rows), :], part, axis=1))
    keep = lax.broadcasted_iota(jnp.int32, (rows, LANES), 1) >= part
    return [jnp.where(keep, moved[t], moved[(t - 1) % tiles]) for t in range(tiles)]


def place_partner(sizes, fields, box, own_offset, offset, active):
    side = sizes[0]
    tiles, lines, _ = box_shape(sizes)
    placed = rolled(sizes, fields, box, 0, side, offset[0], offset[1] * side + offset[2])
    lane = lax.broadcasted_iota(jnp.int32, (1, LANES), 1)
    lows = [jnp.maximum(jnp.maximum(a, b), 0) for a, b in zip(own_offset, offset)]
    highs = [side + jnp.minimum(jnp.minimum(a, b), 0) for a, b in zip(own_offset, offset)]
    point_ok = (lane % side >= lows[2]) & (lane % side < highs[2]) & active
    result = []
    for tile in range(tiles):
        line = lane // side + tile * lines
        ok = jnp.where(point_ok & (line >= lows[1]) & (line < highs[1]), 1.0, 0.0)
        result.append(placed[tile] * ok)
    return result


def own_kernel(
    sizes, match_hbm, centers_hbm, own_hbm, mine_ref, partner_ref, match_ref, centers_ref, boxes_ref, fields, sems
):
    side, rounds, own_count, _, _ = sizes
    tiles, _, _ = box_shape(sizes)
    first_member = lax.axis_index("pair") * own_count
    sources = (match_hbm, centers_hbm, own_hbm)
    targets = (match_ref, centers_ref, boxes_ref.at[0])
    copies = [pltpu.make_async_copy(s, t, sems.at[i]) for i, (s, t) in enumerate(zip(sources, targets))]
    for copy in copies:
        copy.start()
    clear_edges(sizes, fields, 0, own_count)
    for copy in copies:
        copy.wait()
    spread(sizes, boxes_ref, fields, 0)

    def place(index, carry):
        member, mate, a, b, active = pair_geometry(sizes, match_ref, centers_ref, index)
        rows = pl.ds(pl.multiple_of(index * side, side), side)
        placed = rolled(sizes, fields, member - first_member, 0, side, a[0], a[1] * side + a[2])
        for tile in range(tiles):
            mine_ref[rows, tile * LANES : (tile + 1) * LANES] = placed[tile].astype(jnp.bfloat16)
        local = mate - first_member

        @pl.when((local >= 0) & (local < own_count))
        def _():
            placed = place_partner(sizes, fields, local, a, b, active)
            for tile in range(tiles):
                partner_ref[rows, tile * LANES : (tile + 1) * LANES] = placed[tile].astype(jnp.bfloat16)

        return carry

    lax.fori_loop(0, own_count * rounds, place, 0)


def force_kernel(sizes, match_hbm, centers_hbm, mine_hbm, partner_hbm, *refs):
    side, rounds, own_count, slab_count, pair_count = sizes
    piece_hbm, refs = refs[: pair_count - 1], refs[pair_count - 1 :]
    constant_hbm, refs = refs[:6], refs[6:]
    out_refs, refs = refs[:slab_count], refs[slab_count:]
    match_ref, centers_ref, mine, partner, boxes_ref, *refs = refs
    constants, refs = refs[:6], refs[6:]
    mix_ref, gain_ref, there_high, there_low, back_high, back_low = constants
    fields, first, second, *terms, total, sems = refs
    planes = side // slab_count
    tiles, lines, pitch = box_shape(sizes)
    solves = own_count * rounds
    group = min(solves, 8)
    group_rows = group * side
    cells = tiles * LANES
    width = cells // 2
    slab_index = lax.axis_index("slab")
    pair_index = lax.axis_index("pair")
    core = pair_index % CORES
    chip = pair_index // CORES
    chips = pair_count // CORES
    first_member = pair_index * own_count

    places = [
        (chip + chips - step) % chips * CORES + (core + core_step) % CORES
        for core_step in range(CORES)
        for step in range(chips)
    ]
    places = places[1:]
    sources = [match_hbm, centers_hbm, *piece_hbm, mine_hbm, partner_hbm, *constant_hbm]
    targets = [match_ref, centers_ref, *[boxes_ref.at[pair] for pair in places], mine, partner, *constants]
    copies = [pltpu.make_async_copy(s, t, sems.at[i]) for i, (s, t) in enumerate(zip(sources, targets))]
    for copy in copies:
        copy.start()
    for pair in places:
        clear_edges(sizes, fields, pair * own_count, own_count)
    for ref in terms:
        clear_edges(sizes, ref, 0, group)
    boxes_count = 2 + len(places)
    for copy in copies[:boxes_count]:
        copy.wait()
    for pair in places:
        spread(sizes, boxes_ref, fields, pair)
    for copy in copies[boxes_count : boxes_count + 2]:
        copy.wait()

    row_count = solves * side
    half_tiles = tiles // 2
    half_cells = cells // 2

    def mirrored(tile):
        line = lax.broadcasted_iota(jnp.int32, tile.shape, 1) // side
        result = None
        for index in range(lines):
            amount = (2 * index - lines + 1) * side % LANES
            if index < 2:
                moved = pltpu.roll(tile, amount, axis=1)
                result = moved if result is None else jnp.where(line % 2 == index, moved, result)
        return result

    def store_split(ref, start, count, columns, value):
        high, low = split_pair(value)
        ref[start : start + count, columns] = high
        ref[row_count + start : row_count + start + count, columns] = low

    def densities(index):
        start = index * side
        rows = slice(start, start + side)
        _, mate, a, b, active = pair_geometry(sizes, match_ref, centers_ref, index)
        is_own = (mate >= first_member) & (mate < first_member + own_count)
        placed = place_partner(sizes, fields, mate, a, b, active)
        density = []
        for tile in range(tiles):
            columns = slice(tile * LANES, (tile + 1) * LANES)
            chosen = jnp.where(is_own, partner[rows, columns].astype(jnp.float32), placed[tile])
            partner[rows, columns] = chosen.astype(jnp.bfloat16)
            density.append(mine[rows, columns].astype(jnp.float32) * chosen)
        for tile in range(half_tiles):
            far = mirrored(density[tiles - 1 - tile])
            for parity, value in enumerate((density[tile] + far, density[tile] - far)):
                column = parity * half_cells + tile * LANES
                store_split(first, start, side, slice(column, column + LANES), value)

    mix_copy, gain_copy, *matrix_copies = copies[boxes_count + 2 :]
    mix_copy.wait()

    def along_x(start, columns, source):
        high = source[start : start + group_rows, columns]
        low = source[row_count + start : row_count + start + group_rows, columns]
        return dot(mix_ref[...], jnp.concatenate([high, low, high], axis=0))

    def in_plane(parity, columns, source, high_ref, low_ref):
        inner = slice(parity * half_cells, (parity + 1) * half_cells)
        high = source[:row_count, inner]
        low = source[row_count:, inner]
        basis = high_ref[parity, :, columns]
        rest = low_ref[parity, :, columns]
        left = jnp.concatenate([high, low, high], axis=1)
        return dot(left, jnp.concatenate([basis, basis, rest], axis=0))

    for start in range(0, row_count, group_rows):
        for index in range(start // side, (start + group_rows) // side):
            densities(index)
        columns = slice(0, cells)
        store_split(second, start, group_rows, columns, along_x(start, columns, first))

    for copy in (gain_copy, *matrix_copies[:2]):
        copy.wait()
    for parity in range(2):
        for column in range(0, half_cells, width):
            columns = slice(column, column + width)
            value = in_plane(parity, columns, second, there_high, there_low)
            columns = slice(parity * half_cells + column, parity * half_cells + column + width)
            gain = gain_ref[:, columns]
            value = (value.reshape(solves, side, width) * gain[None]).reshape(row_count, width)
            store_split(first, 0, row_count, columns, value)

    for copy in matrix_copies[2:]:
        copy.wait()
    for parity in range(2):
        for column in range(0, half_cells, width):
            value = in_plane(parity, slice(column, column + width), first, back_high, back_low)
            columns = slice(parity * half_cells + column, parity * half_cells + column + width)
            store_split(second, 0, row_count, columns, value)

    for start in range(0, row_count, group_rows):
        for column in range(0, half_cells, width):
            even = along_x(start, slice(column, column + width), second)
            odd = along_x(start, slice(half_cells + column, half_cells + column + width), second)
            for part in range(width // LANES):
                tile = column // LANES + part
                lanes = slice(part * LANES, (part + 1) * LANES)
                near = even[:, lanes] + odd[:, lanes]
                far = mirrored(even[:, lanes] - odd[:, lanes])
                for place, value in ((tile, near), (tiles - 1 - tile, far)):
                    columns = slice(place * LANES, (place + 1) * LANES)
                    value = value * partner[start : start + group_rows, columns].astype(jnp.float32)
                    for solve in range(group):
                        row = (solve * tiles + place) * pitch + REACH
                        terms[start // group_rows][row : row + side, :] = value[solve * side : (solve + 1) * side, :]

    step_rows = 16

    def collect(own, row):
        sums = None
        for turn in range(rounds):
            index = own * rounds + turn
            _, _, a, _, _ = pair_geometry(sizes, match_ref, centers_ref, index)
            ref = terms[index // group]
            term = rolled(sizes, ref, index % group, row, step_rows, -a[0], -(a[1] * side + a[2]))
            sums = term if sums is None else [s + t for s, t in zip(sums, term)]
        for tile in range(tiles):
            start = (own * tiles + tile) * side + row
            total[start : start + step_rows, :] = sums[tile]

    for own in range(own_count):
        for row in range(0, side, step_rows):
            collect(own, row)

    lane_index = lax.broadcasted_iota(jnp.int32, (tiles, LANES), 1)
    for step in range(slab_count):
        slab = partner_of(slab_index, step, slab_count)[0]
        exponents = jnp.zeros((tiles, LANES), jnp.float32)
        factors = jnp.zeros((tiles, LANES), jnp.float32)
        codes = []
        for chunk in range(own_count * planes):
            own, plane = divmod(chunk, planes)
            start = own * tiles * side + slab * planes + plane
            value = total[pl.ds(start, tiles, stride=side), :]
            code, exponent, factor = encode(value)
            codes.append(code)
            exponents = jnp.where(lane_index == chunk, exponent, exponents)
            factors = jnp.where(lane_index == chunk, factor, factors)
            if chunk % 2:
                pair = jnp.concatenate(codes[-2:], axis=0)
                out_refs[step][tiles * (chunk - 1) : tiles * (chunk + 1), :] = whole_codes(pair)
        header = jnp.concatenate([exponents, factors], axis=0)
        out_refs[step][tiles * own_count * planes :, :] = whole_codes(header)


def whole_codes(value):
    return value.astype(jnp.int32).astype(jnp.int16)


def encode(value):
    largest = jnp.max(jnp.abs(value), axis=1, keepdims=True)
    exponent = jnp.maximum(jnp.floor(jnp.log2(jnp.maximum(largest, TINY))), LOWEST_EXPONENT)
    lifted = 1.0 / jnp.exp2(exponent)
    factor = jnp.maximum(jnp.ceil(largest * lifted * FACTOR_UNIT), 1.0)
    code = jnp.floor(value * lifted * (CODE_LIMIT * FACTOR_UNIT / factor) + 0.5)
    return jnp.clip(code, -CODE_LIMIT, CODE_LIMIT), exponent, factor


def swap_cores(block, pair_count):
    return lax.ppermute(block, "pair", [(i, i ^ 1) for i in range(pair_count)])


def gather_chips(boxes, pair_count):
    pieces = []
    for step in range(1, pair_count // CORES):
        perm = [(i, (i + step * CORES) % pair_count) for i in range(pair_count)]
        pieces.append(lax.ppermute(boxes, "pair", perm))
    return pieces


def unpack_kernel(sizes, *refs):
    own_count, slab_count, tiles = sizes
    block_refs, out_ref, blocks, sems = refs[:slab_count], *refs[slab_count:]
    slab_index = lax.axis_index("slab")
    copies = []
    for index in range(slab_count):
        copies.append(pltpu.make_async_copy(block_refs[index], blocks.at[index], sems.at[index]))
        copies[-1].start()
    for index in reversed(range(slab_count)):
        step = slab_count - 1 - index
        copies[index].wait()
        first = partner_of(slab_index, step, slab_count)[1] * own_count
        row_count = own_count * tiles
        header = blocks[index, row_count:, :].astype(jnp.int32).astype(jnp.float32)
        units = jnp.exp2(header[:8, :])
        factors = header[8:, :] * (1.0 / (CODE_LIMIT * FACTOR_UNIT))
        for pair in range(row_count // 16):
            codes = blocks[index, 16 * pair : 16 * pair + 16, :].astype(jnp.int32).astype(jnp.float32)
            for half in range(2):
                chunk = 2 * pair + half
                own, tile = divmod(8 * chunk, tiles)
                row = first + own
                start = (row // 8 * tiles + tile) * 8 + row % 8
                value = codes[8 * half : 8 * half + 8, :] * factors[:, chunk : chunk + 1]
                out_ref[pl.ds(start, 8, stride=8), :] = value * units[:, chunk : chunk + 1]


def unpack(blocks, own_count, cells):
    slab_count = len(blocks)
    row_count = own_count * slab_count
    tiles = cells // LANES
    out = pl.pallas_call(
        functools.partial(unpack_kernel, (own_count, slab_count, tiles)),
        out_shape=jax.ShapeDtypeStruct((row_count * tiles, LANES), jnp.float32),
        in_specs=[pl.BlockSpec(memory_space=pl.ANY)] * slab_count,
        out_specs=pl.BlockSpec(memory_space=pltpu.VMEM),
        scratch_shapes=[
            pltpu.VMEM((slab_count,) + blocks[0].shape, jnp.int16),
            pltpu.SemaphoreType.DMA((slab_count,)),
        ],
        compiler_params=pltpu.CompilerParams(vmem_limit_bytes=8 * 1024 * 1024),
    )(*blocks)
    return out.reshape(row_count // 8, tiles, 8, LANES).transpose(0, 2, 1, 3).reshape(row_count, cells)


def place_own(sizes, match, centers, boxes):
    side, rounds, own_count, slab_count, _ = sizes
    tiles, _, pitch = box_shape(sizes)
    placed = (own_count * rounds * side, side * side)
    either = pl.BlockSpec(memory_space=pl.ANY)
    vectors = pl.BlockSpec(memory_space=pltpu.VMEM)
    return pl.pallas_call(
        functools.partial(own_kernel, sizes),
        out_shape=[jax.ShapeDtypeStruct(placed, jnp.bfloat16)] * 2,
        in_specs=[either] * 3,
        out_specs=[vectors] * 2,
        scratch_shapes=[
            pltpu.SMEM(match.shape, jnp.int32),
            pltpu.SMEM(centers.shape, jnp.int32),
            pltpu.VMEM((1,) + boxes.shape, jnp.bfloat16),
            pltpu.VMEM((own_count * tiles * pitch, LANES), jnp.float32),
            pltpu.SemaphoreType.DMA((3,)),
        ],
        compiler_params=pltpu.CompilerParams(vmem_limit_bytes=60 * 1024 * 1024),
        cost_estimate=pl.CostEstimate(flops=5 * 10**9, bytes_accessed=4 * 1024 * 1024, transcendentals=0),
    )(match, centers, boxes)


def team_forces(sizes, match, centers, mine, partner, pieces):
    side, rounds, own_count, slab_count, pair_count = sizes
    tiles, _, pitch = box_shape(sizes)
    _, rows, _ = pieces[0].shape
    solves = own_count * rounds
    group = min(solves, 8)
    cells = side * side
    basis = sine_basis(side)
    mix_high, mix_low = split_constant(np.kron(np.eye(group), basis))
    mix = np.concatenate([mix_high, mix_high, mix_low], axis=1)
    there = np.stack([np.kron(basis[parity::2, : side // 2].T, basis) for parity in range(2)])
    gain = chebyshev_gain(side).reshape(side, side, side)
    gain = np.concatenate([gain[:, parity::2].reshape(side, -1) for parity in range(2)], axis=1)
    constants = (mix, gain, *split_constant(there), *split_constant(there.transpose(0, 2, 1)))
    either = pl.BlockSpec(memory_space=pl.ANY)
    distant = pl.BlockSpec(memory_space=pltpu.HBM)
    vectors = pl.BlockSpec(memory_space=pltpu.VMEM)
    wide = pltpu.VMEM((2 * solves * side, cells), jnp.bfloat16)
    flops = 2 * solves * side * 3 * 2 * (cells * cells // 2 + cells * group * side)
    inputs = [match, centers, mine, partner, *pieces, *[jnp.asarray(constant) for constant in constants]]
    return pl.pallas_call(
        functools.partial(force_kernel, sizes),
        out_shape=[jax.ShapeDtypeStruct((rows + HEADER_ROWS, LANES), jnp.int16)] * slab_count,
        in_specs=[distant] * 2 + [either] * (len(inputs) - 2 - len(constants)) + [distant] * len(constants),
        out_specs=[vectors] * slab_count,
        scratch_shapes=[
            pltpu.SMEM(match.shape, jnp.int32),
            pltpu.SMEM(centers.shape, jnp.int32),
            pltpu.VMEM(mine.shape, jnp.bfloat16),
            pltpu.VMEM(partner.shape, jnp.bfloat16),
            pltpu.VMEM((pair_count, slab_count, rows, LANES), jnp.bfloat16),
            *[pltpu.VMEM(constant.shape, constant.dtype) for constant in constants],
            pltpu.VMEM((own_count * pair_count * tiles * pitch, LANES), jnp.float32),
            wide,
            wide,
            *[pltpu.VMEM((group * tiles * pitch, LANES), jnp.float32)] * (solves // group),
            pltpu.VMEM((own_count * tiles * side, LANES), jnp.float32),
            pltpu.SemaphoreType.DMA((len(inputs),)),
        ],
        compiler_params=pltpu.CompilerParams(vmem_limit_bytes=60 * 1024 * 1024),
        cost_estimate=pl.CostEstimate(flops=flops, bytes_accessed=8 * 1024 * 1024, transcendentals=0),
    )(*inputs)


def shards(orbitals, centers, matchings):
    slab_count = lax.axis_size("slab")
    pair_count = lax.axis_size("pair")
    local_rows, plane_cells = orbitals.shape
    own_count = local_rows // slab_count
    side = round((plane_cells * slab_count) ** (1.0 / 3.0))
    blocks = orbitals.reshape(slab_count, own_count * plane_cells // LANES, LANES)
    boxes = lax.all_to_all(blocks, "slab", split_axis=0, concat_axis=0, tiled=True)
    sizes = (side, matchings.shape[1], own_count, slab_count, pair_count)
    pieces = gather_chips(boxes, pair_count)
    mine, partner = place_own(sizes, matchings, centers.T, boxes)
    boxes, mine, partner = lax.optimization_barrier((boxes, mine, partner))
    swapped = [swap_cores(boxes, pair_count)]
    pieces, mine, partner = lax.optimization_barrier((pieces, mine, partner))
    pieces = pieces + swapped + [swap_cores(piece, pair_count) for piece in pieces]
    codes = team_forces(sizes, matchings, centers.T, mine, partner, pieces)
    received = []
    for step in reversed(range(1, slab_count)):
        perm = [(i, partner_of(i, step, slab_count)[0]) for i in range(slab_count)]
        received.append(lax.ppermute(codes[step], "slab", perm))
    return unpack(received + [codes[0]], own_count, plane_cells)


def solution(mesh):
    in_specs = (P("pair", "slab"), P(), P("slab", None, None))
    out_specs = P("pair", "slab")
    return jax.shard_map(shards, mesh=mesh, in_specs=in_specs, out_specs=out_specs, check_vma=False)
```

```python
import functools

import jax
import jax.numpy as jnp
import ml_dtypes
import numpy as np
from jax import lax
from jax.experimental import pallas as pl
from jax.experimental.pallas import tpu as pltpu
from jax.sharding import PartitionSpec as P

STEPS = 16
CUT2 = 192
REACH = 8
SCREEN = 0.1
LOWER_BOUND = 0.1
UPPER_BOUND = 12.1
LANES = 128
CORES = 2
CODE_LIMIT = 32767.0
FACTOR_UNIT = 8192.0
LOWEST_EXPONENT = -120.0
TINY = 1e-37
HEADER_ROWS = 16


def split_constant(matrix):
    high = matrix.astype(ml_dtypes.bfloat16)
    low = (matrix - high.astype(np.float64)).astype(ml_dtypes.bfloat16)
    return high, low


def sine_basis(side):
    index = np.arange(1, side + 1, dtype=np.float64)
    return np.sqrt(2.0 / (side + 1)) * np.sin(np.pi * np.outer(index, index) / (side + 1))


def chebyshev_gain(side):
    shifts = -2.0 * np.cos(np.pi * np.arange(1, side + 1, dtype=np.float64) / (side + 1))
    eigenvalue = 6.0 + SCREEN + shifts[:, None, None] + shifts[None, :, None] + shifts[None, None, :]
    middle = (UPPER_BOUND + LOWER_BOUND) / 2.0
    spread = (UPPER_BOUND - LOWER_BOUND) / 2.0
    ratio = middle / spread
    total = np.zeros_like(eigenvalue)
    residual = np.ones_like(eigenvalue)
    direction = residual / middle
    factor = 1.0 / ratio
    for _ in range(STEPS):
        total = total + direction
        residual = residual - eigenvalue * direction
        factor_next = 1.0 / (2.0 * ratio - factor)
        direction = factor_next * factor * direction + 2.0 * factor_next / spread * residual
        factor = factor_next
    return total.reshape(side, side * side).astype(np.float32)


def split_pair(value):
    high = value.astype(jnp.bfloat16)
    low = (value - high.astype(jnp.float32)).astype(jnp.bfloat16)
    return high, low


def dot(left, right):
    return jnp.dot(left, right, preferred_element_type=jnp.float32)


def partner_of(index, step, count):
    if count & (count - 1) == 0:
        return index ^ step, index ^ step
    return (index + step) % count, (index + count - step) % count


def pair_geometry(sizes, match_ref, centers_ref, index):
    _, rounds, own_count, slab_count, _ = sizes
    slab_index = lax.axis_index("slab")
    pair_index = lax.axis_index("pair")

    def orbital_of(member):
        return (member // own_count * slab_count + slab_index) * own_count + member % own_count

    member = pair_index * own_count + index // rounds
    mate = match_ref[0, index % rounds, member]
    own_offset = []
    mate_offset = []
    distance = 0
    for axis in range(3):
        mine = centers_ref[axis, orbital_of(member)]
        other = centers_ref[axis, orbital_of(mate)]
        anchor = (mine + other) >> 1
        own_offset.append(mine - anchor)
        mate_offset.append(other - anchor)
        distance = distance + (mine - other) * (mine - other)
    return member, mate, own_offset, mate_offset, distance <= CUT2


def box_shape(sizes):
    side = sizes[0]
    return side * side // LANES, LANES // side, side + 2 * REACH


def clear_edges(sizes, ref, first, count):
    side = sizes[0]
    tiles, _, pitch = box_shape(sizes)
    zeros = jnp.zeros((REACH, LANES), jnp.float32)

    def clear(index, carry):
        start = (first * tiles + index) * pitch
        ref[pl.ds(pl.multiple_of(start, 8), REACH), :] = zeros
        ref[pl.ds(pl.multiple_of(start + REACH + side, 8), REACH), :] = zeros
        return carry

    lax.fori_loop(0, count * tiles, clear, 0, unroll=8)


def turned(tiles):
    row = lax.broadcasted_iota(jnp.int32, (8, LANES), 0)
    tiles = list(tiles)
    for distance in (4, 2, 1):
        low = (row & distance) == 0
        for index in range(8):
            if index & distance == 0:
                first, second = tiles[index], tiles[index + distance]
                tiles[index] = jnp.where(low, first, pltpu.roll(second, distance, axis=0))
                tiles[index + distance] = jnp.where(low, pltpu.roll(first, 8 - distance, axis=0), second)
    return tiles


def spread(sizes, boxes_ref, fields, pair):
    side, _, own_count, slab_count, _ = sizes
    planes = side // slab_count
    tiles, _, pitch = box_shape(sizes)
    for group in range(side // 8):
        halves = {}
        for slab in range(8 * group // planes, (8 * group + 7) // planes + 1):
            for chunk in range(own_count * planes // 2):
                block = boxes_ref[pair, slab, 16 * chunk : 16 * chunk + 16, :].astype(jnp.float32)
                for half in range(2):
                    own, plane = divmod(2 * chunk + half, planes)
                    halves[own, slab * planes + plane] = block[8 * half : 8 * half + 8, :]
        for own in range(own_count):
            rows = turned([halves[own, 8 * group + index] for index in range(8)])
            for tile in range(tiles):
                start = ((pair * own_count + own) * tiles + tile) * pitch + REACH + 8 * group
                fields[pl.ds(pl.multiple_of(start, 8), 8), :] = rows[tile]


def rolled(sizes, ref, box, row, rows, offset_x, offset_flat):
    tiles, _, pitch = box_shape(sizes)
    whole = (offset_flat >> 7) & (tiles - 1)
    part = offset_flat & (LANES - 1)
    start = box * tiles * pitch + REACH + row - offset_x
    moved = []
    for tile in range(tiles):
        first_row = start + ((tile - whole) & (tiles - 1)) * pitch
        moved.append(pltpu.roll(ref[pl.ds(first_row, rows), :], part, axis=1))
    keep = lax.broadcasted_iota(jnp.int32, (rows, LANES), 1) >= part
    return [jnp.where(keep, moved[t], moved[(t - 1) % tiles]) for t in range(tiles)]


def place_partner(sizes, fields, box, own_offset, offset, active):
    side = sizes[0]
    tiles, lines, _ = box_shape(sizes)
    placed = rolled(sizes, fields, box, 0, side, offset[0], offset[1] * side + offset[2])
    lane = lax.broadcasted_iota(jnp.int32, (1, LANES), 1)
    lows = [jnp.maximum(jnp.maximum(a, b), 0) for a, b in zip(own_offset, offset)]
    highs = [side + jnp.minimum(jnp.minimum(a, b), 0) for a, b in zip(own_offset, offset)]
    point_ok = (lane % side >= lows[2]) & (lane % side < highs[2]) & active
    result = []
    for tile in range(tiles):
        line = lane // side + tile * lines
        ok = jnp.where(point_ok & (line >= lows[1]) & (line < highs[1]), 1.0, 0.0)
        result.append(placed[tile] * ok)
    return result


def own_kernel(
    sizes, match_hbm, centers_hbm, own_hbm, mine_ref, partner_ref, match_ref, centers_ref, boxes_ref, fields, sems
):
    side, rounds, own_count, _, _ = sizes
    tiles, _, _ = box_shape(sizes)
    first_member = lax.axis_index("pair") * own_count
    sources = (match_hbm, centers_hbm, own_hbm)
    targets = (match_ref, centers_ref, boxes_ref.at[0])
    copies = [pltpu.make_async_copy(s, t, sems.at[i]) for i, (s, t) in enumerate(zip(sources, targets))]
    for copy in copies:
        copy.start()
    clear_edges(sizes, fields, 0, own_count)
    for copy in copies:
        copy.wait()
    spread(sizes, boxes_ref, fields, 0)

    def place(index, carry):
        member, mate, a, b, active = pair_geometry(sizes, match_ref, centers_ref, index)
        rows = pl.ds(pl.multiple_of(index * side, side), side)
        placed = rolled(sizes, fields, member - first_member, 0, side, a[0], a[1] * side + a[2])
        for tile in range(tiles):
            mine_ref[rows, tile * LANES : (tile + 1) * LANES] = placed[tile].astype(jnp.bfloat16)
        local = mate - first_member

        @pl.when((local >= 0) & (local < own_count))
        def _():
            placed = place_partner(sizes, fields, local, a, b, active)
            for tile in range(tiles):
                partner_ref[rows, tile * LANES : (tile + 1) * LANES] = placed[tile].astype(jnp.bfloat16)

        return carry

    lax.fori_loop(0, own_count * rounds, place, 0)


def force_kernel(sizes, match_hbm, centers_hbm, mine_hbm, partner_hbm, *refs):
    side, rounds, own_count, slab_count, pair_count = sizes
    piece_hbm, refs = refs[: pair_count - 1], refs[pair_count - 1 :]
    constant_hbm, refs = refs[:6], refs[6:]
    out_refs, refs = refs[:slab_count], refs[slab_count:]
    match_ref, centers_ref, mine, partner, boxes_ref, *refs = refs
    constants, refs = refs[:6], refs[6:]
    mix_ref, gain_ref, there_high, there_low, back_high, back_low = constants
    fields, first, second, *terms, all_codes, sems = refs
    planes = side // slab_count
    tiles, lines, pitch = box_shape(sizes)
    solves = own_count * rounds
    group = min(solves, 8)
    group_rows = group * side
    cells = tiles * LANES
    width = cells // 2
    slab_index = lax.axis_index("slab")
    pair_index = lax.axis_index("pair")
    core = pair_index % CORES
    chip = pair_index // CORES
    chips = pair_count // CORES
    first_member = pair_index * own_count

    places = [
        (chip + chips - step) % chips * CORES + (core + core_step) % CORES
        for core_step in range(CORES)
        for step in range(chips)
    ]
    places = places[1:]
    sources = [match_hbm, centers_hbm, *piece_hbm, mine_hbm, partner_hbm, *constant_hbm]
    targets = [match_ref, centers_ref, *[boxes_ref.at[pair] for pair in places], mine, partner, *constants]
    copies = [pltpu.make_async_copy(s, t, sems.at[i]) for i, (s, t) in enumerate(zip(sources, targets))]
    for copy in copies:
        copy.start()
    for pair in places:
        clear_edges(sizes, fields, pair * own_count, own_count)
    for ref in terms:
        clear_edges(sizes, ref, 0, group)
    boxes_count = 2 + len(places)
    for copy in copies[:boxes_count]:
        copy.wait()
    for pair in places:
        spread(sizes, boxes_ref, fields, pair)
    for copy in copies[boxes_count : boxes_count + 2]:
        copy.wait()

    row_count = solves * side
    half_tiles = tiles // 2
    half_cells = cells // 2

    def mirrored(tile):
        line = lax.broadcasted_iota(jnp.int32, tile.shape, 1) // side
        result = None
        for index in range(lines):
            amount = (2 * index - lines + 1) * side % LANES
            if index < 2:
                moved = pltpu.roll(tile, amount, axis=1)
                result = moved if result is None else jnp.where(line % 2 == index, moved, result)
        return result

    def store_split(ref, start, count, columns, value):
        high, low = split_pair(value)
        ref[start : start + count, columns] = high
        ref[row_count + start : row_count + start + count, columns] = low

    def densities(index):
        start = index * side
        rows = slice(start, start + side)
        _, mate, a, b, active = pair_geometry(sizes, match_ref, centers_ref, index)
        is_own = (mate >= first_member) & (mate < first_member + own_count)
        placed = place_partner(sizes, fields, mate, a, b, active)
        density = []
        for tile in range(tiles):
            columns = slice(tile * LANES, (tile + 1) * LANES)
            chosen = jnp.where(is_own, partner[rows, columns].astype(jnp.float32), placed[tile])
            partner[rows, columns] = chosen.astype(jnp.bfloat16)
            density.append(mine[rows, columns].astype(jnp.float32) * chosen)
        for tile in range(half_tiles):
            far = mirrored(density[tiles - 1 - tile])
            for parity, value in enumerate((density[tile] + far, density[tile] - far)):
                column = parity * half_cells + tile * LANES
                store_split(first, start, side, slice(column, column + LANES), value)

    mix_copy, gain_copy, *matrix_copies = copies[boxes_count + 2 :]
    mix_copy.wait()

    def along_x(start, columns, source):
        high = source[start : start + group_rows, columns]
        low = source[row_count + start : row_count + start + group_rows, columns]
        return dot(mix_ref[...], jnp.concatenate([high, low, high], axis=0))

    def in_plane(parity, columns, source, high_ref, low_ref):
        inner = slice(parity * half_cells, (parity + 1) * half_cells)
        high = source[:row_count, inner]
        low = source[row_count:, inner]
        basis = high_ref[parity, :, columns]
        rest = low_ref[parity, :, columns]
        left = jnp.concatenate([high, low, high], axis=1)
        return dot(left, jnp.concatenate([basis, basis, rest], axis=0))

    for start in range(0, row_count, group_rows):
        for index in range(start // side, (start + group_rows) // side):
            densities(index)
        columns = slice(0, cells)
        store_split(second, start, group_rows, columns, along_x(start, columns, first))

    for copy in (gain_copy, *matrix_copies[:2]):
        copy.wait()
    for parity in range(2):
        for column in range(0, half_cells, width):
            columns = slice(column, column + width)
            value = in_plane(parity, columns, second, there_high, there_low)
            columns = slice(parity * half_cells + column, parity * half_cells + column + width)
            gain = gain_ref[:, columns]
            value = (value.reshape(solves, side, width) * gain[None]).reshape(row_count, width)
            store_split(first, 0, row_count, columns, value)

    for copy in matrix_copies[2:]:
        copy.wait()
    for parity in range(2):
        for column in range(0, half_cells, width):
            value = in_plane(parity, slice(column, column + width), first, back_high, back_low)
            columns = slice(parity * half_cells + column, parity * half_cells + column + width)
            store_split(second, 0, row_count, columns, value)

    for start in range(0, row_count, group_rows):
        for column in range(0, half_cells, width):
            even = along_x(start, slice(column, column + width), second)
            odd = along_x(start, slice(half_cells + column, half_cells + column + width), second)
            for part in range(width // LANES):
                tile = column // LANES + part
                lanes = slice(part * LANES, (part + 1) * LANES)
                near = even[:, lanes] + odd[:, lanes]
                far = mirrored(even[:, lanes] - odd[:, lanes])
                for place, value in ((tile, near), (tiles - 1 - tile, far)):
                    columns = slice(place * LANES, (place + 1) * LANES)
                    value = value * partner[start : start + group_rows, columns].astype(jnp.float32)
                    for solve in range(group):
                        row = (solve * tiles + place) * pitch + REACH
                        terms[start // group_rows][row : row + side, :] = value[solve * side : (solve + 1) * side, :]

    step_rows = 16

    def collect(own, row):
        sums = None
        for turn in range(rounds):
            index = own * rounds + turn
            _, _, a, _, _ = pair_geometry(sizes, match_ref, centers_ref, index)
            ref = terms[index // group]
            term = rolled(sizes, ref, index % group, row, step_rows, -a[0], -(a[1] * side + a[2]))
            sums = term if sums is None else [s + t for s, t in zip(sums, term)]
        return sums

    lane_index = lax.broadcasted_iota(jnp.int32, (tiles, LANES), 1)
    exponents = [jnp.zeros((tiles, LANES), jnp.float32)] * slab_count
    factors = [jnp.zeros((tiles, LANES), jnp.float32)] * slab_count
    codes = {}
    for own in range(own_count):
        for row in range(0, side, step_rows):
            sums = collect(own, row)
            for half in range(0, step_rows, 8):
                for index, value in enumerate(turned([tile[half : half + 8, :] for tile in sums])):
                    slab, plane = divmod(row + half + index, planes)
                    chunk = own * planes + plane
                    codes[slab, chunk], exponent, factor = encode(value)
                    exponents[slab] = jnp.where(lane_index == chunk, exponent, exponents[slab])
                    factors[slab] = jnp.where(lane_index == chunk, factor, factors[slab])
                    if chunk % 2:
                        pair = jnp.concatenate([codes[slab, chunk - 1], codes[slab, chunk]], axis=0)
                        all_codes[slab, tiles * (chunk - 1) : tiles * (chunk + 1), :] = whole_codes(pair)
    for slab in range(slab_count):
        header = jnp.concatenate([exponents[slab], factors[slab]], axis=0)
        all_codes[slab, tiles * own_count * planes :, :] = whole_codes(header)
    for step in range(slab_count):
        out_refs[step][...] = all_codes[partner_of(slab_index, step, slab_count)[0]]


def whole_codes(value):
    return value.astype(jnp.int32).astype(jnp.int16)


def encode(value):
    largest = jnp.max(jnp.abs(value), axis=1, keepdims=True)
    exponent = jnp.maximum(jnp.floor(jnp.log2(jnp.maximum(largest, TINY))), LOWEST_EXPONENT)
    lifted = 1.0 / jnp.exp2(exponent)
    factor = jnp.maximum(jnp.ceil(largest * lifted * FACTOR_UNIT), 1.0)
    code = jnp.floor(value * lifted * (CODE_LIMIT * FACTOR_UNIT / factor) + 0.5)
    return jnp.clip(code, -CODE_LIMIT, CODE_LIMIT), exponent, factor


def swap_cores(block, pair_count):
    return lax.ppermute(block, "pair", [(i, i ^ 1) for i in range(pair_count)])


def gather_chips(boxes, pair_count):
    pieces = []
    for step in range(1, pair_count // CORES):
        perm = [(i, (i + step * CORES) % pair_count) for i in range(pair_count)]
        pieces.append(lax.ppermute(boxes, "pair", perm))
    return pieces


def unpack_kernel(sizes, *refs):
    own_count, slab_count, tiles = sizes
    block_refs, out_ref, blocks, sems = refs[:slab_count], *refs[slab_count:]
    slab_index = lax.axis_index("slab")
    copies = []
    for index in range(slab_count):
        slab = partner_of(slab_index, slab_count - 1 - index, slab_count)[1]
        copies.append(pltpu.make_async_copy(block_refs[index], blocks.at[slab], sems.at[index]))
        copies[-1].start()
    for copy in copies:
        copy.wait()
    row_count = own_count * tiles
    values = {}
    for slab in range(slab_count):
        header = blocks[slab, row_count:, :].astype(jnp.int32).astype(jnp.float32)
        units = jnp.exp2(header[:8, :])
        factors = header[8:, :] * (1.0 / (CODE_LIMIT * FACTOR_UNIT))
        for pair in range(row_count // 16):
            codes = blocks[slab, 16 * pair : 16 * pair + 16, :].astype(jnp.int32).astype(jnp.float32)
            for half in range(2):
                chunk = 2 * pair + half
                own, plane = divmod(8 * chunk, tiles)
                value = codes[8 * half : 8 * half + 8, :] * factors[:, chunk : chunk + 1]
                values[slab * own_count + own, plane // 8] = value * units[:, chunk : chunk + 1]
        if (slab + 1) * own_count % 8 == 0:
            band = (slab + 1) * own_count // 8 - 1
            for plane in range(tiles // 8):
                rows = turned([values[8 * band + index, plane] for index in range(8)])
                for tile in range(8):
                    start = (band * tiles + 8 * plane + tile) * 8
                    out_ref[start : start + 8, :] = rows[tile]


def unpack(blocks, own_count, cells):
    slab_count = len(blocks)
    row_count = own_count * slab_count
    tiles = cells // LANES
    out = pl.pallas_call(
        functools.partial(unpack_kernel, (own_count, slab_count, tiles)),
        out_shape=jax.ShapeDtypeStruct((row_count * tiles, LANES), jnp.float32),
        in_specs=[pl.BlockSpec(memory_space=pl.ANY)] * slab_count,
        out_specs=pl.BlockSpec(memory_space=pltpu.VMEM),
        scratch_shapes=[
            pltpu.VMEM((slab_count,) + blocks[0].shape, jnp.int16),
            pltpu.SemaphoreType.DMA((slab_count,)),
        ],
        compiler_params=pltpu.CompilerParams(vmem_limit_bytes=8 * 1024 * 1024),
    )(*blocks)
    return out.reshape(row_count // 8, tiles, 8, LANES).transpose(0, 2, 1, 3).reshape(row_count, cells)


def place_own(sizes, match, centers, boxes):
    side, rounds, own_count, slab_count, _ = sizes
    tiles, _, pitch = box_shape(sizes)
    placed = (own_count * rounds * side, side * side)
    either = pl.BlockSpec(memory_space=pl.ANY)
    vectors = pl.BlockSpec(memory_space=pltpu.VMEM)
    return pl.pallas_call(
        functools.partial(own_kernel, sizes),
        out_shape=[jax.ShapeDtypeStruct(placed, jnp.bfloat16)] * 2,
        in_specs=[either] * 3,
        out_specs=[vectors] * 2,
        scratch_shapes=[
            pltpu.SMEM(match.shape, jnp.int32),
            pltpu.SMEM(centers.shape, jnp.int32),
            pltpu.VMEM((1,) + boxes.shape, jnp.bfloat16),
            pltpu.VMEM((own_count * tiles * pitch, LANES), jnp.float32),
            pltpu.SemaphoreType.DMA((3,)),
        ],
        compiler_params=pltpu.CompilerParams(vmem_limit_bytes=60 * 1024 * 1024),
        cost_estimate=pl.CostEstimate(flops=5 * 10**9, bytes_accessed=4 * 1024 * 1024, transcendentals=0),
    )(match, centers, boxes)


def team_forces(sizes, match, centers, mine, partner, pieces):
    side, rounds, own_count, slab_count, pair_count = sizes
    tiles, _, pitch = box_shape(sizes)
    _, rows, _ = pieces[0].shape
    solves = own_count * rounds
    group = min(solves, 8)
    cells = side * side
    basis = sine_basis(side)
    mix_high, mix_low = split_constant(np.kron(np.eye(group), basis))
    mix = np.concatenate([mix_high, mix_high, mix_low], axis=1)
    there = np.stack([np.kron(basis[parity::2, : side // 2].T, basis) for parity in range(2)])
    gain = chebyshev_gain(side).reshape(side, side, side)
    gain = np.concatenate([gain[:, parity::2].reshape(side, -1) for parity in range(2)], axis=1)
    constants = (mix, gain, *split_constant(there), *split_constant(there.transpose(0, 2, 1)))
    either = pl.BlockSpec(memory_space=pl.ANY)
    distant = pl.BlockSpec(memory_space=pltpu.HBM)
    vectors = pl.BlockSpec(memory_space=pltpu.VMEM)
    wide = pltpu.VMEM((2 * solves * side, cells), jnp.bfloat16)
    flops = 2 * solves * side * 3 * 2 * (cells * cells // 2 + cells * group * side)
    inputs = [match, centers, mine, partner, *pieces, *[jnp.asarray(constant) for constant in constants]]
    return pl.pallas_call(
        functools.partial(force_kernel, sizes),
        out_shape=[jax.ShapeDtypeStruct((rows + HEADER_ROWS, LANES), jnp.int16)] * slab_count,
        in_specs=[distant] * 2 + [either] * (len(inputs) - 2 - len(constants)) + [distant] * len(constants),
        out_specs=[vectors] * slab_count,
        scratch_shapes=[
            pltpu.SMEM(match.shape, jnp.int32),
            pltpu.SMEM(centers.shape, jnp.int32),
            pltpu.VMEM(mine.shape, jnp.bfloat16),
            pltpu.VMEM(partner.shape, jnp.bfloat16),
            pltpu.VMEM((pair_count, slab_count, rows, LANES), jnp.bfloat16),
            *[pltpu.VMEM(constant.shape, constant.dtype) for constant in constants],
            pltpu.VMEM((own_count * pair_count * tiles * pitch, LANES), jnp.float32),
            wide,
            wide,
            *[pltpu.VMEM((group * tiles * pitch, LANES), jnp.float32)] * (solves // group),
            pltpu.VMEM((slab_count, rows + HEADER_ROWS, LANES), jnp.int16),
            pltpu.SemaphoreType.DMA((len(inputs),)),
        ],
        compiler_params=pltpu.CompilerParams(vmem_limit_bytes=60 * 1024 * 1024),
        cost_estimate=pl.CostEstimate(flops=flops, bytes_accessed=8 * 1024 * 1024, transcendentals=0),
    )(*inputs)


def shards(orbitals, centers, matchings):
    slab_count = lax.axis_size("slab")
    pair_count = lax.axis_size("pair")
    local_rows, plane_cells = orbitals.shape
    own_count = local_rows // slab_count
    side = round((plane_cells * slab_count) ** (1.0 / 3.0))
    blocks = orbitals.reshape(slab_count, own_count * plane_cells // LANES, LANES)
    boxes = lax.all_to_all(blocks, "slab", split_axis=0, concat_axis=0, tiled=True)
    sizes = (side, matchings.shape[1], own_count, slab_count, pair_count)
    pieces = gather_chips(boxes, pair_count)
    mine, partner = place_own(sizes, matchings, centers.T, boxes)
    boxes, mine, partner = lax.optimization_barrier((boxes, mine, partner))
    swapped = [swap_cores(boxes, pair_count)]
    pieces, mine, partner = lax.optimization_barrier((pieces, mine, partner))
    pieces = pieces + swapped + [swap_cores(piece, pair_count) for piece in pieces]
    codes = team_forces(sizes, matchings, centers.T, mine, partner, pieces)
    received = []
    for step in reversed(range(1, slab_count)):
        perm = [(i, partner_of(i, step, slab_count)[0]) for i in range(slab_count)]
        received.append(lax.ppermute(codes[step], "slab", perm))
    return unpack(received + [codes[0]], own_count, plane_cells)


def solution(mesh):
    in_specs = (P("pair", "slab"), P(), P("slab", None, None))
    out_specs = P("pair", "slab")
    return jax.shard_map(shards, mesh=mesh, in_specs=in_specs, out_specs=out_specs, check_vma=False)
```

```python
import functools

import jax
import jax.numpy as jnp
import numpy as np
from jax import lax
from jax.experimental import pallas as pl
from jax.experimental.pallas import tpu as pltpu
from jax.sharding import PartitionSpec as P

STEPS = 16
CUT2 = 192
REACH = 8
SCREEN = 0.1
LOWER_BOUND = 0.1
UPPER_BOUND = 12.1
LANES = 128
CORES = 2
CODE_LIMIT = 32767.0
FACTOR_UNIT = 8192.0
LOWEST_EXPONENT = -120.0
TINY = 1e-37
HEADER_ROWS = 16


def sine_basis(side):
    index = np.arange(1, side + 1, dtype=np.float64)
    return np.sqrt(2.0 / (side + 1)) * np.sin(np.pi * np.outer(index, index) / (side + 1))


def chebyshev_gain(side):
    shifts = -2.0 * np.cos(np.pi * np.arange(1, side + 1, dtype=np.float64) / (side + 1))
    eigenvalue = 6.0 + SCREEN + shifts[:, None, None] + shifts[None, :, None] + shifts[None, None, :]
    middle = (UPPER_BOUND + LOWER_BOUND) / 2.0
    spread = (UPPER_BOUND - LOWER_BOUND) / 2.0
    ratio = middle / spread
    total = np.zeros_like(eigenvalue)
    residual = np.ones_like(eigenvalue)
    direction = residual / middle
    factor = 1.0 / ratio
    for _ in range(STEPS):
        total = total + direction
        residual = residual - eigenvalue * direction
        factor_next = 1.0 / (2.0 * ratio - factor)
        direction = factor_next * factor * direction + 2.0 * factor_next / spread * residual
        factor = factor_next
    return total.reshape(side, side * side).astype(np.float32)


def split_pair(value):
    high = value.astype(jnp.bfloat16)
    low = (value - high.astype(jnp.float32)).astype(jnp.bfloat16)
    return high, low


def dot(left, right):
    return jnp.dot(left, right, preferred_element_type=jnp.float32)


def partner_of(index, step, count):
    if count & (count - 1) == 0:
        return index ^ step, index ^ step
    return (index + step) % count, (index + count - step) % count


def pair_geometry(sizes, match_ref, centers_ref, index):
    _, rounds, own_count, slab_count, _ = sizes
    slab_index = lax.axis_index("slab")
    pair_index = lax.axis_index("pair")

    def orbital_of(member):
        return (member // own_count * slab_count + slab_index) * own_count + member % own_count

    member = pair_index * own_count + index // rounds
    mate = match_ref[0, index % rounds, member]
    own_offset = []
    mate_offset = []
    distance = 0
    for axis in range(3):
        mine = centers_ref[axis, orbital_of(member)]
        other = centers_ref[axis, orbital_of(mate)]
        anchor = (mine + other) >> 1
        own_offset.append(mine - anchor)
        mate_offset.append(other - anchor)
        distance = distance + (mine - other) * (mine - other)
    return member, mate, own_offset, mate_offset, distance <= CUT2


def box_shape(sizes):
    side = sizes[0]
    return side * side // LANES, LANES // side, side + 2 * REACH


def clear_edges(sizes, ref, first, count):
    side = sizes[0]
    tiles, _, pitch = box_shape(sizes)
    zeros = jnp.zeros((REACH, LANES), jnp.float32)

    def clear(index, carry):
        start = (first * tiles + index) * pitch
        ref[pl.ds(pl.multiple_of(start, 8), REACH), :] = zeros
        ref[pl.ds(pl.multiple_of(start + REACH + side, 8), REACH), :] = zeros
        return carry

    lax.fori_loop(0, count * tiles, clear, 0, unroll=8)


def turned(tiles):
    row = lax.broadcasted_iota(jnp.int32, (8, LANES), 0)
    tiles = list(tiles)
    for distance in (4, 2, 1):
        low = (row & distance) == 0
        for index in range(8):
            if index & distance == 0:
                first, second = tiles[index], tiles[index + distance]
                tiles[index] = jnp.where(low, first, pltpu.roll(second, distance, axis=0))
                tiles[index + distance] = jnp.where(low, pltpu.roll(first, 8 - distance, axis=0), second)
    return tiles


def spread(sizes, boxes_ref, fields, pair):
    side, _, own_count, slab_count, _ = sizes
    planes = side // slab_count
    tiles, _, pitch = box_shape(sizes)
    for group in range(side // 8):
        halves = {}
        for slab in range(8 * group // planes, (8 * group + 7) // planes + 1):
            for chunk in range(own_count * planes // 2):
                block = boxes_ref[pair, slab, 16 * chunk : 16 * chunk + 16, :].astype(jnp.float32)
                for half in range(2):
                    own, plane = divmod(2 * chunk + half, planes)
                    halves[own, slab * planes + plane] = block[8 * half : 8 * half + 8, :]
        for own in range(own_count):
            rows = turned([halves[own, 8 * group + index] for index in range(8)])
            for tile in range(tiles):
                start = ((pair * own_count + own) * tiles + tile) * pitch + REACH + 8 * group
                fields[pl.ds(pl.multiple_of(start, 8), 8), :] = rows[tile]


def rolled(sizes, ref, box, row, rows, offset_x, offset_flat):
    tiles, _, pitch = box_shape(sizes)
    whole = (offset_flat >> 7) & (tiles - 1)
    part = offset_flat & (LANES - 1)
    start = box * tiles * pitch + REACH + row - offset_x
    moved = []
    for tile in range(tiles):
        first_row = start + ((tile - whole) & (tiles - 1)) * pitch
        moved.append(pltpu.roll(ref[pl.ds(first_row, rows), :], part, axis=1))
    keep = lax.broadcasted_iota(jnp.int32, (rows, LANES), 1) >= part
    return [jnp.where(keep, moved[t], moved[(t - 1) % tiles]) for t in range(tiles)]


def place_partner(sizes, fields, box, own_offset, offset, active):
    side = sizes[0]
    tiles, lines, _ = box_shape(sizes)
    placed = rolled(sizes, fields, box, 0, side, offset[0], offset[1] * side + offset[2])
    lane = lax.broadcasted_iota(jnp.int32, (1, LANES), 1)
    lows = [jnp.maximum(jnp.maximum(a, b), 0) for a, b in zip(own_offset, offset)]
    highs = [side + jnp.minimum(jnp.minimum(a, b), 0) for a, b in zip(own_offset, offset)]
    point_ok = (lane % side >= lows[2]) & (lane % side < highs[2]) & active
    result = []
    for tile in range(tiles):
        line = lane // side + tile * lines
        ok = jnp.where(point_ok & (line >= lows[1]) & (line < highs[1]), 1.0, 0.0)
        result.append(placed[tile] * ok)
    return result


def own_kernel(
    sizes, match_hbm, centers_hbm, own_hbm, mine_ref, match_ref, centers_ref, boxes_ref, fields, sems
):
    side, rounds, own_count, _, _ = sizes
    tiles, _, _ = box_shape(sizes)
    first_member = lax.axis_index("pair") * own_count
    sources = (match_hbm, centers_hbm, own_hbm)
    targets = (match_ref, centers_ref, boxes_ref.at[0])
    copies = [pltpu.make_async_copy(s, t, sems.at[i]) for i, (s, t) in enumerate(zip(sources, targets))]
    for copy in copies:
        copy.start()
    clear_edges(sizes, fields, 0, own_count)
    for copy in copies:
        copy.wait()
    spread(sizes, boxes_ref, fields, 0)

    def place(index, carry):
        member, _, a, _, _ = pair_geometry(sizes, match_ref, centers_ref, index)
        rows = pl.ds(pl.multiple_of(index * side, side), side)
        placed = rolled(sizes, fields, member - first_member, 0, side, a[0], a[1] * side + a[2])
        for tile in range(tiles):
            mine_ref[rows, tile * LANES : (tile + 1) * LANES] = placed[tile].astype(jnp.bfloat16)
        return carry

    lax.fori_loop(0, own_count * rounds, place, 0)


def force_kernel(sizes, match_hbm, centers_hbm, mine_hbm, *refs):
    side, rounds, own_count, slab_count, pair_count = sizes
    piece_hbm, refs = refs[:pair_count], refs[pair_count:]
    constant_hbm, refs = refs[:3], refs[3:]
    out_refs, refs = refs[:slab_count], refs[slab_count:]
    match_ref, centers_ref, mine, partner, boxes_ref, *refs = refs
    constants, refs = refs[:3], refs[3:]
    basis_ref, line_ref, gain_ref = constants
    mix_ref, there_high, there_low, back_high, back_low, *refs = refs
    fields, first, second, *terms, all_codes, sems = refs
    planes = side // slab_count
    tiles, lines, pitch = box_shape(sizes)
    solves = own_count * rounds
    group = min(solves, 8)
    group_rows = group * side
    cells = tiles * LANES
    width = cells // 2
    slab_index = lax.axis_index("slab")
    pair_index = lax.axis_index("pair")
    core = pair_index % CORES
    chip = pair_index // CORES
    chips = pair_count // CORES

    places = [
        (chip + chips - step) % chips * CORES + (core + core_step) % CORES
        for core_step in range(CORES)
        for step in range(chips)
    ]
    sources = [match_hbm, centers_hbm, *constant_hbm, *piece_hbm, mine_hbm]
    targets = [match_ref, centers_ref, *constants, *[boxes_ref.at[pair] for pair in places], mine]
    copies = [pltpu.make_async_copy(s, t, sems.at[i]) for i, (s, t) in enumerate(zip(sources, targets))]
    for copy in copies:
        copy.start()
    for pair in places:
        clear_edges(sizes, fields, pair * own_count, own_count)
    for ref in terms:
        clear_edges(sizes, ref, 0, group)
    for copy in copies[:5]:
        copy.wait()

    def make_matrices(first_line, high_ref, low_ref):
        count = side // 2
        for parity in range(2):
            for index in range(count):
                line = first_line + parity * count + index
                rows = slice(index * side, (index + 1) * side)
                value = basis_ref[...] * line_ref[line : line + 1, :]
                high_ref[parity, rows, :], low_ref[parity, rows, :] = split_pair(value)

    block = lax.broadcasted_iota(jnp.int32, (side, group_rows), 1) // side
    for index in range(group):
        rows = slice(index * side, (index + 1) * side)
        value = jnp.where(block == index, basis_ref[:, :group_rows], 0.0)
        high, low = split_pair(value)
        for part, piece in enumerate((high, high, low)):
            mix_ref[rows, part * group_rows : (part + 1) * group_rows] = piece
    make_matrices(0, there_high, there_low)

    for copy in copies[5:-1]:
        copy.wait()
    for pair in places:
        spread(sizes, boxes_ref, fields, pair)
    copies[-1].wait()

    row_count = solves * side
    half_tiles = tiles // 2
    half_cells = cells // 2

    def mirrored(tile):
        line = lax.broadcasted_iota(jnp.int32, tile.shape, 1) // side
        result = None
        for index in range(lines):
            amount = (2 * index - lines + 1) * side % LANES
            if index < 2:
                moved = pltpu.roll(tile, amount, axis=1)
                result = moved if result is None else jnp.where(line % 2 == index, moved, result)
        return result

    def store_split(ref, start, count, columns, value):
        high, low = split_pair(value)
        ref[start : start + count, columns] = high
        ref[row_count + start : row_count + start + count, columns] = low

    def densities(index):
        start = index * side
        rows = slice(start, start + side)
        _, mate, a, b, active = pair_geometry(sizes, match_ref, centers_ref, index)
        placed = place_partner(sizes, fields, mate, a, b, active)
        density = []
        for tile in range(tiles):
            columns = slice(tile * LANES, (tile + 1) * LANES)
            partner[rows, columns] = placed[tile].astype(jnp.bfloat16)
            density.append(mine[rows, columns].astype(jnp.float32) * placed[tile])
        for tile in range(half_tiles):
            far = mirrored(density[tiles - 1 - tile])
            for parity, value in enumerate((density[tile] + far, density[tile] - far)):
                column = parity * half_cells + tile * LANES
                store_split(first, start, side, slice(column, column + LANES), value)

    def along_x(start, columns, source):
        high = source[start : start + group_rows, columns]
        low = source[row_count + start : row_count + start + group_rows, columns]
        return dot(mix_ref[...], jnp.concatenate([high, low, high], axis=0))

    def in_plane(parity, columns, source, high_ref, low_ref):
        inner = slice(parity * half_cells, (parity + 1) * half_cells)
        high = source[:row_count, inner]
        low = source[row_count:, inner]
        basis = high_ref[parity, :, columns]
        rest = low_ref[parity, :, columns]
        left = jnp.concatenate([high, low, high], axis=1)
        return dot(left, jnp.concatenate([basis, basis, rest], axis=0))

    for start in range(0, row_count, group_rows):
        for index in range(start // side, (start + group_rows) // side):
            densities(index)
        columns = slice(0, cells)
        store_split(second, start, group_rows, columns, along_x(start, columns, first))

    make_matrices(side, back_high, back_low)
    for parity in range(2):
        for column in range(0, half_cells, width):
            columns = slice(column, column + width)
            value = in_plane(parity, columns, second, there_high, there_low)
            columns = slice(parity * half_cells + column, parity * half_cells + column + width)
            gain = gain_ref[:, columns]
            value = (value.reshape(solves, side, width) * gain[None]).reshape(row_count, width)
            store_split(first, 0, row_count, columns, value)

    for parity in range(2):
        for column in range(0, half_cells, width):
            value = in_plane(parity, slice(column, column + width), first, back_high, back_low)
            columns = slice(parity * half_cells + column, parity * half_cells + column + width)
            store_split(second, 0, row_count, columns, value)

    for start in range(0, row_count, group_rows):
        for column in range(0, half_cells, width):
            even = along_x(start, slice(column, column + width), second)
            odd = along_x(start, slice(half_cells + column, half_cells + column + width), second)
            for part in range(width // LANES):
                tile = column // LANES + part
                lanes = slice(part * LANES, (part + 1) * LANES)
                near = even[:, lanes] + odd[:, lanes]
                far = mirrored(even[:, lanes] - odd[:, lanes])
                for place, value in ((tile, near), (tiles - 1 - tile, far)):
                    columns = slice(place * LANES, (place + 1) * LANES)
                    value = value * partner[start : start + group_rows, columns].astype(jnp.float32)
                    for solve in range(group):
                        row = (solve * tiles + place) * pitch + REACH
                        terms[start // group_rows][row : row + side, :] = value[solve * side : (solve + 1) * side, :]

    step_rows = 16

    def collect(own, row):
        sums = None
        for turn in range(rounds):
            index = own * rounds + turn
            _, _, a, _, _ = pair_geometry(sizes, match_ref, centers_ref, index)
            ref = terms[index // group]
            term = rolled(sizes, ref, index % group, row, step_rows, -a[0], -(a[1] * side + a[2]))
            sums = term if sums is None else [s + t for s, t in zip(sums, term)]
        return sums

    lane_index = lax.broadcasted_iota(jnp.int32, (tiles, LANES), 1)
    exponents = [jnp.zeros((tiles, LANES), jnp.float32)] * slab_count
    factors = [jnp.zeros((tiles, LANES), jnp.float32)] * slab_count
    codes = {}
    for own in range(own_count):
        for row in range(0, side, step_rows):
            sums = collect(own, row)
            for half in range(0, step_rows, 8):
                for index, value in enumerate(turned([tile[half : half + 8, :] for tile in sums])):
                    slab, plane = divmod(row + half + index, planes)
                    chunk = own * planes + plane
                    codes[slab, chunk], exponent, factor = encode(value)
                    exponents[slab] = jnp.where(lane_index == chunk, exponent, exponents[slab])
                    factors[slab] = jnp.where(lane_index == chunk, factor, factors[slab])
                    if chunk % 2:
                        pair = jnp.concatenate([codes[slab, chunk - 1], codes[slab, chunk]], axis=0)
                        all_codes[slab, tiles * (chunk - 1) : tiles * (chunk + 1), :] = whole_codes(pair)
    for slab in range(slab_count):
        header = jnp.concatenate([exponents[slab], factors[slab]], axis=0)
        all_codes[slab, tiles * own_count * planes :, :] = whole_codes(header)
    for step in range(slab_count):
        out_refs[step][...] = all_codes[partner_of(slab_index, step, slab_count)[0]]


def whole_codes(value):
    return value.astype(jnp.int32).astype(jnp.int16)


def encode(value):
    largest = jnp.max(jnp.abs(value), axis=1, keepdims=True)
    exponent = jnp.maximum(jnp.floor(jnp.log2(jnp.maximum(largest, TINY))), LOWEST_EXPONENT)
    lifted = 1.0 / jnp.exp2(exponent)
    factor = jnp.maximum(jnp.ceil(largest * lifted * FACTOR_UNIT), 1.0)
    code = jnp.floor(value * lifted * (CODE_LIMIT * FACTOR_UNIT / factor) + 0.5)
    return jnp.clip(code, -CODE_LIMIT, CODE_LIMIT), exponent, factor


def swap_cores(block, pair_count):
    return lax.ppermute(block, "pair", [(i, i ^ 1) for i in range(pair_count)])


def gather_chips(boxes, pair_count):
    pieces = []
    for step in range(1, pair_count // CORES):
        perm = [(i, (i + step * CORES) % pair_count) for i in range(pair_count)]
        pieces.append(lax.ppermute(boxes, "pair", perm))
    return pieces


def unpack_kernel(sizes, *refs):
    own_count, slab_count, tiles = sizes
    block_refs, out_ref, blocks, sems = refs[:slab_count], *refs[slab_count:]
    slab_index = lax.axis_index("slab")
    copies = []
    for index in range(slab_count):
        slab = partner_of(slab_index, slab_count - 1 - index, slab_count)[1]
        copies.append(pltpu.make_async_copy(block_refs[index], blocks.at[slab], sems.at[index]))
        copies[-1].start()
    for copy in copies:
        copy.wait()
    row_count = own_count * tiles
    values = {}
    for slab in range(slab_count):
        header = blocks[slab, row_count:, :].astype(jnp.int32).astype(jnp.float32)
        units = jnp.exp2(header[:8, :])
        factors = header[8:, :] * (1.0 / (CODE_LIMIT * FACTOR_UNIT))
        for pair in range(row_count // 16):
            codes = blocks[slab, 16 * pair : 16 * pair + 16, :].astype(jnp.int32).astype(jnp.float32)
            for half in range(2):
                chunk = 2 * pair + half
                own, plane = divmod(8 * chunk, tiles)
                value = codes[8 * half : 8 * half + 8, :] * factors[:, chunk : chunk + 1]
                values[slab * own_count + own, plane // 8] = value * units[:, chunk : chunk + 1]
        if (slab + 1) * own_count % 8 == 0:
            band = (slab + 1) * own_count // 8 - 1
            for plane in range(tiles // 8):
                rows = turned([values[8 * band + index, plane] for index in range(8)])
                for tile in range(8):
                    start = (band * tiles + 8 * plane + tile) * 8
                    out_ref[start : start + 8, :] = rows[tile]


def unpack(blocks, own_count, cells):
    slab_count = len(blocks)
    row_count = own_count * slab_count
    tiles = cells // LANES
    out = pl.pallas_call(
        functools.partial(unpack_kernel, (own_count, slab_count, tiles)),
        out_shape=jax.ShapeDtypeStruct((row_count * tiles, LANES), jnp.float32),
        in_specs=[pl.BlockSpec(memory_space=pl.ANY)] * slab_count,
        out_specs=pl.BlockSpec(memory_space=pltpu.VMEM),
        scratch_shapes=[
            pltpu.VMEM((slab_count,) + blocks[0].shape, jnp.int16),
            pltpu.SemaphoreType.DMA((slab_count,)),
        ],
        compiler_params=pltpu.CompilerParams(vmem_limit_bytes=8 * 1024 * 1024),
    )(*blocks)
    return out.reshape(row_count // 8, tiles, 8, LANES).transpose(0, 2, 1, 3).reshape(row_count, cells)


def place_own(sizes, match, centers, boxes):
    side, rounds, own_count, slab_count, _ = sizes
    tiles, _, pitch = box_shape(sizes)
    placed = (own_count * rounds * side, side * side)
    either = pl.BlockSpec(memory_space=pl.ANY)
    vectors = pl.BlockSpec(memory_space=pltpu.VMEM)
    return pl.pallas_call(
        functools.partial(own_kernel, sizes),
        out_shape=jax.ShapeDtypeStruct(placed, jnp.bfloat16),
        in_specs=[either] * 3,
        out_specs=vectors,
        scratch_shapes=[
            pltpu.SMEM(match.shape, jnp.int32),
            pltpu.SMEM(centers.shape, jnp.int32),
            pltpu.VMEM((1,) + boxes.shape, jnp.bfloat16),
            pltpu.VMEM((own_count * tiles * pitch, LANES), jnp.float32),
            pltpu.SemaphoreType.DMA((3,)),
        ],
        compiler_params=pltpu.CompilerParams(vmem_limit_bytes=60 * 1024 * 1024),
        cost_estimate=pl.CostEstimate(flops=5 * 10**9, bytes_accessed=4 * 1024 * 1024, transcendentals=0),
    )(match, centers, boxes)


def team_forces(sizes, match, centers, mine, pieces):
    side, rounds, own_count, slab_count, pair_count = sizes
    tiles, _, pitch = box_shape(sizes)
    _, rows, _ = pieces[0].shape
    solves = own_count * rounds
    group = min(solves, 8)
    cells = side * side
    basis = sine_basis(side)
    halves = [basis[parity::2, : side // 2].T for parity in range(2)]
    lines = np.concatenate(halves + [half.T for half in halves])
    lines = np.repeat(lines, side, axis=1).astype(np.float32)
    tile = np.tile(basis, (1, side // 2)).astype(np.float32)
    gain = chebyshev_gain(side).reshape(side, side, side)
    gain = np.concatenate([gain[:, parity::2].reshape(side, -1) for parity in range(2)], axis=1)
    constants = (tile, lines, gain)
    either = pl.BlockSpec(memory_space=pl.ANY)
    distant = pl.BlockSpec(memory_space=pltpu.HBM)
    vectors = pl.BlockSpec(memory_space=pltpu.VMEM)
    wide = pltpu.VMEM((2 * solves * side, cells), jnp.bfloat16)
    flops = 2 * solves * side * 3 * 2 * (cells * cells // 2 + cells * group * side)
    inputs = [match, centers, mine, *pieces, *[jnp.asarray(constant) for constant in constants]]
    return pl.pallas_call(
        functools.partial(force_kernel, sizes),
        out_shape=[jax.ShapeDtypeStruct((rows + HEADER_ROWS, LANES), jnp.int16)] * slab_count,
        in_specs=[distant] * 2 + [either] * (len(inputs) - 2 - len(constants)) + [distant] * len(constants),
        out_specs=[vectors] * slab_count,
        scratch_shapes=[
            pltpu.SMEM(match.shape, jnp.int32),
            pltpu.SMEM(centers.shape, jnp.int32),
            pltpu.VMEM(mine.shape, jnp.bfloat16),
            pltpu.VMEM(mine.shape, jnp.bfloat16),
            pltpu.VMEM((pair_count, slab_count, rows, LANES), jnp.bfloat16),
            *[pltpu.VMEM(constant.shape, constant.dtype) for constant in constants],
            pltpu.VMEM((group * side, 3 * group * side), jnp.bfloat16),
            *[pltpu.VMEM((2, cells // 2, cells // 2), jnp.bfloat16)] * 4,
            pltpu.VMEM((own_count * pair_count * tiles * pitch, LANES), jnp.float32),
            wide,
            wide,
            *[pltpu.VMEM((group * tiles * pitch, LANES), jnp.float32)] * (solves // group),
            pltpu.VMEM((slab_count, rows + HEADER_ROWS, LANES), jnp.int16),
            pltpu.SemaphoreType.DMA((len(inputs),)),
        ],
        compiler_params=pltpu.CompilerParams(vmem_limit_bytes=60 * 1024 * 1024),
        cost_estimate=pl.CostEstimate(flops=flops, bytes_accessed=8 * 1024 * 1024, transcendentals=0),
    )(*inputs)


def shards(orbitals, centers, matchings):
    slab_count = lax.axis_size("slab")
    pair_count = lax.axis_size("pair")
    local_rows, plane_cells = orbitals.shape
    own_count = local_rows // slab_count
    side = round((plane_cells * slab_count) ** (1.0 / 3.0))
    blocks = orbitals.reshape(slab_count, own_count * plane_cells // LANES, LANES)
    boxes = lax.all_to_all(blocks, "slab", split_axis=0, concat_axis=0, tiled=True)
    sizes = (side, matchings.shape[1], own_count, slab_count, pair_count)
    pieces = gather_chips(boxes, pair_count)
    mine = place_own(sizes, matchings, centers.T, boxes)
    boxes, mine = lax.optimization_barrier((boxes, mine))
    swapped = [swap_cores(boxes, pair_count)]
    pieces, mine = lax.optimization_barrier((pieces, mine))
    swapped += [swap_cores(piece, pair_count) for piece in pieces]
    codes = team_forces(sizes, matchings, centers.T, mine, [boxes] + pieces + swapped)
    received = []
    for step in reversed(range(1, slab_count)):
        perm = [(i, partner_of(i, step, slab_count)[0]) for i in range(slab_count)]
        received.append(lax.ppermute(codes[step], "slab", perm))
    return unpack(received + [codes[0]], own_count, plane_cells)


def solution(mesh):
    in_specs = (P("pair", "slab"), P(), P("slab", None, None))
    out_specs = P("pair", "slab")
    return jax.shard_map(shards, mesh=mesh, in_specs=in_specs, out_specs=out_specs, check_vma=False)
```

```python
import functools

import jax
import jax.numpy as jnp
import numpy as np
from jax import lax
from jax.experimental import pallas as pl
from jax.experimental.pallas import tpu as pltpu
from jax.sharding import PartitionSpec as P

STEPS = 16
CUT2 = 192
REACH = 8
SCREEN = 0.1
LOWER_BOUND = 0.1
UPPER_BOUND = 12.1
LANES = 128
CORES = 2
CODE_LIMIT = 32767.0
FACTOR_UNIT = 8192.0
LOWEST_EXPONENT = -120.0
TINY = 1e-37
HEADER_ROWS = 16
ENTRIES = 8


def sine_basis(side):
    index = np.arange(1, side + 1, dtype=np.float64)
    return np.sqrt(2.0 / (side + 1)) * np.sin(np.pi * np.outer(index, index) / (side + 1))


def chebyshev_gain(side):
    shifts = -2.0 * np.cos(np.pi * np.arange(1, side + 1, dtype=np.float64) / (side + 1))
    eigenvalue = 6.0 + SCREEN + shifts[:, None, None] + shifts[None, :, None] + shifts[None, None, :]
    middle = (UPPER_BOUND + LOWER_BOUND) / 2.0
    spread = (UPPER_BOUND - LOWER_BOUND) / 2.0
    ratio = middle / spread
    total = np.zeros_like(eigenvalue)
    residual = np.ones_like(eigenvalue)
    direction = residual / middle
    factor = 1.0 / ratio
    for _ in range(STEPS):
        total = total + direction
        residual = residual - eigenvalue * direction
        factor_next = 1.0 / (2.0 * ratio - factor)
        direction = factor_next * factor * direction + 2.0 * factor_next / spread * residual
        factor = factor_next
    return total.reshape(side, side * side).astype(np.float32)


def split_pair(value):
    high = value.astype(jnp.bfloat16)
    low = (value - high.astype(jnp.float32)).astype(jnp.bfloat16)
    return high, low


def dot(left, right):
    return jnp.dot(left, right, preferred_element_type=jnp.float32)


def partner_of(index, step, count):
    if count & (count - 1) == 0:
        return index ^ step, index ^ step
    return (index + step) % count, (index + count - step) % count


def pair_geometry(sizes, match_ref, centers_ref, index):
    _, rounds, own_count, slab_count, _ = sizes
    slab_index = lax.axis_index("slab")
    pair_index = lax.axis_index("pair")

    def orbital_of(member):
        return (member // own_count * slab_count + slab_index) * own_count + member % own_count

    member = pair_index * own_count + index // rounds
    mate = match_ref[0, index % rounds, member]
    own_offset = []
    mate_offset = []
    distance = 0
    for axis in range(3):
        mine = centers_ref[axis, orbital_of(member)]
        other = centers_ref[axis, orbital_of(mate)]
        anchor = (mine + other) >> 1
        own_offset.append(mine - anchor)
        mate_offset.append(other - anchor)
        distance = distance + (mine - other) * (mine - other)
    return member, mate, own_offset, mate_offset, distance <= CUT2


def box_shape(sizes):
    side = sizes[0]
    return side * side // LANES, LANES // side, side + 2 * REACH


def clear_edges(sizes, ref, first, count):
    side = sizes[0]
    tiles, _, pitch = box_shape(sizes)
    zeros = jnp.zeros((REACH, LANES), jnp.float32)

    def clear(index, carry):
        start = (first * tiles + index) * pitch
        ref[pl.ds(pl.multiple_of(start, 8), REACH), :] = zeros
        ref[pl.ds(pl.multiple_of(start + REACH + side, 8), REACH), :] = zeros
        return carry

    lax.fori_loop(0, count * tiles, clear, 0, unroll=8)


def turned(tiles):
    row = lax.broadcasted_iota(jnp.int32, (8, LANES), 0)
    tiles = list(tiles)
    for distance in (4, 2, 1):
        low = (row & distance) == 0
        for index in range(8):
            if index & distance == 0:
                first, second = tiles[index], tiles[index + distance]
                tiles[index] = jnp.where(low, first, pltpu.roll(second, distance, axis=0))
                tiles[index + distance] = jnp.where(low, pltpu.roll(first, 8 - distance, axis=0), second)
    return tiles


def spread(sizes, boxes_ref, fields, pair):
    side, _, own_count, slab_count, _ = sizes
    planes = side // slab_count
    tiles, _, pitch = box_shape(sizes)
    for group in range(side // 8):
        halves = {}
        for slab in range(8 * group // planes, (8 * group + 7) // planes + 1):
            for chunk in range(own_count * planes // 2):
                block = boxes_ref[pair, slab, 16 * chunk : 16 * chunk + 16, :].astype(jnp.float32)
                for half in range(2):
                    own, plane = divmod(2 * chunk + half, planes)
                    halves[own, slab * planes + plane] = block[8 * half : 8 * half + 8, :]
        for own in range(own_count):
            rows = turned([halves[own, 8 * group + index] for index in range(8)])
            for tile in range(tiles):
                start = ((pair * own_count + own) * tiles + tile) * pitch + REACH + 8 * group
                fields[pl.ds(pl.multiple_of(start, 8), 8), :] = rows[tile]


def rolled(sizes, ref, box, row, rows, offset_x, offset_flat):
    tiles, _, pitch = box_shape(sizes)
    whole = (offset_flat >> 7) & (tiles - 1)
    part = offset_flat & (LANES - 1)
    start = box * tiles * pitch + REACH + row - offset_x
    moved = []
    for tile in range(tiles):
        first_row = start + ((tile - whole) & (tiles - 1)) * pitch
        moved.append(pltpu.roll(ref[pl.ds(first_row, rows), :], part, axis=1))
    keep = lax.broadcasted_iota(jnp.int32, (rows, LANES), 1) >= part
    return [jnp.where(keep, moved[t], moved[(t - 1) % tiles]) for t in range(tiles)]


def place_partner(sizes, fields, box, own_offset, offset, active):
    side = sizes[0]
    tiles, lines, _ = box_shape(sizes)
    placed = rolled(sizes, fields, box, 0, side, offset[0], offset[1] * side + offset[2])
    lane = lax.broadcasted_iota(jnp.int32, (1, LANES), 1)
    lows = [jnp.maximum(jnp.maximum(a, b), 0) for a, b in zip(own_offset, offset)]
    highs = [side + jnp.minimum(jnp.minimum(a, b), 0) for a, b in zip(own_offset, offset)]
    point_ok = (lane % side >= lows[2]) & (lane % side < highs[2]) & active
    result = []
    for tile in range(tiles):
        line = lane // side + tile * lines
        ok = jnp.where(point_ok & (line >= lows[1]) & (line < highs[1]), 1.0, 0.0)
        result.append(placed[tile] * ok)
    return result


def own_kernel(sizes, match_hbm, centers_hbm, own_hbm, *refs):
    constant_hbm, refs = refs[:3], refs[3:]
    mine_ref, table_ref, *constant_refs = refs[:5]
    match_ref, centers_ref, boxes_ref, fields, sems = refs[5:]
    side, rounds, own_count, _, _ = sizes
    tiles, _, _ = box_shape(sizes)
    first_member = lax.axis_index("pair") * own_count
    sources = (match_hbm, centers_hbm, own_hbm, *constant_hbm)
    targets = (match_ref, centers_ref, boxes_ref.at[0], *constant_refs)
    copies = [pltpu.make_async_copy(s, t, sems.at[i]) for i, (s, t) in enumerate(zip(sources, targets))]
    for copy in copies:
        copy.start()
    clear_edges(sizes, fields, 0, own_count)
    for copy in copies:
        copy.wait()
    spread(sizes, boxes_ref, fields, 0)

    def place(index, carry):
        member, mate, a, b, active = pair_geometry(sizes, match_ref, centers_ref, index)
        for place, entry in enumerate((mate, *a, *b, jnp.where(active, 1, 0))):
            table_ref[index * ENTRIES + place] = entry
        rows = pl.ds(pl.multiple_of(index * side, side), side)
        placed = rolled(sizes, fields, member - first_member, 0, side, a[0], a[1] * side + a[2])
        for tile in range(tiles):
            mine_ref[rows, tile * LANES : (tile + 1) * LANES] = placed[tile].astype(jnp.bfloat16)
        return carry

    lax.fori_loop(0, own_count * rounds, place, 0)


def force_kernel(sizes, mine_hbm, table_hbm, *refs):
    side, rounds, own_count, slab_count, pair_count = sizes
    piece_hbm, refs = refs[:pair_count], refs[pair_count:]
    constant_hbm, refs = refs[:3], refs[3:]
    out_refs, refs = refs[:slab_count], refs[slab_count:]
    table_ref, mine, partner, boxes_ref, *refs = refs
    constants, refs = refs[:3], refs[3:]
    basis_ref, line_ref, gain_ref = constants
    mix_ref, there_high, there_low, back_high, back_low, *refs = refs
    fields, first, second, *terms, all_codes, sems = refs
    planes = side // slab_count
    tiles, lines, pitch = box_shape(sizes)
    solves = own_count * rounds
    group = min(solves, 8)
    group_rows = group * side
    cells = tiles * LANES
    width = cells // 2
    slab_index = lax.axis_index("slab")
    pair_index = lax.axis_index("pair")
    core = pair_index % CORES
    chip = pair_index // CORES
    chips = pair_count // CORES

    places = [
        (chip + chips - step) % chips * CORES + (core + core_step) % CORES
        for core_step in range(CORES)
        for step in range(chips)
    ]
    sources = [table_hbm, *constant_hbm, *piece_hbm, mine_hbm]
    targets = [table_ref, *constants, *[boxes_ref.at[pair] for pair in places], mine]
    copies = [pltpu.make_async_copy(s, t, sems.at[i]) for i, (s, t) in enumerate(zip(sources, targets))]
    for copy in copies:
        copy.start()
    for pair in places:
        clear_edges(sizes, fields, pair * own_count, own_count)
    for ref in terms:
        clear_edges(sizes, ref, 0, group)
    for copy in copies[:4]:
        copy.wait()

    def make_matrices(first_line, high_ref, low_ref):
        count = side // 2
        for parity in range(2):
            for index in range(count):
                line = first_line + parity * count + index
                rows = slice(index * side, (index + 1) * side)
                value = basis_ref[...] * line_ref[line : line + 1, :]
                high_ref[parity, rows, :], low_ref[parity, rows, :] = split_pair(value)

    block = lax.broadcasted_iota(jnp.int32, (side, group_rows), 1) // side
    for index in range(group):
        rows = slice(index * side, (index + 1) * side)
        value = jnp.where(block == index, basis_ref[:, :group_rows], 0.0)
        high, low = split_pair(value)
        for part, piece in enumerate((high, high, low)):
            mix_ref[rows, part * group_rows : (part + 1) * group_rows] = piece
    make_matrices(0, there_high, there_low)

    for copy in copies[4:-1]:
        copy.wait()
    for pair in places:
        spread(sizes, boxes_ref, fields, pair)
    copies[-1].wait()

    row_count = solves * side
    half_tiles = tiles // 2
    half_cells = cells // 2

    def mirrored(tile):
        line = lax.broadcasted_iota(jnp.int32, tile.shape, 1) // side
        result = None
        for index in range(lines):
            amount = (2 * index - lines + 1) * side % LANES
            if index < 2:
                moved = pltpu.roll(tile, amount, axis=1)
                result = moved if result is None else jnp.where(line % 2 == index, moved, result)
        return result

    def store_split(ref, start, count, columns, value):
        high, low = split_pair(value)
        ref[start : start + count, columns] = high
        ref[row_count + start : row_count + start + count, columns] = low

    def densities(index):
        start = index * side
        rows = slice(start, start + side)
        mate, *offsets, active = [table_ref[index * ENTRIES + place] for place in range(ENTRIES)]
        placed = place_partner(sizes, fields, mate, offsets[:3], offsets[3:], active == 1)
        density = []
        for tile in range(tiles):
            columns = slice(tile * LANES, (tile + 1) * LANES)
            partner[rows, columns] = placed[tile].astype(jnp.bfloat16)
            density.append(mine[rows, columns].astype(jnp.float32) * placed[tile])
        for tile in range(half_tiles):
            far = mirrored(density[tiles - 1 - tile])
            for parity, value in enumerate((density[tile] + far, density[tile] - far)):
                column = parity * half_cells + tile * LANES
                store_split(first, start, side, slice(column, column + LANES), value)

    def along_x(start, columns, source):
        high = source[start : start + group_rows, columns]
        low = source[row_count + start : row_count + start + group_rows, columns]
        return dot(mix_ref[...], jnp.concatenate([high, low, high], axis=0))

    def in_plane(parity, columns, source, high_ref, low_ref):
        inner = slice(parity * half_cells, (parity + 1) * half_cells)
        high = source[:row_count, inner]
        low = source[row_count:, inner]
        basis = high_ref[parity, :, columns]
        rest = low_ref[parity, :, columns]
        left = jnp.concatenate([high, low, high], axis=1)
        return dot(left, jnp.concatenate([basis, basis, rest], axis=0))

    for start in range(0, row_count, group_rows):
        for index in range(start // side, (start + group_rows) // side):
            densities(index)
        columns = slice(0, cells)
        store_split(second, start, group_rows, columns, along_x(start, columns, first))

    make_matrices(side, back_high, back_low)
    for parity in range(2):
        for column in range(0, half_cells, width):
            columns = slice(column, column + width)
            value = in_plane(parity, columns, second, there_high, there_low)
            columns = slice(parity * half_cells + column, parity * half_cells + column + width)
            gain = gain_ref[:, columns]
            value = (value.reshape(solves, side, width) * gain[None]).reshape(row_count, width)
            store_split(first, 0, row_count, columns, value)

    for parity in range(2):
        for column in range(0, half_cells, width):
            value = in_plane(parity, slice(column, column + width), first, back_high, back_low)
            columns = slice(parity * half_cells + column, parity * half_cells + column + width)
            store_split(second, 0, row_count, columns, value)

    for start in range(0, row_count, group_rows):
        for column in range(0, half_cells, width):
            even = along_x(start, slice(column, column + width), second)
            odd = along_x(start, slice(half_cells + column, half_cells + column + width), second)
            for part in range(width // LANES):
                tile = column // LANES + part
                lanes = slice(part * LANES, (part + 1) * LANES)
                near = even[:, lanes] + odd[:, lanes]
                far = mirrored(even[:, lanes] - odd[:, lanes])
                for place, value in ((tile, near), (tiles - 1 - tile, far)):
                    columns = slice(place * LANES, (place + 1) * LANES)
                    value = value * partner[start : start + group_rows, columns].astype(jnp.float32)
                    for solve in range(group):
                        row = (solve * tiles + place) * pitch + REACH
                        terms[start // group_rows][row : row + side, :] = value[solve * side : (solve + 1) * side, :]

    step_rows = 16

    def collect(own, row):
        sums = None
        for turn in range(rounds):
            index = own * rounds + turn
            a = [table_ref[index * ENTRIES + 1 + axis] for axis in range(3)]
            ref = terms[index // group]
            term = rolled(sizes, ref, index % group, row, step_rows, -a[0], -(a[1] * side + a[2]))
            sums = term if sums is None else [s + t for s, t in zip(sums, term)]
        return sums

    lane_index = lax.broadcasted_iota(jnp.int32, (tiles, LANES), 1)
    exponents = [jnp.zeros((tiles, LANES), jnp.float32)] * slab_count
    factors = [jnp.zeros((tiles, LANES), jnp.float32)] * slab_count
    codes = {}
    for own in range(own_count):
        for row in range(0, side, step_rows):
            sums = collect(own, row)
            for half in range(0, step_rows, 8):
                for index, value in enumerate(turned([tile[half : half + 8, :] for tile in sums])):
                    slab, plane = divmod(row + half + index, planes)
                    chunk = own * planes + plane
                    codes[slab, chunk], exponent, factor = encode(value)
                    exponents[slab] = jnp.where(lane_index == chunk, exponent, exponents[slab])
                    factors[slab] = jnp.where(lane_index == chunk, factor, factors[slab])
                    if chunk % 2:
                        pair = jnp.concatenate([codes[slab, chunk - 1], codes[slab, chunk]], axis=0)
                        all_codes[slab, tiles * (chunk - 1) : tiles * (chunk + 1), :] = whole_codes(pair)
    for slab in range(slab_count):
        header = jnp.concatenate([exponents[slab], factors[slab]], axis=0)
        all_codes[slab, tiles * own_count * planes :, :] = whole_codes(header)
    for step in range(slab_count):
        out_refs[step][...] = all_codes[partner_of(slab_index, step, slab_count)[0]]


def whole_codes(value):
    return value.astype(jnp.int32).astype(jnp.int16)


def encode(value):
    largest = jnp.max(jnp.abs(value), axis=1, keepdims=True)
    exponent = jnp.maximum(jnp.floor(jnp.log2(jnp.maximum(largest, TINY))), LOWEST_EXPONENT)
    lifted = 1.0 / jnp.exp2(exponent)
    factor = jnp.maximum(jnp.ceil(largest * lifted * FACTOR_UNIT), 1.0)
    code = jnp.floor(value * lifted * (CODE_LIMIT * FACTOR_UNIT / factor) + 0.5)
    return jnp.clip(code, -CODE_LIMIT, CODE_LIMIT), exponent, factor


def swap_cores(block, pair_count):
    return lax.ppermute(block, "pair", [(i, i ^ 1) for i in range(pair_count)])


def gather_chips(boxes, pair_count):
    pieces = []
    for step in range(1, pair_count // CORES):
        perm = [(i, (i + step * CORES) % pair_count) for i in range(pair_count)]
        pieces.append(lax.ppermute(boxes, "pair", perm))
    return pieces


def unpack_kernel(sizes, *refs):
    own_count, slab_count, tiles = sizes
    block_refs, out_ref, blocks, sems = refs[:slab_count], *refs[slab_count:]
    slab_index = lax.axis_index("slab")
    copies = []
    for index in range(slab_count):
        slab = partner_of(slab_index, slab_count - 1 - index, slab_count)[1]
        copies.append(pltpu.make_async_copy(block_refs[index], blocks.at[slab], sems.at[index]))
        copies[-1].start()
    for copy in copies:
        copy.wait()
    row_count = own_count * tiles
    values = {}
    for slab in range(slab_count):
        header = blocks[slab, row_count:, :].astype(jnp.int32).astype(jnp.float32)
        units = jnp.exp2(header[:8, :])
        factors = header[8:, :] * (1.0 / (CODE_LIMIT * FACTOR_UNIT))
        for pair in range(row_count // 16):
            codes = blocks[slab, 16 * pair : 16 * pair + 16, :].astype(jnp.int32).astype(jnp.float32)
            for half in range(2):
                chunk = 2 * pair + half
                own, plane = divmod(8 * chunk, tiles)
                value = codes[8 * half : 8 * half + 8, :] * factors[:, chunk : chunk + 1]
                values[slab * own_count + own, plane // 8] = value * units[:, chunk : chunk + 1]
        if (slab + 1) * own_count % 8 == 0:
            band = (slab + 1) * own_count // 8 - 1
            for plane in range(tiles // 8):
                rows = turned([values[8 * band + index, plane] for index in range(8)])
                for tile in range(8):
                    start = (band * tiles + 8 * plane + tile) * 8
                    out_ref[start : start + 8, :] = rows[tile]


def unpack(blocks, own_count, cells):
    slab_count = len(blocks)
    row_count = own_count * slab_count
    tiles = cells // LANES
    out = pl.pallas_call(
        functools.partial(unpack_kernel, (own_count, slab_count, tiles)),
        out_shape=jax.ShapeDtypeStruct((row_count * tiles, LANES), jnp.float32),
        in_specs=[pl.BlockSpec(memory_space=pl.ANY)] * slab_count,
        out_specs=pl.BlockSpec(memory_space=pltpu.VMEM),
        scratch_shapes=[
            pltpu.VMEM((slab_count,) + blocks[0].shape, jnp.int16),
            pltpu.SemaphoreType.DMA((slab_count,)),
        ],
        compiler_params=pltpu.CompilerParams(vmem_limit_bytes=8 * 1024 * 1024),
    )(*blocks)
    return out.reshape(row_count // 8, tiles, 8, LANES).transpose(0, 2, 1, 3).reshape(row_count, cells)


def kernel_constants(side):
    basis = sine_basis(side)
    halves = [basis[parity::2, : side // 2].T for parity in range(2)]
    lines = np.concatenate(halves + [half.T for half in halves])
    lines = np.repeat(lines, side, axis=1).astype(np.float32)
    tile = np.tile(basis, (1, side // 2)).astype(np.float32)
    gain = chebyshev_gain(side).reshape(side, side, side)
    gain = np.concatenate([gain[:, parity::2].reshape(side, -1) for parity in range(2)], axis=1)
    return [jnp.asarray(constant) for constant in (tile, lines, gain)]


def place_own(sizes, match, centers, boxes):
    side, rounds, own_count, slab_count, _ = sizes
    tiles, _, pitch = box_shape(sizes)
    solves = own_count * rounds
    constants = kernel_constants(side)
    inputs = [match, centers, boxes, *constants]
    either = pl.BlockSpec(memory_space=pl.ANY)
    vectors = pl.BlockSpec(memory_space=pltpu.VMEM)
    return pl.pallas_call(
        functools.partial(own_kernel, sizes),
        out_shape=[
            jax.ShapeDtypeStruct((solves * side, side * side), jnp.bfloat16),
            jax.ShapeDtypeStruct((solves * ENTRIES,), jnp.int32),
            *[jax.ShapeDtypeStruct(constant.shape, constant.dtype) for constant in constants],
        ],
        in_specs=[either] * len(inputs),
        out_specs=[vectors, pl.BlockSpec(memory_space=pltpu.SMEM)] + [vectors] * len(constants),
        scratch_shapes=[
            pltpu.SMEM(match.shape, jnp.int32),
            pltpu.SMEM(centers.shape, jnp.int32),
            pltpu.VMEM((1,) + boxes.shape, jnp.bfloat16),
            pltpu.VMEM((own_count * tiles * pitch, LANES), jnp.float32),
            pltpu.SemaphoreType.DMA((len(inputs),)),
        ],
        compiler_params=pltpu.CompilerParams(vmem_limit_bytes=32 * 1024 * 1024),
        cost_estimate=pl.CostEstimate(flops=5 * 10**9, bytes_accessed=4 * 1024 * 1024, transcendentals=0),
    )(*inputs)


def team_forces(sizes, mine, table, constants, pieces):
    side, rounds, own_count, slab_count, pair_count = sizes
    tiles, _, pitch = box_shape(sizes)
    _, rows, _ = pieces[0].shape
    solves = own_count * rounds
    group = min(solves, 8)
    cells = side * side
    either = pl.BlockSpec(memory_space=pl.ANY)
    vectors = pl.BlockSpec(memory_space=pltpu.VMEM)
    wide = pltpu.VMEM((2 * solves * side, cells), jnp.bfloat16)
    flops = 2 * solves * side * 3 * 2 * (cells * cells // 2 + cells * group * side)
    inputs = [mine, table, *pieces, *constants]
    return pl.pallas_call(
        functools.partial(force_kernel, sizes),
        out_shape=[jax.ShapeDtypeStruct((rows + HEADER_ROWS, LANES), jnp.int16)] * slab_count,
        in_specs=[either] * len(inputs),
        out_specs=[vectors] * slab_count,
        scratch_shapes=[
            pltpu.SMEM(table.shape, jnp.int32),
            pltpu.VMEM(mine.shape, jnp.bfloat16),
            pltpu.VMEM(mine.shape, jnp.bfloat16),
            pltpu.VMEM((pair_count, slab_count, rows, LANES), jnp.bfloat16),
            *[pltpu.VMEM(constant.shape, constant.dtype) for constant in constants],
            pltpu.VMEM((group * side, 3 * group * side), jnp.bfloat16),
            *[pltpu.VMEM((2, cells // 2, cells // 2), jnp.bfloat16)] * 4,
            pltpu.VMEM((own_count * pair_count * tiles * pitch, LANES), jnp.float32),
            wide,
            wide,
            *[pltpu.VMEM((group * tiles * pitch, LANES), jnp.float32)] * (solves // group),
            pltpu.VMEM((slab_count, rows + HEADER_ROWS, LANES), jnp.int16),
            pltpu.SemaphoreType.DMA((len(inputs),)),
        ],
        compiler_params=pltpu.CompilerParams(vmem_limit_bytes=32 * 1024 * 1024),
        cost_estimate=pl.CostEstimate(flops=flops, bytes_accessed=8 * 1024 * 1024, transcendentals=0),
    )(*inputs)


def shards(orbitals, centers, matchings):
    slab_count = lax.axis_size("slab")
    pair_count = lax.axis_size("pair")
    local_rows, plane_cells = orbitals.shape
    own_count = local_rows // slab_count
    side = round((plane_cells * slab_count) ** (1.0 / 3.0))
    blocks = orbitals.reshape(slab_count, own_count * plane_cells // LANES, LANES)
    boxes = lax.all_to_all(blocks, "slab", split_axis=0, concat_axis=0, tiled=True)
    sizes = (side, matchings.shape[1], own_count, slab_count, pair_count)
    pieces = gather_chips(boxes, pair_count)
    mine, table, *constants = place_own(sizes, matchings, centers.T, boxes)
    boxes, mine = lax.optimization_barrier((boxes, mine))
    swapped = [swap_cores(boxes, pair_count)]
    pieces, mine = lax.optimization_barrier((pieces, mine))
    swapped += [swap_cores(piece, pair_count) for piece in pieces]
    codes = team_forces(sizes, mine, table, constants, [boxes] + pieces + swapped)
    received = []
    for step in reversed(range(1, slab_count)):
        perm = [(i, partner_of(i, step, slab_count)[0]) for i in range(slab_count)]
        received.append(lax.ppermute(codes[step], "slab", perm))
    return unpack(received + [codes[0]], own_count, plane_cells)


def solution(mesh):
    in_specs = (P("pair", "slab"), P(), P("slab", None, None))
    out_specs = P("pair", "slab")
    return jax.shard_map(shards, mesh=mesh, in_specs=in_specs, out_specs=out_specs, check_vma=False)
```

```python
import functools

import jax
import jax.numpy as jnp
import numpy as np
from jax import lax
from jax.experimental import pallas as pl
from jax.experimental.pallas import tpu as pltpu
from jax.sharding import PartitionSpec as P

STEPS = 16
CUT2 = 192
REACH = 8
SCREEN = 0.1
LOWER_BOUND = 0.1
UPPER_BOUND = 12.1
LANES = 128
CORES = 2
CODE_LIMIT = 32767.0
FACTOR_UNIT = 8192.0
LOWEST_EXPONENT = -120.0
TINY = 1e-37
HEADER_ROWS = 16
ENTRIES = 8


def sine_basis(side):
    index = np.arange(1, side + 1, dtype=np.float64)
    return np.sqrt(2.0 / (side + 1)) * np.sin(np.pi * np.outer(index, index) / (side + 1))


def chebyshev_gain(side):
    shifts = -2.0 * np.cos(np.pi * np.arange(1, side + 1, dtype=np.float64) / (side + 1))
    eigenvalue = 6.0 + SCREEN + shifts[:, None, None] + shifts[None, :, None] + shifts[None, None, :]
    middle = (UPPER_BOUND + LOWER_BOUND) / 2.0
    spread = (UPPER_BOUND - LOWER_BOUND) / 2.0
    ratio = middle / spread
    total = np.zeros_like(eigenvalue)
    residual = np.ones_like(eigenvalue)
    direction = residual / middle
    factor = 1.0 / ratio
    for _ in range(STEPS):
        total = total + direction
        residual = residual - eigenvalue * direction
        factor_next = 1.0 / (2.0 * ratio - factor)
        direction = factor_next * factor * direction + 2.0 * factor_next / spread * residual
        factor = factor_next
    return total.reshape(side, side * side).astype(np.float32)


def split_pair(value):
    high = value.astype(jnp.bfloat16)
    low = (value - high.astype(jnp.float32)).astype(jnp.bfloat16)
    return high, low


def dot(left, right):
    return jnp.dot(left, right, preferred_element_type=jnp.float32)


def pair_geometry(sizes, match_ref, centers_ref, index):
    _, rounds, own_count, slab_count, _ = sizes
    slab_index = lax.axis_index("slab")
    pair_index = lax.axis_index("pair")

    def orbital_of(member):
        return (member // own_count * slab_count + slab_index) * own_count + member % own_count

    member = pair_index * own_count + index // rounds
    mate = match_ref[0, index % rounds, member]
    own_offset = []
    mate_offset = []
    distance = 0
    for axis in range(3):
        mine = centers_ref[axis, orbital_of(member)]
        other = centers_ref[axis, orbital_of(mate)]
        anchor = (mine + other) >> 1
        own_offset.append(mine - anchor)
        mate_offset.append(other - anchor)
        distance = distance + (mine - other) * (mine - other)
    return member, mate, own_offset, mate_offset, distance <= CUT2


def box_shape(sizes):
    side = sizes[0]
    return side * side // LANES, LANES // side, side + 2 * REACH


def clear_edges(sizes, ref, first, count):
    side = sizes[0]
    tiles, _, pitch = box_shape(sizes)
    zeros = jnp.zeros((REACH, LANES), jnp.float32)

    def clear(index, carry):
        start = (first * tiles + index) * pitch
        ref[pl.ds(pl.multiple_of(start, 8), REACH), :] = zeros
        ref[pl.ds(pl.multiple_of(start + REACH + side, 8), REACH), :] = zeros
        return carry

    lax.fori_loop(0, count * tiles, clear, 0, unroll=8)


def turned(tiles):
    row = lax.broadcasted_iota(jnp.int32, (8, LANES), 0)
    tiles = list(tiles)
    for distance in (4, 2, 1):
        low = (row & distance) == 0
        for index in range(8):
            if index & distance == 0:
                first, second = tiles[index], tiles[index + distance]
                tiles[index] = jnp.where(low, first, pltpu.roll(second, distance, axis=0))
                tiles[index + distance] = jnp.where(low, pltpu.roll(first, 8 - distance, axis=0), second)
    return tiles


def spread(sizes, boxes_ref, fields, pair):
    side, _, own_count, slab_count, _ = sizes
    planes = side // slab_count
    tiles, _, pitch = box_shape(sizes)
    for group in range(side // 8):
        halves = {}
        for slab in range(8 * group // planes, (8 * group + 7) // planes + 1):
            for chunk in range(own_count * planes // 2):
                block = boxes_ref[pair, slab, 16 * chunk : 16 * chunk + 16, :].astype(jnp.float32)
                for half in range(2):
                    own, plane = divmod(2 * chunk + half, planes)
                    halves[own, slab * planes + plane] = block[8 * half : 8 * half + 8, :]
        for own in range(own_count):
            rows = turned([halves[own, 8 * group + index] for index in range(8)])
            for tile in range(tiles):
                start = ((pair * own_count + own) * tiles + tile) * pitch + REACH + 8 * group
                fields[pl.ds(pl.multiple_of(start, 8), 8), :] = rows[tile]


def rolled(sizes, ref, box, row, rows, offset_x, offset_flat):
    tiles, _, pitch = box_shape(sizes)
    whole = (offset_flat >> 7) & (tiles - 1)
    part = offset_flat & (LANES - 1)
    start = box * tiles * pitch + REACH + row - offset_x
    moved = []
    for tile in range(tiles):
        first_row = start + ((tile - whole) & (tiles - 1)) * pitch
        moved.append(pltpu.roll(ref[pl.ds(first_row, rows), :], part, axis=1))
    keep = lax.broadcasted_iota(jnp.int32, (rows, LANES), 1) >= part
    return [jnp.where(keep, moved[t], moved[(t - 1) % tiles]) for t in range(tiles)]


def place_partner(sizes, fields, box, own_offset, offset, active):
    side = sizes[0]
    tiles, lines, _ = box_shape(sizes)
    placed = rolled(sizes, fields, box, 0, side, offset[0], offset[1] * side + offset[2])
    lane = lax.broadcasted_iota(jnp.int32, (1, LANES), 1)
    lows = [jnp.maximum(jnp.maximum(a, b), 0) for a, b in zip(own_offset, offset)]
    highs = [side + jnp.minimum(jnp.minimum(a, b), 0) for a, b in zip(own_offset, offset)]
    point_ok = (lane % side >= lows[2]) & (lane % side < highs[2]) & active
    result = []
    for tile in range(tiles):
        line = lane // side + tile * lines
        ok = jnp.where(point_ok & (line >= lows[1]) & (line < highs[1]), 1.0, 0.0)
        result.append(placed[tile] * ok)
    return result


def own_kernel(sizes, match_hbm, centers_hbm, own_hbm, *refs):
    constant_hbm, refs = refs[:3], refs[3:]
    mine_ref, table_ref, *constant_refs = refs[:5]
    match_ref, centers_ref, boxes_ref, fields, sems = refs[5:]
    side, rounds, own_count, _, _ = sizes
    tiles, _, _ = box_shape(sizes)
    first_member = lax.axis_index("pair") * own_count
    sources = (match_hbm, centers_hbm, own_hbm, *constant_hbm)
    targets = (match_ref, centers_ref, boxes_ref.at[0], *constant_refs)
    copies = [pltpu.make_async_copy(s, t, sems.at[i]) for i, (s, t) in enumerate(zip(sources, targets))]
    for copy in copies:
        copy.start()
    clear_edges(sizes, fields, 0, own_count)
    for copy in copies:
        copy.wait()
    spread(sizes, boxes_ref, fields, 0)

    def place(index, carry):
        member, mate, a, b, active = pair_geometry(sizes, match_ref, centers_ref, index)
        for place, entry in enumerate((mate, *a, *b, jnp.where(active, 1, 0))):
            table_ref[index * ENTRIES + place] = entry
        rows = pl.ds(pl.multiple_of(index * side, side), side)
        placed = rolled(sizes, fields, member - first_member, 0, side, a[0], a[1] * side + a[2])
        for tile in range(tiles):
            mine_ref[rows, tile * LANES : (tile + 1) * LANES] = placed[tile].astype(jnp.bfloat16)
        return carry

    lax.fori_loop(0, own_count * rounds, place, 0)


def force_kernel(sizes, mine_hbm, table_hbm, *refs):
    side, rounds, own_count, slab_count, pair_count = sizes
    piece_hbm, refs = refs[:pair_count], refs[pair_count:]
    constant_hbm, refs = refs[:3], refs[3:]
    all_codes, refs = refs[0], refs[1:]
    table_ref, mine, partner, boxes_ref, *refs = refs
    constants, refs = refs[:3], refs[3:]
    basis_ref, line_ref, gain_ref = constants
    mix_ref, there_high, there_low, back_high, back_low, *refs = refs
    fields, first, second, *terms, sems = refs
    planes = side // slab_count
    tiles, lines, pitch = box_shape(sizes)
    solves = own_count * rounds
    group = min(solves, 8)
    group_rows = group * side
    cells = tiles * LANES
    width = cells // 2
    pair_index = lax.axis_index("pair")
    core = pair_index % CORES
    chip = pair_index // CORES
    chips = pair_count // CORES

    places = [
        (chip + chips - step) % chips * CORES + (core + core_step) % CORES
        for core_step in range(CORES)
        for step in range(chips)
    ]
    sources = [table_hbm, *constant_hbm, *piece_hbm, mine_hbm]
    targets = [table_ref, *constants, *[boxes_ref.at[pair] for pair in places], mine]
    copies = [pltpu.make_async_copy(s, t, sems.at[i]) for i, (s, t) in enumerate(zip(sources, targets))]
    for copy in copies:
        copy.start()
    for pair in places:
        clear_edges(sizes, fields, pair * own_count, own_count)
    for ref in terms:
        clear_edges(sizes, ref, 0, group)
    for copy in copies[:4]:
        copy.wait()

    def make_matrices(first_line, high_ref, low_ref):
        count = side // 2
        for parity in range(2):
            for index in range(count):
                line = first_line + parity * count + index
                rows = slice(index * side, (index + 1) * side)
                value = basis_ref[...] * line_ref[line : line + 1, :]
                high_ref[parity, rows, :], low_ref[parity, rows, :] = split_pair(value)

    block = lax.broadcasted_iota(jnp.int32, (side, group_rows), 1) // side
    for index in range(group):
        rows = slice(index * side, (index + 1) * side)
        value = jnp.where(block == index, basis_ref[:, :group_rows], 0.0)
        high, low = split_pair(value)
        for part, piece in enumerate((high, high, low)):
            mix_ref[rows, part * group_rows : (part + 1) * group_rows] = piece
    make_matrices(0, there_high, there_low)

    for copy in copies[4:-1]:
        copy.wait()
    for pair in places:
        spread(sizes, boxes_ref, fields, pair)
    copies[-1].wait()

    row_count = solves * side
    half_tiles = tiles // 2
    half_cells = cells // 2

    def mirrored(tile):
        line = lax.broadcasted_iota(jnp.int32, tile.shape, 1) // side
        result = None
        for index in range(lines):
            amount = (2 * index - lines + 1) * side % LANES
            if index < 2:
                moved = pltpu.roll(tile, amount, axis=1)
                result = moved if result is None else jnp.where(line % 2 == index, moved, result)
        return result

    def store_split(ref, start, count, columns, value):
        high, low = split_pair(value)
        ref[start : start + count, columns] = high
        ref[row_count + start : row_count + start + count, columns] = low

    def densities(index):
        start = index * side
        rows = slice(start, start + side)
        mate, *offsets, active = [table_ref[index * ENTRIES + place] for place in range(ENTRIES)]
        placed = place_partner(sizes, fields, mate, offsets[:3], offsets[3:], active == 1)
        density = []
        for tile in range(tiles):
            columns = slice(tile * LANES, (tile + 1) * LANES)
            partner[rows, columns] = placed[tile].astype(jnp.bfloat16)
            density.append(mine[rows, columns].astype(jnp.float32) * placed[tile])
        for tile in range(half_tiles):
            far = mirrored(density[tiles - 1 - tile])
            for parity, value in enumerate((density[tile] + far, density[tile] - far)):
                column = parity * half_cells + tile * LANES
                store_split(first, start, side, slice(column, column + LANES), value)

    def along_x(start, columns, source):
        high = source[start : start + group_rows, columns]
        low = source[row_count + start : row_count + start + group_rows, columns]
        return dot(mix_ref[...], jnp.concatenate([high, low, high], axis=0))

    def in_plane(parity, columns, source, high_ref, low_ref):
        inner = slice(parity * half_cells, (parity + 1) * half_cells)
        high = source[:row_count, inner]
        low = source[row_count:, inner]
        basis = high_ref[parity, :, columns]
        rest = low_ref[parity, :, columns]
        left = jnp.concatenate([high, low, high], axis=1)
        return dot(left, jnp.concatenate([basis, basis, rest], axis=0))

    for start in range(0, row_count, group_rows):
        for index in range(start // side, (start + group_rows) // side):
            densities(index)
        columns = slice(0, cells)
        store_split(second, start, group_rows, columns, along_x(start, columns, first))

    make_matrices(side, back_high, back_low)
    for parity in range(2):
        for column in range(0, half_cells, width):
            columns = slice(column, column + width)
            value = in_plane(parity, columns, second, there_high, there_low)
            columns = slice(parity * half_cells + column, parity * half_cells + column + width)
            gain = gain_ref[:, columns]
            value = (value.reshape(solves, side, width) * gain[None]).reshape(row_count, width)
            store_split(first, 0, row_count, columns, value)

    for parity in range(2):
        for column in range(0, half_cells, width):
            value = in_plane(parity, slice(column, column + width), first, back_high, back_low)
            columns = slice(parity * half_cells + column, parity * half_cells + column + width)
            store_split(second, 0, row_count, columns, value)

    for start in range(0, row_count, group_rows):
        for column in range(0, half_cells, width):
            even = along_x(start, slice(column, column + width), second)
            odd = along_x(start, slice(half_cells + column, half_cells + column + width), second)
            for part in range(width // LANES):
                tile = column // LANES + part
                lanes = slice(part * LANES, (part + 1) * LANES)
                near = even[:, lanes] + odd[:, lanes]
                far = mirrored(even[:, lanes] - odd[:, lanes])
                for place, value in ((tile, near), (tiles - 1 - tile, far)):
                    columns = slice(place * LANES, (place + 1) * LANES)
                    value = value * partner[start : start + group_rows, columns].astype(jnp.float32)
                    for solve in range(group):
                        row = (solve * tiles + place) * pitch + REACH
                        terms[start // group_rows][row : row + side, :] = value[solve * side : (solve + 1) * side, :]

    step_rows = 16

    def collect(own, row):
        sums = None
        for turn in range(rounds):
            index = own * rounds + turn
            a = [table_ref[index * ENTRIES + 1 + axis] for axis in range(3)]
            ref = terms[index // group]
            term = rolled(sizes, ref, index % group, row, step_rows, -a[0], -(a[1] * side + a[2]))
            sums = term if sums is None else [s + t for s, t in zip(sums, term)]
        return sums

    lane_index = lax.broadcasted_iota(jnp.int32, (tiles, LANES), 1)
    exponents = [jnp.zeros((tiles, LANES), jnp.float32)] * slab_count
    factors = [jnp.zeros((tiles, LANES), jnp.float32)] * slab_count
    codes = {}
    for own in range(own_count):
        for row in range(0, side, step_rows):
            sums = collect(own, row)
            for half in range(0, step_rows, 8):
                for index, value in enumerate(turned([tile[half : half + 8, :] for tile in sums])):
                    slab, plane = divmod(row + half + index, planes)
                    chunk = own * planes + plane
                    codes[slab, chunk], exponent, factor = encode(value)
                    exponents[slab] = jnp.where(lane_index == chunk, exponent, exponents[slab])
                    factors[slab] = jnp.where(lane_index == chunk, factor, factors[slab])
                    if chunk % 2:
                        pair = jnp.concatenate([codes[slab, chunk - 1], codes[slab, chunk]], axis=0)
                        all_codes[slab, tiles * (chunk - 1) : tiles * (chunk + 1), :] = whole_codes(pair)
    for slab in range(slab_count):
        header = jnp.concatenate([exponents[slab], factors[slab]], axis=0)
        all_codes[slab, tiles * own_count * planes :, :] = whole_codes(header)


def whole_codes(value):
    return value.astype(jnp.int32).astype(jnp.int16)


def encode(value):
    largest = jnp.max(jnp.abs(value), axis=1, keepdims=True)
    exponent = jnp.maximum(jnp.floor(jnp.log2(jnp.maximum(largest, TINY))), LOWEST_EXPONENT)
    lifted = 1.0 / jnp.exp2(exponent)
    factor = jnp.maximum(jnp.ceil(largest * lifted * FACTOR_UNIT), 1.0)
    code = jnp.floor(value * lifted * (CODE_LIMIT * FACTOR_UNIT / factor) + 0.5)
    return jnp.clip(code, -CODE_LIMIT, CODE_LIMIT), exponent, factor


def swap_cores(block, pair_count):
    return lax.ppermute(block, "pair", [(i, i ^ 1) for i in range(pair_count)])


def gather_chips(boxes, pair_count):
    pieces = []
    for step in range(1, pair_count // CORES):
        perm = [(i, (i + step * CORES) % pair_count) for i in range(pair_count)]
        pieces.append(lax.ppermute(boxes, "pair", perm))
    return pieces


def unpack_kernel(sizes, *refs):
    own_count, slab_count, tiles = sizes
    blocks_hbm, out_ref, blocks, sems = refs
    copies = [pltpu.make_async_copy(blocks_hbm.at[slab], blocks.at[slab], sems.at[slab]) for slab in range(slab_count)]
    for copy in copies:
        copy.start()
    row_count = own_count * tiles
    values = {}
    for slab in range(slab_count):
        copies[slab].wait()
        header = blocks[slab, row_count:, :].astype(jnp.int32).astype(jnp.float32)
        units = jnp.exp2(header[:8, :])
        factors = header[8:, :] * (1.0 / (CODE_LIMIT * FACTOR_UNIT))
        for pair in range(row_count // 16):
            codes = blocks[slab, 16 * pair : 16 * pair + 16, :].astype(jnp.int32).astype(jnp.float32)
            for half in range(2):
                chunk = 2 * pair + half
                own, plane = divmod(8 * chunk, tiles)
                value = codes[8 * half : 8 * half + 8, :] * factors[:, chunk : chunk + 1]
                values[slab * own_count + own, plane // 8] = value * units[:, chunk : chunk + 1]
        if (slab + 1) * own_count % 8 == 0:
            band = (slab + 1) * own_count // 8 - 1
            for plane in range(tiles // 8):
                rows = turned([values[8 * band + index, plane] for index in range(8)])
                for tile in range(8):
                    start = (band * tiles + 8 * plane + tile) * 8
                    out_ref[start : start + 8, :] = rows[tile]


def unpack(blocks, own_count, cells):
    slab_count = blocks.shape[0]
    row_count = own_count * slab_count
    tiles = cells // LANES
    out = pl.pallas_call(
        functools.partial(unpack_kernel, (own_count, slab_count, tiles)),
        out_shape=jax.ShapeDtypeStruct((row_count * tiles, LANES), jnp.float32),
        in_specs=[pl.BlockSpec(memory_space=pl.ANY)],
        out_specs=pl.BlockSpec(memory_space=pltpu.VMEM),
        scratch_shapes=[
            pltpu.VMEM(blocks.shape, jnp.int16),
            pltpu.SemaphoreType.DMA((slab_count,)),
        ],
        compiler_params=pltpu.CompilerParams(vmem_limit_bytes=8 * 1024 * 1024),
    )(blocks)
    return out.reshape(row_count // 8, tiles, 8, LANES).transpose(0, 2, 1, 3).reshape(row_count, cells)


def kernel_constants(side):
    basis = sine_basis(side)
    halves = [basis[parity::2, : side // 2].T for parity in range(2)]
    lines = np.concatenate(halves + [half.T for half in halves])
    lines = np.repeat(lines, side, axis=1).astype(np.float32)
    tile = np.tile(basis, (1, side // 2)).astype(np.float32)
    gain = chebyshev_gain(side).reshape(side, side, side)
    gain = np.concatenate([gain[:, parity::2].reshape(side, -1) for parity in range(2)], axis=1)
    return [jnp.asarray(constant) for constant in (tile, lines, gain)]


def place_own(sizes, match, centers, boxes):
    side, rounds, own_count, slab_count, _ = sizes
    tiles, _, pitch = box_shape(sizes)
    solves = own_count * rounds
    constants = kernel_constants(side)
    inputs = [match, centers, boxes, *constants]
    either = pl.BlockSpec(memory_space=pl.ANY)
    vectors = pl.BlockSpec(memory_space=pltpu.VMEM)
    return pl.pallas_call(
        functools.partial(own_kernel, sizes),
        out_shape=[
            jax.ShapeDtypeStruct((solves * side, side * side), jnp.bfloat16),
            jax.ShapeDtypeStruct((solves * ENTRIES,), jnp.int32),
            *[jax.ShapeDtypeStruct(constant.shape, constant.dtype) for constant in constants],
        ],
        in_specs=[either] * len(inputs),
        out_specs=[vectors, pl.BlockSpec(memory_space=pltpu.SMEM)] + [vectors] * len(constants),
        scratch_shapes=[
            pltpu.SMEM(match.shape, jnp.int32),
            pltpu.SMEM(centers.shape, jnp.int32),
            pltpu.VMEM((1,) + boxes.shape, jnp.bfloat16),
            pltpu.VMEM((own_count * tiles * pitch, LANES), jnp.float32),
            pltpu.SemaphoreType.DMA((len(inputs),)),
        ],
        compiler_params=pltpu.CompilerParams(vmem_limit_bytes=32 * 1024 * 1024),
        cost_estimate=pl.CostEstimate(flops=5 * 10**9, bytes_accessed=4 * 1024 * 1024, transcendentals=0),
    )(*inputs)


def team_forces(sizes, mine, table, constants, pieces):
    side, rounds, own_count, slab_count, pair_count = sizes
    tiles, _, pitch = box_shape(sizes)
    _, rows, _ = pieces[0].shape
    solves = own_count * rounds
    group = min(solves, 8)
    cells = side * side
    either = pl.BlockSpec(memory_space=pl.ANY)
    vectors = pl.BlockSpec(memory_space=pltpu.VMEM)
    wide = pltpu.VMEM((2 * solves * side, cells), jnp.bfloat16)
    flops = 2 * solves * side * 3 * 2 * (cells * cells // 2 + cells * group * side)
    inputs = [mine, table, *pieces, *constants]
    return pl.pallas_call(
        functools.partial(force_kernel, sizes),
        out_shape=jax.ShapeDtypeStruct((slab_count, rows + HEADER_ROWS, LANES), jnp.int16),
        in_specs=[either] * len(inputs),
        out_specs=vectors,
        scratch_shapes=[
            pltpu.SMEM(table.shape, jnp.int32),
            pltpu.VMEM(mine.shape, jnp.bfloat16),
            pltpu.VMEM(mine.shape, jnp.bfloat16),
            pltpu.VMEM((pair_count, slab_count, rows, LANES), jnp.bfloat16),
            *[pltpu.VMEM(constant.shape, constant.dtype) for constant in constants],
            pltpu.VMEM((group * side, 3 * group * side), jnp.bfloat16),
            *[pltpu.VMEM((2, cells // 2, cells // 2), jnp.bfloat16)] * 4,
            pltpu.VMEM((own_count * pair_count * tiles * pitch, LANES), jnp.float32),
            wide,
            wide,
            *[pltpu.VMEM((group * tiles * pitch, LANES), jnp.float32)] * (solves // group),
            pltpu.SemaphoreType.DMA((len(inputs),)),
        ],
        compiler_params=pltpu.CompilerParams(vmem_limit_bytes=32 * 1024 * 1024),
        cost_estimate=pl.CostEstimate(flops=flops, bytes_accessed=8 * 1024 * 1024, transcendentals=0),
    )(*inputs)


def shards(orbitals, centers, matchings):
    slab_count = lax.axis_size("slab")
    pair_count = lax.axis_size("pair")
    local_rows, plane_cells = orbitals.shape
    own_count = local_rows // slab_count
    side = round((plane_cells * slab_count) ** (1.0 / 3.0))
    blocks = orbitals.reshape(slab_count, own_count * plane_cells // LANES, LANES)
    boxes = lax.all_to_all(blocks, "slab", split_axis=0, concat_axis=0, tiled=True)
    sizes = (side, matchings.shape[1], own_count, slab_count, pair_count)
    pieces = gather_chips(boxes, pair_count)
    mine, table, *constants = place_own(sizes, matchings, centers.T, boxes)
    boxes, mine = lax.optimization_barrier((boxes, mine))
    swapped = [swap_cores(boxes, pair_count)]
    pieces, mine = lax.optimization_barrier((pieces, mine))
    swapped += [swap_cores(piece, pair_count) for piece in pieces]
    codes = team_forces(sizes, mine, table, constants, [boxes] + pieces + swapped)
    codes = lax.all_to_all(codes, "slab", split_axis=0, concat_axis=0, tiled=True)
    return unpack(codes, own_count, plane_cells)


def solution(mesh):
    in_specs = (P("pair", "slab"), P(), P("slab", None, None))
    out_specs = P("pair", "slab")
    return jax.shard_map(shards, mesh=mesh, in_specs=in_specs, out_specs=out_specs, check_vma=False)
```

```python
import functools

import jax
import jax.numpy as jnp
import numpy as np
from jax import lax
from jax.experimental import pallas as pl
from jax.experimental.pallas import tpu as pltpu
from jax.sharding import PartitionSpec as P

STEPS = 16
CUT2 = 192
REACH = 8
SCREEN = 0.1
LOWER_BOUND = 0.1
UPPER_BOUND = 12.1
LANES = 128
CORES = 2
CODE_LIMIT = 32767.0
FACTOR_UNIT = 8192.0
LOWEST_EXPONENT = -120.0
TINY = 1e-37
HEADER_ROWS = 16
ENTRIES = 8


def sine_basis(side):
    index = np.arange(1, side + 1, dtype=np.float64)
    return np.sqrt(2.0 / (side + 1)) * np.sin(np.pi * np.outer(index, index) / (side + 1))


def chebyshev_gain(side):
    shifts = -2.0 * np.cos(np.pi * np.arange(1, side + 1, dtype=np.float64) / (side + 1))
    eigenvalue = 6.0 + SCREEN + shifts[:, None, None] + shifts[None, :, None] + shifts[None, None, :]
    middle = (UPPER_BOUND + LOWER_BOUND) / 2.0
    spread = (UPPER_BOUND - LOWER_BOUND) / 2.0
    ratio = middle / spread
    total = np.zeros_like(eigenvalue)
    residual = np.ones_like(eigenvalue)
    direction = residual / middle
    factor = 1.0 / ratio
    for _ in range(STEPS):
        total = total + direction
        residual = residual - eigenvalue * direction
        factor_next = 1.0 / (2.0 * ratio - factor)
        direction = factor_next * factor * direction + 2.0 * factor_next / spread * residual
        factor = factor_next
    return total.reshape(side, side * side).astype(np.float32)


def split_pair(value):
    high = value.astype(jnp.bfloat16)
    low = (value - high.astype(jnp.float32)).astype(jnp.bfloat16)
    return high, low


def dot(left, right):
    return jnp.dot(left, right, preferred_element_type=jnp.float32)


def partner_of(index, step, count):
    if count & (count - 1) == 0:
        return index ^ step, index ^ step
    return (index + step) % count, (index + count - step) % count


def pair_geometry(sizes, match_ref, centers_ref, index):
    _, rounds, own_count, slab_count, _ = sizes
    slab_index = lax.axis_index("slab")
    pair_index = lax.axis_index("pair")

    def orbital_of(member):
        return (member // own_count * slab_count + slab_index) * own_count + member % own_count

    member = pair_index * own_count + index // rounds
    mate = match_ref[0, index % rounds, member]
    own_offset = []
    mate_offset = []
    distance = 0
    for axis in range(3):
        mine = centers_ref[axis, orbital_of(member)]
        other = centers_ref[axis, orbital_of(mate)]
        anchor = (mine + other) >> 1
        own_offset.append(mine - anchor)
        mate_offset.append(other - anchor)
        distance = distance + (mine - other) * (mine - other)
    return member, mate, own_offset, mate_offset, distance <= CUT2


def box_shape(sizes):
    side = sizes[0]
    return side * side // LANES, LANES // side, side + 2 * REACH


def clear_edges(sizes, ref, first, count):
    side = sizes[0]
    tiles, _, pitch = box_shape(sizes)
    zeros = jnp.zeros((REACH, LANES), jnp.float32)

    def clear(index, carry):
        start = (first * tiles + index) * pitch
        ref[pl.ds(pl.multiple_of(start, 8), REACH), :] = zeros
        ref[pl.ds(pl.multiple_of(start + REACH + side, 8), REACH), :] = zeros
        return carry

    lax.fori_loop(0, count * tiles, clear, 0, unroll=8)


def turned(tiles):
    row = lax.broadcasted_iota(jnp.int32, (8, LANES), 0)
    tiles = list(tiles)
    for distance in (4, 2, 1):
        low = (row & distance) == 0
        for index in range(8):
            if index & distance == 0:
                first, second = tiles[index], tiles[index + distance]
                tiles[index] = jnp.where(low, first, pltpu.roll(second, distance, axis=0))
                tiles[index + distance] = jnp.where(low, pltpu.roll(first, 8 - distance, axis=0), second)
    return tiles


def spread(sizes, boxes_ref, fields, pair):
    side, _, own_count, slab_count, _ = sizes
    planes = side // slab_count
    tiles, _, pitch = box_shape(sizes)
    for group in range(side // 8):
        halves = {}
        for slab in range(8 * group // planes, (8 * group + 7) // planes + 1):
            for chunk in range(own_count * planes // 2):
                block = boxes_ref[pair, slab, 16 * chunk : 16 * chunk + 16, :].astype(jnp.float32)
                for half in range(2):
                    own, plane = divmod(2 * chunk + half, planes)
                    halves[own, slab * planes + plane] = block[8 * half : 8 * half + 8, :]
        for own in range(own_count):
            rows = turned([halves[own, 8 * group + index] for index in range(8)])
            for tile in range(tiles):
                start = ((pair * own_count + own) * tiles + tile) * pitch + REACH + 8 * group
                fields[pl.ds(pl.multiple_of(start, 8), 8), :] = rows[tile]


def rolled(sizes, ref, box, row, rows, offset_x, offset_flat):
    tiles, _, pitch = box_shape(sizes)
    whole = (offset_flat >> 7) & (tiles - 1)
    part = offset_flat & (LANES - 1)
    start = box * tiles * pitch + REACH + row - offset_x
    moved = []
    for tile in range(tiles):
        first_row = start + ((tile - whole) & (tiles - 1)) * pitch
        moved.append(pltpu.roll(ref[pl.ds(first_row, rows), :], part, axis=1))
    keep = lax.broadcasted_iota(jnp.int32, (rows, LANES), 1) >= part
    return [jnp.where(keep, moved[t], moved[(t - 1) % tiles]) for t in range(tiles)]


def place_partner(sizes, fields, box, own_offset, offset, active):
    side = sizes[0]
    tiles, lines, _ = box_shape(sizes)
    placed = rolled(sizes, fields, box, 0, side, offset[0], offset[1] * side + offset[2])
    lane = lax.broadcasted_iota(jnp.int32, (1, LANES), 1)
    lows = [jnp.maximum(jnp.maximum(a, b), 0) for a, b in zip(own_offset, offset)]
    highs = [side + jnp.minimum(jnp.minimum(a, b), 0) for a, b in zip(own_offset, offset)]
    point_ok = (lane % side >= lows[2]) & (lane % side < highs[2]) & active
    result = []
    for tile in range(tiles):
        line = lane // side + tile * lines
        ok = jnp.where(point_ok & (line >= lows[1]) & (line < highs[1]), 1.0, 0.0)
        result.append(placed[tile] * ok)
    return result


def make_matrices(basis_ref, line_ref, first_line, high_ref, low_ref):
    side = basis_ref.shape[0]
    count = side // 2
    for parity in range(2):
        for index in range(count):
            line = first_line + parity * count + index
            rows = slice(index * side, (index + 1) * side)
            value = basis_ref[...] * line_ref[line : line + 1, :]
            high_ref[parity, rows, :], low_ref[parity, rows, :] = split_pair(value)


def make_mix(basis_ref, mix_ref):
    side = basis_ref.shape[0]
    width = mix_ref.shape[0]
    block = lax.broadcasted_iota(jnp.int32, (side, width), 1) // side
    for index in range(width // side):
        rows = slice(index * side, (index + 1) * side)
        high, low = split_pair(jnp.where(block == index, basis_ref[:, :width], 0.0))
        for part, piece in enumerate((high, high, low)):
            mix_ref[rows, part * width : (part + 1) * width] = piece


def own_kernel(sizes, match_hbm, centers_hbm, own_hbm, *refs):
    constant_hbm, refs = refs[:3], refs[3:]
    mine_ref, table_ref, mix_ref, gain_ref, there_high, there_low, back_high, back_low = refs[:8]
    match_ref, centers_ref, boxes_ref, basis_ref, line_ref, fields, sems = refs[8:]
    side, rounds, own_count, _, _ = sizes
    tiles, _, _ = box_shape(sizes)
    first_member = lax.axis_index("pair") * own_count
    sources = (*constant_hbm, match_hbm, centers_hbm, own_hbm)
    targets = (basis_ref, line_ref, gain_ref, match_ref, centers_ref, boxes_ref.at[0])
    copies = [pltpu.make_async_copy(s, t, sems.at[i]) for i, (s, t) in enumerate(zip(sources, targets))]
    for copy in copies:
        copy.start()
    clear_edges(sizes, fields, 0, own_count)
    for copy in copies[:2]:
        copy.wait()
    make_mix(basis_ref, mix_ref)
    make_matrices(basis_ref, line_ref, 0, there_high, there_low)
    make_matrices(basis_ref, line_ref, side, back_high, back_low)
    for copy in copies[2:]:
        copy.wait()
    spread(sizes, boxes_ref, fields, 0)

    def place(index, carry):
        member, mate, a, b, active = pair_geometry(sizes, match_ref, centers_ref, index)
        for place, entry in enumerate((mate, *a, *b, jnp.where(active, 1, 0))):
            table_ref[index * ENTRIES + place] = entry
        rows = pl.ds(pl.multiple_of(index * side, side), side)
        placed = rolled(sizes, fields, member - first_member, 0, side, a[0], a[1] * side + a[2])
        for tile in range(tiles):
            mine_ref[rows, tile * LANES : (tile + 1) * LANES] = placed[tile].astype(jnp.bfloat16)
        return carry

    lax.fori_loop(0, own_count * rounds, place, 0)


def force_kernel(sizes, mine_hbm, table_hbm, *refs):
    side, rounds, own_count, slab_count, pair_count = sizes
    piece_hbm, refs = refs[:pair_count], refs[pair_count:]
    constant_hbm, refs = refs[:6], refs[6:]
    out_refs, refs = refs[:slab_count], refs[slab_count:]
    table_ref, mine, partner, boxes_ref, *refs = refs
    constants, refs = refs[:6], refs[6:]
    mix_ref, gain_ref, there_high, there_low, back_high, back_low = constants
    fields, first, second, *terms, all_codes, sems = refs
    planes = side // slab_count
    tiles, lines, pitch = box_shape(sizes)
    solves = own_count * rounds
    group = min(solves, 8)
    group_rows = group * side
    cells = tiles * LANES
    width = cells // 2
    slab_index = lax.axis_index("slab")
    pair_index = lax.axis_index("pair")
    core = pair_index % CORES
    chip = pair_index // CORES
    chips = pair_count // CORES

    places = [
        (chip + chips - step) % chips * CORES + (core + core_step) % CORES
        for core_step in range(CORES)
        for step in range(chips)
    ]
    sources = [table_hbm, *piece_hbm, mine_hbm, *constant_hbm]
    targets = [table_ref, *[boxes_ref.at[pair] for pair in places], mine, *constants]
    copies = [pltpu.make_async_copy(s, t, sems.at[i]) for i, (s, t) in enumerate(zip(sources, targets))]
    for copy in copies:
        copy.start()
    for pair in places:
        clear_edges(sizes, fields, pair * own_count, own_count)
    for ref in terms:
        clear_edges(sizes, ref, 0, group)
    table_copy, *piece_copies, mine_copy, mix_copy, gain_copy = copies[: pair_count + 4]
    there_copies, back_copies = copies[pair_count + 4 : pair_count + 6], copies[pair_count + 6 :]
    for copy in (table_copy, *piece_copies):
        copy.wait()
    for pair in places:
        spread(sizes, boxes_ref, fields, pair)
    mine_copy.wait()

    row_count = solves * side
    half_tiles = tiles // 2
    half_cells = cells // 2

    def mirrored(tile):
        line = lax.broadcasted_iota(jnp.int32, tile.shape, 1) // side
        result = None
        for index in range(lines):
            amount = (2 * index - lines + 1) * side % LANES
            if index < 2:
                moved = pltpu.roll(tile, amount, axis=1)
                result = moved if result is None else jnp.where(line % 2 == index, moved, result)
        return result

    def store_split(ref, start, count, columns, value):
        high, low = split_pair(value)
        ref[start : start + count, columns] = high
        ref[row_count + start : row_count + start + count, columns] = low

    def densities(index):
        start = index * side
        rows = slice(start, start + side)
        mate, *offsets, active = [table_ref[index * ENTRIES + place] for place in range(ENTRIES)]
        placed = place_partner(sizes, fields, mate, offsets[:3], offsets[3:], active == 1)
        density = []
        for tile in range(tiles):
            columns = slice(tile * LANES, (tile + 1) * LANES)
            partner[rows, columns] = placed[tile].astype(jnp.bfloat16)
            density.append(mine[rows, columns].astype(jnp.float32) * placed[tile])
        for tile in range(half_tiles):
            far = mirrored(density[tiles - 1 - tile])
            for parity, value in enumerate((density[tile] + far, density[tile] - far)):
                column = parity * half_cells + tile * LANES
                store_split(first, start, side, slice(column, column + LANES), value)

    def along_x(start, columns, source):
        high = source[start : start + group_rows, columns]
        low = source[row_count + start : row_count + start + group_rows, columns]
        return dot(mix_ref[...], jnp.concatenate([high, low, high], axis=0))

    def in_plane(parity, columns, source, high_ref, low_ref):
        inner = slice(parity * half_cells, (parity + 1) * half_cells)
        high = source[:row_count, inner]
        low = source[row_count:, inner]
        basis = high_ref[parity, :, columns]
        rest = low_ref[parity, :, columns]
        left = jnp.concatenate([high, low, high], axis=1)
        return dot(left, jnp.concatenate([basis, basis, rest], axis=0))

    mix_copy.wait()
    for start in range(0, row_count, group_rows):
        for index in range(start // side, (start + group_rows) // side):
            densities(index)
        columns = slice(0, cells)
        store_split(second, start, group_rows, columns, along_x(start, columns, first))

    for copy in (gain_copy, *there_copies):
        copy.wait()
    for parity in range(2):
        for column in range(0, half_cells, width):
            columns = slice(column, column + width)
            value = in_plane(parity, columns, second, there_high, there_low)
            columns = slice(parity * half_cells + column, parity * half_cells + column + width)
            gain = gain_ref[:, columns]
            value = (value.reshape(solves, side, width) * gain[None]).reshape(row_count, width)
            store_split(first, 0, row_count, columns, value)

    for copy in back_copies:
        copy.wait()
    for parity in range(2):
        for column in range(0, half_cells, width):
            value = in_plane(parity, slice(column, column + width), first, back_high, back_low)
            columns = slice(parity * half_cells + column, parity * half_cells + column + width)
            store_split(second, 0, row_count, columns, value)

    for start in range(0, row_count, group_rows):
        for column in range(0, half_cells, width):
            even = along_x(start, slice(column, column + width), second)
            odd = along_x(start, slice(half_cells + column, half_cells + column + width), second)
            for part in range(width // LANES):
                tile = column // LANES + part
                lanes = slice(part * LANES, (part + 1) * LANES)
                near = even[:, lanes] + odd[:, lanes]
                far = mirrored(even[:, lanes] - odd[:, lanes])
                for place, value in ((tile, near), (tiles - 1 - tile, far)):
                    columns = slice(place * LANES, (place + 1) * LANES)
                    value = value * partner[start : start + group_rows, columns].astype(jnp.float32)
                    for solve in range(group):
                        row = (solve * tiles + place) * pitch + REACH
                        terms[start // group_rows][row : row + side, :] = value[solve * side : (solve + 1) * side, :]

    step_rows = 16

    def collect(own, row):
        sums = None
        for turn in range(rounds):
            index = own * rounds + turn
            a = [table_ref[index * ENTRIES + 1 + axis] for axis in range(3)]
            ref = terms[index // group]
            term = rolled(sizes, ref, index % group, row, step_rows, -a[0], -(a[1] * side + a[2]))
            sums = term if sums is None else [s + t for s, t in zip(sums, term)]
        return sums

    lane_index = lax.broadcasted_iota(jnp.int32, (tiles, LANES), 1)
    exponents = [jnp.zeros((tiles, LANES), jnp.float32)] * slab_count
    factors = [jnp.zeros((tiles, LANES), jnp.float32)] * slab_count
    codes = {}
    for own in range(own_count):
        for row in range(0, side, step_rows):
            sums = collect(own, row)
            for half in range(0, step_rows, 8):
                for index, value in enumerate(turned([tile[half : half + 8, :] for tile in sums])):
                    slab, plane = divmod(row + half + index, planes)
                    chunk = own * planes + plane
                    codes[slab, chunk], exponent, factor = encode(value)
                    exponents[slab] = jnp.where(lane_index == chunk, exponent, exponents[slab])
                    factors[slab] = jnp.where(lane_index == chunk, factor, factors[slab])
                    if chunk % 2:
                        pair = jnp.concatenate([codes[slab, chunk - 1], codes[slab, chunk]], axis=0)
                        all_codes[slab, tiles * (chunk - 1) : tiles * (chunk + 1), :] = whole_codes(pair)
    for slab in range(slab_count):
        header = jnp.concatenate([exponents[slab], factors[slab]], axis=0)
        all_codes[slab, tiles * own_count * planes :, :] = whole_codes(header)
    for step in range(slab_count):
        out_refs[step][...] = all_codes[partner_of(slab_index, step, slab_count)[0]]


def whole_codes(value):
    return value.astype(jnp.int32).astype(jnp.int16)


def encode(value):
    largest = jnp.max(jnp.abs(value), axis=1, keepdims=True)
    exponent = jnp.maximum(jnp.floor(jnp.log2(jnp.maximum(largest, TINY))), LOWEST_EXPONENT)
    lifted = 1.0 / jnp.exp2(exponent)
    factor = jnp.maximum(jnp.ceil(largest * lifted * FACTOR_UNIT), 1.0)
    code = jnp.floor(value * lifted * (CODE_LIMIT * FACTOR_UNIT / factor) + 0.5)
    return jnp.clip(code, -CODE_LIMIT, CODE_LIMIT), exponent, factor


def swap_cores(block, pair_count):
    return lax.ppermute(block, "pair", [(i, i ^ 1) for i in range(pair_count)])


def gather_chips(boxes, pair_count):
    pieces = []
    for step in range(1, pair_count // CORES):
        perm = [(i, (i + step * CORES) % pair_count) for i in range(pair_count)]
        pieces.append(lax.ppermute(boxes, "pair", perm))
    return pieces


def unpack_kernel(sizes, *refs):
    own_count, slab_count, tiles = sizes
    block_refs, out_ref, blocks, sems = refs[:slab_count], *refs[slab_count:]
    slab_index = lax.axis_index("slab")
    copies = []
    for index in range(slab_count):
        slab = partner_of(slab_index, slab_count - 1 - index, slab_count)[1]
        copies.append(pltpu.make_async_copy(block_refs[index], blocks.at[slab], sems.at[index]))
        copies[-1].start()
    for copy in copies:
        copy.wait()
    row_count = own_count * tiles
    values = {}
    for slab in range(slab_count):
        header = blocks[slab, row_count:, :].astype(jnp.int32).astype(jnp.float32)
        units = jnp.exp2(header[:8, :])
        factors = header[8:, :] * (1.0 / (CODE_LIMIT * FACTOR_UNIT))
        for pair in range(row_count // 16):
            codes = blocks[slab, 16 * pair : 16 * pair + 16, :].astype(jnp.int32).astype(jnp.float32)
            for half in range(2):
                chunk = 2 * pair + half
                own, plane = divmod(8 * chunk, tiles)
                value = codes[8 * half : 8 * half + 8, :] * factors[:, chunk : chunk + 1]
                values[slab * own_count + own, plane // 8] = value * units[:, chunk : chunk + 1]
        if (slab + 1) * own_count % 8 == 0:
            band = (slab + 1) * own_count // 8 - 1
            for plane in range(tiles // 8):
                rows = turned([values[8 * band + index, plane] for index in range(8)])
                for tile in range(8):
                    start = (band * tiles + 8 * plane + tile) * 8
                    out_ref[start : start + 8, :] = rows[tile]


def unpack(blocks, own_count, cells):
    slab_count = len(blocks)
    row_count = own_count * slab_count
    tiles = cells // LANES
    out = pl.pallas_call(
        functools.partial(unpack_kernel, (own_count, slab_count, tiles)),
        out_shape=jax.ShapeDtypeStruct((row_count * tiles, LANES), jnp.float32),
        in_specs=[pl.BlockSpec(memory_space=pl.ANY)] * slab_count,
        out_specs=pl.BlockSpec(memory_space=pltpu.VMEM),
        scratch_shapes=[
            pltpu.VMEM((slab_count,) + blocks[0].shape, jnp.int16),
            pltpu.SemaphoreType.DMA((slab_count,)),
        ],
        compiler_params=pltpu.CompilerParams(vmem_limit_bytes=8 * 1024 * 1024),
    )(*blocks)
    return out.reshape(row_count // 8, tiles, 8, LANES).transpose(0, 2, 1, 3).reshape(row_count, cells)


def kernel_constants(side):
    basis = sine_basis(side)
    halves = [basis[parity::2, : side // 2].T for parity in range(2)]
    lines = np.concatenate(halves + [half.T for half in halves])
    lines = np.repeat(lines, side, axis=1).astype(np.float32)
    tile = np.tile(basis, (1, side // 2)).astype(np.float32)
    gain = chebyshev_gain(side).reshape(side, side, side)
    gain = np.concatenate([gain[:, parity::2].reshape(side, -1) for parity in range(2)], axis=1)
    return [jnp.asarray(constant) for constant in (tile, lines, gain)]


def place_own(sizes, match, centers, boxes):
    side, rounds, own_count, slab_count, _ = sizes
    tiles, _, pitch = box_shape(sizes)
    solves = own_count * rounds
    constants = kernel_constants(side)
    group_rows = min(solves, 8) * side
    half_cells = side * side // 2
    matrix = jax.ShapeDtypeStruct((2, half_cells, half_cells), jnp.bfloat16)
    inputs = [match, centers, boxes, *constants]
    either = pl.BlockSpec(memory_space=pl.ANY)
    vectors = pl.BlockSpec(memory_space=pltpu.VMEM)
    return pl.pallas_call(
        functools.partial(own_kernel, sizes),
        out_shape=[
            jax.ShapeDtypeStruct((solves * side, side * side), jnp.bfloat16),
            jax.ShapeDtypeStruct((solves * ENTRIES,), jnp.int32),
            jax.ShapeDtypeStruct((group_rows, 3 * group_rows), jnp.bfloat16),
            jax.ShapeDtypeStruct(constants[2].shape, jnp.float32),
            *[matrix] * 4,
        ],
        in_specs=[either] * len(inputs),
        out_specs=[vectors, pl.BlockSpec(memory_space=pltpu.SMEM)] + [vectors] * 6,
        scratch_shapes=[
            pltpu.SMEM(match.shape, jnp.int32),
            pltpu.SMEM(centers.shape, jnp.int32),
            pltpu.VMEM((1,) + boxes.shape, jnp.bfloat16),
            pltpu.VMEM(constants[0].shape, jnp.float32),
            pltpu.VMEM(constants[1].shape, jnp.float32),
            pltpu.VMEM((own_count * tiles * pitch, LANES), jnp.float32),
            pltpu.SemaphoreType.DMA((len(inputs),)),
        ],
        compiler_params=pltpu.CompilerParams(vmem_limit_bytes=32 * 1024 * 1024),
        cost_estimate=pl.CostEstimate(flops=5 * 10**9, bytes_accessed=4 * 1024 * 1024, transcendentals=0),
    )(*inputs)


def team_forces(sizes, mine, table, constants, pieces):
    side, rounds, own_count, slab_count, pair_count = sizes
    tiles, _, pitch = box_shape(sizes)
    _, rows, _ = pieces[0].shape
    solves = own_count * rounds
    group = min(solves, 8)
    cells = side * side
    either = pl.BlockSpec(memory_space=pl.ANY)
    vectors = pl.BlockSpec(memory_space=pltpu.VMEM)
    wide = pltpu.VMEM((2 * solves * side, cells), jnp.bfloat16)
    flops = 2 * solves * side * 3 * 2 * (cells * cells // 2 + cells * group * side)
    inputs = [mine, table, *pieces, *constants]
    return pl.pallas_call(
        functools.partial(force_kernel, sizes),
        out_shape=[jax.ShapeDtypeStruct((rows + HEADER_ROWS, LANES), jnp.int16)] * slab_count,
        in_specs=[either] * len(inputs),
        out_specs=[vectors] * slab_count,
        scratch_shapes=[
            pltpu.SMEM(table.shape, jnp.int32),
            pltpu.VMEM(mine.shape, jnp.bfloat16),
            pltpu.VMEM(mine.shape, jnp.bfloat16),
            pltpu.VMEM((pair_count, slab_count, rows, LANES), jnp.bfloat16),
            *[pltpu.VMEM(constant.shape, constant.dtype) for constant in constants],
            pltpu.VMEM((own_count * pair_count * tiles * pitch, LANES), jnp.float32),
            wide,
            wide,
            *[pltpu.VMEM((group * tiles * pitch, LANES), jnp.float32)] * (solves // group),
            pltpu.VMEM((slab_count, rows + HEADER_ROWS, LANES), jnp.int16),
            pltpu.SemaphoreType.DMA((len(inputs),)),
        ],
        compiler_params=pltpu.CompilerParams(vmem_limit_bytes=32 * 1024 * 1024),
        cost_estimate=pl.CostEstimate(flops=flops, bytes_accessed=8 * 1024 * 1024, transcendentals=0),
    )(*inputs)


def shards(orbitals, centers, matchings):
    slab_count = lax.axis_size("slab")
    pair_count = lax.axis_size("pair")
    local_rows, plane_cells = orbitals.shape
    own_count = local_rows // slab_count
    side = round((plane_cells * slab_count) ** (1.0 / 3.0))
    blocks = orbitals.reshape(slab_count, own_count * plane_cells // LANES, LANES)
    boxes = lax.all_to_all(blocks, "slab", split_axis=0, concat_axis=0, tiled=True)
    sizes = (side, matchings.shape[1], own_count, slab_count, pair_count)
    pieces = gather_chips(boxes, pair_count)
    mine, table, *constants = place_own(sizes, matchings, centers.T, boxes)
    boxes, mine = lax.optimization_barrier((boxes, mine))
    swapped = [swap_cores(boxes, pair_count)]
    pieces, mine = lax.optimization_barrier((pieces, mine))
    swapped += [swap_cores(piece, pair_count) for piece in pieces]
    codes = team_forces(sizes, mine, table, constants, [boxes] + pieces + swapped)
    received = []
    for step in reversed(range(1, slab_count)):
        perm = [(i, partner_of(i, step, slab_count)[0]) for i in range(slab_count)]
        received.append(lax.ppermute(codes[step], "slab", perm))
    return unpack(received + [codes[0]], own_count, plane_cells)


def solution(mesh):
    in_specs = (P("pair", "slab"), P(), P("slab", None, None))
    out_specs = P("pair", "slab")
    return jax.shard_map(shards, mesh=mesh, in_specs=in_specs, out_specs=out_specs, check_vma=False)
```

```python
import functools

import jax
import jax.numpy as jnp
import numpy as np
from jax import lax
from jax.experimental import pallas as pl
from jax.experimental.pallas import tpu as pltpu
from jax.sharding import PartitionSpec as P

STEPS = 16
CUT2 = 192
REACH = 8
SCREEN = 0.1
LOWER_BOUND = 0.1
UPPER_BOUND = 12.1
LANES = 128
CORES = 2
CODE_LIMIT = 32767.0
FACTOR_UNIT = 8192.0
LOWEST_EXPONENT = -120.0
TINY = 1e-37
HEADER_ROWS = 16
ENTRIES = 8


def sine_basis(side):
    index = np.arange(1, side + 1, dtype=np.float64)
    return np.sqrt(2.0 / (side + 1)) * np.sin(np.pi * np.outer(index, index) / (side + 1))


def chebyshev_gain(side):
    shifts = -2.0 * np.cos(np.pi * np.arange(1, side + 1, dtype=np.float64) / (side + 1))
    eigenvalue = 6.0 + SCREEN + shifts[:, None, None] + shifts[None, :, None] + shifts[None, None, :]
    middle = (UPPER_BOUND + LOWER_BOUND) / 2.0
    spread = (UPPER_BOUND - LOWER_BOUND) / 2.0
    ratio = middle / spread
    total = np.zeros_like(eigenvalue)
    residual = np.ones_like(eigenvalue)
    direction = residual / middle
    factor = 1.0 / ratio
    for _ in range(STEPS):
        total = total + direction
        residual = residual - eigenvalue * direction
        factor_next = 1.0 / (2.0 * ratio - factor)
        direction = factor_next * factor * direction + 2.0 * factor_next / spread * residual
        factor = factor_next
    return total.reshape(side, side * side).astype(np.float32)


def split_pair(value):
    high = value.astype(jnp.bfloat16)
    low = (value - high.astype(jnp.float32)).astype(jnp.bfloat16)
    return high, low


def dot(left, right):
    return jnp.dot(left, right, preferred_element_type=jnp.float32)


def partner_of(index, step, count):
    if count & (count - 1) == 0:
        return index ^ step, index ^ step
    return (index + step) % count, (index + count - step) % count


def pair_geometry(sizes, match_ref, centers_ref, index):
    _, rounds, own_count, slab_count, _ = sizes
    slab_index = lax.axis_index("slab")
    pair_index = lax.axis_index("pair")

    def orbital_of(member):
        return (member // own_count * slab_count + slab_index) * own_count + member % own_count

    member = pair_index * own_count + index // rounds
    mate = match_ref[0, index % rounds, member]
    own_offset = []
    mate_offset = []
    distance = 0
    for axis in range(3):
        mine = centers_ref[axis, orbital_of(member)]
        other = centers_ref[axis, orbital_of(mate)]
        anchor = (mine + other) >> 1
        own_offset.append(mine - anchor)
        mate_offset.append(other - anchor)
        distance = distance + (mine - other) * (mine - other)
    return member, mate, own_offset, mate_offset, distance <= CUT2


def box_shape(sizes):
    side = sizes[0]
    return side * side // LANES, LANES // side, side + 2 * REACH


def clear_edges(sizes, ref, first, count):
    side = sizes[0]
    tiles, _, pitch = box_shape(sizes)
    zeros = jnp.zeros((REACH, LANES), jnp.float32)

    def clear(index, carry):
        start = (first * tiles + index) * pitch
        ref[pl.ds(pl.multiple_of(start, 8), REACH), :] = zeros
        ref[pl.ds(pl.multiple_of(start + REACH + side, 8), REACH), :] = zeros
        return carry

    lax.fori_loop(0, count * tiles, clear, 0, unroll=8)


def turned(tiles):
    row = lax.broadcasted_iota(jnp.int32, (8, LANES), 0)
    tiles = list(tiles)
    for distance in (4, 2, 1):
        low = (row & distance) == 0
        for index in range(8):
            if index & distance == 0:
                first, second = tiles[index], tiles[index + distance]
                tiles[index] = jnp.where(low, first, pltpu.roll(second, distance, axis=0))
                tiles[index + distance] = jnp.where(low, pltpu.roll(first, 8 - distance, axis=0), second)
    return tiles


def spread(sizes, boxes_ref, fields, pair):
    side, _, own_count, slab_count, _ = sizes
    planes = side // slab_count
    tiles, _, pitch = box_shape(sizes)
    for group in range(side // 8):
        halves = {}
        for slab in range(8 * group // planes, (8 * group + 7) // planes + 1):
            for chunk in range(own_count * planes // 2):
                block = boxes_ref[pair, slab, 16 * chunk : 16 * chunk + 16, :].astype(jnp.float32)
                for half in range(2):
                    own, plane = divmod(2 * chunk + half, planes)
                    halves[own, slab * planes + plane] = block[8 * half : 8 * half + 8, :]
        for own in range(own_count):
            rows = turned([halves[own, 8 * group + index] for index in range(8)])
            for tile in range(tiles):
                start = ((pair * own_count + own) * tiles + tile) * pitch + REACH + 8 * group
                fields[pl.ds(pl.multiple_of(start, 8), 8), :] = rows[tile]


def rolled(sizes, ref, box, row, rows, offset_x, offset_flat):
    tiles, _, pitch = box_shape(sizes)
    whole = (offset_flat >> 7) & (tiles - 1)
    part = offset_flat & (LANES - 1)
    start = box * tiles * pitch + REACH + row - offset_x
    moved = []
    for tile in range(tiles):
        first_row = start + ((tile - whole) & (tiles - 1)) * pitch
        moved.append(pltpu.roll(ref[pl.ds(first_row, rows), :], part, axis=1))
    keep = lax.broadcasted_iota(jnp.int32, (rows, LANES), 1) >= part
    return [jnp.where(keep, moved[t], moved[(t - 1) % tiles]) for t in range(tiles)]


def place_partner(sizes, fields, box, own_offset, offset, active):
    side = sizes[0]
    tiles, lines, _ = box_shape(sizes)
    placed = rolled(sizes, fields, box, 0, side, offset[0], offset[1] * side + offset[2])
    lane = lax.broadcasted_iota(jnp.int32, (1, LANES), 1)
    lows = [jnp.maximum(jnp.maximum(a, b), 0) for a, b in zip(own_offset, offset)]
    highs = [side + jnp.minimum(jnp.minimum(a, b), 0) for a, b in zip(own_offset, offset)]
    point_ok = (lane % side >= lows[2]) & (lane % side < highs[2]) & active
    result = []
    for tile in range(tiles):
        line = lane // side + tile * lines
        ok = jnp.where(point_ok & (line >= lows[1]) & (line < highs[1]), 1.0, 0.0)
        result.append(placed[tile] * ok)
    return result


def own_kernel(sizes, match_hbm, centers_hbm, own_hbm, *refs):
    constant_hbm, refs = refs[:3], refs[3:]
    mine_ref, table_ref, *constant_refs = refs[:5]
    match_ref, centers_ref, boxes_ref, fields, sems = refs[5:]
    side, rounds, own_count, _, _ = sizes
    tiles, _, _ = box_shape(sizes)
    first_member = lax.axis_index("pair") * own_count
    sources = (match_hbm, centers_hbm, own_hbm, *constant_hbm)
    targets = (match_ref, centers_ref, boxes_ref.at[0], *constant_refs)
    copies = [pltpu.make_async_copy(s, t, sems.at[i]) for i, (s, t) in enumerate(zip(sources, targets))]
    for copy in copies:
        copy.start()
    clear_edges(sizes, fields, 0, own_count)
    for copy in copies:
        copy.wait()
    spread(sizes, boxes_ref, fields, 0)

    def place(index, carry):
        member, mate, a, b, active = pair_geometry(sizes, match_ref, centers_ref, index)
        for place, entry in enumerate((mate, *a, *b, jnp.where(active, 1, 0))):
            table_ref[index * ENTRIES + place] = entry
        rows = pl.ds(pl.multiple_of(index * side, side), side)
        placed = rolled(sizes, fields, member - first_member, 0, side, a[0], a[1] * side + a[2])
        for tile in range(tiles):
            mine_ref[rows, tile * LANES : (tile + 1) * LANES] = placed[tile].astype(jnp.bfloat16)
        return carry

    lax.fori_loop(0, own_count * rounds, place, 0)


def force_kernel(sizes, mine_hbm, table_hbm, *refs):
    side, rounds, own_count, slab_count, pair_count = sizes
    piece_hbm, refs = refs[:pair_count], refs[pair_count:]
    constant_hbm, refs = refs[:3], refs[3:]
    out_refs, refs = refs[:slab_count], refs[slab_count:]
    table_ref, mine, partner, boxes_ref, *refs = refs
    constants, refs = refs[:3], refs[3:]
    basis_ref, line_ref, gain_ref = constants
    mix_ref, there_high, there_low, back_high, back_low, *refs = refs
    fields, first, second, *terms, all_codes, sems = refs
    planes = side // slab_count
    tiles, lines, pitch = box_shape(sizes)
    solves = own_count * rounds
    group = min(solves, 8)
    group_rows = group * side
    cells = tiles * LANES
    width = cells // 2
    slab_index = lax.axis_index("slab")
    pair_index = lax.axis_index("pair")
    core = pair_index % CORES
    chip = pair_index // CORES
    chips = pair_count // CORES

    places = [
        (chip + chips - step) % chips * CORES + (core + core_step) % CORES
        for core_step in range(CORES)
        for step in range(chips)
    ]
    sources = [table_hbm, *constant_hbm, *piece_hbm, mine_hbm]
    targets = [table_ref, *constants, *[boxes_ref.at[pair] for pair in places], mine]
    copies = [pltpu.make_async_copy(s, t, sems.at[i]) for i, (s, t) in enumerate(zip(sources, targets))]
    for copy in copies:
        copy.start()
    for pair in places:
        clear_edges(sizes, fields, pair * own_count, own_count)
    for ref in terms:
        clear_edges(sizes, ref, 0, group)
    for copy in copies[:4]:
        copy.wait()

    def make_matrices(first_line, high_ref, low_ref):
        count = side // 2
        for parity in range(2):
            for index in range(count):
                line = first_line + parity * count + index
                rows = slice(index * side, (index + 1) * side)
                value = basis_ref[...] * line_ref[line : line + 1, :]
                high_ref[parity, rows, :], low_ref[parity, rows, :] = split_pair(value)

    block = lax.broadcasted_iota(jnp.int32, (side, group_rows), 1) // side
    for index in range(group):
        rows = slice(index * side, (index + 1) * side)
        value = jnp.where(block == index, basis_ref[:, :group_rows], 0.0)
        high, low = split_pair(value)
        for part, piece in enumerate((high, high, low)):
            mix_ref[rows, part * group_rows : (part + 1) * group_rows] = piece
    make_matrices(0, there_high, there_low)

    for copy in copies[4:-1]:
        copy.wait()
    for pair in places:
        spread(sizes, boxes_ref, fields, pair)
    copies[-1].wait()

    row_count = solves * side
    half_tiles = tiles // 2
    half_cells = cells // 2

    def mirrored(tile):
        line = lax.broadcasted_iota(jnp.int32, tile.shape, 1) // side
        result = None
        for index in range(lines):
            amount = (2 * index - lines + 1) * side % LANES
            if index < 2:
                moved = pltpu.roll(tile, amount, axis=1)
                result = moved if result is None else jnp.where(line % 2 == index, moved, result)
        return result

    def store_split(ref, start, count, columns, value):
        high, low = split_pair(value)
        ref[start : start + count, columns] = high
        ref[row_count + start : row_count + start + count, columns] = low

    def densities(index):
        start = index * side
        rows = slice(start, start + side)
        mate, *offsets, active = [table_ref[index * ENTRIES + place] for place in range(ENTRIES)]
        placed = place_partner(sizes, fields, mate, offsets[:3], offsets[3:], active == 1)
        density = []
        for tile in range(tiles):
            columns = slice(tile * LANES, (tile + 1) * LANES)
            partner[rows, columns] = placed[tile].astype(jnp.bfloat16)
            density.append(mine[rows, columns].astype(jnp.float32) * placed[tile])
        for tile in range(half_tiles):
            far = mirrored(density[tiles - 1 - tile])
            for parity, value in enumerate((density[tile] + far, density[tile] - far)):
                column = parity * half_cells + tile * LANES
                store_split(first, start, side, slice(column, column + LANES), value)

    def along_x(start, columns, source):
        high = source[start : start + group_rows, columns]
        low = source[row_count + start : row_count + start + group_rows, columns]
        return dot(mix_ref[...], jnp.concatenate([high, low, high], axis=0))

    def in_plane(parity, columns, source, high_ref, low_ref):
        inner = slice(parity * half_cells, (parity + 1) * half_cells)
        high = source[:row_count, inner]
        low = source[row_count:, inner]
        basis = high_ref[parity, :, columns]
        rest = low_ref[parity, :, columns]
        left = jnp.concatenate([high, low, high], axis=1)
        return dot(left, jnp.concatenate([basis, basis, rest], axis=0))

    for start in range(0, row_count, group_rows):
        for index in range(start // side, (start + group_rows) // side):
            densities(index)
        columns = slice(0, cells)
        store_split(second, start, group_rows, columns, along_x(start, columns, first))

    make_matrices(side, back_high, back_low)
    for parity in range(2):
        for column in range(0, half_cells, width):
            columns = slice(column, column + width)
            value = in_plane(parity, columns, second, there_high, there_low)
            columns = slice(parity * half_cells + column, parity * half_cells + column + width)
            gain = gain_ref[:, columns]
            value = (value.reshape(solves, side, width) * gain[None]).reshape(row_count, width)
            store_split(first, 0, row_count, columns, value)

    for parity in range(2):
        for column in range(0, half_cells, width):
            value = in_plane(parity, slice(column, column + width), first, back_high, back_low)
            columns = slice(parity * half_cells + column, parity * half_cells + column + width)
            store_split(second, 0, row_count, columns, value)

    for start in range(0, row_count, group_rows):
        for column in range(0, half_cells, width):
            even = along_x(start, slice(column, column + width), second)
            odd = along_x(start, slice(half_cells + column, half_cells + column + width), second)
            for part in range(width // LANES):
                tile = column // LANES + part
                lanes = slice(part * LANES, (part + 1) * LANES)
                near = even[:, lanes] + odd[:, lanes]
                far = mirrored(even[:, lanes] - odd[:, lanes])
                for place, value in ((tile, near), (tiles - 1 - tile, far)):
                    columns = slice(place * LANES, (place + 1) * LANES)
                    value = value * partner[start : start + group_rows, columns].astype(jnp.float32)
                    for solve in range(group):
                        row = (solve * tiles + place) * pitch + REACH
                        terms[start // group_rows][row : row + side, :] = value[solve * side : (solve + 1) * side, :]

    step_rows = 16

    def collect(own, row):
        sums = None
        for turn in range(rounds):
            index = own * rounds + turn
            a = [table_ref[index * ENTRIES + 1 + axis] for axis in range(3)]
            ref = terms[index // group]
            term = rolled(sizes, ref, index % group, row, step_rows, -a[0], -(a[1] * side + a[2]))
            sums = term if sums is None else [s + t for s, t in zip(sums, term)]
        return sums

    lane_index = lax.broadcasted_iota(jnp.int32, (tiles, LANES), 1)
    exponents = [jnp.zeros((tiles, LANES), jnp.float32)] * slab_count
    factors = [jnp.zeros((tiles, LANES), jnp.float32)] * slab_count
    codes = {}
    for own in range(own_count):
        for row in range(0, side, step_rows):
            sums = collect(own, row)
            for half in range(0, step_rows, 8):
                for index, value in enumerate(turned([tile[half : half + 8, :] for tile in sums])):
                    slab, plane = divmod(row + half + index, planes)
                    chunk = own * planes + plane
                    codes[slab, chunk], exponent, factor = encode(value)
                    exponents[slab] = jnp.where(lane_index == chunk, exponent, exponents[slab])
                    factors[slab] = jnp.where(lane_index == chunk, factor, factors[slab])
                    if chunk % 2:
                        pair = jnp.concatenate([codes[slab, chunk - 1], codes[slab, chunk]], axis=0)
                        all_codes[slab, tiles * (chunk - 1) : tiles * (chunk + 1), :] = whole_codes(pair)
    for slab in range(slab_count):
        header = jnp.concatenate([exponents[slab], factors[slab]], axis=0)
        all_codes[slab, tiles * own_count * planes :, :] = whole_codes(header)
    copies = []
    for step in range(slab_count):
        slab = partner_of(slab_index, step, slab_count)[0]
        copies.append(pltpu.make_async_copy(all_codes.at[slab], out_refs[step], sems.at[step]))
        copies[-1].start()
    for copy in copies:
        copy.wait()


def whole_codes(value):
    return value.astype(jnp.int32).astype(jnp.int16)


def encode(value):
    largest = jnp.max(jnp.abs(value), axis=1, keepdims=True)
    exponent = jnp.maximum(jnp.floor(jnp.log2(jnp.maximum(largest, TINY))), LOWEST_EXPONENT)
    lifted = 1.0 / jnp.exp2(exponent)
    factor = jnp.maximum(jnp.ceil(largest * lifted * FACTOR_UNIT), 1.0)
    code = jnp.floor(value * lifted * (CODE_LIMIT * FACTOR_UNIT / factor) + 0.5)
    return jnp.clip(code, -CODE_LIMIT, CODE_LIMIT), exponent, factor


def swap_cores(block, pair_count):
    return lax.ppermute(block, "pair", [(i, i ^ 1) for i in range(pair_count)])


def gather_chips(boxes, pair_count):
    pieces = []
    for step in range(1, pair_count // CORES):
        perm = [(i, (i + step * CORES) % pair_count) for i in range(pair_count)]
        pieces.append(lax.ppermute(boxes, "pair", perm))
    return pieces


def unpack_kernel(sizes, *refs):
    own_count, slab_count, tiles = sizes
    block_refs, out_hbm, blocks, out_ref, sems, out_sems = refs[:slab_count], *refs[slab_count:]
    slab_index = lax.axis_index("slab")
    copies = []
    for index in range(slab_count):
        slab = partner_of(slab_index, slab_count - 1 - index, slab_count)[1]
        copies.append(pltpu.make_async_copy(block_refs[index], blocks.at[slab], sems.at[index]))
        copies[-1].start()
    for copy in copies:
        copy.wait()
    row_count = own_count * tiles
    values = {}
    copies = []
    for slab in range(slab_count):
        header = blocks[slab, row_count:, :].astype(jnp.int32).astype(jnp.float32)
        units = jnp.exp2(header[:8, :])
        factors = header[8:, :] * (1.0 / (CODE_LIMIT * FACTOR_UNIT))
        for pair in range(row_count // 16):
            codes = blocks[slab, 16 * pair : 16 * pair + 16, :].astype(jnp.int32).astype(jnp.float32)
            for half in range(2):
                chunk = 2 * pair + half
                own, plane = divmod(8 * chunk, tiles)
                value = codes[8 * half : 8 * half + 8, :] * factors[:, chunk : chunk + 1]
                values[slab * own_count + own, plane // 8] = value * units[:, chunk : chunk + 1]
        if (slab + 1) * own_count % 8 == 0:
            band = (slab + 1) * own_count // 8 - 1
            for plane in range(tiles // 8):
                rows = turned([values[8 * band + index, plane] for index in range(8)])
                for tile in range(8):
                    start = (band * tiles + 8 * plane + tile) * 8
                    out_ref[start : start + 8, :] = rows[tile]
            rows = slice(band * tiles * 8, (band + 1) * tiles * 8)
            copies.append(pltpu.make_async_copy(out_ref.at[rows], out_hbm.at[rows], out_sems.at[band]))
            copies[-1].start()
    for copy in copies:
        copy.wait()


def unpack(blocks, own_count, cells):
    slab_count = len(blocks)
    row_count = own_count * slab_count
    tiles = cells // LANES
    out = pl.pallas_call(
        functools.partial(unpack_kernel, (own_count, slab_count, tiles)),
        out_shape=jax.ShapeDtypeStruct((row_count * tiles, LANES), jnp.float32),
        in_specs=[pl.BlockSpec(memory_space=pl.ANY)] * slab_count,
        out_specs=pl.BlockSpec(memory_space=pl.ANY),
        scratch_shapes=[
            pltpu.VMEM((slab_count,) + blocks[0].shape, jnp.int16),
            pltpu.VMEM((row_count * tiles, LANES), jnp.float32),
            pltpu.SemaphoreType.DMA((slab_count,)),
            pltpu.SemaphoreType.DMA((row_count // 8,)),
        ],
        compiler_params=pltpu.CompilerParams(vmem_limit_bytes=8 * 1024 * 1024),
    )(*blocks)
    return out.reshape(row_count // 8, tiles, 8, LANES).transpose(0, 2, 1, 3).reshape(row_count, cells)


def kernel_constants(side):
    basis = sine_basis(side)
    halves = [basis[parity::2, : side // 2].T for parity in range(2)]
    lines = np.concatenate(halves + [half.T for half in halves])
    lines = np.repeat(lines, side, axis=1).astype(np.float32)
    tile = np.tile(basis, (1, side // 2)).astype(np.float32)
    gain = chebyshev_gain(side).reshape(side, side, side)
    gain = np.concatenate([gain[:, parity::2].reshape(side, -1) for parity in range(2)], axis=1)
    return [jnp.asarray(constant) for constant in (tile, lines, gain)]


def place_own(sizes, match, centers, boxes):
    side, rounds, own_count, slab_count, _ = sizes
    tiles, _, pitch = box_shape(sizes)
    solves = own_count * rounds
    constants = kernel_constants(side)
    inputs = [match, centers, boxes, *constants]
    either = pl.BlockSpec(memory_space=pl.ANY)
    vectors = pl.BlockSpec(memory_space=pltpu.VMEM)
    return pl.pallas_call(
        functools.partial(own_kernel, sizes),
        out_shape=[
            jax.ShapeDtypeStruct((solves * side, side * side), jnp.bfloat16),
            jax.ShapeDtypeStruct((solves * ENTRIES,), jnp.int32),
            *[jax.ShapeDtypeStruct(constant.shape, constant.dtype) for constant in constants],
        ],
        in_specs=[either] * len(inputs),
        out_specs=[vectors, pl.BlockSpec(memory_space=pltpu.SMEM)] + [vectors] * len(constants),
        scratch_shapes=[
            pltpu.SMEM(match.shape, jnp.int32),
            pltpu.SMEM(centers.shape, jnp.int32),
            pltpu.VMEM((1,) + boxes.shape, jnp.bfloat16),
            pltpu.VMEM((own_count * tiles * pitch, LANES), jnp.float32),
            pltpu.SemaphoreType.DMA((len(inputs),)),
        ],
        compiler_params=pltpu.CompilerParams(vmem_limit_bytes=32 * 1024 * 1024),
        cost_estimate=pl.CostEstimate(flops=5 * 10**9, bytes_accessed=4 * 1024 * 1024, transcendentals=0),
    )(*inputs)


def team_forces(sizes, mine, table, constants, pieces):
    side, rounds, own_count, slab_count, pair_count = sizes
    tiles, _, pitch = box_shape(sizes)
    _, rows, _ = pieces[0].shape
    solves = own_count * rounds
    group = min(solves, 8)
    cells = side * side
    either = pl.BlockSpec(memory_space=pl.ANY)
    wide = pltpu.VMEM((2 * solves * side, cells), jnp.bfloat16)
    flops = 2 * solves * side * 3 * 2 * (cells * cells // 2 + cells * group * side)
    inputs = [mine, table, *pieces, *constants]
    return pl.pallas_call(
        functools.partial(force_kernel, sizes),
        out_shape=[jax.ShapeDtypeStruct((rows + HEADER_ROWS, LANES), jnp.int16)] * slab_count,
        in_specs=[either] * len(inputs),
        out_specs=[either] * slab_count,
        scratch_shapes=[
            pltpu.SMEM(table.shape, jnp.int32),
            pltpu.VMEM(mine.shape, jnp.bfloat16),
            pltpu.VMEM(mine.shape, jnp.bfloat16),
            pltpu.VMEM((pair_count, slab_count, rows, LANES), jnp.bfloat16),
            *[pltpu.VMEM(constant.shape, constant.dtype) for constant in constants],
            pltpu.VMEM((group * side, 3 * group * side), jnp.bfloat16),
            *[pltpu.VMEM((2, cells // 2, cells // 2), jnp.bfloat16)] * 4,
            pltpu.VMEM((own_count * pair_count * tiles * pitch, LANES), jnp.float32),
            wide,
            wide,
            *[pltpu.VMEM((group * tiles * pitch, LANES), jnp.float32)] * (solves // group),
            pltpu.VMEM((slab_count, rows + HEADER_ROWS, LANES), jnp.int16),
            pltpu.SemaphoreType.DMA((max(len(inputs), slab_count),)),
        ],
        compiler_params=pltpu.CompilerParams(vmem_limit_bytes=32 * 1024 * 1024),
        cost_estimate=pl.CostEstimate(flops=flops, bytes_accessed=8 * 1024 * 1024, transcendentals=0),
    )(*inputs)


def shards(orbitals, centers, matchings):
    slab_count = lax.axis_size("slab")
    pair_count = lax.axis_size("pair")
    local_rows, plane_cells = orbitals.shape
    own_count = local_rows // slab_count
    side = round((plane_cells * slab_count) ** (1.0 / 3.0))
    blocks = orbitals.reshape(slab_count, own_count * plane_cells // LANES, LANES)
    boxes = lax.all_to_all(blocks, "slab", split_axis=0, concat_axis=0, tiled=True)
    sizes = (side, matchings.shape[1], own_count, slab_count, pair_count)
    pieces = gather_chips(boxes, pair_count)
    mine, table, *constants = place_own(sizes, matchings, centers.T, boxes)
    boxes, mine = lax.optimization_barrier((boxes, mine))
    swapped = [swap_cores(boxes, pair_count)]
    pieces, mine = lax.optimization_barrier((pieces, mine))
    swapped += [swap_cores(piece, pair_count) for piece in pieces]
    codes = team_forces(sizes, mine, table, constants, [boxes] + pieces + swapped)
    received = []
    for step in reversed(range(1, slab_count)):
        perm = [(i, partner_of(i, step, slab_count)[0]) for i in range(slab_count)]
        received.append(lax.ppermute(codes[step], "slab", perm))
    return unpack(received + [codes[0]], own_count, plane_cells)


def solution(mesh):
    in_specs = (P("pair", "slab"), P(), P("slab", None, None))
    out_specs = P("pair", "slab")
    return jax.shard_map(shards, mesh=mesh, in_specs=in_specs, out_specs=out_specs, check_vma=False)
```

```python
import functools

import jax
import jax.numpy as jnp
import numpy as np
from jax import lax
from jax.experimental import pallas as pl
from jax.experimental.pallas import tpu as pltpu
from jax.sharding import PartitionSpec as P

STEPS = 16
CUT2 = 192
REACH = 8
SCREEN = 0.1
LOWER_BOUND = 0.1
UPPER_BOUND = 12.1
LANES = 128
CORES = 2
CODE_LIMIT = 32767.0
FACTOR_UNIT = 8192.0
LOWEST_EXPONENT = -120.0
TINY = 1e-37
HEADER_ROWS = 16
ENTRIES = 8


def sine_basis(side):
    index = np.arange(1, side + 1, dtype=np.float64)
    return np.sqrt(2.0 / (side + 1)) * np.sin(np.pi * np.outer(index, index) / (side + 1))


def chebyshev_gain(side):
    shifts = -2.0 * np.cos(np.pi * np.arange(1, side + 1, dtype=np.float64) / (side + 1))
    eigenvalue = 6.0 + SCREEN + shifts[:, None, None] + shifts[None, :, None] + shifts[None, None, :]
    middle = (UPPER_BOUND + LOWER_BOUND) / 2.0
    spread = (UPPER_BOUND - LOWER_BOUND) / 2.0
    ratio = middle / spread
    total = np.zeros_like(eigenvalue)
    residual = np.ones_like(eigenvalue)
    direction = residual / middle
    factor = 1.0 / ratio
    for _ in range(STEPS):
        total = total + direction
        residual = residual - eigenvalue * direction
        factor_next = 1.0 / (2.0 * ratio - factor)
        direction = factor_next * factor * direction + 2.0 * factor_next / spread * residual
        factor = factor_next
    return total.reshape(side, side * side).astype(np.float32)


def split_pair(value):
    high = value.astype(jnp.bfloat16)
    low = (value - high.astype(jnp.float32)).astype(jnp.bfloat16)
    return high, low


def dot(left, right):
    return jnp.dot(left, right, preferred_element_type=jnp.float32)


def partner_of(index, step, count):
    if count & (count - 1) == 0:
        return index ^ step, index ^ step
    return (index + step) % count, (index + count - step) % count


def pair_geometry(sizes, match_ref, centers_ref, index):
    _, rounds, own_count, slab_count, _ = sizes
    slab_index = lax.axis_index("slab")
    pair_index = lax.axis_index("pair")

    def orbital_of(member):
        return (member // own_count * slab_count + slab_index) * own_count + member % own_count

    member = pair_index * own_count + index // rounds
    mate = match_ref[0, index % rounds, member]
    own_offset = []
    mate_offset = []
    distance = 0
    for axis in range(3):
        mine = centers_ref[axis, orbital_of(member)]
        other = centers_ref[axis, orbital_of(mate)]
        anchor = (mine + other) >> 1
        own_offset.append(mine - anchor)
        mate_offset.append(other - anchor)
        distance = distance + (mine - other) * (mine - other)
    return member, mate, own_offset, mate_offset, distance <= CUT2


def box_shape(sizes):
    side = sizes[0]
    return side * side // LANES, LANES // side, side + 2 * REACH


def clear_edges(sizes, ref, first, count):
    side = sizes[0]
    tiles, _, pitch = box_shape(sizes)
    zeros = jnp.zeros((REACH, LANES), jnp.float32)

    def clear(index, carry):
        start = (first * tiles + index) * pitch
        ref[pl.ds(pl.multiple_of(start, 8), REACH), :] = zeros
        ref[pl.ds(pl.multiple_of(start + REACH + side, 8), REACH), :] = zeros
        return carry

    lax.fori_loop(0, count * tiles, clear, 0, unroll=8)


def turned(tiles):
    row = lax.broadcasted_iota(jnp.int32, (8, LANES), 0)
    tiles = list(tiles)
    for distance in (4, 2, 1):
        low = (row & distance) == 0
        for index in range(8):
            if index & distance == 0:
                first, second = tiles[index], tiles[index + distance]
                tiles[index] = jnp.where(low, first, pltpu.roll(second, distance, axis=0))
                tiles[index + distance] = jnp.where(low, pltpu.roll(first, 8 - distance, axis=0), second)
    return tiles


def spread(sizes, boxes_ref, fields, pair):
    side, _, own_count, slab_count, _ = sizes
    planes = side // slab_count
    tiles, _, pitch = box_shape(sizes)
    for group in range(side // 8):
        halves = {}
        for slab in range(8 * group // planes, (8 * group + 7) // planes + 1):
            for chunk in range(own_count * planes // 2):
                block = boxes_ref[slab, 16 * chunk : 16 * chunk + 16, :].astype(jnp.float32)
                for half in range(2):
                    own, plane = divmod(2 * chunk + half, planes)
                    halves[own, slab * planes + plane] = block[8 * half : 8 * half + 8, :]
        for own in range(own_count):
            rows = turned([halves[own, 8 * group + index] for index in range(8)])
            for tile in range(tiles):
                start = ((pair * own_count + own) * tiles + tile) * pitch + REACH + 8 * group
                fields[pl.ds(pl.multiple_of(start, 8), 8), :] = rows[tile]


def rolled(sizes, ref, box, row, rows, offset_x, offset_flat):
    tiles, _, pitch = box_shape(sizes)
    whole = (offset_flat >> 7) & (tiles - 1)
    part = offset_flat & (LANES - 1)
    start = box * tiles * pitch + REACH + row - offset_x
    moved = []
    for tile in range(tiles):
        first_row = start + ((tile - whole) & (tiles - 1)) * pitch
        moved.append(pltpu.roll(ref[pl.ds(first_row, rows), :], part, axis=1))
    keep = lax.broadcasted_iota(jnp.int32, (rows, LANES), 1) >= part
    return [jnp.where(keep, moved[t], moved[(t - 1) % tiles]) for t in range(tiles)]


def place_partner(sizes, fields, box, own_offset, offset, active):
    side = sizes[0]
    tiles, lines, _ = box_shape(sizes)
    placed = rolled(sizes, fields, box, 0, side, offset[0], offset[1] * side + offset[2])
    lane = lax.broadcasted_iota(jnp.int32, (1, LANES), 1)
    lows = [jnp.maximum(jnp.maximum(a, b), 0) for a, b in zip(own_offset, offset)]
    highs = [side + jnp.minimum(jnp.minimum(a, b), 0) for a, b in zip(own_offset, offset)]
    point_ok = (lane % side >= lows[2]) & (lane % side < highs[2]) & active
    result = []
    for tile in range(tiles):
        line = lane // side + tile * lines
        ok = jnp.where(point_ok & (line >= lows[1]) & (line < highs[1]), 1.0, 0.0)
        result.append(placed[tile] * ok)
    return result


def make_matrices(basis_ref, line_ref, first_line, high_ref, low_ref):
    side = basis_ref.shape[0]
    count = side // 2
    for parity in range(2):
        for index in range(count):
            line = first_line + parity * count + index
            rows = slice(index * side, (index + 1) * side)
            value = basis_ref[...] * line_ref[line : line + 1, :]
            high_ref[parity, rows, :], low_ref[parity, rows, :] = split_pair(value)


def make_mix(basis_ref, mix_ref):
    side = basis_ref.shape[0]
    width = mix_ref.shape[0]
    block = lax.broadcasted_iota(jnp.int32, (side, width), 1) // side
    for index in range(width // side):
        rows = slice(index * side, (index + 1) * side)
        high, low = split_pair(jnp.where(block == index, basis_ref[:, :width], 0.0))
        for part, piece in enumerate((high, high, low)):
            mix_ref[rows, part * width : (part + 1) * width] = piece


def own_kernel(sizes, match_hbm, centers_hbm, boxes_ref, *refs):
    basis_ref, line_ref, gain_hbm, *refs = refs
    mine_ref, table_ref, mix_ref, gain_ref, there_high, there_low, back_high, back_low = refs[:8]
    match_ref, centers_ref, fields, sems = refs[8:]
    side, rounds, own_count, _, _ = sizes
    tiles, _, _ = box_shape(sizes)
    first_member = lax.axis_index("pair") * own_count
    sources = (gain_hbm, match_hbm, centers_hbm)
    targets = (gain_ref, match_ref, centers_ref)
    copies = [pltpu.make_async_copy(s, t, sems.at[i]) for i, (s, t) in enumerate(zip(sources, targets))]
    for copy in copies:
        copy.start()
    clear_edges(sizes, fields, 0, own_count)
    make_mix(basis_ref, mix_ref)
    make_matrices(basis_ref, line_ref, 0, there_high, there_low)
    make_matrices(basis_ref, line_ref, side, back_high, back_low)
    for copy in copies:
        copy.wait()
    spread(sizes, boxes_ref, fields, 0)

    def place(index, carry):
        member, mate, a, b, active = pair_geometry(sizes, match_ref, centers_ref, index)
        for place, entry in enumerate((mate, *a, *b, jnp.where(active, 1, 0))):
            table_ref[index * ENTRIES + place] = entry
        rows = pl.ds(pl.multiple_of(index * side, side), side)
        placed = rolled(sizes, fields, member - first_member, 0, side, a[0], a[1] * side + a[2])
        for tile in range(tiles):
            mine_ref[rows, tile * LANES : (tile + 1) * LANES] = placed[tile].astype(jnp.bfloat16)
        return carry

    lax.fori_loop(0, own_count * rounds, place, 0)


def force_kernel(sizes, mine, table_hbm, *refs):
    side, rounds, own_count, slab_count, pair_count = sizes
    piece_refs, refs = refs[:pair_count], refs[pair_count:]
    constants, refs = refs[:6], refs[6:]
    mix_ref, gain_ref, there_high, there_low, back_high, back_low = constants
    out_refs, refs = refs[:slab_count], refs[slab_count:]
    table_ref, partner, *refs = refs
    fields, first, second, *terms, all_codes, sems = refs
    planes = side // slab_count
    tiles, lines, pitch = box_shape(sizes)
    solves = own_count * rounds
    group = min(solves, 8)
    group_rows = group * side
    cells = tiles * LANES
    width = cells // 2
    slab_index = lax.axis_index("slab")
    pair_index = lax.axis_index("pair")
    core = pair_index % CORES
    chip = pair_index // CORES
    chips = pair_count // CORES

    places = [
        (chip + chips - step) % chips * CORES + (core + core_step) % CORES
        for core_step in range(CORES)
        for step in range(chips)
    ]
    table_copy = pltpu.make_async_copy(table_hbm, table_ref, sems.at[0])
    table_copy.start()
    for pair in places:
        clear_edges(sizes, fields, pair * own_count, own_count)
    for ref in terms:
        clear_edges(sizes, ref, 0, group)
    for piece_ref, pair in zip(piece_refs, places):
        spread(sizes, piece_ref, fields, pair)
    table_copy.wait()

    row_count = solves * side
    half_tiles = tiles // 2
    half_cells = cells // 2

    def mirrored(tile):
        line = lax.broadcasted_iota(jnp.int32, tile.shape, 1) // side
        result = None
        for index in range(lines):
            amount = (2 * index - lines + 1) * side % LANES
            if index < 2:
                moved = pltpu.roll(tile, amount, axis=1)
                result = moved if result is None else jnp.where(line % 2 == index, moved, result)
        return result

    def store_split(ref, start, count, columns, value):
        high, low = split_pair(value)
        ref[start : start + count, columns] = high
        ref[row_count + start : row_count + start + count, columns] = low

    def densities(index):
        start = index * side
        rows = slice(start, start + side)
        mate, *offsets, active = [table_ref[index * ENTRIES + place] for place in range(ENTRIES)]
        placed = place_partner(sizes, fields, mate, offsets[:3], offsets[3:], active == 1)
        density = []
        for tile in range(tiles):
            columns = slice(tile * LANES, (tile + 1) * LANES)
            partner[rows, columns] = placed[tile].astype(jnp.bfloat16)
            density.append(mine[rows, columns].astype(jnp.float32) * placed[tile])
        for tile in range(half_tiles):
            far = mirrored(density[tiles - 1 - tile])
            for parity, value in enumerate((density[tile] + far, density[tile] - far)):
                column = parity * half_cells + tile * LANES
                store_split(first, start, side, slice(column, column + LANES), value)

    def along_x(start, columns, source):
        high = source[start : start + group_rows, columns]
        low = source[row_count + start : row_count + start + group_rows, columns]
        return dot(mix_ref[...], jnp.concatenate([high, low, high], axis=0))

    def in_plane(parity, columns, source, high_ref, low_ref):
        inner = slice(parity * half_cells, (parity + 1) * half_cells)
        high = source[:row_count, inner]
        low = source[row_count:, inner]
        basis = high_ref[parity, :, columns]
        rest = low_ref[parity, :, columns]
        left = jnp.concatenate([high, low, high], axis=1)
        return dot(left, jnp.concatenate([basis, basis, rest], axis=0))

    for start in range(0, row_count, group_rows):
        for index in range(start // side, (start + group_rows) // side):
            densities(index)
        columns = slice(0, cells)
        store_split(second, start, group_rows, columns, along_x(start, columns, first))

    for parity in range(2):
        for column in range(0, half_cells, width):
            columns = slice(column, column + width)
            value = in_plane(parity, columns, second, there_high, there_low)
            columns = slice(parity * half_cells + column, parity * half_cells + column + width)
            gain = gain_ref[:, columns]
            value = (value.reshape(solves, side, width) * gain[None]).reshape(row_count, width)
            store_split(first, 0, row_count, columns, value)

    for parity in range(2):
        for column in range(0, half_cells, width):
            value = in_plane(parity, slice(column, column + width), first, back_high, back_low)
            columns = slice(parity * half_cells + column, parity * half_cells + column + width)
            store_split(second, 0, row_count, columns, value)

    for start in range(0, row_count, group_rows):
        for column in range(0, half_cells, width):
            even = along_x(start, slice(column, column + width), second)
            odd = along_x(start, slice(half_cells + column, half_cells + column + width), second)
            for part in range(width // LANES):
                tile = column // LANES + part
                lanes = slice(part * LANES, (part + 1) * LANES)
                near = even[:, lanes] + odd[:, lanes]
                far = mirrored(even[:, lanes] - odd[:, lanes])
                for place, value in ((tile, near), (tiles - 1 - tile, far)):
                    columns = slice(place * LANES, (place + 1) * LANES)
                    value = value * partner[start : start + group_rows, columns].astype(jnp.float32)
                    for solve in range(group):
                        row = (solve * tiles + place) * pitch + REACH
                        terms[start // group_rows][row : row + side, :] = value[solve * side : (solve + 1) * side, :]

    step_rows = 16

    def collect(own, row):
        sums = None
        for turn in range(rounds):
            index = own * rounds + turn
            a = [table_ref[index * ENTRIES + 1 + axis] for axis in range(3)]
            ref = terms[index // group]
            term = rolled(sizes, ref, index % group, row, step_rows, -a[0], -(a[1] * side + a[2]))
            sums = term if sums is None else [s + t for s, t in zip(sums, term)]
        return sums

    lane_index = lax.broadcasted_iota(jnp.int32, (tiles, LANES), 1)
    exponents = [jnp.zeros((tiles, LANES), jnp.float32)] * slab_count
    factors = [jnp.zeros((tiles, LANES), jnp.float32)] * slab_count
    codes = {}
    for own in range(own_count):
        for row in range(0, side, step_rows):
            sums = collect(own, row)
            for half in range(0, step_rows, 8):
                for index, value in enumerate(turned([tile[half : half + 8, :] for tile in sums])):
                    slab, plane = divmod(row + half + index, planes)
                    chunk = own * planes + plane
                    codes[slab, chunk], exponent, factor = encode(value)
                    exponents[slab] = jnp.where(lane_index == chunk, exponent, exponents[slab])
                    factors[slab] = jnp.where(lane_index == chunk, factor, factors[slab])
                    if chunk % 2:
                        pair = jnp.concatenate([codes[slab, chunk - 1], codes[slab, chunk]], axis=0)
                        all_codes[slab, tiles * (chunk - 1) : tiles * (chunk + 1), :] = whole_codes(pair)
    for slab in range(slab_count):
        header = jnp.concatenate([exponents[slab], factors[slab]], axis=0)
        all_codes[slab, tiles * own_count * planes :, :] = whole_codes(header)
    for step in range(slab_count):
        out_refs[step][...] = all_codes[partner_of(slab_index, step, slab_count)[0]]


def whole_codes(value):
    return value.astype(jnp.int32).astype(jnp.int16)


def encode(value):
    largest = jnp.max(jnp.abs(value), axis=1, keepdims=True)
    exponent = jnp.maximum(jnp.floor(jnp.log2(jnp.maximum(largest, TINY))), LOWEST_EXPONENT)
    lifted = 1.0 / jnp.exp2(exponent)
    factor = jnp.maximum(jnp.ceil(largest * lifted * FACTOR_UNIT), 1.0)
    code = jnp.floor(value * lifted * (CODE_LIMIT * FACTOR_UNIT / factor) + 0.5)
    return jnp.clip(code, -CODE_LIMIT, CODE_LIMIT), exponent, factor


def swap_cores(block, pair_count):
    return lax.ppermute(block, "pair", [(i, i ^ 1) for i in range(pair_count)])


def gather_chips(boxes, pair_count):
    pieces = []
    for step in range(1, pair_count // CORES):
        perm = [(i, (i + step * CORES) % pair_count) for i in range(pair_count)]
        pieces.append(lax.ppermute(boxes, "pair", perm))
    return pieces


def unpack_kernel(sizes, *refs):
    own_count, slab_count, tiles = sizes
    block_refs, out_hbm, blocks, out_ref, sems, out_sems = refs[:slab_count], *refs[slab_count:]
    slab_index = lax.axis_index("slab")
    copies = []
    for index in range(slab_count):
        slab = partner_of(slab_index, slab_count - 1 - index, slab_count)[1]
        copies.append(pltpu.make_async_copy(block_refs[index], blocks.at[slab], sems.at[index]))
        copies[-1].start()
    for copy in copies:
        copy.wait()
    row_count = own_count * tiles
    values = {}
    copies = []
    for slab in range(slab_count):
        header = blocks[slab, row_count:, :].astype(jnp.int32).astype(jnp.float32)
        units = jnp.exp2(header[:8, :])
        factors = header[8:, :] * (1.0 / (CODE_LIMIT * FACTOR_UNIT))
        for pair in range(row_count // 16):
            codes = blocks[slab, 16 * pair : 16 * pair + 16, :].astype(jnp.int32).astype(jnp.float32)
            for half in range(2):
                chunk = 2 * pair + half
                own, plane = divmod(8 * chunk, tiles)
                value = codes[8 * half : 8 * half + 8, :] * factors[:, chunk : chunk + 1]
                values[slab * own_count + own, plane // 8] = value * units[:, chunk : chunk + 1]
        if (slab + 1) * own_count % 8 == 0:
            band = (slab + 1) * own_count // 8 - 1
            for plane in range(tiles // 8):
                rows = turned([values[8 * band + index, plane] for index in range(8)])
                for tile in range(8):
                    start = (band * tiles + 8 * plane + tile) * 8
                    out_ref[start : start + 8, :] = rows[tile]
            rows = slice(band * tiles * 8, (band + 1) * tiles * 8)
            copies.append(pltpu.make_async_copy(out_ref.at[rows], out_hbm.at[rows], out_sems.at[band]))
            copies[-1].start()
    for copy in copies:
        copy.wait()


def unpack(blocks, own_count, cells):
    slab_count = len(blocks)
    row_count = own_count * slab_count
    tiles = cells // LANES
    out = pl.pallas_call(
        functools.partial(unpack_kernel, (own_count, slab_count, tiles)),
        out_shape=jax.ShapeDtypeStruct((row_count * tiles, LANES), jnp.float32),
        in_specs=[pl.BlockSpec(memory_space=pl.ANY)] * slab_count,
        out_specs=pl.BlockSpec(memory_space=pl.ANY),
        scratch_shapes=[
            pltpu.VMEM((slab_count,) + blocks[0].shape, jnp.int16),
            pltpu.VMEM((row_count * tiles, LANES), jnp.float32),
            pltpu.SemaphoreType.DMA((slab_count,)),
            pltpu.SemaphoreType.DMA((row_count // 8,)),
        ],
        compiler_params=pltpu.CompilerParams(vmem_limit_bytes=8 * 1024 * 1024),
    )(*blocks)
    return out.reshape(row_count // 8, tiles, 8, LANES).transpose(0, 2, 1, 3).reshape(row_count, cells)


def kernel_constants(side):
    basis = sine_basis(side)
    halves = [basis[parity::2, : side // 2].T for parity in range(2)]
    lines = np.concatenate(halves + [half.T for half in halves])
    lines = np.repeat(lines, side, axis=1).astype(np.float32)
    tile = np.tile(basis, (1, side // 2)).astype(np.float32)
    gain = chebyshev_gain(side).reshape(side, side, side)
    gain = np.concatenate([gain[:, parity::2].reshape(side, -1) for parity in range(2)], axis=1)
    return [jnp.asarray(constant) for constant in (tile, lines, gain)]


def place_own(sizes, match, centers, boxes):
    side, rounds, own_count, slab_count, _ = sizes
    tiles, _, pitch = box_shape(sizes)
    solves = own_count * rounds
    constants = kernel_constants(side)
    group_rows = min(solves, 8) * side
    half_cells = side * side // 2
    matrix = jax.ShapeDtypeStruct((2, half_cells, half_cells), jnp.bfloat16)
    inputs = [match, centers, boxes, *constants]
    either = pl.BlockSpec(memory_space=pl.ANY)
    vectors = pl.BlockSpec(memory_space=pltpu.VMEM)
    return pl.pallas_call(
        functools.partial(own_kernel, sizes),
        out_shape=[
            jax.ShapeDtypeStruct((solves * side, side * side), jnp.bfloat16),
            jax.ShapeDtypeStruct((solves * ENTRIES,), jnp.int32),
            jax.ShapeDtypeStruct((group_rows, 3 * group_rows), jnp.bfloat16),
            jax.ShapeDtypeStruct(constants[2].shape, jnp.float32),
            *[matrix] * 4,
        ],
        in_specs=[either] * 2 + [vectors] * 3 + [either],
        out_specs=[vectors, pl.BlockSpec(memory_space=pltpu.SMEM)] + [vectors] * 6,
        scratch_shapes=[
            pltpu.SMEM(match.shape, jnp.int32),
            pltpu.SMEM(centers.shape, jnp.int32),
            pltpu.VMEM((own_count * tiles * pitch, LANES), jnp.float32),
            pltpu.SemaphoreType.DMA((len(inputs),)),
        ],
        compiler_params=pltpu.CompilerParams(vmem_limit_bytes=32 * 1024 * 1024),
        cost_estimate=pl.CostEstimate(flops=5 * 10**9, bytes_accessed=4 * 1024 * 1024, transcendentals=0),
    )(*inputs)


def team_forces(sizes, mine, table, constants, pieces):
    side, rounds, own_count, slab_count, pair_count = sizes
    tiles, _, pitch = box_shape(sizes)
    _, rows, _ = pieces[0].shape
    solves = own_count * rounds
    group = min(solves, 8)
    cells = side * side
    either = pl.BlockSpec(memory_space=pl.ANY)
    vectors = pl.BlockSpec(memory_space=pltpu.VMEM)
    wide = pltpu.VMEM((2 * solves * side, cells), jnp.bfloat16)
    flops = 2 * solves * side * 3 * 2 * (cells * cells // 2 + cells * group * side)
    inputs = [mine, table, *pieces, *constants]
    return pl.pallas_call(
        functools.partial(force_kernel, sizes),
        out_shape=[jax.ShapeDtypeStruct((rows + HEADER_ROWS, LANES), jnp.int16)] * slab_count,
        in_specs=[vectors, either] + [vectors] * (len(pieces) + len(constants)),
        out_specs=[vectors] * slab_count,
        scratch_shapes=[
            pltpu.SMEM(table.shape, jnp.int32),
            pltpu.VMEM(mine.shape, jnp.bfloat16),
            pltpu.VMEM((own_count * pair_count * tiles * pitch, LANES), jnp.float32),
            wide,
            wide,
            *[pltpu.VMEM((group * tiles * pitch, LANES), jnp.float32)] * (solves // group),
            pltpu.VMEM((slab_count, rows + HEADER_ROWS, LANES), jnp.int16),
            pltpu.SemaphoreType.DMA((1,)),
        ],
        compiler_params=pltpu.CompilerParams(vmem_limit_bytes=32 * 1024 * 1024),
        cost_estimate=pl.CostEstimate(flops=flops, bytes_accessed=8 * 1024 * 1024, transcendentals=0),
    )(*inputs)


def shards(orbitals, centers, matchings):
    slab_count = lax.axis_size("slab")
    pair_count = lax.axis_size("pair")
    local_rows, plane_cells = orbitals.shape
    own_count = local_rows // slab_count
    side = round((plane_cells * slab_count) ** (1.0 / 3.0))
    blocks = orbitals.reshape(slab_count, own_count * plane_cells // LANES, LANES)
    boxes = lax.all_to_all(blocks, "slab", split_axis=0, concat_axis=0, tiled=True)
    sizes = (side, matchings.shape[1], own_count, slab_count, pair_count)
    pieces = gather_chips(boxes, pair_count)
    mine, table, *constants = place_own(sizes, matchings, centers.T, boxes)
    boxes, mine = lax.optimization_barrier((boxes, mine))
    swapped = [swap_cores(boxes, pair_count)]
    pieces, mine = lax.optimization_barrier((pieces, mine))
    swapped += [swap_cores(piece, pair_count) for piece in pieces]
    codes = team_forces(sizes, mine, table, constants, [boxes] + pieces + swapped)
    received = []
    for step in reversed(range(1, slab_count)):
        perm = [(i, partner_of(i, step, slab_count)[0]) for i in range(slab_count)]
        received.append(lax.ppermute(codes[step], "slab", perm))
    return unpack(received + [codes[0]], own_count, plane_cells)


def solution(mesh):
    in_specs = (P("pair", "slab"), P(), P("slab", None, None))
    out_specs = P("pair", "slab")
    return jax.shard_map(shards, mesh=mesh, in_specs=in_specs, out_specs=out_specs, check_vma=False)
```

```python
import functools

import jax
import jax.numpy as jnp
import numpy as np
from jax import lax
from jax.experimental import pallas as pl
from jax.experimental.pallas import tpu as pltpu
from jax.sharding import PartitionSpec as P

STEPS = 16
CUT2 = 192
REACH = 8
SCREEN = 0.1
LOWER_BOUND = 0.1
UPPER_BOUND = 12.1
LANES = 128
CORES = 2
CODE_LIMIT = 32767.0
FACTOR_UNIT = 8192.0
LOWEST_EXPONENT = -120.0
TINY = 1e-37
HEADER_ROWS = 16
ENTRIES = 8


def sine_basis(side):
    index = np.arange(1, side + 1, dtype=np.float64)
    return np.sqrt(2.0 / (side + 1)) * np.sin(np.pi * np.outer(index, index) / (side + 1))


def chebyshev_gain(side):
    shifts = -2.0 * np.cos(np.pi * np.arange(1, side + 1, dtype=np.float64) / (side + 1))
    eigenvalue = 6.0 + SCREEN + shifts[:, None, None] + shifts[None, :, None] + shifts[None, None, :]
    middle = (UPPER_BOUND + LOWER_BOUND) / 2.0
    spread = (UPPER_BOUND - LOWER_BOUND) / 2.0
    ratio = middle / spread
    total = np.zeros_like(eigenvalue)
    residual = np.ones_like(eigenvalue)
    direction = residual / middle
    factor = 1.0 / ratio
    for _ in range(STEPS):
        total = total + direction
        residual = residual - eigenvalue * direction
        factor_next = 1.0 / (2.0 * ratio - factor)
        direction = factor_next * factor * direction + 2.0 * factor_next / spread * residual
        factor = factor_next
    return total.reshape(side, side * side).astype(np.float32)


def split_pair(value):
    high = value.astype(jnp.bfloat16)
    low = (value - high.astype(jnp.float32)).astype(jnp.bfloat16)
    return high, low


def dot(left, right):
    return jnp.dot(left, right, preferred_element_type=jnp.float32)


def partner_of(index, step, count):
    if count & (count - 1) == 0:
        return index ^ step, index ^ step
    return (index + step) % count, (index + count - step) % count


def pair_geometry(sizes, match_ref, centers_ref, index):
    _, rounds, own_count, slab_count, _ = sizes
    slab_index = lax.axis_index("slab")
    pair_index = lax.axis_index("pair")

    def orbital_of(member):
        return (member // own_count * slab_count + slab_index) * own_count + member % own_count

    member = pair_index * own_count + index // rounds
    mate = match_ref[0, index % rounds, member]
    own_offset = []
    mate_offset = []
    distance = 0
    for axis in range(3):
        mine = centers_ref[axis, orbital_of(member)]
        other = centers_ref[axis, orbital_of(mate)]
        anchor = (mine + other) >> 1
        own_offset.append(mine - anchor)
        mate_offset.append(other - anchor)
        distance = distance + (mine - other) * (mine - other)
    return member, mate, own_offset, mate_offset, distance <= CUT2


def box_shape(sizes):
    side = sizes[0]
    return side * side // LANES, LANES // side, side + REACH


def clear_edges(sizes, ref, count):
    tiles, _, pitch = box_shape(sizes)
    for index in range(count * tiles + 1):
        ref[index * pitch : index * pitch + REACH, :] = jnp.zeros((REACH, LANES), jnp.float32)


def turned(tiles):
    row = lax.broadcasted_iota(jnp.int32, (8, LANES), 0)
    tiles = list(tiles)
    for distance in (4, 2, 1):
        low = (row & distance) == 0
        for index in range(8):
            if index & distance == 0:
                first, second = tiles[index], tiles[index + distance]
                tiles[index] = jnp.where(low, first, pltpu.roll(second, distance, axis=0))
                tiles[index + distance] = jnp.where(low, pltpu.roll(first, 8 - distance, axis=0), second)
    return tiles


def spread(sizes, boxes_ref, fields, pair):
    side, _, own_count, slab_count, _ = sizes
    planes = side // slab_count
    tiles, _, pitch = box_shape(sizes)
    for group in range(side // 8):
        halves = {}
        for slab in range(8 * group // planes, (8 * group + 7) // planes + 1):
            for chunk in range(own_count * planes // 2):
                block = boxes_ref[slab, 16 * chunk : 16 * chunk + 16, :].astype(jnp.float32)
                for half in range(2):
                    own, plane = divmod(2 * chunk + half, planes)
                    halves[own, slab * planes + plane] = block[8 * half : 8 * half + 8, :]
        for own in range(own_count):
            rows = turned([halves[own, 8 * group + index] for index in range(8)])
            for tile in range(tiles):
                start = ((pair * own_count + own) * tiles + tile) * pitch + REACH + 8 * group
                fields[pl.ds(pl.multiple_of(start, 8), 8), :] = rows[tile]


def rolled(sizes, ref, box, row, rows, offset_x, offset_flat):
    tiles, _, pitch = box_shape(sizes)
    whole = (offset_flat >> 7) & (tiles - 1)
    part = offset_flat & (LANES - 1)
    start = box * tiles * pitch + REACH + row - offset_x
    moved = []
    for tile in range(tiles):
        first_row = start + ((tile - whole) & (tiles - 1)) * pitch
        moved.append(pltpu.roll(ref[pl.ds(first_row, rows), :], part, axis=1))
    keep = lax.broadcasted_iota(jnp.int32, (rows, LANES), 1) >= part
    return [jnp.where(keep, moved[t], moved[(t - 1) % tiles]) for t in range(tiles)]


def place_partner(sizes, fields, box, own_offset, offset, active):
    side = sizes[0]
    tiles, lines, _ = box_shape(sizes)
    placed = rolled(sizes, fields, box, 0, side, offset[0], offset[1] * side + offset[2])
    lane = lax.broadcasted_iota(jnp.int32, (1, LANES), 1)
    lows = [jnp.maximum(jnp.maximum(a, b), 0) for a, b in zip(own_offset, offset)]
    highs = [side + jnp.minimum(jnp.minimum(a, b), 0) for a, b in zip(own_offset, offset)]
    point_ok = (lane % side >= lows[2]) & (lane % side < highs[2]) & active
    result = []
    for tile in range(tiles):
        line = lane // side + tile * lines
        ok = jnp.where(point_ok & (line >= lows[1]) & (line < highs[1]), 1.0, 0.0)
        result.append(placed[tile] * ok)
    return result


def make_matrices(basis_ref, line_ref, first_line, high_ref, low_ref):
    side = basis_ref.shape[0]
    count = side // 2
    for parity in range(2):
        for index in range(count):
            line = first_line + parity * count + index
            rows = slice(index * side, (index + 1) * side)
            value = basis_ref[...] * line_ref[line : line + 1, :]
            high_ref[parity, rows, :], low_ref[parity, rows, :] = split_pair(value)


def make_mix(basis_ref, mix_ref):
    side = basis_ref.shape[0]
    width = mix_ref.shape[0]
    block = lax.broadcasted_iota(jnp.int32, (side, width), 1) // side
    for index in range(width // side):
        rows = slice(index * side, (index + 1) * side)
        high, low = split_pair(jnp.where(block == index, basis_ref[:, :width], 0.0))
        for part, piece in enumerate((high, high, low)):
            mix_ref[rows, part * width : (part + 1) * width] = piece


def own_kernel(sizes, match_hbm, centers_hbm, boxes_ref, *refs):
    basis_ref, line_ref, gain_hbm, *refs = refs
    mine_ref, table_ref, mix_ref, gain_ref, there_high, there_low, back_high, back_low = refs[:8]
    match_ref, centers_ref, fields, sems = refs[8:]
    side, rounds, own_count, _, _ = sizes
    tiles, _, _ = box_shape(sizes)
    first_member = lax.axis_index("pair") * own_count
    sources = (gain_hbm, match_hbm, centers_hbm)
    targets = (gain_ref, match_ref, centers_ref)
    copies = [pltpu.make_async_copy(s, t, sems.at[i]) for i, (s, t) in enumerate(zip(sources, targets))]
    for copy in copies:
        copy.start()
    clear_edges(sizes, fields, own_count)
    make_mix(basis_ref, mix_ref)
    make_matrices(basis_ref, line_ref, 0, there_high, there_low)
    make_matrices(basis_ref, line_ref, side, back_high, back_low)
    for copy in copies:
        copy.wait()
    spread(sizes, boxes_ref, fields, 0)

    def place(index, carry):
        member, mate, a, b, active = pair_geometry(sizes, match_ref, centers_ref, index)
        for place, entry in enumerate((mate, *a, *b, jnp.where(active, 1, 0))):
            table_ref[index * ENTRIES + place] = entry
        rows = pl.ds(pl.multiple_of(index * side, side), side)
        placed = rolled(sizes, fields, member - first_member, 0, side, a[0], a[1] * side + a[2])
        for tile in range(tiles):
            mine_ref[rows, tile * LANES : (tile + 1) * LANES] = placed[tile].astype(jnp.bfloat16)
        return carry

    lax.fori_loop(0, own_count * rounds, place, 0)


def force_kernel(sizes, mine, table_hbm, *refs):
    side, rounds, own_count, slab_count, pair_count = sizes
    piece_refs, refs = refs[:pair_count], refs[pair_count:]
    constants, refs = refs[:6], refs[6:]
    mix_ref, gain_ref, there_high, there_low, back_high, back_low = constants
    out_refs, refs = refs[:slab_count], refs[slab_count:]
    table_ref, partner, *refs = refs
    fields, first, second, *terms, all_codes, sems = refs
    planes = side // slab_count
    tiles, lines, pitch = box_shape(sizes)
    solves = own_count * rounds
    group = min(solves, 8)
    group_rows = group * side
    cells = tiles * LANES
    width = cells // 2
    slab_index = lax.axis_index("slab")
    pair_index = lax.axis_index("pair")
    core = pair_index % CORES
    chip = pair_index // CORES
    chips = pair_count // CORES

    places = [
        (chip + chips - step) % chips * CORES + (core + core_step) % CORES
        for core_step in range(CORES)
        for step in range(chips)
    ]
    table_copy = pltpu.make_async_copy(table_hbm, table_ref, sems.at[0])
    table_copy.start()
    clear_edges(sizes, fields, pair_count * own_count)
    for ref in terms:
        clear_edges(sizes, ref, group)
    for piece_ref, pair in zip(piece_refs, places):
        spread(sizes, piece_ref, fields, pair)
    table_copy.wait()

    row_count = solves * side
    half_tiles = tiles // 2
    half_cells = cells // 2

    def mirrored(tile):
        line = lax.broadcasted_iota(jnp.int32, tile.shape, 1) // side
        result = None
        for index in range(lines):
            amount = (2 * index - lines + 1) * side % LANES
            if index < 2:
                moved = pltpu.roll(tile, amount, axis=1)
                result = moved if result is None else jnp.where(line % 2 == index, moved, result)
        return result

    def store_split(ref, start, count, columns, value):
        high, low = split_pair(value)
        ref[start : start + count, columns] = high
        ref[row_count + start : row_count + start + count, columns] = low

    def densities(index):
        start = index * side
        rows = slice(start, start + side)
        mate, *offsets, active = [table_ref[index * ENTRIES + place] for place in range(ENTRIES)]
        placed = place_partner(sizes, fields, mate, offsets[:3], offsets[3:], active == 1)
        density = []
        for tile in range(tiles):
            columns = slice(tile * LANES, (tile + 1) * LANES)
            partner[rows, columns] = placed[tile].astype(jnp.bfloat16)
            density.append(mine[rows, columns].astype(jnp.float32) * placed[tile])
        for tile in range(half_tiles):
            far = mirrored(density[tiles - 1 - tile])
            for parity, value in enumerate((density[tile] + far, density[tile] - far)):
                column = parity * half_cells + tile * LANES
                store_split(first, start, side, slice(column, column + LANES), value)

    def along_x(start, columns, source):
        high = source[start : start + group_rows, columns]
        low = source[row_count + start : row_count + start + group_rows, columns]
        return dot(mix_ref[...], jnp.concatenate([high, low, high], axis=0))

    def in_plane(parity, columns, source, high_ref, low_ref):
        inner = slice(parity * half_cells, (parity + 1) * half_cells)
        high = source[:row_count, inner]
        low = source[row_count:, inner]
        basis = high_ref[parity, :, columns]
        rest = low_ref[parity, :, columns]
        left = jnp.concatenate([high, low, high], axis=1)
        return dot(left, jnp.concatenate([basis, basis, rest], axis=0))

    for start in range(0, row_count, group_rows):
        for index in range(start // side, (start + group_rows) // side):
            densities(index)
        columns = slice(0, cells)
        store_split(second, start, group_rows, columns, along_x(start, columns, first))

    for parity in range(2):
        for column in range(0, half_cells, width):
            columns = slice(column, column + width)
            value = in_plane(parity, columns, second, there_high, there_low)
            columns = slice(parity * half_cells + column, parity * half_cells + column + width)
            gain = gain_ref[:, columns]
            value = (value.reshape(solves, side, width) * gain[None]).reshape(row_count, width)
            store_split(first, 0, row_count, columns, value)

    for parity in range(2):
        for column in range(0, half_cells, width):
            value = in_plane(parity, slice(column, column + width), first, back_high, back_low)
            columns = slice(parity * half_cells + column, parity * half_cells + column + width)
            store_split(second, 0, row_count, columns, value)

    for start in range(0, row_count, group_rows):
        for column in range(0, half_cells, width):
            even = along_x(start, slice(column, column + width), second)
            odd = along_x(start, slice(half_cells + column, half_cells + column + width), second)
            for part in range(width // LANES):
                tile = column // LANES + part
                lanes = slice(part * LANES, (part + 1) * LANES)
                near = even[:, lanes] + odd[:, lanes]
                far = mirrored(even[:, lanes] - odd[:, lanes])
                for place, value in ((tile, near), (tiles - 1 - tile, far)):
                    columns = slice(place * LANES, (place + 1) * LANES)
                    value = value * partner[start : start + group_rows, columns].astype(jnp.float32)
                    for solve in range(group):
                        row = (solve * tiles + place) * pitch + REACH
                        terms[start // group_rows][row : row + side, :] = value[solve * side : (solve + 1) * side, :]

    step_rows = 16

    def collect(own, row):
        sums = None
        for turn in range(rounds):
            index = own * rounds + turn
            a = [table_ref[index * ENTRIES + 1 + axis] for axis in range(3)]
            ref = terms[index // group]
            term = rolled(sizes, ref, index % group, row, step_rows, -a[0], -(a[1] * side + a[2]))
            sums = term if sums is None else [s + t for s, t in zip(sums, term)]
        return sums

    lane_index = lax.broadcasted_iota(jnp.int32, (tiles, LANES), 1)
    exponents = [jnp.zeros((tiles, LANES), jnp.float32)] * slab_count
    factors = [jnp.zeros((tiles, LANES), jnp.float32)] * slab_count
    codes = {}
    for own in range(own_count):
        for row in range(0, side, step_rows):
            sums = collect(own, row)
            for half in range(0, step_rows, 8):
                for index, value in enumerate(turned([tile[half : half + 8, :] for tile in sums])):
                    slab, plane = divmod(row + half + index, planes)
                    chunk = own * planes + plane
                    codes[slab, chunk], exponent, factor = encode(value)
                    exponents[slab] = jnp.where(lane_index == chunk, exponent, exponents[slab])
                    factors[slab] = jnp.where(lane_index == chunk, factor, factors[slab])
                    if chunk % 2:
                        pair = jnp.concatenate([codes[slab, chunk - 1], codes[slab, chunk]], axis=0)
                        all_codes[slab, tiles * (chunk - 1) : tiles * (chunk + 1), :] = whole_codes(pair)
    for slab in range(slab_count):
        header = jnp.concatenate([exponents[slab], factors[slab]], axis=0)
        all_codes[slab, tiles * own_count * planes :, :] = whole_codes(header)
    for step in range(slab_count):
        out_refs[step][...] = all_codes[partner_of(slab_index, step, slab_count)[0]]


def whole_codes(value):
    return value.astype(jnp.int32).astype(jnp.int16)


def encode(value):
    largest = jnp.max(jnp.abs(value), axis=1, keepdims=True)
    exponent = jnp.maximum(jnp.floor(jnp.log2(jnp.maximum(largest, TINY))), LOWEST_EXPONENT)
    lifted = 1.0 / jnp.exp2(exponent)
    factor = jnp.maximum(jnp.ceil(largest * lifted * FACTOR_UNIT), 1.0)
    code = jnp.floor(value * lifted * (CODE_LIMIT * FACTOR_UNIT / factor) + 0.5)
    return jnp.clip(code, -CODE_LIMIT, CODE_LIMIT), exponent, factor


def swap_cores(block, pair_count):
    return lax.ppermute(block, "pair", [(i, i ^ 1) for i in range(pair_count)])


def gather_chips(boxes, pair_count):
    pieces = []
    for step in range(1, pair_count // CORES):
        perm = [(i, (i + step * CORES) % pair_count) for i in range(pair_count)]
        pieces.append(lax.ppermute(boxes, "pair", perm))
    return pieces


def unpack_kernel(sizes, *refs):
    own_count, slab_count, tiles = sizes
    block_refs, out_hbm, out_ref, out_sems = refs[:slab_count], *refs[slab_count:]
    slab_index = lax.axis_index("slab")
    band_slabs = 8 // own_count
    assert slab_count & (slab_count - 1) == 0 and band_slabs * own_count == 8
    row = lax.broadcasted_iota(jnp.int32, (8, LANES), 0)

    def ordered(value):
        distance = own_count
        while distance < 8:
            near = pltpu.roll(value, 8 - distance, axis=0)
            far = pltpu.roll(value, distance, axis=0)
            swapped = jnp.where((row & distance) == 0, near, far)
            value = jnp.where(slab_index // (distance // own_count) % 2 == 1, swapped, value)
            distance *= 2
        return value

    row_count = own_count * tiles
    copies = []
    for band in range(slab_count // band_slabs):
        values = {}
        for part in range(band_slabs):
            block_ref = block_refs[slab_count - 1 - band * band_slabs - part]
            header = block_ref[row_count:, :].astype(jnp.int32).astype(jnp.float32)
            units = jnp.exp2(header[:8, :])
            factors = header[8:, :] * (1.0 / (CODE_LIMIT * FACTOR_UNIT))
            for pair in range(row_count // 16):
                codes = block_ref[16 * pair : 16 * pair + 16, :].astype(jnp.int32).astype(jnp.float32)
                for half in range(2):
                    chunk = 2 * pair + half
                    own, plane = divmod(8 * chunk, tiles)
                    value = codes[8 * half : 8 * half + 8, :] * factors[:, chunk : chunk + 1]
                    values[part * own_count + own, plane // 8] = value * units[:, chunk : chunk + 1]
        for plane in range(tiles // 8):
            rows = turned([values[index, plane] for index in range(8)])
            for tile in range(8):
                start = (band * tiles + 8 * plane + tile) * 8
                out_ref[start : start + 8, :] = ordered(rows[tile])
        target = (slab_index // band_slabs ^ band) * (tiles * 8)
        source = out_ref.at[band * tiles * 8 : (band + 1) * tiles * 8]
        target = out_hbm.at[pl.ds(pl.multiple_of(target, 8), tiles * 8)]
        copies.append(pltpu.make_async_copy(source, target, out_sems.at[band]))
        copies[-1].start()
    for copy in copies:
        copy.wait()


def unpack(blocks, own_count, cells):
    slab_count = len(blocks)
    row_count = own_count * slab_count
    tiles = cells // LANES
    out = pl.pallas_call(
        functools.partial(unpack_kernel, (own_count, slab_count, tiles)),
        out_shape=jax.ShapeDtypeStruct((row_count * tiles, LANES), jnp.float32),
        in_specs=[pl.BlockSpec(memory_space=pltpu.VMEM)] * slab_count,
        out_specs=pl.BlockSpec(memory_space=pl.ANY),
        scratch_shapes=[
            pltpu.VMEM((row_count * tiles, LANES), jnp.float32),
            pltpu.SemaphoreType.DMA((row_count // 8,)),
        ],
        compiler_params=pltpu.CompilerParams(vmem_limit_bytes=8 * 1024 * 1024),
    )(*blocks)
    return out.reshape(row_count // 8, tiles, 8, LANES).transpose(0, 2, 1, 3).reshape(row_count, cells)


def kernel_constants(side):
    basis = sine_basis(side)
    halves = [basis[parity::2, : side // 2].T for parity in range(2)]
    lines = np.concatenate(halves + [half.T for half in halves])
    lines = np.repeat(lines, side, axis=1).astype(np.float32)
    tile = np.tile(basis, (1, side // 2)).astype(np.float32)
    gain = chebyshev_gain(side).reshape(side, side, side)
    gain = np.concatenate([gain[:, parity::2].reshape(side, -1) for parity in range(2)], axis=1)
    return [jnp.asarray(constant) for constant in (tile, lines, gain)]


def place_own(sizes, match, centers, boxes):
    side, rounds, own_count, slab_count, _ = sizes
    tiles, _, pitch = box_shape(sizes)
    solves = own_count * rounds
    constants = kernel_constants(side)
    group_rows = min(solves, 8) * side
    half_cells = side * side // 2
    matrix = jax.ShapeDtypeStruct((2, half_cells, half_cells), jnp.bfloat16)
    inputs = [match, centers, boxes, *constants]
    either = pl.BlockSpec(memory_space=pl.ANY)
    vectors = pl.BlockSpec(memory_space=pltpu.VMEM)
    return pl.pallas_call(
        functools.partial(own_kernel, sizes),
        out_shape=[
            jax.ShapeDtypeStruct((solves * side, side * side), jnp.bfloat16),
            jax.ShapeDtypeStruct((solves * ENTRIES,), jnp.int32),
            jax.ShapeDtypeStruct((group_rows, 3 * group_rows), jnp.bfloat16),
            jax.ShapeDtypeStruct(constants[2].shape, jnp.float32),
            *[matrix] * 4,
        ],
        in_specs=[either] * 2 + [vectors] * 3 + [either],
        out_specs=[vectors, pl.BlockSpec(memory_space=pltpu.SMEM)] + [vectors] * 6,
        scratch_shapes=[
            pltpu.SMEM(match.shape, jnp.int32),
            pltpu.SMEM(centers.shape, jnp.int32),
            pltpu.VMEM((own_count * tiles * pitch + REACH, LANES), jnp.float32),
            pltpu.SemaphoreType.DMA((len(inputs),)),
        ],
        compiler_params=pltpu.CompilerParams(vmem_limit_bytes=32 * 1024 * 1024),
        cost_estimate=pl.CostEstimate(flops=5 * 10**9, bytes_accessed=4 * 1024 * 1024, transcendentals=0),
    )(*inputs)


def team_forces(sizes, mine, table, constants, pieces):
    side, rounds, own_count, slab_count, pair_count = sizes
    tiles, _, pitch = box_shape(sizes)
    _, rows, _ = pieces[0].shape
    solves = own_count * rounds
    group = min(solves, 8)
    cells = side * side
    either = pl.BlockSpec(memory_space=pl.ANY)
    vectors = pl.BlockSpec(memory_space=pltpu.VMEM)
    wide = pltpu.VMEM((2 * solves * side, cells), jnp.bfloat16)
    flops = 2 * solves * side * 3 * 2 * (cells * cells // 2 + cells * group * side)
    inputs = [mine, table, *pieces, *constants]
    return pl.pallas_call(
        functools.partial(force_kernel, sizes),
        out_shape=[jax.ShapeDtypeStruct((rows + HEADER_ROWS, LANES), jnp.int16)] * slab_count,
        in_specs=[vectors, either] + [vectors] * (len(pieces) + len(constants)),
        out_specs=[vectors] * slab_count,
        scratch_shapes=[
            pltpu.SMEM(table.shape, jnp.int32),
            pltpu.VMEM(mine.shape, jnp.bfloat16),
            pltpu.VMEM((own_count * pair_count * tiles * pitch + REACH, LANES), jnp.float32),
            wide,
            wide,
            *[pltpu.VMEM((group * tiles * pitch + REACH, LANES), jnp.float32)] * (solves // group),
            pltpu.VMEM((slab_count, rows + HEADER_ROWS, LANES), jnp.int16),
            pltpu.SemaphoreType.DMA((1,)),
        ],
        compiler_params=pltpu.CompilerParams(vmem_limit_bytes=32 * 1024 * 1024),
        cost_estimate=pl.CostEstimate(flops=flops, bytes_accessed=8 * 1024 * 1024, transcendentals=0),
    )(*inputs)


def shards(orbitals, centers, matchings):
    slab_count = lax.axis_size("slab")
    pair_count = lax.axis_size("pair")
    local_rows, plane_cells = orbitals.shape
    own_count = local_rows // slab_count
    side = round((plane_cells * slab_count) ** (1.0 / 3.0))
    blocks = orbitals.reshape(slab_count, own_count * plane_cells // LANES, LANES)
    boxes = lax.all_to_all(blocks, "slab", split_axis=0, concat_axis=0, tiled=True)
    sizes = (side, matchings.shape[1], own_count, slab_count, pair_count)
    pieces = gather_chips(boxes, pair_count)
    mine, table, *constants = place_own(sizes, matchings, centers.T, boxes)
    boxes, mine = lax.optimization_barrier((boxes, mine))
    swapped = [swap_cores(boxes, pair_count)]
    pieces, mine = lax.optimization_barrier((pieces, mine))
    swapped += [swap_cores(piece, pair_count) for piece in pieces]
    codes = team_forces(sizes, mine, table, constants, [boxes] + pieces + swapped)
    received = []
    for step in reversed(range(1, slab_count)):
        perm = [(i, partner_of(i, step, slab_count)[0]) for i in range(slab_count)]
        received.append(lax.ppermute(codes[step], "slab", perm))
    return unpack(received + [codes[0]], own_count, plane_cells)


def solution(mesh):
    in_specs = (P("pair", "slab"), P(), P("slab", None, None))
    out_specs = P("pair", "slab")
    return jax.shard_map(shards, mesh=mesh, in_specs=in_specs, out_specs=out_specs, check_vma=False)
```

```python
import functools

import jax
import jax.numpy as jnp
import numpy as np
from jax import lax
from jax.experimental import pallas as pl
from jax.experimental.pallas import tpu as pltpu
from jax.sharding import PartitionSpec as P

STEPS = 16
CUT2 = 192
REACH = 8
SCREEN = 0.1
LOWER_BOUND = 0.1
UPPER_BOUND = 12.1
LANES = 128
CORES = 2
CODE_LIMIT = 32767.0
FACTOR_UNIT = 8192.0
LOWEST_EXPONENT = -120.0
TINY = 1e-37
HEADER_ROWS = 16
ENTRIES = 8


def sine_basis(side):
    index = np.arange(1, side + 1, dtype=np.float64)
    return np.sqrt(2.0 / (side + 1)) * np.sin(np.pi * np.outer(index, index) / (side + 1))


def chebyshev_gain(side):
    shifts = -2.0 * np.cos(np.pi * np.arange(1, side + 1, dtype=np.float64) / (side + 1))
    eigenvalue = 6.0 + SCREEN + shifts[:, None, None] + shifts[None, :, None] + shifts[None, None, :]
    middle = (UPPER_BOUND + LOWER_BOUND) / 2.0
    spread = (UPPER_BOUND - LOWER_BOUND) / 2.0
    ratio = middle / spread
    total = np.zeros_like(eigenvalue)
    residual = np.ones_like(eigenvalue)
    direction = residual / middle
    factor = 1.0 / ratio
    for _ in range(STEPS):
        total = total + direction
        residual = residual - eigenvalue * direction
        factor_next = 1.0 / (2.0 * ratio - factor)
        direction = factor_next * factor * direction + 2.0 * factor_next / spread * residual
        factor = factor_next
    return total.reshape(side, side * side).astype(np.float32)


def split_pair(value):
    high = value.astype(jnp.bfloat16)
    low = (value - high.astype(jnp.float32)).astype(jnp.bfloat16)
    return high, low


def dot(left, right):
    return jnp.dot(left, right, preferred_element_type=jnp.float32)


def partner_of(index, step, count):
    if count & (count - 1) == 0:
        return index ^ step, index ^ step
    return (index + step) % count, (index + count - step) % count


def pair_geometry(sizes, match_ref, centers_ref, index):
    _, rounds, own_count, slab_count, _ = sizes
    slab_index = lax.axis_index("slab")
    pair_index = lax.axis_index("pair")

    def orbital_of(member):
        return (member // own_count * slab_count + slab_index) * own_count + member % own_count

    member = pair_index * own_count + index // rounds
    mate = match_ref[0, index % rounds, member]
    own_offset = []
    mate_offset = []
    distance = 0
    for axis in range(3):
        mine = centers_ref[axis, orbital_of(member)]
        other = centers_ref[axis, orbital_of(mate)]
        anchor = (mine + other) >> 1
        own_offset.append(mine - anchor)
        mate_offset.append(other - anchor)
        distance = distance + (mine - other) * (mine - other)
    return member, mate, own_offset, mate_offset, distance <= CUT2


def box_shape(sizes):
    side = sizes[0]
    return side * side // LANES, LANES // side, side + REACH


def clear_edges(sizes, ref, count):
    tiles, _, pitch = box_shape(sizes)
    for index in range(count * tiles + 1):
        ref[index * pitch : index * pitch + REACH, :] = jnp.zeros((REACH, LANES), jnp.float32)


def turned(tiles):
    row = lax.broadcasted_iota(jnp.int32, (8, LANES), 0)
    tiles = list(tiles)
    for distance in (4, 2, 1):
        low = (row & distance) == 0
        for index in range(8):
            if index & distance == 0:
                first, second = tiles[index], tiles[index + distance]
                tiles[index] = jnp.where(low, first, pltpu.roll(second, distance, axis=0))
                tiles[index + distance] = jnp.where(low, pltpu.roll(first, 8 - distance, axis=0), second)
    return tiles


def spread(sizes, boxes_ref, fields, pair):
    side, _, own_count, slab_count, _ = sizes
    planes = side // slab_count
    tiles, _, pitch = box_shape(sizes)
    for group in range(side // 8):
        halves = {}
        for slab in range(8 * group // planes, (8 * group + 7) // planes + 1):
            for chunk in range(own_count * planes // 2):
                block = boxes_ref[slab, 16 * chunk : 16 * chunk + 16, :].astype(jnp.float32)
                for half in range(2):
                    own, plane = divmod(2 * chunk + half, planes)
                    halves[own, slab * planes + plane] = block[8 * half : 8 * half + 8, :]
        for own in range(own_count):
            rows = turned([halves[own, 8 * group + index] for index in range(8)])
            for tile in range(tiles):
                start = ((pair * own_count + own) * tiles + tile) * pitch + REACH + 8 * group
                fields[pl.ds(pl.multiple_of(start, 8), 8), :] = rows[tile]


def rolled(sizes, ref, box, row, rows, offset_x, offset_flat):
    tiles, _, pitch = box_shape(sizes)
    whole = (offset_flat >> 7) & (tiles - 1)
    part = offset_flat & (LANES - 1)
    start = box * tiles * pitch + REACH + row - offset_x
    moved = []
    for tile in range(tiles):
        first_row = start + ((tile - whole) & (tiles - 1)) * pitch
        moved.append(pltpu.roll(ref[pl.ds(first_row, rows), :], part, axis=1))
    keep = lax.broadcasted_iota(jnp.int32, (rows, LANES), 1) >= part
    return [jnp.where(keep, moved[t], moved[(t - 1) % tiles]) for t in range(tiles)]


def place_partner(sizes, fields, box, own_offset, offset, active):
    side = sizes[0]
    tiles, lines, _ = box_shape(sizes)
    placed = rolled(sizes, fields, box, 0, side, offset[0], offset[1] * side + offset[2])
    lane = lax.broadcasted_iota(jnp.int32, (1, LANES), 1)
    lows = [jnp.maximum(jnp.maximum(a, b), 0) for a, b in zip(own_offset, offset)]
    highs = [side + jnp.minimum(jnp.minimum(a, b), 0) for a, b in zip(own_offset, offset)]
    point_ok = (lane % side >= lows[2]) & (lane % side < highs[2]) & active
    result = []
    for tile in range(tiles):
        line = lane // side + tile * lines
        ok = jnp.where(point_ok & (line >= lows[1]) & (line < highs[1]), 1.0, 0.0)
        result.append(placed[tile] * ok)
    return result


def make_matrices(basis_ref, line_ref, first_line, high_ref, low_ref):
    side = basis_ref.shape[0]
    count = side // 2
    for parity in range(2):
        for index in range(count):
            line = first_line + parity * count + index
            rows = slice(index * side, (index + 1) * side)
            value = basis_ref[...] * line_ref[line : line + 1, :]
            high_ref[parity, rows, :], low_ref[parity, rows, :] = split_pair(value)


def make_mix(basis_ref, mix_ref):
    side = basis_ref.shape[0]
    width = mix_ref.shape[0]
    block = lax.broadcasted_iota(jnp.int32, (side, width), 1) // side
    for index in range(width // side):
        rows = slice(index * side, (index + 1) * side)
        high, low = split_pair(jnp.where(block == index, basis_ref[:, :width], 0.0))
        for part, piece in enumerate((high, high, low)):
            mix_ref[rows, part * width : (part + 1) * width] = piece


def own_kernel(sizes, match_hbm, centers_hbm, boxes_ref, *refs):
    basis_ref, line_ref, gain_hbm, *refs = refs
    mine_ref, table_ref, mix_ref, gain_ref, there_high, there_low, back_high, back_low = refs[:8]
    match_ref, centers_ref, fields, sems = refs[8:]
    side, rounds, own_count, _, _ = sizes
    tiles, _, _ = box_shape(sizes)
    first_member = lax.axis_index("pair") * own_count
    sources = (gain_hbm, match_hbm, centers_hbm)
    targets = (gain_ref, match_ref, centers_ref)
    copies = [pltpu.make_async_copy(s, t, sems.at[i]) for i, (s, t) in enumerate(zip(sources, targets))]
    for copy in copies:
        copy.start()
    clear_edges(sizes, fields, own_count)
    make_mix(basis_ref, mix_ref)
    make_matrices(basis_ref, line_ref, 0, there_high, there_low)
    make_matrices(basis_ref, line_ref, side, back_high, back_low)
    for copy in copies:
        copy.wait()
    spread(sizes, boxes_ref, fields, 0)

    def place(index, carry):
        member, mate, a, b, active = pair_geometry(sizes, match_ref, centers_ref, index)
        for place, entry in enumerate((mate, *a, *b, jnp.where(active, 1, 0))):
            table_ref[index * ENTRIES + place] = entry
        rows = pl.ds(pl.multiple_of(index * side, side), side)
        placed = rolled(sizes, fields, member - first_member, 0, side, a[0], a[1] * side + a[2])
        for tile in range(tiles):
            mine_ref[rows, tile * LANES : (tile + 1) * LANES] = placed[tile].astype(jnp.bfloat16)
        return carry

    lax.fori_loop(0, own_count * rounds, place, 0)


def force_kernel(sizes, mine, table_hbm, *refs):
    side, rounds, own_count, slab_count, pair_count = sizes
    piece_refs, refs = refs[:pair_count], refs[pair_count:]
    constants, refs = refs[:6], refs[6:]
    mix_ref, gain_ref, there_high, there_low, back_high, back_low = constants
    out_refs, refs = refs[:slab_count], refs[slab_count:]
    table_ref, partner, *refs = refs
    fields, first, second, *terms, all_codes, sems = refs
    planes = side // slab_count
    tiles, lines, pitch = box_shape(sizes)
    solves = own_count * rounds
    group = min(solves, 8)
    group_rows = group * side
    cells = tiles * LANES
    slab_index = lax.axis_index("slab")
    pair_index = lax.axis_index("pair")
    core = pair_index % CORES
    chip = pair_index // CORES
    chips = pair_count // CORES

    places = [
        (chip + chips - step) % chips * CORES + (core + core_step) % CORES
        for core_step in range(CORES)
        for step in range(chips)
    ]
    table_copy = pltpu.make_async_copy(table_hbm, table_ref, sems.at[0])
    table_copy.start()
    clear_edges(sizes, fields, pair_count * own_count)
    for ref in terms:
        clear_edges(sizes, ref, group)
    for piece_ref, pair in zip(piece_refs, places):
        spread(sizes, piece_ref, fields, pair)
    table_copy.wait()

    row_count = solves * side
    half_tiles = tiles // 2
    half_cells = cells // 2

    def mirrored(tile):
        line = lax.broadcasted_iota(jnp.int32, tile.shape, 1) // side
        result = None
        for index in range(lines):
            amount = (2 * index - lines + 1) * side % LANES
            if index < 2:
                moved = pltpu.roll(tile, amount, axis=1)
                result = moved if result is None else jnp.where(line % 2 == index, moved, result)
        return result

    def store_split(ref, start, count, columns, value):
        high, low = split_pair(value)
        ref[start : start + count, columns] = high
        ref[row_count + start : row_count + start + count, columns] = low

    def densities(index):
        start = index * side
        rows = slice(start, start + side)
        mate, *offsets, active = [table_ref[index * ENTRIES + place] for place in range(ENTRIES)]
        placed = place_partner(sizes, fields, mate, offsets[:3], offsets[3:], active == 1)
        density = []
        for tile in range(tiles):
            columns = slice(tile * LANES, (tile + 1) * LANES)
            partner[rows, columns] = placed[tile].astype(jnp.bfloat16)
            density.append(mine[rows, columns].astype(jnp.float32) * placed[tile])
        for tile in range(half_tiles):
            far = mirrored(density[tiles - 1 - tile])
            for parity, value in enumerate((density[tile] + far, density[tile] - far)):
                column = parity * half_cells + tile * LANES
                store_split(first, start, side, slice(column, column + LANES), value)

    def along_x(start, columns, source):
        high = source[start : start + group_rows, columns]
        low = source[row_count + start : row_count + start + group_rows, columns]
        return dot(mix_ref[...], jnp.concatenate([high, low, high], axis=0))

    def in_plane(start, parity, source, high_ref, low_ref):
        inner = slice(parity * half_cells, (parity + 1) * half_cells)
        high = source[start : start + group_rows, inner]
        low = source[row_count + start : row_count + start + group_rows, inner]
        basis = high_ref[parity]
        left = jnp.concatenate([high, low, high], axis=1)
        return dot(left, jnp.concatenate([basis, basis, low_ref[parity]], axis=0))

    def solve_group(start):
        for index in range(start // side, (start + group_rows) // side):
            densities(index)
        columns = slice(0, cells)
        store_split(second, start, group_rows, columns, along_x(start, columns, first))
        for parity in range(2):
            columns = slice(parity * half_cells, (parity + 1) * half_cells)
            value = in_plane(start, parity, second, there_high, there_low)
            value = value.reshape(group, side, half_cells) * gain_ref[:, columns][None]
            store_split(first, start, group_rows, columns, value.reshape(group_rows, half_cells))
        for parity in range(2):
            columns = slice(parity * half_cells, (parity + 1) * half_cells)
            store_split(second, start, group_rows, columns, in_plane(start, parity, first, back_high, back_low))
        even = along_x(start, slice(0, half_cells), second)
        odd = along_x(start, slice(half_cells, cells), second)
        for tile in range(half_tiles):
            lanes = slice(tile * LANES, (tile + 1) * LANES)
            near = even[:, lanes] + odd[:, lanes]
            far = mirrored(even[:, lanes] - odd[:, lanes])
            for place, value in ((tile, near), (tiles - 1 - tile, far)):
                columns = slice(place * LANES, (place + 1) * LANES)
                value = value * partner[start : start + group_rows, columns].astype(jnp.float32)
                for solve in range(group):
                    row = (solve * tiles + place) * pitch + REACH
                    terms[start // group_rows][row : row + side, :] = value[solve * side : (solve + 1) * side, :]

    step_rows = 16

    def collect(own, row):
        sums = None
        for turn in range(rounds):
            index = own * rounds + turn
            a = [table_ref[index * ENTRIES + 1 + axis] for axis in range(3)]
            ref = terms[index // group]
            term = rolled(sizes, ref, index % group, row, step_rows, -a[0], -(a[1] * side + a[2]))
            sums = term if sums is None else [s + t for s, t in zip(sums, term)]
        return sums

    lane_index = lax.broadcasted_iota(jnp.int32, (tiles, LANES), 1)
    exponents = [jnp.zeros((tiles, LANES), jnp.float32)] * slab_count
    factors = [jnp.zeros((tiles, LANES), jnp.float32)] * slab_count
    codes = {}
    for own in range(own_count):
        if own * rounds % group == 0:
            solve_group(own * rounds * side)
        for row in range(0, side, step_rows):
            sums = collect(own, row)
            for half in range(0, step_rows, 8):
                for index, value in enumerate(turned([tile[half : half + 8, :] for tile in sums])):
                    slab, plane = divmod(row + half + index, planes)
                    chunk = own * planes + plane
                    codes[slab, chunk], exponent, factor = encode(value)
                    exponents[slab] = jnp.where(lane_index == chunk, exponent, exponents[slab])
                    factors[slab] = jnp.where(lane_index == chunk, factor, factors[slab])
                    if chunk % 2:
                        pair = jnp.concatenate([codes[slab, chunk - 1], codes[slab, chunk]], axis=0)
                        all_codes[slab, tiles * (chunk - 1) : tiles * (chunk + 1), :] = whole_codes(pair)
    for slab in range(slab_count):
        header = jnp.concatenate([exponents[slab], factors[slab]], axis=0)
        all_codes[slab, tiles * own_count * planes :, :] = whole_codes(header)
    for step in range(slab_count):
        out_refs[step][...] = all_codes[partner_of(slab_index, step, slab_count)[0]]


def whole_codes(value):
    return value.astype(jnp.int32).astype(jnp.int16)


def encode(value):
    largest = jnp.max(jnp.abs(value), axis=1, keepdims=True)
    exponent = jnp.maximum(jnp.floor(jnp.log2(jnp.maximum(largest, TINY))), LOWEST_EXPONENT)
    lifted = 1.0 / jnp.exp2(exponent)
    factor = jnp.maximum(jnp.ceil(largest * lifted * FACTOR_UNIT), 1.0)
    code = jnp.floor(value * lifted * (CODE_LIMIT * FACTOR_UNIT / factor) + 0.5)
    return jnp.clip(code, -CODE_LIMIT, CODE_LIMIT), exponent, factor


def swap_cores(block, pair_count):
    return lax.ppermute(block, "pair", [(i, i ^ 1) for i in range(pair_count)])


def gather_chips(boxes, pair_count):
    pieces = []
    for step in range(1, pair_count // CORES):
        perm = [(i, (i + step * CORES) % pair_count) for i in range(pair_count)]
        pieces.append(lax.ppermute(boxes, "pair", perm))
    return pieces


def unpack_kernel(sizes, *refs):
    own_count, slab_count, tiles = sizes
    block_refs, out_hbm, out_ref, out_sems = refs[:slab_count], *refs[slab_count:]
    slab_index = lax.axis_index("slab")
    band_slabs = 8 // own_count
    assert slab_count & (slab_count - 1) == 0 and band_slabs * own_count == 8
    row = lax.broadcasted_iota(jnp.int32, (8, LANES), 0)

    def ordered(value):
        distance = own_count
        while distance < 8:
            near = pltpu.roll(value, 8 - distance, axis=0)
            far = pltpu.roll(value, distance, axis=0)
            swapped = jnp.where((row & distance) == 0, near, far)
            value = jnp.where(slab_index // (distance // own_count) % 2 == 1, swapped, value)
            distance *= 2
        return value

    row_count = own_count * tiles
    copies = []
    for band in range(slab_count // band_slabs):
        values = {}
        for part in range(band_slabs):
            block_ref = block_refs[slab_count - 1 - band * band_slabs - part]
            header = block_ref[row_count:, :].astype(jnp.int32).astype(jnp.float32)
            units = jnp.exp2(header[:8, :])
            factors = header[8:, :] * (1.0 / (CODE_LIMIT * FACTOR_UNIT))
            for pair in range(row_count // 16):
                codes = block_ref[16 * pair : 16 * pair + 16, :].astype(jnp.int32).astype(jnp.float32)
                for half in range(2):
                    chunk = 2 * pair + half
                    own, plane = divmod(8 * chunk, tiles)
                    value = codes[8 * half : 8 * half + 8, :] * factors[:, chunk : chunk + 1]
                    values[part * own_count + own, plane // 8] = value * units[:, chunk : chunk + 1]
        for plane in range(tiles // 8):
            rows = turned([values[index, plane] for index in range(8)])
            for tile in range(8):
                start = (band * tiles + 8 * plane + tile) * 8
                out_ref[start : start + 8, :] = ordered(rows[tile])
        target = (slab_index // band_slabs ^ band) * (tiles * 8)
        source = out_ref.at[band * tiles * 8 : (band + 1) * tiles * 8]
        target = out_hbm.at[pl.ds(pl.multiple_of(target, 8), tiles * 8)]
        copies.append(pltpu.make_async_copy(source, target, out_sems.at[band]))
        copies[-1].start()
    for copy in copies:
        copy.wait()


def unpack(blocks, own_count, cells):
    slab_count = len(blocks)
    row_count = own_count * slab_count
    tiles = cells // LANES
    out = pl.pallas_call(
        functools.partial(unpack_kernel, (own_count, slab_count, tiles)),
        out_shape=jax.ShapeDtypeStruct((row_count * tiles, LANES), jnp.float32),
        in_specs=[pl.BlockSpec(memory_space=pltpu.VMEM)] * slab_count,
        out_specs=pl.BlockSpec(memory_space=pl.ANY),
        scratch_shapes=[
            pltpu.VMEM((row_count * tiles, LANES), jnp.float32),
            pltpu.SemaphoreType.DMA((row_count // 8,)),
        ],
        compiler_params=pltpu.CompilerParams(vmem_limit_bytes=8 * 1024 * 1024),
    )(*blocks)
    return out.reshape(row_count // 8, tiles, 8, LANES).transpose(0, 2, 1, 3).reshape(row_count, cells)


def kernel_constants(side):
    basis = sine_basis(side)
    halves = [basis[parity::2, : side // 2].T for parity in range(2)]
    lines = np.concatenate(halves + [half.T for half in halves])
    lines = np.repeat(lines, side, axis=1).astype(np.float32)
    tile = np.tile(basis, (1, side // 2)).astype(np.float32)
    gain = chebyshev_gain(side).reshape(side, side, side)
    gain = np.concatenate([gain[:, parity::2].reshape(side, -1) for parity in range(2)], axis=1)
    return [jnp.asarray(constant) for constant in (tile, lines, gain)]


def place_own(sizes, match, centers, boxes):
    side, rounds, own_count, slab_count, _ = sizes
    tiles, _, pitch = box_shape(sizes)
    solves = own_count * rounds
    constants = kernel_constants(side)
    group_rows = min(solves, 8) * side
    half_cells = side * side // 2
    matrix = jax.ShapeDtypeStruct((2, half_cells, half_cells), jnp.bfloat16)
    inputs = [match, centers, boxes, *constants]
    either = pl.BlockSpec(memory_space=pl.ANY)
    vectors = pl.BlockSpec(memory_space=pltpu.VMEM)
    return pl.pallas_call(
        functools.partial(own_kernel, sizes),
        out_shape=[
            jax.ShapeDtypeStruct((solves * side, side * side), jnp.bfloat16),
            jax.ShapeDtypeStruct((solves * ENTRIES,), jnp.int32),
            jax.ShapeDtypeStruct((group_rows, 3 * group_rows), jnp.bfloat16),
            jax.ShapeDtypeStruct(constants[2].shape, jnp.float32),
            *[matrix] * 4,
        ],
        in_specs=[either] * 2 + [vectors] * 3 + [either],
        out_specs=[vectors, pl.BlockSpec(memory_space=pltpu.SMEM)] + [vectors] * 6,
        scratch_shapes=[
            pltpu.SMEM(match.shape, jnp.int32),
            pltpu.SMEM(centers.shape, jnp.int32),
            pltpu.VMEM((own_count * tiles * pitch + REACH, LANES), jnp.float32),
            pltpu.SemaphoreType.DMA((len(inputs),)),
        ],
        compiler_params=pltpu.CompilerParams(vmem_limit_bytes=32 * 1024 * 1024),
        cost_estimate=pl.CostEstimate(flops=5 * 10**9, bytes_accessed=4 * 1024 * 1024, transcendentals=0),
    )(*inputs)


def team_forces(sizes, mine, table, constants, pieces):
    side, rounds, own_count, slab_count, pair_count = sizes
    tiles, _, pitch = box_shape(sizes)
    _, rows, _ = pieces[0].shape
    solves = own_count * rounds
    group = min(solves, 8)
    cells = side * side
    either = pl.BlockSpec(memory_space=pl.ANY)
    vectors = pl.BlockSpec(memory_space=pltpu.VMEM)
    wide = pltpu.VMEM((2 * solves * side, cells), jnp.bfloat16)
    flops = 2 * solves * side * 3 * 2 * (cells * cells // 2 + cells * group * side)
    inputs = [mine, table, *pieces, *constants]
    return pl.pallas_call(
        functools.partial(force_kernel, sizes),
        out_shape=[jax.ShapeDtypeStruct((rows + HEADER_ROWS, LANES), jnp.int16)] * slab_count,
        in_specs=[vectors, either] + [vectors] * (len(pieces) + len(constants)),
        out_specs=[vectors] * slab_count,
        scratch_shapes=[
            pltpu.SMEM(table.shape, jnp.int32),
            pltpu.VMEM(mine.shape, jnp.bfloat16),
            pltpu.VMEM((own_count * pair_count * tiles * pitch + REACH, LANES), jnp.float32),
            wide,
            wide,
            *[pltpu.VMEM((group * tiles * pitch + REACH, LANES), jnp.float32)] * (solves // group),
            pltpu.VMEM((slab_count, rows + HEADER_ROWS, LANES), jnp.int16),
            pltpu.SemaphoreType.DMA((1,)),
        ],
        compiler_params=pltpu.CompilerParams(vmem_limit_bytes=32 * 1024 * 1024),
        cost_estimate=pl.CostEstimate(flops=flops, bytes_accessed=8 * 1024 * 1024, transcendentals=0),
    )(*inputs)


def shards(orbitals, centers, matchings):
    slab_count = lax.axis_size("slab")
    pair_count = lax.axis_size("pair")
    local_rows, plane_cells = orbitals.shape
    own_count = local_rows // slab_count
    side = round((plane_cells * slab_count) ** (1.0 / 3.0))
    blocks = orbitals.reshape(slab_count, own_count * plane_cells // LANES, LANES)
    boxes = lax.all_to_all(blocks, "slab", split_axis=0, concat_axis=0, tiled=True)
    sizes = (side, matchings.shape[1], own_count, slab_count, pair_count)
    pieces = gather_chips(boxes, pair_count)
    mine, table, *constants = place_own(sizes, matchings, centers.T, boxes)
    boxes, mine = lax.optimization_barrier((boxes, mine))
    swapped = [swap_cores(boxes, pair_count)]
    pieces, mine = lax.optimization_barrier((pieces, mine))
    swapped += [swap_cores(piece, pair_count) for piece in pieces]
    codes = team_forces(sizes, mine, table, constants, [boxes] + pieces + swapped)
    received = []
    for step in reversed(range(1, slab_count)):
        perm = [(i, partner_of(i, step, slab_count)[0]) for i in range(slab_count)]
        received.append(lax.ppermute(codes[step], "slab", perm))
    return unpack(received + [codes[0]], own_count, plane_cells)


def solution(mesh):
    in_specs = (P("pair", "slab"), P(), P("slab", None, None))
    out_specs = P("pair", "slab")
    return jax.shard_map(shards, mesh=mesh, in_specs=in_specs, out_specs=out_specs, check_vma=False)
```

```python
import functools

import jax
import jax.numpy as jnp
import numpy as np
from jax import lax
from jax.experimental import pallas as pl
from jax.experimental.pallas import tpu as pltpu
from jax.sharding import PartitionSpec as P

STEPS = 16
CUT2 = 192
REACH = 8
SCREEN = 0.1
LOWER_BOUND = 0.1
UPPER_BOUND = 12.1
LANES = 128
CORES = 2
CODE_LIMIT = 32767.0
FACTOR_UNIT = 8192.0
LOWEST_EXPONENT = -120.0
TINY = 1e-37
HEADER_ROWS = 16
ENTRIES = 8


def sine_basis(side):
    index = np.arange(1, side + 1, dtype=np.float64)
    return np.sqrt(2.0 / (side + 1)) * np.sin(np.pi * np.outer(index, index) / (side + 1))


def chebyshev_gain(side):
    shifts = -2.0 * np.cos(np.pi * np.arange(1, side + 1, dtype=np.float64) / (side + 1))
    eigenvalue = 6.0 + SCREEN + shifts[:, None, None] + shifts[None, :, None] + shifts[None, None, :]
    middle = (UPPER_BOUND + LOWER_BOUND) / 2.0
    spread = (UPPER_BOUND - LOWER_BOUND) / 2.0
    ratio = middle / spread
    total = np.zeros_like(eigenvalue)
    residual = np.ones_like(eigenvalue)
    direction = residual / middle
    factor = 1.0 / ratio
    for _ in range(STEPS):
        total = total + direction
        residual = residual - eigenvalue * direction
        factor_next = 1.0 / (2.0 * ratio - factor)
        direction = factor_next * factor * direction + 2.0 * factor_next / spread * residual
        factor = factor_next
    return total.reshape(side, side * side).astype(np.float32)


def split_pair(value):
    high = value.astype(jnp.bfloat16)
    low = (value - high.astype(jnp.float32)).astype(jnp.bfloat16)
    return high, low


def dot(left, right):
    return jnp.dot(left, right, preferred_element_type=jnp.float32)


def partner_of(index, step, count):
    if count & (count - 1) == 0:
        return index ^ step, index ^ step
    return (index + step) % count, (index + count - step) % count


def pair_geometry(sizes, match_ref, centers_ref, index):
    _, rounds, own_count, slab_count, _ = sizes
    slab_index = lax.axis_index("slab")
    pair_index = lax.axis_index("pair")

    def orbital_of(member):
        return (member // own_count * slab_count + slab_index) * own_count + member % own_count

    member = pair_index * own_count + index // rounds
    mate = match_ref[0, index % rounds, member]
    own_offset = []
    mate_offset = []
    distance = 0
    for axis in range(3):
        mine = centers_ref[axis, orbital_of(member)]
        other = centers_ref[axis, orbital_of(mate)]
        anchor = (mine + other) >> 1
        own_offset.append(mine - anchor)
        mate_offset.append(other - anchor)
        distance = distance + (mine - other) * (mine - other)
    return member, mate, own_offset, mate_offset, distance <= CUT2


def box_shape(sizes):
    side = sizes[0]
    return side * side // LANES, LANES // side, side + REACH


def clear_edges(sizes, ref, count):
    tiles, _, pitch = box_shape(sizes)
    for index in range(count * tiles + 1):
        ref[index * pitch : index * pitch + REACH, :] = jnp.zeros((REACH, LANES), jnp.float32)


def turned(tiles):
    row = lax.broadcasted_iota(jnp.int32, (8, LANES), 0)
    tiles = list(tiles)
    for distance in (4, 2, 1):
        low = (row & distance) == 0
        for index in range(8):
            if index & distance == 0:
                first, second = tiles[index], tiles[index + distance]
                tiles[index] = jnp.where(low, first, pltpu.roll(second, distance, axis=0))
                tiles[index + distance] = jnp.where(low, pltpu.roll(first, 8 - distance, axis=0), second)
    return tiles


def spread(sizes, boxes_ref, fields, pair):
    side, _, own_count, slab_count, _ = sizes
    planes = side // slab_count
    tiles, _, pitch = box_shape(sizes)
    for group in range(side // 8):
        halves = {}
        for slab in range(8 * group // planes, (8 * group + 7) // planes + 1):
            for chunk in range(own_count * planes // 2):
                block = boxes_ref[slab, 16 * chunk : 16 * chunk + 16, :].astype(jnp.float32)
                for half in range(2):
                    own, plane = divmod(2 * chunk + half, planes)
                    halves[own, slab * planes + plane] = block[8 * half : 8 * half + 8, :]
        for own in range(own_count):
            rows = turned([halves[own, 8 * group + index] for index in range(8)])
            for tile in range(tiles):
                start = ((pair * own_count + own) * tiles + tile) * pitch + REACH + 8 * group
                fields[pl.ds(pl.multiple_of(start, 8), 8), :] = rows[tile]


def rolled(sizes, ref, box, row, rows, offset_x, offset_flat):
    tiles, _, pitch = box_shape(sizes)
    whole = (offset_flat >> 7) & (tiles - 1)
    part = offset_flat & (LANES - 1)
    start = box * tiles * pitch + REACH + row - offset_x
    moved = []
    for tile in range(tiles):
        first_row = start + ((tile - whole) & (tiles - 1)) * pitch
        moved.append(pltpu.roll(ref[pl.ds(first_row, rows), :], part, axis=1))
    keep = lax.broadcasted_iota(jnp.int32, (rows, LANES), 1) >= part
    return [jnp.where(keep, moved[t], moved[(t - 1) % tiles]) for t in range(tiles)]


def place_partner(sizes, fields, box, own_offset, offset, active):
    side = sizes[0]
    tiles, lines, _ = box_shape(sizes)
    placed = rolled(sizes, fields, box, 0, side, offset[0], offset[1] * side + offset[2])
    lane = lax.broadcasted_iota(jnp.int32, (1, LANES), 1)
    lows = [jnp.maximum(jnp.maximum(a, b), 0) for a, b in zip(own_offset, offset)]
    highs = [side + jnp.minimum(jnp.minimum(a, b), 0) for a, b in zip(own_offset, offset)]
    point_ok = (lane % side >= lows[2]) & (lane % side < highs[2]) & active
    result = []
    for tile in range(tiles):
        line = lane // side + tile * lines
        ok = jnp.where(point_ok & (line >= lows[1]) & (line < highs[1]), 1.0, 0.0)
        result.append(placed[tile] * ok)
    return result


def make_matrices(basis_ref, line_ref, first_line, high_ref, low_ref):
    side = basis_ref.shape[0]
    count = side // 2
    for parity in range(2):
        for index in range(count):
            line = first_line + parity * count + index
            rows = slice(index * side, (index + 1) * side)
            value = basis_ref[...] * line_ref[line : line + 1, :]
            high_ref[parity, rows, :], low_ref[parity, rows, :] = split_pair(value)


def make_mix(basis_ref, mix_ref):
    side = basis_ref.shape[0]
    width = mix_ref.shape[0]
    block = lax.broadcasted_iota(jnp.int32, (side, width), 1) // side
    for index in range(width // side):
        rows = slice(index * side, (index + 1) * side)
        high, low = split_pair(jnp.where(block == index, basis_ref[:, :width], 0.0))
        for part, piece in enumerate((high, high, low)):
            mix_ref[rows, part * width : (part + 1) * width] = piece


def own_kernel(sizes, match_hbm, centers_hbm, boxes_ref, *refs):
    basis_ref, line_ref, gain_hbm, *refs = refs
    mine_ref, table_ref, mix_ref, gain_ref, there_high, there_low, back_high, back_low = refs[:8]
    match_ref, centers_ref, fields, sems = refs[8:]
    side, rounds, own_count, _, _ = sizes
    tiles, _, _ = box_shape(sizes)
    first_member = lax.axis_index("pair") * own_count
    sources = (gain_hbm, match_hbm, centers_hbm)
    targets = (gain_ref, match_ref, centers_ref)
    copies = [pltpu.make_async_copy(s, t, sems.at[i]) for i, (s, t) in enumerate(zip(sources, targets))]
    for copy in copies:
        copy.start()
    clear_edges(sizes, fields, own_count)
    make_mix(basis_ref, mix_ref)
    make_matrices(basis_ref, line_ref, 0, there_high, there_low)
    make_matrices(basis_ref, line_ref, side, back_high, back_low)
    for copy in copies:
        copy.wait()
    spread(sizes, boxes_ref, fields, 0)

    def place(index, carry):
        member, mate, a, b, active = pair_geometry(sizes, match_ref, centers_ref, index)
        for place, entry in enumerate((mate, *a, *b, jnp.where(active, 1, 0))):
            table_ref[index * ENTRIES + place] = entry
        rows = pl.ds(pl.multiple_of(index * side, side), side)
        placed = rolled(sizes, fields, member - first_member, 0, side, a[0], a[1] * side + a[2])
        for tile in range(tiles):
            mine_ref[rows, tile * LANES : (tile + 1) * LANES] = placed[tile].astype(jnp.bfloat16)
        return carry

    lax.fori_loop(0, own_count * rounds, place, 0)


def force_kernel(sizes, mine, table_hbm, *refs):
    side, rounds, own_count, slab_count, pair_count = sizes
    piece_refs, refs = refs[:pair_count], refs[pair_count:]
    constants, refs = refs[:6], refs[6:]
    mix_ref, gain_ref, there_high, there_low, back_high, back_low = constants
    out_refs, refs = refs[:slab_count], refs[slab_count:]
    table_ref, partner, *refs = refs
    fields, first, second, *terms, all_codes, sems = refs
    planes = side // slab_count
    tiles, lines, pitch = box_shape(sizes)
    solves = own_count * rounds
    group = min(solves, 8)
    group_rows = group * side
    cells = tiles * LANES
    slab_index = lax.axis_index("slab")
    pair_index = lax.axis_index("pair")
    core = pair_index % CORES
    chip = pair_index // CORES
    chips = pair_count // CORES

    places = [
        (chip + chips - step) % chips * CORES + (core + core_step) % CORES
        for core_step in range(CORES)
        for step in range(chips)
    ]
    table_copy = pltpu.make_async_copy(table_hbm, table_ref, sems.at[0])
    table_copy.start()
    clear_edges(sizes, fields, pair_count * own_count)
    for ref in terms:
        clear_edges(sizes, ref, group)
    for piece_ref, pair in zip(piece_refs, places):
        spread(sizes, piece_ref, fields, pair)
    table_copy.wait()

    row_count = solves * side
    half_tiles = tiles // 2
    half_cells = cells // 2

    def mirrored(tile):
        line = lax.broadcasted_iota(jnp.int32, tile.shape, 1) // side
        result = None
        for index in range(lines):
            amount = (2 * index - lines + 1) * side % LANES
            if index < 2:
                moved = pltpu.roll(tile, amount, axis=1)
                result = moved if result is None else jnp.where(line % 2 == index, moved, result)
        return result

    def store_split(ref, start, count, columns, value):
        high, low = split_pair(value)
        ref[start : start + count, columns] = high
        ref[row_count + start : row_count + start + count, columns] = low

    def densities(index):
        start = index * side
        rows = slice(start, start + side)
        mate, *offsets, active = [table_ref[index * ENTRIES + place] for place in range(ENTRIES)]
        placed = place_partner(sizes, fields, mate, offsets[:3], offsets[3:], active == 1)
        density = []
        for tile in range(tiles):
            columns = slice(tile * LANES, (tile + 1) * LANES)
            partner[rows, columns] = placed[tile].astype(jnp.bfloat16)
            density.append(mine[rows, columns].astype(jnp.float32) * placed[tile])
        for tile in range(half_tiles):
            far = mirrored(density[tiles - 1 - tile])
            for parity, value in enumerate((density[tile] + far, density[tile] - far)):
                column = parity * half_cells + tile * LANES
                store_split(first, start, side, slice(column, column + LANES), value)

    def along_x(start, columns, source):
        high = source[start : start + group_rows, columns]
        low = source[row_count + start : row_count + start + group_rows, columns]
        return dot(mix_ref[...], jnp.concatenate([high, low, high], axis=0))

    def in_plane(start, parity, source, high_ref, low_ref):
        inner = slice(parity * half_cells, (parity + 1) * half_cells)
        high = source[start : start + group_rows, inner]
        low = source[row_count + start : row_count + start + group_rows, inner]
        basis = high_ref[parity]
        left = jnp.concatenate([high, low, high], axis=1)
        return dot(left, jnp.concatenate([basis, basis, low_ref[parity]], axis=0))

    def solve_group(start):
        for index in range(start // side, (start + group_rows) // side):
            densities(index)
        columns = slice(0, cells)
        store_split(second, start, group_rows, columns, along_x(start, columns, first))
        for parity in range(2):
            columns = slice(parity * half_cells, (parity + 1) * half_cells)
            value = in_plane(start, parity, second, there_high, there_low)
            value = value.reshape(group, side, half_cells) * gain_ref[:, columns][None]
            store_split(first, start, group_rows, columns, value.reshape(group_rows, half_cells))
        for parity in range(2):
            columns = slice(parity * half_cells, (parity + 1) * half_cells)
            store_split(second, start, group_rows, columns, in_plane(start, parity, first, back_high, back_low))
        even = along_x(start, slice(0, half_cells), second)
        odd = along_x(start, slice(half_cells, cells), second)
        for tile in range(half_tiles):
            lanes = slice(tile * LANES, (tile + 1) * LANES)
            near = even[:, lanes] + odd[:, lanes]
            far = mirrored(even[:, lanes] - odd[:, lanes])
            for place, value in ((tile, near), (tiles - 1 - tile, far)):
                columns = slice(place * LANES, (place + 1) * LANES)
                value = value * partner[start : start + group_rows, columns].astype(jnp.float32)
                for solve in range(group):
                    row = (solve * tiles + place) * pitch + REACH
                    terms[start // group_rows][row : row + side, :] = value[solve * side : (solve + 1) * side, :]

    step_rows = 16

    def collect(own, row):
        sums = None
        for turn in range(rounds):
            index = own * rounds + turn
            a = [table_ref[index * ENTRIES + 1 + axis] for axis in range(3)]
            ref = terms[index // group]
            term = rolled(sizes, ref, index % group, row, step_rows, -a[0], -(a[1] * side + a[2]))
            sums = term if sums is None else [s + t for s, t in zip(sums, term)]
        return sums

    lane_index = lax.broadcasted_iota(jnp.int32, (tiles, LANES), 1)
    exponents = [jnp.zeros((tiles, LANES), jnp.float32)] * slab_count
    factors = [jnp.zeros((tiles, LANES), jnp.float32)] * slab_count
    codes = {}
    for own in range(own_count):
        if own * rounds % group == 0:
            solve_group(own * rounds * side)
        for row in range(0, side, step_rows):
            sums = collect(own, row)
            for half in range(0, step_rows, 8):
                for index, value in enumerate(turned([tile[half : half + 8, :] for tile in sums])):
                    slab, plane = divmod(row + half + index, planes)
                    chunk = own * planes + plane
                    codes[slab, chunk], exponent, factor = encode(value)
                    exponents[slab] = jnp.where(lane_index == chunk, exponent, exponents[slab])
                    factors[slab] = jnp.where(lane_index == chunk, factor, factors[slab])
                    if chunk % 2:
                        pair = jnp.concatenate([codes[slab, chunk - 1], codes[slab, chunk]], axis=0)
                        all_codes[slab, tiles * (chunk - 1) : tiles * (chunk + 1), :] = whole_codes(pair)
    for slab in range(slab_count):
        header = jnp.concatenate([exponents[slab], factors[slab]], axis=0)
        all_codes[slab, tiles * own_count * planes :, :] = whole_codes(header)
    for step in range(slab_count):
        out_refs[step][...] = all_codes[partner_of(slab_index, step, slab_count)[0]]


def whole_codes(value):
    return value.astype(jnp.int32).astype(jnp.int16)


def encode(value):
    largest = jnp.max(jnp.abs(value), axis=1, keepdims=True)
    exponent = jnp.maximum(jnp.floor(jnp.log2(jnp.maximum(largest, TINY))), LOWEST_EXPONENT)
    lifted = 1.0 / jnp.exp2(exponent)
    factor = jnp.maximum(jnp.ceil(largest * lifted * FACTOR_UNIT), 1.0)
    code = jnp.floor(value * lifted * (CODE_LIMIT * FACTOR_UNIT / factor) + 0.5)
    return jnp.clip(code, -CODE_LIMIT, CODE_LIMIT), exponent, factor


def swap_cores(block, pair_count):
    return lax.ppermute(block, "pair", [(i, i ^ 1) for i in range(pair_count)])


def gather_chips(boxes, pair_count):
    pieces = []
    for step in range(1, pair_count // CORES):
        perm = [(i, (i + step * CORES) % pair_count) for i in range(pair_count)]
        pieces.append(lax.ppermute(boxes, "pair", perm))
    return pieces


def unpack_kernel(sizes, *refs):
    own_count, slab_count, tiles = sizes
    block_refs, out_hbm, out_ref, out_sems = refs[:slab_count], *refs[slab_count:]
    slab_index = lax.axis_index("slab")
    band_slabs = 8 // own_count
    assert slab_count & (slab_count - 1) == 0 and band_slabs * own_count == 8
    row = lax.broadcasted_iota(jnp.int32, (8, LANES), 0)

    def ordered(value):
        distance = own_count
        while distance < 8:
            near = pltpu.roll(value, 8 - distance, axis=0)
            far = pltpu.roll(value, distance, axis=0)
            swapped = jnp.where((row & distance) == 0, near, far)
            value = jnp.where(slab_index // (distance // own_count) % 2 == 1, swapped, value)
            distance *= 2
        return value

    row_count = own_count * tiles
    copies = []
    for band in range(slab_count // band_slabs):
        values = {}
        for part in range(band_slabs):
            block_ref = block_refs[band * band_slabs + part]
            header = block_ref[row_count:, :].astype(jnp.int32).astype(jnp.float32)
            units = jnp.exp2(header[:8, :])
            factors = header[8:, :] * (1.0 / (CODE_LIMIT * FACTOR_UNIT))
            for pair in range(row_count // 16):
                codes = block_ref[16 * pair : 16 * pair + 16, :].astype(jnp.int32).astype(jnp.float32)
                for half in range(2):
                    chunk = 2 * pair + half
                    own, plane = divmod(8 * chunk, tiles)
                    value = codes[8 * half : 8 * half + 8, :] * factors[:, chunk : chunk + 1]
                    values[part * own_count + own, plane // 8] = value * units[:, chunk : chunk + 1]
        for plane in range(tiles // 8):
            rows = turned([values[index, plane] for index in range(8)])
            for tile in range(8):
                start = (band * tiles + 8 * plane + tile) * 8
                out_ref[start : start + 8, :] = ordered(rows[tile])
        target = (slab_index // band_slabs ^ band) * (tiles * 8)
        source = out_ref.at[band * tiles * 8 : (band + 1) * tiles * 8]
        target = out_hbm.at[pl.ds(pl.multiple_of(target, 8), tiles * 8)]
        copies.append(pltpu.make_async_copy(source, target, out_sems.at[band]))
        copies[-1].start()
    for copy in copies:
        copy.wait()


def unpack(blocks, own_count, cells):
    slab_count = len(blocks)
    row_count = own_count * slab_count
    tiles = cells // LANES
    out = pl.pallas_call(
        functools.partial(unpack_kernel, (own_count, slab_count, tiles)),
        out_shape=jax.ShapeDtypeStruct((row_count * tiles, LANES), jnp.float32),
        in_specs=[pl.BlockSpec(memory_space=pltpu.VMEM)] * slab_count,
        out_specs=pl.BlockSpec(memory_space=pl.ANY),
        scratch_shapes=[
            pltpu.VMEM((row_count * tiles, LANES), jnp.float32),
            pltpu.SemaphoreType.DMA((row_count // 8,)),
        ],
        compiler_params=pltpu.CompilerParams(vmem_limit_bytes=8 * 1024 * 1024),
    )(*blocks)
    return out.reshape(row_count // 8, tiles, 8, LANES).transpose(0, 2, 1, 3).reshape(row_count, cells)


def kernel_constants(side):
    basis = sine_basis(side)
    halves = [basis[parity::2, : side // 2].T for parity in range(2)]
    lines = np.concatenate(halves + [half.T for half in halves])
    lines = np.repeat(lines, side, axis=1).astype(np.float32)
    tile = np.tile(basis, (1, side // 2)).astype(np.float32)
    gain = chebyshev_gain(side).reshape(side, side, side)
    gain = np.concatenate([gain[:, parity::2].reshape(side, -1) for parity in range(2)], axis=1)
    return [jnp.asarray(constant) for constant in (tile, lines, gain)]


def place_own(sizes, match, centers, boxes):
    side, rounds, own_count, slab_count, _ = sizes
    tiles, _, pitch = box_shape(sizes)
    solves = own_count * rounds
    constants = kernel_constants(side)
    group_rows = min(solves, 8) * side
    half_cells = side * side // 2
    matrix = jax.ShapeDtypeStruct((2, half_cells, half_cells), jnp.bfloat16)
    inputs = [match, centers, boxes, *constants]
    either = pl.BlockSpec(memory_space=pl.ANY)
    vectors = pl.BlockSpec(memory_space=pltpu.VMEM)
    return pl.pallas_call(
        functools.partial(own_kernel, sizes),
        out_shape=[
            jax.ShapeDtypeStruct((solves * side, side * side), jnp.bfloat16),
            jax.ShapeDtypeStruct((solves * ENTRIES,), jnp.int32),
            jax.ShapeDtypeStruct((group_rows, 3 * group_rows), jnp.bfloat16),
            jax.ShapeDtypeStruct(constants[2].shape, jnp.float32),
            *[matrix] * 4,
        ],
        in_specs=[either] * 2 + [vectors] * 3 + [either],
        out_specs=[vectors, pl.BlockSpec(memory_space=pltpu.SMEM)] + [vectors] * 6,
        scratch_shapes=[
            pltpu.SMEM(match.shape, jnp.int32),
            pltpu.SMEM(centers.shape, jnp.int32),
            pltpu.VMEM((own_count * tiles * pitch + REACH, LANES), jnp.float32),
            pltpu.SemaphoreType.DMA((len(inputs),)),
        ],
        compiler_params=pltpu.CompilerParams(vmem_limit_bytes=32 * 1024 * 1024),
        cost_estimate=pl.CostEstimate(flops=5 * 10**9, bytes_accessed=4 * 1024 * 1024, transcendentals=0),
    )(*inputs)


def team_forces(sizes, mine, table, constants, pieces):
    side, rounds, own_count, slab_count, pair_count = sizes
    tiles, _, pitch = box_shape(sizes)
    _, rows, _ = pieces[0].shape
    solves = own_count * rounds
    group = min(solves, 8)
    cells = side * side
    either = pl.BlockSpec(memory_space=pl.ANY)
    vectors = pl.BlockSpec(memory_space=pltpu.VMEM)
    wide = pltpu.VMEM((2 * solves * side, cells), jnp.bfloat16)
    flops = 2 * solves * side * 3 * 2 * (cells * cells // 2 + cells * group * side)
    inputs = [mine, table, *pieces, *constants]
    return pl.pallas_call(
        functools.partial(force_kernel, sizes),
        out_shape=[jax.ShapeDtypeStruct((rows + HEADER_ROWS, LANES), jnp.int16)] * slab_count,
        in_specs=[vectors, either] + [vectors] * (len(pieces) + len(constants)),
        out_specs=[vectors] * slab_count,
        scratch_shapes=[
            pltpu.SMEM(table.shape, jnp.int32),
            pltpu.VMEM(mine.shape, jnp.bfloat16),
            pltpu.VMEM((own_count * pair_count * tiles * pitch + REACH, LANES), jnp.float32),
            wide,
            wide,
            *[pltpu.VMEM((group * tiles * pitch + REACH, LANES), jnp.float32)] * (solves // group),
            pltpu.VMEM((slab_count, rows + HEADER_ROWS, LANES), jnp.int16),
            pltpu.SemaphoreType.DMA((1,)),
        ],
        compiler_params=pltpu.CompilerParams(vmem_limit_bytes=32 * 1024 * 1024),
        cost_estimate=pl.CostEstimate(flops=flops, bytes_accessed=8 * 1024 * 1024, transcendentals=0),
    )(*inputs)


def shards(orbitals, centers, matchings):
    slab_count = lax.axis_size("slab")
    pair_count = lax.axis_size("pair")
    local_rows, plane_cells = orbitals.shape
    own_count = local_rows // slab_count
    side = round((plane_cells * slab_count) ** (1.0 / 3.0))
    blocks = orbitals.reshape(slab_count, own_count * plane_cells // LANES, LANES)
    boxes = lax.all_to_all(blocks, "slab", split_axis=0, concat_axis=0, tiled=True)
    sizes = (side, matchings.shape[1], own_count, slab_count, pair_count)
    pieces = gather_chips(boxes, pair_count)
    mine, table, *constants = place_own(sizes, matchings, centers.T, boxes)
    boxes, mine = lax.optimization_barrier((boxes, mine))
    swapped = [swap_cores(boxes, pair_count)]
    pieces, mine = lax.optimization_barrier((pieces, mine))
    swapped += [swap_cores(piece, pair_count) for piece in pieces]
    codes = team_forces(sizes, mine, table, constants, [boxes] + pieces + swapped)
    received = [codes[0]]
    for step in range(1, slab_count):
        perm = [(i, partner_of(i, step, slab_count)[0]) for i in range(slab_count)]
        received.append(lax.ppermute(codes[step], "slab", perm))
    return unpack(received, own_count, plane_cells)


def solution(mesh):
    in_specs = (P("pair", "slab"), P(), P("slab", None, None))
    out_specs = P("pair", "slab")
    return jax.shard_map(shards, mesh=mesh, in_specs=in_specs, out_specs=out_specs, check_vma=False)
```
